32 devices in a mesh: dp: 8 (over z, y), tensor: 4 (over x, core).
Axes of the slice: x: 2, y: 2, z: 4, core: 2. Of those that a mesh axis runs over, the one named last changes fastest.
Arguments:
- tokens: bfloat16 [24, 1024, 1024], P(None, 'dp', 'tensor'), may hold values from -6 to 6
- cotangent: bfloat16 [24, 1024, 1024], P(None, 'dp', 'tensor'), may hold values from -6 to 6
- lengths: int32 [24], replicated, may hold values from 512 to 1024, as said below
- packing: int32 [24], replicated, may hold values from 0 to 23, as said below
- pre_gain: bfloat16 [2, 1024], P(None, 'dp'), may hold values from 0.099609375 to 1.8984375
- w_z: bfloat16 [2, 1024, 2048], P(None, 'dp', 'tensor'), may hold values from -0.1875 to 0.1875
- w_x: bfloat16 [2, 1024, 2048], P(None, 'dp', 'tensor'), may hold values from -0.1875 to 0.1875
- w_bc: bfloat16 [2, 1024, 256], P(None, 'dp'), may hold values from -0.1875 to 0.1875
- w_dt: bfloat16 [2, 1024, 32], P(None, 'dp', 'tensor'), may hold values from -0.1875 to 0.1875
- conv_x: bfloat16 [2, 5, 2048], P(None, None, 'tensor'), may hold values from -3 to 3
- conv_bc: bfloat16 [2, 5, 256], replicated, may hold values from -3 to 3
- head_params: float32 [2, 3, 32], P(None, None, 'tensor'), may hold values from -6.9 to 2.77, as said below
- norm_gain: bfloat16 [2, 2048], P(None, 'tensor'), may hold values from 0.099609375 to 1.8984375
- w_out: bfloat16 [2, 2048, 1024], P(None, 'tensor', 'dp'), may hold values from -0.125 to 0.125
Outputs:
- activations: bfloat16 [24, 1024, 1024], P(None, 'dp', 'tensor')
- input_grad: bfloat16 [24, 1024, 1024], P(None, 'dp', 'tensor')
- grad_pre_gain: float32 [2, 1024], P(None, 'dp')
- grad_w_z: float32 [2, 1024, 2048], P(None, 'dp', 'tensor')
- grad_w_x: float32 [2, 1024, 2048], P(None, 'dp', 'tensor')
- grad_w_bc: float32 [2, 1024, 256], P(None, 'dp')
- grad_w_dt: float32 [2, 1024, 32], P(None, 'dp', 'tensor')
- grad_conv_x: float32 [2, 5, 2048], P(None, None, 'tensor')
- grad_conv_bc: float32 [2, 5, 256], replicated
- grad_head_params: float32 [2, 3, 32], P(None, None, 'tensor')
- grad_norm_gain: float32 [2, 2048], P(None, 'tensor')
- grad_w_out: float32 [2, 2048, 1024], P(None, 'tensor', 'dp')
The draws below stay inside these ranges and needn't reach their ends.
Inputs may be any that keep to these rules, and one draw needn't show every extreme that they name: Each value is a whole number; in every bin the three lengths add up to 2048. `packing`: A permutation of the 24 sequences. `head_params`: row 0 lies in -6.9 to -2.3, row 1 in 0 to 2.77, row 2 in 0.5 to 1.5.
All inputs are finite; a program needn't handle non-finite values.
Results may differ from the reference program's by a relative error of at most 0.02.
Values may be sent and summed in bfloat16 or wider, within the bound.
A program may use at most 256 MiB of HBM per device.

```python
import jax
import jax.numpy as jnp
from jax import lax

D = 1024
INNER = 2048
HEADS = 32
STATE = 128
CONV = 4
SCAN_BLOCK = 256
LAYERS = 2
SEQ_MIN = 512
SEQ_MAX = 1024
BIN = 2048
SEQS = 24
N_TENSOR = 4


def bin_triples(key):
    bin_count = SEQS // 3
    lead_key, middle_key, order_key = jax.random.split(key, 3)
    leading = jax.random.randint(lead_key, (bin_count,), SEQ_MIN, 2 * SEQ_MIN + 1)
    leading = leading.at[0].set(2 * SEQ_MIN)
    middle = jax.random.randint(middle_key, (bin_count,), SEQ_MIN, 3 * SEQ_MIN - leading + 1)
    trailing = BIN - leading - middle
    triples = jnp.stack([leading, middle, trailing], axis=1).reshape(-1).astype(jnp.int32)
    shuffled = jax.random.permutation(order_key, SEQS).astype(jnp.int32)
    return (triples, shuffled)


def draw_lengths(key, part):
    triples, shuffled = bin_triples(key)
    return jnp.zeros((SEQS,), jnp.int32).at[shuffled].set(triples)


def draw_packing(key, part):
    triples, shuffled = bin_triples(key)
    return shuffled


def draw_head_params(key, part):
    key = jax.random.fold_in(key, 7)
    bias_key, rate_key, skip_key = jax.random.split(key, 3)
    shape = (LAYERS, 1, HEADS)
    skip_gain = jax.random.uniform(skip_key, shape, jnp.float32, 0.5, 1.5)
    step_bias = jax.random.uniform(bias_key, shape, jnp.float32, -6.9, -2.3)
    spread = jax.random.uniform(rate_key, shape, jnp.float32, 0.0, 1.0)
    log_rate = spread * (step_bias + 6.9) * 0.6
    return jnp.concatenate([step_bias, log_rate, skip_gain], axis=1)


def levels(key, dims, shards, smallest, top_value):
    level, own = 1.0, jax.random.fold_in(key, 6)
    for dim, parts in shards:
        draws = jnp.exp(jax.random.uniform(jax.random.fold_in(own, dim), (parts,), jnp.float32, smallest / len(shards), top_value / len(shards)))
        level = level * jnp.repeat(draws, dims[dim] // parts).reshape([-1 if axis == dim else 1 for axis in range(len(dims))])
    return level


def gaussian(own_key, dims, deviation, bound, cuts=(), held_as=jnp.bfloat16):
    entries = jax.random.normal(own_key, dims, jnp.float32) * deviation
    if len(cuts) > 0:
        entries = levels(own_key, dims, cuts, -0.22, 0.18) * entries
    return jnp.clip(entries, min=-bound, max=bound).astype(held_as)


def setup_inputs(seed: int = 0) -> dict:
    arg_keys = jax.random.split(jax.random.key(seed), 15)
    return {
        "tokens": gaussian(arg_keys[0], (SEQS, SEQ_MAX, D), 1.0, 6.0, ((1, 8), (2, 4))),
        "cotangent": gaussian(arg_keys[1], (SEQS, SEQ_MAX, D), 1.0, 6.0, ((1, 8), (2, 4))),
        "lengths": draw_lengths(jax.random.fold_in(arg_keys[14], 71), 0),
        "packing": draw_packing(jax.random.fold_in(arg_keys[14], 71), 0),
        "pre_gain": jnp.clip(1.0 + 0.18 * jax.random.normal(arg_keys[4], (LAYERS, D), jnp.float32), 0.099609375, 1.8984375).astype(jnp.bfloat16),
        "w_z": gaussian(arg_keys[5], (LAYERS, D, INNER), D ** -0.5, 0.1875, ((1, 8), (2, 4))),
        "w_x": gaussian(arg_keys[6], (LAYERS, D, INNER), D ** -0.5, 0.1875, ((1, 8), (2, 4))),
        "w_bc": gaussian(arg_keys[7], (LAYERS, D, 2 * STATE), D ** -0.5, 0.1875, ((1, 8),)),
        "w_dt": gaussian(arg_keys[8], (LAYERS, D, HEADS), D ** -0.5, 0.1875, ((1, 8), (2, 4))),
        "conv_x": gaussian(arg_keys[9], (LAYERS, CONV + 1, INNER), CONV ** -0.5, 3.0, ((2, 4),)),
        "conv_bc": gaussian(arg_keys[10], (LAYERS, CONV + 1, 2 * STATE), CONV ** -0.5, 3.0),
        "head_params": draw_head_params(jax.random.fold_in(arg_keys[14], 71), 0),
        "norm_gain": jnp.clip(1.0 + 0.18 * jax.random.normal(arg_keys[12], (LAYERS, INNER), jnp.float32), 0.099609375, 1.8984375).astype(jnp.bfloat16),
        "w_out": gaussian(arg_keys[13], (LAYERS, INNER, D), INNER ** -0.5, 0.125, ((1, 4), (2, 8))),
    }


eps = 1e-05
precise = lax.Precision.HIGHEST

@jax.custom_vjp
def low(v):
    return lax.optimization_barrier(v.astype(jnp.bfloat16)).astype(jnp.float32)

@jax.custom_vjp
def low_back(v):
    return v

def low_keep(v):
    return (low(v), None)

def low_pass(kept, grad):
    return (grad,)

def back_keep(v):
    return (v, None)

def back_low(kept, grad):
    return (low(grad),)
low.defvjp(low_keep, low_pass)
low_back.defvjp(back_keep, back_low)

def causal_conv(values, conv_taps, segment):
    row_count = values.shape[0]
    running = jnp.broadcast_to(conv_taps[CONV], values.shape)
    for delay_step in range(CONV):
        shifted = jnp.pad(values, ((delay_step, 0), (0, 0)))[:row_count]
        earlier = jnp.pad(segment, (delay_step, 0), constant_values=-1)[:row_count]
        running = running + conv_taps[CONV - 1 - delay_step] * jnp.where((earlier == segment)[:, None], shifted, 0.0)
    return running

def state_space(inputs, step_sizes, decay_rates, b_rows, c_rows, segment):
    row_count, heads_here, head_dim = inputs.shape
    blocks = row_count // SCAN_BLOCK
    log_decay = step_sizes * decay_rates[None, :]
    seg_blocks = segment.reshape(blocks, SCAN_BLOCK)
    previous = jnp.concatenate([jnp.full((1,), -1, jnp.int32), seg_blocks[:-1, -1].astype(jnp.int32)])

    def one_block(state, block_data):
        x_blk, dt_blk, a_blk, b_blk, c_blk, s_blk, prior_seg = block_data
        cumulative = jnp.cumsum(a_blk, axis=0)
        positions = jnp.arange(SCAN_BLOCK)
        allowed = (s_blk[:, None] == s_blk[None, :]) & (positions[:, None] >= positions[None, :])
        log_gaps = jnp.where(allowed[:, :, None], cumulative[:, None, :] - cumulative[None, :, :], 0.0)
        decays = jnp.where(allowed[:, :, None], jnp.exp(log_gaps), 0.0)
        scores = jnp.dot(c_blk, b_blk.T, precision=precise)
        coupling = decays * scores[:, :, None] * dt_blk[None, :, :]
        inside = jnp.einsum('pqh,qhd->phd', coupling, x_blk, precision=precise)
        entering = jnp.where((s_blk == prior_seg)[:, None], jnp.exp(cumulative), 0.0)
        carried = jnp.einsum('pn,hdn->phd', c_blk, state, precision=precise) * entering[:, :, None]
        final_log = cumulative[-1]
        tail_weight = jnp.where((s_blk == s_blk[-1])[:, None], jnp.exp(final_log[None, :] - cumulative), 0.0) * dt_blk
        retained = jnp.where(s_blk[-1] == prior_seg, jnp.exp(final_log), 0.0)
        new_state = state * retained[:, None, None] + jnp.einsum('qh,qhd,qn->hdn', tail_weight, x_blk, b_blk, precision=precise)
        return (new_state, inside + carried)
    blocked = (inputs.reshape(blocks, SCAN_BLOCK, heads_here, head_dim), step_sizes.reshape(blocks, SCAN_BLOCK, heads_here), log_decay.reshape(blocks, SCAN_BLOCK, heads_here), b_rows.reshape(blocks, SCAN_BLOCK, -1), c_rows.reshape(blocks, SCAN_BLOCK, -1), seg_blocks, previous)
    start_state = jnp.zeros((heads_here, head_dim, b_rows.shape[1]), jnp.float32)
    end_state, outputs = lax.scan(jax.checkpoint(one_block), start_state, blocked)
    return outputs.reshape(row_count, heads_here, head_dim)

def core_piece(inputs, b_rows, c_rows, gate_in, dt_raw, head_part, segment):
    row_count, inner_part = inputs.shape
    heads_here = head_part.shape[1]
    step_sizes = jax.nn.softplus(dt_raw + head_part[0])
    decay_rates = -jnp.exp(head_part[1])
    shaped = inputs.reshape(row_count, heads_here, inner_part // heads_here)
    mixed_out = state_space(shaped, step_sizes, decay_rates, b_rows, c_rows, segment) + head_part[2][None, :, None] * shaped
    return mixed_out.reshape(row_count, inner_part) * jax.nn.silu(gate_in)

def pre_norm(hidden, gain_full):
    return hidden * lax.rsqrt(lax.optimization_barrier(jnp.mean(hidden * hidden, axis=-1, keepdims=True)) + eps) * gain_full

def post_scale(gated_out, squares, gain_part):
    return gated_out * lax.rsqrt(squares / INNER + eps)[:, None] * gain_part

def mamba_layer(hidden, layer_params, segment):
    pre_gain, w_z, w_x, w_bc, w_dt, conv_x, conv_bc, head_params, norm_gain, w_out = layer_params
    normed = low(pre_norm(hidden, pre_gain))
    inner_part = INNER // N_TENSOR
    heads_part = HEADS // N_TENSOR
    gated_list = []
    for member in range(N_TENSOR):
        columns = slice(member * inner_part, (member + 1) * inner_part)
        heads_cut = slice(member * heads_part, (member + 1) * heads_part)
        weights = jnp.concatenate([w_z[:, columns], w_x[:, columns], w_bc, w_dt[:, heads_cut]], axis=1)
        projected = low_back(jnp.dot(low_back(normed), weights, precision=precise))
        conv_taps = jnp.concatenate([conv_x[:, columns], conv_bc], axis=1)
        conv_out = jax.nn.silu(causal_conv(projected[:, inner_part:2 * inner_part + 2 * STATE], conv_taps, segment))
        inputs = low(conv_out[:, :inner_part])
        b_rows = low(conv_out[:, inner_part:inner_part + STATE])
        c_rows = low(conv_out[:, inner_part + STATE:])
        gated_list.append(core_piece(inputs, b_rows, c_rows, projected[:, :inner_part], projected[:, 2 * inner_part + 2 * STATE:], head_params[:, heads_cut], segment))
    squares = sum((lax.optimization_barrier(jnp.sum(gated_out * gated_out, axis=-1)) for gated_out in gated_list))
    branch = jnp.zeros_like(hidden)
    for member in range(N_TENSOR):
        columns = slice(member * inner_part, (member + 1) * inner_part)
        scaled = low(post_scale(gated_list[member], squares, norm_gain[columns]))
        branch = branch + low(jnp.dot(scaled, w_out[columns], precision=precise))
    return hidden + low_back(branch)

def reference(tokens, cotangent, lengths, packing, pre_gain, w_z, w_x, w_bc, w_dt, conv_x, conv_bc, head_params, norm_gain, w_out):
    seq_total = lengths.shape[0]
    bin_count = seq_total // 3
    triples = lengths[packing].reshape(bin_count, 3)
    offsets = jnp.cumsum(triples, axis=1) - triples
    bin_rows = jnp.arange(BIN, dtype=jnp.int32)
    segment = (bin_rows[None, :] >= offsets[:, 1:2]).astype(jnp.int32) + (bin_rows[None, :] >= offsets[:, 2:3]).astype(jnp.int32)
    within = bin_rows[None, :] - jnp.take_along_axis(offsets, segment, axis=1)
    seq_ids = jnp.take_along_axis(packing.reshape(bin_count, 3), segment, axis=1)
    rank_of = jnp.zeros_like(packing).at[packing].set(jnp.arange(seq_total, dtype=jnp.int32))
    home_bin = rank_of // 3
    home_offset = offsets.reshape(-1)[rank_of]
    positions = jnp.arange(SEQ_MAX, dtype=jnp.int32)
    live_slot = positions[None, :] < lengths[:, None]
    source_row = home_bin[:, None] * BIN + jnp.minimum(home_offset[:, None] + positions[None, :], BIN - 1)
    params = tuple((values.astype(jnp.float32) for values in (pre_gain, w_z, w_x, w_bc, w_dt, conv_x, conv_bc, head_params, norm_gain, w_out)))

    def forward(layer_stack, given_rows):
        binned = given_rows[seq_ids, within]

        def one_bin(bin_data):
            hidden, bin_segment = bin_data
            for layer_index in range(LAYERS):
                hidden = mamba_layer(hidden, tuple((values[layer_index] for values in layer_stack)), bin_segment)
            return hidden
        results = lax.map(jax.checkpoint(one_bin), (binned, segment))
        flat_rows = results.reshape(bin_count * BIN, -1)[source_row]
        return jnp.where(live_slot[:, :, None], flat_rows, 0.0)
    outputs, pullback = jax.vjp(forward, params, tokens.astype(jnp.float32))
    param_grads, token_grads = pullback(cotangent.astype(jnp.float32))
    g_pre, g_z, g_x, g_bc, g_dt, g_convx, g_convbc, g_head, g_norm, g_out = param_grads
    return (outputs.astype(jnp.bfloat16), token_grads.astype(jnp.bfloat16), g_pre, g_z, g_x, g_bc, g_dt, g_convx, g_convbc, g_head, g_norm, g_out)
```

```python
import functools
import jax
import jax.numpy as jnp
from jax import lax
from jax.experimental import pallas as pl
from jax.experimental.pallas import tpu as pltpu
from jax.sharding import PartitionSpec as P

CONV = 4
INNER = 2048
LAYERS = 2
BIN = 2048
eps = 1e-05
STATE = 128
BLK = 256
LANES = 128
LOG2E = 1.4426950408889634
F32 = jnp.float32
BF16 = jnp.bfloat16


def dot_nn(left, right):
    return lax.dot_general(left, right, (((1,), (0,)), ((), ())), preferred_element_type=F32)


def dot_nt(left, right):
    return lax.dot_general(left, right, (((1,), (1,)), ((), ())), preferred_element_type=F32)


def dot_tn(left, right):
    return lax.dot_general(left, right, (((0,), (0,)), ((), ())), preferred_element_type=F32)


def split_two(values):
    high = values.astype(BF16)
    return high, (values - high.astype(F32)).astype(BF16)


def split_three(values):
    high = values.astype(BF16)
    rest = values - high.astype(F32)
    middle = rest.astype(BF16)
    return high, middle, (rest - middle.astype(F32)).astype(BF16)


def spread_heads(values, spread):
    high, low = split_two(values)
    return dot_nn(jnp.concatenate([high, low], axis=1), spread)


def gather_heads(values, spread):
    high, low = split_two(values)
    half = spread[:LANES]
    return dot_nt(high, half) + dot_nt(low, half)


def sigmoid(values):
    return 0.5 * jnp.tanh(0.5 * values) + 0.5


def softplus(values):
    return jnp.maximum(values, 0.0) + jnp.log1p(jnp.exp(-jnp.abs(values)))


def segment_of(rows, first, second):
    return (rows >= first).astype(jnp.int32) + (rows >= second).astype(jnp.int32)


def block_frame(block, first, second):
    row_col = block * BLK + lax.broadcasted_iota(jnp.int32, (BLK, 1), 0)
    row_row = block * BLK + lax.broadcasted_iota(jnp.int32, (1, BLK), 1)
    return row_col, row_row, segment_of(row_col, first, second), segment_of(row_row, first, second)


def decay_parts(block, dt_raw, head, seg_col, first, second):
    shifted = dt_raw + head[0:1]
    steps = softplus(shifted)
    log_decay = steps * head[1:2]
    above = lax.broadcasted_iota(jnp.int32, (BLK, BLK), 0)
    below = lax.broadcasted_iota(jnp.int32, (BLK, BLK), 1)
    lower = jnp.where(above >= below, 1.0, 0.0).astype(BF16)
    parts = dot_nn(lower, jnp.concatenate(split_three(log_decay), axis=1))
    cumulative = parts[:, :LANES] + parts[:, LANES : 2 * LANES] + parts[:, 2 * LANES :]
    cum2 = cumulative * LOG2E
    final2 = cum2[BLK - 1 : BLK]
    last_seg = segment_of(block * BLK + BLK - 1, first, second)
    prior_seg = jnp.where(block == 0, -1, segment_of(block * BLK - 1, first, second))
    entering = jnp.where(seg_col == prior_seg, jnp.exp2(cum2), 0.0)
    tail = jnp.where(seg_col == last_seg, jnp.exp2(final2 - cum2), 0.0)
    retained = jnp.where(last_seg == prior_seg, jnp.exp2(final2), 0.0)
    return shifted, steps, cum2, entering, tail, retained


def head_half(pair, head):
    lanes = lax.broadcasted_iota(jnp.int32, pair.shape, 1)
    keep = (lanes < LANES // 2) if head % 2 == 0 else (lanes >= LANES // 2)
    return jnp.where(keep, pair, jnp.zeros_like(pair))


def forward_kernel(
    off_ref, rows_ref, w_ref, taps_ref, head_ref, wide_ref, spread_ref,
    part_ref, sq_ref, z_ref, in_ref, pre_ref, dt_ref, y_ref, gg_ref, st_ref,
    state, padded,
):
    block = pl.program_id(0)
    inner = y_ref.shape[1]
    mixed = in_ref.shape[1]
    first, second = off_ref[0], off_ref[1]

    @pl.when(block == 0)
    def _():
        state[...] = jnp.zeros_like(state)
        padded[pl.ds(0, 8), :] = jnp.zeros((8, mixed), F32)

    row_col, row_row, seg_col, seg_row = block_frame(block, first, second)
    seg_start = jnp.where(seg_col == 0, 0, jnp.where(seg_col == 1, first, second))
    within = row_col - seg_start
    product = dot_nn(rows_ref[...], w_ref[:, inner:])
    gate = product[:, :inner]
    mixed_in = product[:, inner : inner + mixed]
    dt_raw = product[:, inner + mixed :]
    z_ref[...] = gate
    in_ref[...] = mixed_in
    dt_ref[...] = dt_raw
    padded[pl.ds(8, BLK), :] = mixed_in
    taps = taps_ref[...]
    conv = taps[CONV : CONV + 1] + taps[CONV - 1 : CONV] * mixed_in
    for delay in range(1, CONV):
        shifted_in = padded[pl.ds(8 - delay, BLK), :]
        conv = conv + taps[CONV - 1 - delay : CONV - delay] * jnp.where(within >= delay, shifted_in, 0.0)
    padded[pl.ds(0, 8), :] = padded[pl.ds(BLK, 8), :]
    pre_ref[...] = conv
    mixed_low = (conv * sigmoid(conv)).astype(BF16)
    x_low = mixed_low[:, :inner]
    b_low = mixed_low[:, inner : inner + STATE]
    c_low = mixed_low[:, inner + STATE :]
    head = head_ref[...]
    spread = spread_ref[...]
    shifted, steps, cum2, entering, tail, retained = decay_parts(block, dt_raw, head, seg_col, first, second)
    cum_row = jnp.transpose(cum2)
    x_in = x_low.astype(F32)
    x_steps = spread_heads(steps, spread) * x_in
    x_steps_low = x_steps.astype(BF16)
    allowed = (seg_col == seg_row) & (row_col >= row_row)
    scores = jnp.where(allowed, dot_nt(c_low, b_low), 0.0)
    old_state = state[...]
    st_ref[0] = old_state
    carried = spread_heads(entering, spread) * dot_nn(c_low, old_state.astype(BF16))
    wide = wide_ref[...]
    pieces = []
    for pair in range(inner // LANES):
        columns = slice(pair * LANES, (pair + 1) * LANES)
        total = None
        for head_index in (2 * pair, 2 * pair + 1):
            gaps = cum2[:, head_index : head_index + 1] - cum_row[head_index : head_index + 1, :]
            coupling = (jnp.exp2(jnp.minimum(gaps, 0.0)) * scores).astype(BF16)
            term = dot_nn(coupling, head_half(x_steps_low[:, columns], head_index))
            total = term if total is None else total + term
        pieces.append(total)
    mixed_out = jnp.concatenate(pieces, axis=1) + carried + wide[0:1] * x_in
    tailed = (spread_heads(tail, spread) * x_steps).astype(BF16)
    keep = spread_heads(jnp.broadcast_to(retained, (8, LANES)), spread)[0:1]
    state[...] = old_state * keep + dot_tn(b_low, tailed)
    y_ref[...] = mixed_out
    gated = mixed_out * (gate * sigmoid(gate))
    sq_ref[...] = jnp.sum(gated * gated, axis=1, keepdims=True)
    gained = (gated * wide[1:2]).astype(BF16)
    gg_ref[...] = gained
    part_ref[...] = dot_nt(gained, w_ref[:, :inner]).astype(BF16)


def backward_kernel(
    off_ref, sg_ref, g2_ref, w_ref, taps_ref, head_ref, wide_ref, spread_ref,
    z_ref, in_ref, pre_ref, dt_ref, y_ref, st_ref,
    part_ref, gproj_ref, gtaps_ref, ghead_ref, gwide_ref,
    dstate, padded,
):
    step = pl.program_id(0)
    block = pl.num_programs(0) - 1 - step
    inner = y_ref.shape[1]
    mixed = in_ref.shape[1]
    first, second = off_ref[0], off_ref[1]

    @pl.when(step == 0)
    def _():
        dstate[...] = jnp.zeros_like(dstate)
        padded[pl.ds(BLK, 8), :] = jnp.zeros((8, mixed), F32)
        gtaps_ref[...] = jnp.zeros_like(gtaps_ref)
        ghead_ref[...] = jnp.zeros_like(ghead_ref)
        gwide_ref[...] = jnp.zeros_like(gwide_ref)

    row_col, row_row, seg_col, seg_row = block_frame(block, first, second)
    seg_end = jnp.where(seg_col == 0, first, jnp.where(seg_col == 1, second, pl.num_programs(0) * BLK))
    remaining = seg_end - row_col
    head = head_ref[...]
    wide = wide_ref[...]
    spread = spread_ref[...]
    skip, gain = wide[0:1], wide[1:2]
    gate = z_ref[...]
    mixed_out = y_ref[...]
    conv = pre_ref[...]
    gate_sig = sigmoid(gate)
    gate_silu = gate * gate_sig
    gated = mixed_out * gate_silu
    grad_scaled = dot_nn(sg_ref[...], w_ref[:, :inner])
    grad_gated = grad_scaled * gain + g2_ref[...] * gated
    grad_out = grad_gated * gate_silu
    grad_gate = grad_gated * mixed_out * (gate_sig * (1.0 + gate * (1.0 - gate_sig)))
    grad_out_low = grad_out.astype(BF16)

    conv_sig = sigmoid(conv)
    mixed_low = (conv * conv_sig).astype(BF16)
    x_low = mixed_low[:, :inner]
    b_low = mixed_low[:, inner : inner + STATE]
    c_low = mixed_low[:, inner + STATE :]
    x_in = x_low.astype(F32)
    shifted, steps, cum2, entering, tail, retained = decay_parts(block, dt_ref[...], head, seg_col, first, second)
    cum_row = jnp.transpose(cum2)
    steps_wide = spread_heads(steps, spread)
    x_steps_low = (steps_wide * x_in).astype(BF16)
    x_steps = x_steps_low.astype(F32)

    allowed = (seg_col == seg_row) & (row_col <= row_row)
    scores = jnp.where(allowed, dot_nt(b_low, c_low), 0.0)
    grad_scores = jnp.zeros((BLK, BLK), F32)
    pieces = []
    for pair in range(inner // LANES):
        columns = slice(pair * LANES, (pair + 1) * LANES)
        total = None
        for head_index in (2 * pair, 2 * pair + 1):
            gaps = cum_row[head_index : head_index + 1, :] - cum2[:, head_index : head_index + 1]
            decays = jnp.exp2(jnp.minimum(gaps, 0.0))
            coupling = (decays * scores).astype(BF16)
            term = dot_nn(coupling, head_half(grad_out_low[:, columns], head_index))
            total = term if total is None else total + term
            grad_scores = grad_scores + decays * dot_nt(
                head_half(x_steps_low[:, columns], head_index), grad_out_low[:, columns]
            )
        pieces.append(total)
    grad_scores_low = jnp.where(allowed, grad_scores, 0.0).astype(BF16)
    old_dstate = dstate[...]
    old_dstate_low = old_dstate.astype(BF16)
    old_state = st_ref[0]
    tail_wide = spread_heads(tail, spread)
    from_state = tail_wide * dot_nn(b_low, old_dstate_low)
    grad_unit = jnp.concatenate(pieces, axis=1) + from_state
    entered = (spread_heads(entering, spread) * grad_out).astype(BF16)
    tailed = (tail_wide * x_steps).astype(BF16)
    grad_c = dot_tn(grad_scores_low, b_low) + dot_nt(entered, old_state.astype(BF16))
    grad_b = dot_nn(grad_scores_low, c_low) + dot_nt(tailed, old_dstate_low)
    keep = spread_heads(jnp.broadcast_to(retained, (8, LANES)), spread)[0:1]
    dstate[...] = old_dstate * keep + dot_tn(c_low, entered)

    balance = gather_heads(grad_out_low.astype(F32) * (mixed_out - skip * x_in) - x_steps * grad_unit, spread)
    direct = gather_heads(x_in * grad_unit, spread)
    final_wide = jnp.sum(x_steps * from_state, axis=0, keepdims=True) + keep * jnp.sum(
        old_dstate * old_state, axis=0, keepdims=True
    )
    final = gather_heads(jnp.broadcast_to(final_wide, (8, inner)), spread)[0:1]
    above = lax.broadcasted_iota(jnp.int32, (BLK, BLK), 0)
    below = lax.broadcasted_iota(jnp.int32, (BLK, BLK), 1)
    upper = jnp.where(above <= below, 1.0, 0.0).astype(BF16)
    parts = dot_nn(upper, jnp.concatenate(split_three(balance), axis=1))
    grad_log = parts[:, :LANES] + parts[:, LANES : 2 * LANES] + parts[:, 2 * LANES :] + final
    grad_steps = direct + grad_log * head[1:2]
    grad_dt = grad_steps * sigmoid(shifted)
    ghead_ref[0:1, :] += jnp.sum(grad_dt, axis=0, keepdims=True)
    ghead_ref[1:2, :] += jnp.sum(grad_log * steps, axis=0, keepdims=True) * head[1:2]
    gwide_ref[0:1, :] += jnp.sum(grad_out * x_in, axis=0, keepdims=True)
    gwide_ref[1:2, :] += jnp.sum(grad_scaled * gated, axis=0, keepdims=True)

    grad_x = steps_wide * grad_unit + skip * grad_out
    grad_conv = jnp.concatenate([grad_x, grad_b, grad_c], axis=1) * (
        conv_sig * (1.0 + conv * (1.0 - conv_sig))
    )
    padded[pl.ds(0, BLK), :] = grad_conv
    mixed_in = in_ref[...]
    taps = taps_ref[...]
    grad_in = taps[CONV - 1 : CONV] * grad_conv
    gtaps_ref[CONV : CONV + 1, :] += jnp.sum(grad_conv, axis=0, keepdims=True)
    gtaps_ref[CONV - 1 : CONV, :] += jnp.sum(mixed_in * grad_conv, axis=0, keepdims=True)
    for delay in range(1, CONV):
        later = jnp.where(remaining > delay, padded[pl.ds(delay, BLK), :], 0.0)
        grad_in = grad_in + taps[CONV - 1 - delay : CONV - delay] * later
        gtaps_ref[CONV - 1 - delay : CONV - delay, :] += jnp.sum(mixed_in * later, axis=0, keepdims=True)
    padded[pl.ds(BLK, 8), :] = padded[pl.ds(0, 8), :]
    gproj = jnp.concatenate([grad_gate.astype(BF16), grad_in.astype(BF16), grad_dt.astype(BF16)], axis=1)
    gproj_ref[...] = gproj
    part_ref[...] = dot_nt(gproj, w_ref[:, inner:]).astype(BF16)


def whole(shape):
    return pl.BlockSpec(shape, lambda b: (0,) * len(shape))


def layer_forward(offsets, rows, weights, taps, head, wide, spread):
    count, width = rows.shape
    inner, mixed = wide.shape[1], taps.shape[1]
    blocks = count // BLK
    total = weights.shape[1]

    def by_block(columns):
        return pl.BlockSpec((BLK, columns), lambda b: (b, 0))

    return pl.pallas_call(
        forward_kernel,
        grid=(blocks,),
        in_specs=[
            pl.BlockSpec(memory_space=pltpu.SMEM),
            by_block(width), whole((width, total)), whole((8, mixed)), whole((8, LANES)), whole((8, inner)),
            whole((2 * LANES, inner)),
        ],
        out_specs=[
            by_block(width), by_block(1), by_block(inner), by_block(mixed), by_block(mixed),
            by_block(LANES), by_block(inner), by_block(inner),
            pl.BlockSpec((1, STATE, inner), lambda b: (b, 0, 0)),
        ],
        out_shape=[
            jax.ShapeDtypeStruct((count, width), BF16),
            jax.ShapeDtypeStruct((count, 1), F32),
            jax.ShapeDtypeStruct((count, inner), F32),
            jax.ShapeDtypeStruct((count, mixed), F32),
            jax.ShapeDtypeStruct((count, mixed), F32),
            jax.ShapeDtypeStruct((count, LANES), F32),
            jax.ShapeDtypeStruct((count, inner), F32),
            jax.ShapeDtypeStruct((count, inner), BF16),
            jax.ShapeDtypeStruct((blocks, STATE, inner), F32),
        ],
        scratch_shapes=[pltpu.VMEM((STATE, inner), F32), pltpu.VMEM((BLK + 8, mixed), F32)],
        compiler_params=pltpu.CompilerParams(vmem_limit_bytes=48 * 1024 * 1024),
        name="layer_forward",
    )(offsets, rows, weights, taps, head, wide, spread)


def layer_backward(offsets, spread_grad, twice, weights, taps, head, wide, spread, saved):
    gate, mixed_in, conv, dt_raw, mixed_out, states = saved
    count, width = spread_grad.shape
    inner, mixed = wide.shape[1], taps.shape[1]
    blocks = count // BLK
    total = weights.shape[1]

    def by_block(columns):
        return pl.BlockSpec((BLK, columns), lambda b: (blocks - 1 - b, 0))

    return pl.pallas_call(
        backward_kernel,
        grid=(blocks,),
        in_specs=[
            pl.BlockSpec(memory_space=pltpu.SMEM),
            by_block(width), by_block(1), whole((width, total)), whole((8, mixed)), whole((8, LANES)),
            whole((8, inner)), whole((2 * LANES, inner)),
            by_block(inner), by_block(mixed), by_block(mixed), by_block(LANES), by_block(inner),
            pl.BlockSpec((1, STATE, inner), lambda b: (blocks - 1 - b, 0, 0)),
        ],
        out_specs=[
            by_block(width), by_block(total - inner),
            whole((8, mixed)), whole((8, LANES)), whole((8, inner)),
        ],
        out_shape=[
            jax.ShapeDtypeStruct((count, width), BF16),
            jax.ShapeDtypeStruct((count, total - inner), BF16),
            jax.ShapeDtypeStruct((8, mixed), F32),
            jax.ShapeDtypeStruct((8, LANES), F32),
            jax.ShapeDtypeStruct((8, inner), F32),
        ],
        scratch_shapes=[pltpu.VMEM((STATE, inner), F32), pltpu.VMEM((BLK + 8, mixed), F32)],
        compiler_params=pltpu.CompilerParams(vmem_limit_bytes=48 * 1024 * 1024),
        name="layer_backward",
    )(offsets, spread_grad, twice, weights, taps, head, wide, spread, gate, mixed_in, conv, dt_raw, mixed_out, states)


def spread_matrix(inner, heads):
    lane_head = lax.broadcasted_iota(jnp.int32, (2 * LANES, inner), 1) // (inner // heads)
    row_head = lax.broadcasted_iota(jnp.int32, (2 * LANES, inner), 0) % LANES
    return jnp.where(lane_head == row_head, 1.0, 0.0).astype(BF16)


def pre_norm(hidden, gain_full):
    return hidden * lax.rsqrt(jnp.mean(hidden * hidden, axis=-1, keepdims=True) + eps) * gain_full


def pad_to(values, rows, columns):
    return jnp.pad(values, ((0, rows - values.shape[0]), (0, columns - values.shape[1])))


def on_device(
    tokens, cotangent, lengths, packing, pre_gain, w_z, w_x, w_bc, w_dt, conv_x, conv_bc, head_params, norm_gain, w_out,
):
    dp_count = lax.axis_size("dp")
    bin_index = lax.axis_index("dp")
    seq_total, pos_here, cols_here = tokens.shape
    inner_part = conv_x.shape[2]
    heads_here = head_params.shape[2]
    dp_rows = w_z.shape[1]
    mixed = inner_part + 2 * STATE
    triples = lengths[packing].reshape(dp_count, 3)
    offsets = jnp.cumsum(triples, axis=1) - triples
    my_offsets = offsets[bin_index]
    my_lengths = triples[bin_index]
    bounds = my_offsets[1:3]
    bin_rows = jnp.arange(BIN, dtype=jnp.int32)
    segment = segment_of(bin_rows, my_offsets[1], my_offsets[2])
    seg_start = jnp.where(segment == 0, my_offsets[0], jnp.where(segment == 1, my_offsets[1], my_offsets[2]))
    within = bin_rows - seg_start
    pick_rows = (within // pos_here * 3 + segment) * pos_here + within % pos_here
    groups = packing.reshape(dp_count, 3)

    def to_bins(given):
        arrived = lax.all_to_all(given[groups], "dp", split_axis=0, concat_axis=0, tiled=True)
        flat = arrived.reshape(-1, cols_here)[pick_rows]
        return lax.all_to_all(flat, "tensor", split_axis=0, concat_axis=1, tiled=True)

    spread = spread_matrix(inner_part, heads_here)
    gains = lax.all_gather(pre_gain, "dp", axis=1, tiled=True).astype(F32)
    packs = []
    for layer in range(LAYERS):
        own = jnp.concatenate(
            [w_out[layer].T, w_z[layer], w_x[layer], w_bc[layer], pad_to(w_dt[layer], dp_rows, LANES)], axis=1
        )
        taps = jnp.concatenate([conv_x[layer], conv_bc[layer]], axis=1).astype(F32)
        head = jnp.stack([head_params[layer, 0], -jnp.exp(head_params[layer, 1])])
        wide = jnp.stack(
            [jnp.repeat(head_params[layer, 2], inner_part // heads_here), norm_gain[layer].astype(F32)]
        )
        packs.append((own, pad_to(taps, 8, mixed), pad_to(head, 8, LANES), pad_to(wide, 8, inner_part)))

    row_tokens = to_bins(tokens)
    hidden = row_tokens.astype(F32)
    records = []
    for layer in range(LAYERS):
        own, taps, head, wide = packs[layer]
        weights = lax.all_gather(own, "dp", axis=0, tiled=True)
        normed, norm_back = jax.vjp(pre_norm, hidden, gains[layer])
        rows = lax.all_gather(normed.astype(BF16), "tensor", axis=0, tiled=True)
        part, squares, gate, mixed_in, conv, dt_raw, mixed_out, gained, states = layer_forward(
            bounds, rows, weights, taps, head, wide, spread
        )
        total = lax.psum_scatter(part, "tensor", scatter_dimension=0, tiled=True).astype(F32)
        own_squares = lax.psum_scatter(squares[:, 0], "tensor", scatter_dimension=0, tiled=True)
        scale = lax.rsqrt(own_squares / INNER + eps)[:, None]
        hidden = hidden + total * scale
        records.append((norm_back, rows, weights, gained, total, scale, (gate, mixed_in, conv, dt_raw, mixed_out, states)))
    final_rows = hidden.astype(BF16)

    grad_hidden = to_bins(cotangent).astype(F32)
    collected = [None] * LAYERS
    for layer in reversed(range(LAYERS)):
        own, taps, head, wide = packs[layer]
        norm_back, rows, weights, gained, total, scale, saved = records[layer]
        grad_branch = grad_hidden.astype(BF16).astype(F32)
        twice = 2.0 * (-(scale**3) / (2 * INNER)) * jnp.sum(grad_branch * total, axis=1, keepdims=True)
        spread_grad = lax.all_gather((grad_branch * scale).astype(BF16), "tensor", axis=0, tiled=True)
        spread_twice = lax.all_gather(twice, "tensor", axis=0, tiled=True)
        part, gproj, gtaps, ghead, gwide = layer_backward(
            bounds, spread_grad, spread_twice, weights, taps, head, wide, spread, saved
        )
        grad_normed = lax.psum_scatter(part, "tensor", scatter_dimension=0, tiled=True).astype(F32)
        grad_weights = jnp.concatenate(
            [dot_tn(spread_grad, gained).astype(BF16), dot_tn(rows, gproj).astype(BF16)], axis=1
        )
        own_weights = lax.psum_scatter(grad_weights, "dp", scatter_dimension=0, tiled=True)
        grad_before, grad_gain = norm_back(grad_normed)
        grad_hidden = grad_hidden + grad_before
        collected[layer] = (own_weights, grad_gain, gtaps, ghead, gwide)

    heads_first = (
        jnp.stack([item[2][: CONV + 1, :inner_part] for item in collected]),
        jnp.stack(
            [
                jnp.concatenate(
                    [item[3][:2, :heads_here], jnp.sum(item[4][0:1].reshape(1, heads_here, -1), axis=2)], axis=0
                )
                for item in collected
            ]
        ),
        jnp.stack([item[4][1] for item in collected]),
    )
    shared = (
        jnp.stack([item[2][: CONV + 1, inner_part:] for item in collected]),
        jnp.stack([item[1] for item in collected]),
    )
    grad_convx, grad_head, grad_norm, shared_convbc, shared_pre = lax.psum(heads_first + shared, "dp")
    own_weights = jnp.stack([item[0] for item in collected])
    shared_bc = own_weights[:, :, 3 * inner_part : 3 * inner_part + 2 * STATE].astype(F32)
    grad_convbc, grad_pre, grad_bc = lax.psum((shared_convbc, shared_pre, shared_bc), "tensor")
    shard_pre = lax.dynamic_slice_in_dim(grad_pre, bin_index * dp_rows, dp_rows, 1)
    own_weights = own_weights.astype(F32)
    grad_out = jnp.swapaxes(own_weights[:, :, :inner_part], 1, 2)
    grad_z = own_weights[:, :, inner_part : 2 * inner_part]
    grad_x = own_weights[:, :, 2 * inner_part : 3 * inner_part]
    grad_dt = own_weights[:, :, 3 * inner_part + 2 * STATE : 3 * inner_part + 2 * STATE + heads_here]

    dev_grid = jnp.arange(dp_count, dtype=jnp.int32)[:, None, None]
    pos_grid = jnp.arange(pos_here, dtype=jnp.int32)[None, None, :]
    seq_pos = dev_grid * pos_here + pos_grid
    live_slot = (seq_pos < my_lengths[None, :, None]).reshape(-1, 1)
    source = jnp.minimum(my_offsets[None, :, None] + seq_pos, BIN - 1).reshape(-1)
    rank_of = jnp.zeros_like(packing).at[packing].set(jnp.arange(seq_total, dtype=jnp.int32))

    def from_bins(rows):
        columns = lax.all_to_all(rows, "tensor", split_axis=1, concat_axis=0, tiled=True)
        slots = jnp.where(live_slot, columns[source], 0).reshape(dp_count, 3, pos_here, cols_here)
        returned = lax.all_to_all(slots, "dp", split_axis=0, concat_axis=0, tiled=True)
        return returned.reshape(seq_total, pos_here, cols_here)[rank_of]

    activations = from_bins(final_rows)
    input_grad = from_bins(grad_hidden.astype(BF16))
    return (
        activations, input_grad, shard_pre, grad_z, grad_x, grad_bc, grad_dt,
        grad_convx, grad_convbc, grad_head, grad_norm, grad_out,
    )


def solution(mesh):
    placed = (
        P(None, "dp", "tensor"), P(None, "dp", "tensor"), P(), P(), P(None, "dp"),
        P(None, "dp", "tensor"), P(None, "dp", "tensor"), P(None, "dp", None), P(None, "dp", "tensor"),
        P(None, None, "tensor"), P(), P(None, None, "tensor"), P(None, "tensor"), P(None, "tensor", "dp"),
    )
    results = (
        P(None, "dp", "tensor"), P(None, "dp", "tensor"), P(None, "dp"),
        P(None, "dp", "tensor"), P(None, "dp", "tensor"), P(None, "dp", None), P(None, "dp", "tensor"),
        P(None, None, "tensor"), P(), P(None, None, "tensor"), P(None, "tensor"), P(None, "tensor", "dp"),
    )
    return jax.shard_map(on_device, mesh=mesh, in_specs=placed, out_specs=results, check_vma=False)
```

```python
import functools
import jax
import jax.numpy as jnp
from jax import lax
from jax.experimental import pallas as pl
from jax.experimental.pallas import tpu as pltpu
from jax.sharding import PartitionSpec as P

CONV = 4
INNER = 2048
LAYERS = 2
BIN = 2048
eps = 1e-05
STATE = 128
BLK = 256
LANES = 128
LOG2E = 1.4426950408889634
F32 = jnp.float32
BF16 = jnp.bfloat16


def dot_nn(left, right):
    return lax.dot_general(left, right, (((1,), (0,)), ((), ())), preferred_element_type=F32)


def dot_nt(left, right):
    return lax.dot_general(left, right, (((1,), (1,)), ((), ())), preferred_element_type=F32)


def dot_tn(left, right):
    return lax.dot_general(left, right, (((0,), (0,)), ((), ())), preferred_element_type=F32)


def split_two(values):
    high = values.astype(BF16)
    return high, (values - high.astype(F32)).astype(BF16)


def split_three(values):
    high = values.astype(BF16)
    rest = values - high.astype(F32)
    middle = rest.astype(BF16)
    return high, middle, (rest - middle.astype(F32)).astype(BF16)


def spread_heads(values, spread):
    high, low = split_two(values)
    return dot_nn(jnp.concatenate([high, low], axis=1), spread)


def gather_heads(values, spread):
    high, low = split_two(values)
    half = spread[:LANES]
    return dot_nt(high, half) + dot_nt(low, half)


def sigmoid(values):
    return 0.5 * jnp.tanh(0.5 * values) + 0.5


def softplus(values):
    return jnp.maximum(values, 0.0) + jnp.log1p(jnp.exp(-jnp.abs(values)))


def segment_of(rows, first, second):
    return (rows >= first).astype(jnp.int32) + (rows >= second).astype(jnp.int32)


def block_frame(block, first, second):
    row_col = block * BLK + lax.broadcasted_iota(jnp.int32, (BLK, 1), 0)
    row_row = block * BLK + lax.broadcasted_iota(jnp.int32, (1, BLK), 1)
    return row_col, row_row, segment_of(row_col, first, second), segment_of(row_row, first, second)


def decay_parts(block, dt_raw, head, seg_col, first, second):
    shifted = dt_raw + head[0:1]
    steps = softplus(shifted)
    log_decay = steps * head[1:2]
    above = lax.broadcasted_iota(jnp.int32, (BLK, BLK), 0)
    below = lax.broadcasted_iota(jnp.int32, (BLK, BLK), 1)
    lower = jnp.where(above >= below, 1.0, 0.0).astype(BF16)
    parts = dot_nn(lower, jnp.concatenate(split_three(log_decay), axis=1))
    cumulative = parts[:, :LANES] + parts[:, LANES : 2 * LANES] + parts[:, 2 * LANES :]
    cum2 = cumulative * LOG2E
    final2 = cum2[BLK - 1 : BLK]
    last_seg = segment_of(block * BLK + BLK - 1, first, second)
    prior_seg = jnp.where(block == 0, -1, segment_of(block * BLK - 1, first, second))
    entering = jnp.where(seg_col == prior_seg, jnp.exp2(cum2), 0.0)
    tail = jnp.where(seg_col == last_seg, jnp.exp2(final2 - cum2), 0.0)
    retained = jnp.where(last_seg == prior_seg, jnp.exp2(final2), 0.0)
    return shifted, steps, cum2, entering, tail, retained


def head_half(pair, head):
    lanes = lax.broadcasted_iota(jnp.int32, pair.shape, 1)
    keep = (lanes < LANES // 2) if head % 2 == 0 else (lanes >= LANES // 2)
    return jnp.where(keep, pair, jnp.zeros_like(pair))


SHARE = BLK // 4
AG_OWN, AG_ACROSS, AG_PASS, RS_PAIR, RS_ACROSS, SM_PAIR, SM_ACROSS = range(7)


class Ring:
    def __init__(self, sems):
        me = lax.axis_index("tensor")
        self.low, self.high = me % 2, me // 2
        self.me = me
        self.sibling = self.high * 2 + (1 - self.low)
        self.across = (1 - self.high) * 2 + self.low
        self.beyond = (1 - self.high) * 2 + (1 - self.low)
        self.sems = sems

    def greet(self):
        barrier = pltpu.get_barrier_semaphore()
        for other in (self.sibling, self.across):
            pl.semaphore_signal(barrier, inc=1, device_id={"tensor": other}, device_id_type=pl.DeviceIdType.MESH)
        pl.semaphore_wait(barrier, 2)

    def slot(self, owner):
        return ((self.low + owner % 2) % 2) * 2 + (self.high + owner // 2) % 2

    def copy(self, kind, block, source, target, other):
        return pltpu.make_async_remote_copy(
            src_ref=source, dst_ref=target,
            send_sem=self.sems.at[kind, block, 0], recv_sem=self.sems.at[kind, block, 1],
            device_id={"tensor": other}, device_id_type=pl.DeviceIdType.MESH,
        )


def gather_copy(ring, kind, block, own, rows):
    if kind == AG_PASS:
        passed = rows.at[block, pl.ds(ring.across * SHARE, SHARE), :]
        return ring.copy(kind, block, passed, passed, ring.sibling)
    mine = own.at[pl.ds(block * SHARE, SHARE), :]
    place = rows.at[block, pl.ds(ring.me * SHARE, SHARE), :]
    return ring.copy(kind, block, mine, place, ring.sibling if kind == AG_OWN else ring.across)


def pair_copy(ring, block, parts, from_pair):
    return ring.copy(RS_PAIR, block, parts.at[block, pl.ds(2 * SHARE, 2 * SHARE), :], from_pair.at[block], ring.sibling)


def across_copy(ring, block, sums, from_across):
    return ring.copy(RS_ACROSS, block, sums.at[block], from_across.at[block], ring.across)


def store_parts(ring, block, part, parts):
    for owner in range(4):
        parts[block, pl.ds(ring.slot(owner) * SHARE, SHARE), :] = part[owner * SHARE : (owner + 1) * SHARE].astype(BF16)


def add_pair(block, parts, from_pair, sums):
    sums[block] = (
        parts[block, pl.ds(SHARE, SHARE), :].astype(F32) + from_pair[block, pl.ds(SHARE, SHARE), :].astype(F32)
    ).astype(BF16)


def add_all(block, parts, from_pair, from_across):
    return (
        parts[block, pl.ds(0, SHARE), :].astype(F32)
        + from_pair[block, pl.ds(0, SHARE), :].astype(F32)
        + from_across[block].astype(F32)
    )


def own_column(line, first_lane):
    lanes = lax.broadcasted_iota(jnp.int32, (SHARE, line.shape[1]), 1)
    rows = lax.broadcasted_iota(jnp.int32, (SHARE, line.shape[1]), 0)
    return jnp.sum(jnp.where(lanes == rows + first_lane, line, 0.0), axis=1, keepdims=True)


def forward_kernel(
    off_ref, own_ref, hid_ref, w_ref, taps_ref, head_ref, wide_ref, spread_ref, next_ref,
    rows_ref, z_ref, in_ref, pre_ref, dt_ref, y_ref, gg_ref, st_ref, hnext_ref, tot_ref, scale_ref, normed_ref,
    state, padded, rows, parts, from_pair, sums, from_across, sq_own, sq_pair, sq_sums, sq_across, sems,
):
    block = pl.program_id(0)
    inner = y_ref.shape[1]
    mixed = in_ref.shape[1]
    first, second = off_ref[0], off_ref[1]
    blocks = rows.shape[0]
    ring = Ring(sems)

    def sq_pair_copy(at):
        return ring.copy(SM_PAIR, at, sq_own.at[at], sq_pair.at[at], ring.sibling)

    def sq_across_copy(at):
        return ring.copy(SM_ACROSS, at, sq_sums.at[at], sq_across.at[at], ring.across)

    @pl.when(block == 0)
    def _():
        ring.greet()

        @pl.loop(0, blocks)
        def _(at):
            gather_copy(ring, AG_ACROSS, at, own_ref, rows).start()
            gather_copy(ring, AG_OWN, at, own_ref, rows).start()

        state[...] = jnp.zeros_like(state)
        padded[pl.ds(0, 8), :] = jnp.zeros((8, mixed), F32)

        @pl.loop(0, blocks)
        def _(at):
            rows[at, pl.ds(ring.me * SHARE, SHARE), :] = own_ref[pl.ds(at * SHARE, SHARE), :]

        gather_copy(ring, AG_ACROSS, 0, own_ref, rows).wait_recv()
        gather_copy(ring, AG_PASS, 0, own_ref, rows).start()

    gather_copy(ring, AG_OWN, block, own_ref, rows).wait_recv()
    gather_copy(ring, AG_PASS, block, own_ref, rows).wait_recv()
    here = rows[block]
    rows_ref[...] = here

    row_col, row_row, seg_col, seg_row = block_frame(block, first, second)
    seg_start = jnp.where(seg_col == 0, 0, jnp.where(seg_col == 1, first, second))
    within = row_col - seg_start
    product = dot_nn(here, w_ref[:, inner:])
    gate = product[:, :inner]
    mixed_in = product[:, inner : inner + mixed]
    dt_raw = product[:, inner + mixed :]
    z_ref[...] = gate
    in_ref[...] = mixed_in
    dt_ref[...] = dt_raw
    padded[pl.ds(8, BLK), :] = mixed_in
    taps = taps_ref[...]
    conv = taps[CONV : CONV + 1] + taps[CONV - 1 : CONV] * mixed_in
    for delay in range(1, CONV):
        shifted_in = padded[pl.ds(8 - delay, BLK), :]
        conv = conv + taps[CONV - 1 - delay : CONV - delay] * jnp.where(within >= delay, shifted_in, 0.0)
    padded[pl.ds(0, 8), :] = padded[pl.ds(BLK, 8), :]
    pre_ref[...] = conv
    mixed_low = (conv * sigmoid(conv)).astype(BF16)
    x_low = mixed_low[:, :inner]
    b_low = mixed_low[:, inner : inner + STATE]
    c_low = mixed_low[:, inner + STATE :]
    head = head_ref[...]
    spread = spread_ref[...]
    shifted, steps, cum2, entering, tail, retained = decay_parts(block, dt_raw, head, seg_col, first, second)
    cum_row = jnp.transpose(cum2)
    x_in = x_low.astype(F32)
    x_steps = spread_heads(steps, spread) * x_in
    x_steps_low = x_steps.astype(BF16)
    allowed = (seg_col == seg_row) & (row_col >= row_row)
    scores = jnp.where(allowed, dot_nt(c_low, b_low), 0.0)
    old_state = state[...]
    st_ref[0] = old_state
    carried = spread_heads(entering, spread) * dot_nn(c_low, old_state.astype(BF16))
    wide = wide_ref[...]
    pieces = []
    for pair in range(inner // LANES):
        columns = slice(pair * LANES, (pair + 1) * LANES)
        total = None
        for head_index in (2 * pair, 2 * pair + 1):
            gaps = cum2[:, head_index : head_index + 1] - cum_row[head_index : head_index + 1, :]
            coupling = (jnp.exp2(jnp.minimum(gaps, 0.0)) * scores).astype(BF16)
            term = dot_nn(coupling, head_half(x_steps_low[:, columns], head_index))
            total = term if total is None else total + term
        pieces.append(total)
    mixed_out = jnp.concatenate(pieces, axis=1) + carried + wide[0:1] * x_in
    tailed = (spread_heads(tail, spread) * x_steps).astype(BF16)
    keep = spread_heads(jnp.broadcast_to(retained, (8, LANES)), spread)[0:1]
    state[...] = old_state * keep + dot_tn(b_low, tailed)
    y_ref[...] = mixed_out
    gated = mixed_out * (gate * sigmoid(gate))
    gained = (gated * wide[1:2]).astype(BF16)
    gg_ref[...] = gained
    store_parts(ring, block, dot_nt(gained, w_ref[:, :inner]), parts)
    high, low = split_two(gated * gated)
    ones = jnp.ones((8, inner), BF16)
    sq_own[block] = dot_nt(ones, high) + dot_nt(ones, low)
    pair_copy(ring, block, parts, from_pair).start()
    sq_pair_copy(block).start()

    def second_stage(at):
        pair_copy(ring, at, parts, from_pair).wait_recv()
        sq_pair_copy(at).wait_recv()
        add_pair(at, parts, from_pair, sums)
        sq_sums[at] = sq_own[at] + sq_pair[at]
        across_copy(ring, at, sums, from_across).start()
        sq_across_copy(at).start()

    def last_stage(at):
        across_copy(ring, at, sums, from_across).wait_recv()
        sq_across_copy(at).wait_recv()
        total = add_all(at, parts, from_pair, from_across)
        squares = own_column((sq_sums[at] + sq_across[at])[0:1], ring.me * SHARE)
        scale = lax.rsqrt(squares / INNER + eps)
        here = pl.ds(at * SHARE, SHARE)
        hidden = hid_ref[here, :] + total * scale
        hnext_ref[here, :] = hidden
        tot_ref[here, :] = total
        scale_ref[here, :] = scale
        mean = jnp.sum(hidden * hidden, axis=1, keepdims=True) / hidden.shape[1]
        normed_ref[here, :] = (hidden * lax.rsqrt(mean + eps) * next_ref[0:1]).astype(BF16)

    @pl.when(block < blocks - 1)
    def _():
        gather_copy(ring, AG_ACROSS, block + 1, own_ref, rows).wait_recv()
        gather_copy(ring, AG_PASS, block + 1, own_ref, rows).start()

    @pl.when(block >= 1)
    def _():
        second_stage(block - 1)

    @pl.when(block >= 2)
    def _():
        last_stage(block - 2)

    @pl.when(block == blocks - 1)
    def _():
        second_stage(block)
        last_stage(block - 1)
        last_stage(block)

        @pl.loop(0, blocks)
        def _(at):
            for kind in (AG_OWN, AG_ACROSS, AG_PASS):
                gather_copy(ring, kind, at, own_ref, rows).wait_send()
            pair_copy(ring, at, parts, from_pair).wait_send()
            across_copy(ring, at, sums, from_across).wait_send()
            sq_pair_copy(at).wait_send()
            sq_across_copy(at).wait_send()


def backward_kernel(
    off_ref, own_ref, tw_ref, w_ref, taps_ref, head_ref, wide_ref, spread_ref,
    z_ref, in_ref, pre_ref, dt_ref, y_ref, st_ref,
    rows_ref, gnormed_ref, gproj_ref, gtaps_ref, ghead_ref, gwide_ref,
    dstate, padded, rows, parts, from_pair, sums, from_across, twice, sems,
):
    step = pl.program_id(0)
    block = pl.num_programs(0) - 1 - step
    inner = y_ref.shape[1]
    mixed = in_ref.shape[1]
    first, second = off_ref[0], off_ref[1]
    blocks = rows.shape[0]
    ring = Ring(sems)

    def twice_copies():
        return (
            ring.copy(SM_PAIR, 0, tw_ref, twice.at[ring.me], ring.sibling),
            ring.copy(SM_ACROSS, 0, tw_ref, twice.at[ring.me], ring.across),
            ring.copy(SM_PAIR, 1, twice.at[ring.across], twice.at[ring.across], ring.sibling),
        )

    @pl.when(step == 0)
    def _():
        ring.greet()
        to_sibling, to_across, onward = twice_copies()
        to_across.start()
        to_sibling.start()

        @pl.loop(0, blocks)
        def _(at):
            gather_copy(ring, AG_ACROSS, blocks - 1 - at, own_ref, rows).start()
            gather_copy(ring, AG_OWN, blocks - 1 - at, own_ref, rows).start()

        @pl.loop(0, blocks)
        def _(at):
            rows[at, pl.ds(ring.me * SHARE, SHARE), :] = own_ref[pl.ds(at * SHARE, SHARE), :]

        twice[ring.me] = tw_ref[...]
        to_across.wait_recv()
        onward.start()
        gather_copy(ring, AG_ACROSS, blocks - 1, own_ref, rows).wait_recv()
        gather_copy(ring, AG_PASS, blocks - 1, own_ref, rows).start()
        to_sibling.wait_recv()
        onward.wait_recv()
        dstate[...] = jnp.zeros_like(dstate)
        padded[pl.ds(BLK, 8), :] = jnp.zeros((8, mixed), F32)
        gtaps_ref[...] = jnp.zeros_like(gtaps_ref)
        ghead_ref[...] = jnp.zeros_like(ghead_ref)
        gwide_ref[...] = jnp.zeros_like(gwide_ref)

    gather_copy(ring, AG_OWN, block, own_ref, rows).wait_recv()
    gather_copy(ring, AG_PASS, block, own_ref, rows).wait_recv()
    here = rows[block]
    rows_ref[...] = here
    twice_here = jnp.concatenate([own_column(twice[owner, block][0:1], 0) for owner in range(4)], axis=0)
    row_col, row_row, seg_col, seg_row = block_frame(block, first, second)
    seg_end = jnp.where(seg_col == 0, first, jnp.where(seg_col == 1, second, pl.num_programs(0) * BLK))
    remaining = seg_end - row_col
    head = head_ref[...]
    wide = wide_ref[...]
    spread = spread_ref[...]
    skip, gain = wide[0:1], wide[1:2]
    gate = z_ref[...]
    mixed_out = y_ref[...]
    conv = pre_ref[...]
    gate_sig = sigmoid(gate)
    gate_silu = gate * gate_sig
    gated = mixed_out * gate_silu
    grad_scaled = dot_nn(here, w_ref[:, :inner])
    grad_gated = grad_scaled * gain + twice_here * gated
    grad_out = grad_gated * gate_silu
    grad_gate = grad_gated * mixed_out * (gate_sig * (1.0 + gate * (1.0 - gate_sig)))
    grad_out_low = grad_out.astype(BF16)

    conv_sig = sigmoid(conv)
    mixed_low = (conv * conv_sig).astype(BF16)
    x_low = mixed_low[:, :inner]
    b_low = mixed_low[:, inner : inner + STATE]
    c_low = mixed_low[:, inner + STATE :]
    x_in = x_low.astype(F32)
    shifted, steps, cum2, entering, tail, retained = decay_parts(block, dt_ref[...], head, seg_col, first, second)
    cum_row = jnp.transpose(cum2)
    steps_wide = spread_heads(steps, spread)
    x_steps_low = (steps_wide * x_in).astype(BF16)
    x_steps = x_steps_low.astype(F32)

    allowed = (seg_col == seg_row) & (row_col <= row_row)
    scores = jnp.where(allowed, dot_nt(b_low, c_low), 0.0)
    grad_scores = jnp.zeros((BLK, BLK), F32)
    pieces = []
    for pair in range(inner // LANES):
        columns = slice(pair * LANES, (pair + 1) * LANES)
        total = None
        for head_index in (2 * pair, 2 * pair + 1):
            gaps = cum_row[head_index : head_index + 1, :] - cum2[:, head_index : head_index + 1]
            decays = jnp.exp2(jnp.minimum(gaps, 0.0))
            coupling = (decays * scores).astype(BF16)
            term = dot_nn(coupling, head_half(grad_out_low[:, columns], head_index))
            total = term if total is None else total + term
            grad_scores = grad_scores + decays * dot_nt(
                head_half(x_steps_low[:, columns], head_index), grad_out_low[:, columns]
            )
        pieces.append(total)
    grad_scores_low = jnp.where(allowed, grad_scores, 0.0).astype(BF16)
    old_dstate = dstate[...]
    old_dstate_low = old_dstate.astype(BF16)
    old_state = st_ref[0]
    tail_wide = spread_heads(tail, spread)
    from_state = tail_wide * dot_nn(b_low, old_dstate_low)
    grad_unit = jnp.concatenate(pieces, axis=1) + from_state
    entered = (spread_heads(entering, spread) * grad_out).astype(BF16)
    tailed = (tail_wide * x_steps).astype(BF16)
    grad_c = dot_tn(grad_scores_low, b_low) + dot_nt(entered, old_state.astype(BF16))
    grad_b = dot_nn(grad_scores_low, c_low) + dot_nt(tailed, old_dstate_low)
    keep = spread_heads(jnp.broadcast_to(retained, (8, LANES)), spread)[0:1]
    dstate[...] = old_dstate * keep + dot_tn(c_low, entered)

    balance = gather_heads(grad_out_low.astype(F32) * (mixed_out - skip * x_in) - x_steps * grad_unit, spread)
    direct = gather_heads(x_in * grad_unit, spread)
    final_wide = jnp.sum(x_steps * from_state, axis=0, keepdims=True) + keep * jnp.sum(
        old_dstate * old_state, axis=0, keepdims=True
    )
    final = gather_heads(jnp.broadcast_to(final_wide, (8, inner)), spread)[0:1]
    above = lax.broadcasted_iota(jnp.int32, (BLK, BLK), 0)
    below = lax.broadcasted_iota(jnp.int32, (BLK, BLK), 1)
    upper = jnp.where(above <= below, 1.0, 0.0).astype(BF16)
    thirds = dot_nn(upper, jnp.concatenate(split_three(balance), axis=1))
    grad_log = thirds[:, :LANES] + thirds[:, LANES : 2 * LANES] + thirds[:, 2 * LANES :] + final
    grad_steps = direct + grad_log * head[1:2]
    grad_dt = grad_steps * sigmoid(shifted)
    ghead_ref[0:1, :] += jnp.sum(grad_dt, axis=0, keepdims=True)
    ghead_ref[1:2, :] += jnp.sum(grad_log * steps, axis=0, keepdims=True) * head[1:2]
    gwide_ref[0:1, :] += jnp.sum(grad_out * x_in, axis=0, keepdims=True)
    gwide_ref[1:2, :] += jnp.sum(grad_scaled * gated, axis=0, keepdims=True)

    grad_x = steps_wide * grad_unit + skip * grad_out
    grad_conv = jnp.concatenate([grad_x, grad_b, grad_c], axis=1) * (
        conv_sig * (1.0 + conv * (1.0 - conv_sig))
    )
    padded[pl.ds(0, BLK), :] = grad_conv
    mixed_in = in_ref[...]
    taps = taps_ref[...]
    grad_in = taps[CONV - 1 : CONV] * grad_conv
    gtaps_ref[CONV : CONV + 1, :] += jnp.sum(grad_conv, axis=0, keepdims=True)
    gtaps_ref[CONV - 1 : CONV, :] += jnp.sum(mixed_in * grad_conv, axis=0, keepdims=True)
    for delay in range(1, CONV):
        later = jnp.where(remaining > delay, padded[pl.ds(delay, BLK), :], 0.0)
        grad_in = grad_in + taps[CONV - 1 - delay : CONV - delay] * later
        gtaps_ref[CONV - 1 - delay : CONV - delay, :] += jnp.sum(mixed_in * later, axis=0, keepdims=True)
    padded[pl.ds(BLK, 8), :] = padded[pl.ds(0, 8), :]
    gproj = jnp.concatenate([grad_gate.astype(BF16), grad_in.astype(BF16), grad_dt.astype(BF16)], axis=1)
    gproj_ref[...] = gproj
    store_parts(ring, block, dot_nt(gproj, w_ref[:, inner:]), parts)
    pair_copy(ring, block, parts, from_pair).start()

    def second_stage(at):
        pair_copy(ring, at, parts, from_pair).wait_recv()
        add_pair(at, parts, from_pair, sums)
        across_copy(ring, at, sums, from_across).start()

    def last_stage(at):
        across_copy(ring, at, sums, from_across).wait_recv()
        gnormed_ref[pl.ds(at * SHARE, SHARE), :] = add_all(at, parts, from_pair, from_across)

    @pl.when(step < blocks - 1)
    def _():
        gather_copy(ring, AG_ACROSS, block - 1, own_ref, rows).wait_recv()
        gather_copy(ring, AG_PASS, block - 1, own_ref, rows).start()

    @pl.when(step >= 1)
    def _():
        second_stage(block + 1)

    @pl.when(step >= 2)
    def _():
        last_stage(block + 2)

    @pl.when(step == blocks - 1)
    def _():
        second_stage(block)
        last_stage(block + 1)
        last_stage(block)
        for copy in twice_copies():
            copy.wait_send()

        @pl.loop(0, blocks)
        def _(at):
            for kind in (AG_OWN, AG_ACROSS, AG_PASS):
                gather_copy(ring, kind, at, own_ref, rows).wait_send()
            pair_copy(ring, at, parts, from_pair).wait_send()
            across_copy(ring, at, sums, from_across).wait_send()


def whole(shape):
    return pl.BlockSpec(shape, lambda b: (0,) * len(shape))


def exchange_scratch(blocks, width):
    return [
        pltpu.VMEM((blocks, BLK, width), BF16),
        pltpu.VMEM((blocks, BLK, width), BF16),
        pltpu.VMEM((blocks, 2 * SHARE, width), BF16),
        pltpu.VMEM((blocks, SHARE, width), BF16),
        pltpu.VMEM((blocks, SHARE, width), BF16),
    ]


def layer_forward(offsets, own, hidden, weights, taps, head, wide, spread, next_gain):
    own_rows, width = own.shape
    count = 4 * own_rows
    inner, mixed = wide.shape[1], taps.shape[1]
    blocks = count // BLK
    total = weights.shape[1]

    def by_block(columns):
        return pl.BlockSpec((BLK, columns), lambda b: (b, 0))

    return pl.pallas_call(
        forward_kernel,
        grid=(blocks,),
        in_specs=[
            pl.BlockSpec(memory_space=pltpu.SMEM),
            whole((own_rows, width)), whole((own_rows, width)), whole((width, total)), whole((8, mixed)),
            whole((8, LANES)), whole((8, inner)), whole((2 * LANES, inner)), whole((8, width)),
        ],
        out_specs=[
            by_block(width), by_block(inner), by_block(mixed), by_block(mixed),
            by_block(LANES), by_block(inner), by_block(inner),
            pl.BlockSpec((1, STATE, inner), lambda b: (b, 0, 0)),
            whole((own_rows, width)), whole((own_rows, width)), whole((own_rows, 1)), whole((own_rows, width)),
        ],
        out_shape=[
            jax.ShapeDtypeStruct((count, width), BF16),
            jax.ShapeDtypeStruct((count, inner), F32),
            jax.ShapeDtypeStruct((count, mixed), F32),
            jax.ShapeDtypeStruct((count, mixed), F32),
            jax.ShapeDtypeStruct((count, LANES), F32),
            jax.ShapeDtypeStruct((count, inner), F32),
            jax.ShapeDtypeStruct((count, inner), BF16),
            jax.ShapeDtypeStruct((blocks, STATE, inner), F32),
            jax.ShapeDtypeStruct((own_rows, width), F32),
            jax.ShapeDtypeStruct((own_rows, width), F32),
            jax.ShapeDtypeStruct((own_rows, 1), F32),
            jax.ShapeDtypeStruct((own_rows, width), BF16),
        ],
        scratch_shapes=[pltpu.VMEM((STATE, inner), F32), pltpu.VMEM((BLK + 8, mixed), F32)]
        + exchange_scratch(blocks, width)
        + [pltpu.VMEM((blocks, 8, BLK), F32)] * 4
        + [pltpu.SemaphoreType.DMA((7, blocks, 2))],
        compiler_params=pltpu.CompilerParams(
            vmem_limit_bytes=56 * 1024 * 1024, collective_id=1, has_side_effects=True
        ),
        name="layer_forward",
    )(offsets, own, hidden, weights, taps, head, wide, spread, next_gain)


def layer_backward(offsets, own, twice, weights, taps, head, wide, spread, saved):
    gate, mixed_in, conv, dt_raw, mixed_out, states = saved
    own_rows, width = own.shape
    count = 4 * own_rows
    inner, mixed = wide.shape[1], taps.shape[1]
    blocks = count // BLK
    total = weights.shape[1]

    def by_block(columns):
        return pl.BlockSpec((BLK, columns), lambda b: (blocks - 1 - b, 0))

    return pl.pallas_call(
        backward_kernel,
        grid=(blocks,),
        in_specs=[
            pl.BlockSpec(memory_space=pltpu.SMEM),
            whole((own_rows, width)), whole((blocks, 8, LANES)), whole((width, total)), whole((8, mixed)),
            whole((8, LANES)), whole((8, inner)), whole((2 * LANES, inner)),
            by_block(inner), by_block(mixed), by_block(mixed), by_block(LANES), by_block(inner),
            pl.BlockSpec((1, STATE, inner), lambda b: (blocks - 1 - b, 0, 0)),
        ],
        out_specs=[
            by_block(width), whole((own_rows, width)), by_block(total - inner),
            whole((8, mixed)), whole((8, LANES)), whole((8, inner)),
        ],
        out_shape=[
            jax.ShapeDtypeStruct((count, width), BF16),
            jax.ShapeDtypeStruct((own_rows, width), F32),
            jax.ShapeDtypeStruct((count, total - inner), BF16),
            jax.ShapeDtypeStruct((8, mixed), F32),
            jax.ShapeDtypeStruct((8, LANES), F32),
            jax.ShapeDtypeStruct((8, inner), F32),
        ],
        scratch_shapes=[pltpu.VMEM((STATE, inner), F32), pltpu.VMEM((BLK + 8, mixed), F32)]
        + exchange_scratch(blocks, width)
        + [pltpu.VMEM((4, blocks, 8, LANES), F32)]
        + [pltpu.SemaphoreType.DMA((7, blocks, 2))],
        compiler_params=pltpu.CompilerParams(
            vmem_limit_bytes=56 * 1024 * 1024, collective_id=2, has_side_effects=True
        ),
        name="layer_backward",
    )(offsets, own, twice, weights, taps, head, wide, spread, gate, mixed_in, conv, dt_raw, mixed_out, states)


def spread_matrix(inner, heads):
    lane_head = lax.broadcasted_iota(jnp.int32, (2 * LANES, inner), 1) // (inner // heads)
    row_head = lax.broadcasted_iota(jnp.int32, (2 * LANES, inner), 0) % LANES
    return jnp.where(lane_head == row_head, 1.0, 0.0).astype(BF16)


def pre_norm(hidden, gain_full):
    return hidden * lax.rsqrt(jnp.mean(hidden * hidden, axis=-1, keepdims=True) + eps) * gain_full


def pad_to(values, rows, columns):
    return jnp.pad(values, ((0, rows - values.shape[0]), (0, columns - values.shape[1])))


def on_device(
    tokens, cotangent, lengths, packing, pre_gain, w_z, w_x, w_bc, w_dt, conv_x, conv_bc, head_params, norm_gain, w_out,
):
    dp_count = lax.axis_size("dp")
    bin_index = lax.axis_index("dp")
    seq_total, pos_here, cols_here = tokens.shape
    inner_part = conv_x.shape[2]
    heads_here = head_params.shape[2]
    dp_rows = w_z.shape[1]
    mixed = inner_part + 2 * STATE
    triples = lengths[packing].reshape(dp_count, 3)
    offsets = jnp.cumsum(triples, axis=1) - triples
    my_offsets = offsets[bin_index]
    my_lengths = triples[bin_index]
    bounds = my_offsets[1:3]
    bin_rows = jnp.arange(BIN, dtype=jnp.int32)
    segment = segment_of(bin_rows, my_offsets[1], my_offsets[2])
    seg_start = jnp.where(segment == 0, my_offsets[0], jnp.where(segment == 1, my_offsets[1], my_offsets[2]))
    within = bin_rows - seg_start
    pick_rows = (within // pos_here * 3 + segment) * pos_here + within % pos_here
    blocks = BIN // BLK
    pick_rows = jnp.swapaxes(pick_rows.reshape(blocks, 4, SHARE), 0, 1).reshape(-1)
    groups = packing.reshape(dp_count, 3)

    def to_bins(given):
        arrived = lax.all_to_all(given[groups], "dp", split_axis=0, concat_axis=0, tiled=True)
        flat = arrived.reshape(-1, cols_here)[pick_rows]
        return lax.all_to_all(flat, "tensor", split_axis=0, concat_axis=1, tiled=True)

    spread = spread_matrix(inner_part, heads_here)
    gains = lax.all_gather(pre_gain, "dp", axis=1, tiled=True).astype(F32)
    packs = []
    for layer in range(LAYERS):
        own = jnp.concatenate(
            [w_out[layer].T, w_z[layer], w_x[layer], w_bc[layer], pad_to(w_dt[layer], dp_rows, LANES)], axis=1
        )
        taps = jnp.concatenate([conv_x[layer], conv_bc[layer]], axis=1).astype(F32)
        head = jnp.stack([head_params[layer, 0], -jnp.exp(head_params[layer, 1])])
        wide = jnp.stack(
            [jnp.repeat(head_params[layer, 2], inner_part // heads_here), norm_gain[layer].astype(F32)]
        )
        packs.append((own, pad_to(taps, 8, mixed), pad_to(head, 8, LANES), pad_to(wide, 8, inner_part)))

    row_tokens = to_bins(tokens)
    hidden = row_tokens.astype(F32)
    records = []
    for layer in range(LAYERS):
        own, taps, head, wide = packs[layer]
        weights = lax.all_gather(own, "dp", axis=0, tiled=True)
        before = hidden
        if layer == 0:
            normed = pre_norm(hidden, gains[layer]).astype(BF16)
        rows, gate, mixed_in, conv, dt_raw, mixed_out, gained, states, hidden, total, scale, normed = layer_forward(
            bounds, normed, hidden, weights, taps, head, wide, spread,
            jnp.broadcast_to(gains[min(layer + 1, LAYERS - 1)], (8, gains.shape[1])),
        )
        saved = (gate, mixed_in, conv, dt_raw, mixed_out, states)
        records.append((before, rows, weights, gained, total, scale, saved))
    final_rows = hidden.astype(BF16)

    grad_hidden = to_bins(cotangent).astype(F32)
    collected = [None] * LAYERS
    for layer in reversed(range(LAYERS)):
        own, taps, head, wide = packs[layer]
        before, rows, weights, gained, total, scale, saved = records[layer]
        normed, norm_back = jax.vjp(pre_norm, before, gains[layer])
        grad_branch = grad_hidden.astype(BF16).astype(F32)
        twice = 2.0 * (-(scale**3) / (2 * INNER)) * jnp.sum(grad_branch * total, axis=1, keepdims=True)
        twice_rows = jnp.broadcast_to(pad_to(twice.reshape(blocks, SHARE), blocks, LANES)[:, None], (blocks, 8, LANES))
        spread_grad, grad_normed, gproj, gtaps, ghead, gwide = layer_backward(
            bounds, (grad_branch * scale).astype(BF16), twice_rows, weights, taps, head, wide, spread, saved
        )
        grad_weights = jnp.concatenate(
            [dot_tn(spread_grad, gained).astype(BF16), dot_tn(rows, gproj).astype(BF16)], axis=1
        )
        own_weights = lax.psum_scatter(grad_weights, "dp", scatter_dimension=0, tiled=True)
        grad_before, grad_gain = norm_back(grad_normed)
        grad_hidden = grad_hidden + grad_before
        collected[layer] = (own_weights, grad_gain, gtaps, ghead, gwide)

    heads_first = (
        jnp.stack([item[2][: CONV + 1, :inner_part] for item in collected]),
        jnp.stack(
            [
                jnp.concatenate(
                    [item[3][:2, :heads_here], jnp.sum(item[4][0:1].reshape(1, heads_here, -1), axis=2)], axis=0
                )
                for item in collected
            ]
        ),
        jnp.stack([item[4][1] for item in collected]),
    )
    shared = (
        jnp.stack([item[2][: CONV + 1, inner_part:] for item in collected]),
        jnp.stack([item[1] for item in collected]),
    )
    grad_convx, grad_head, grad_norm, shared_convbc, shared_pre = lax.psum(heads_first + shared, "dp")
    own_weights = jnp.stack([item[0] for item in collected])
    shared_bc = own_weights[:, :, 3 * inner_part : 3 * inner_part + 2 * STATE].astype(F32)
    grad_convbc, grad_pre, grad_bc = lax.psum((shared_convbc, shared_pre, shared_bc), "tensor")
    shard_pre = lax.dynamic_slice_in_dim(grad_pre, bin_index * dp_rows, dp_rows, 1)
    own_weights = own_weights.astype(F32)
    grad_out = jnp.swapaxes(own_weights[:, :, :inner_part], 1, 2)
    grad_z = own_weights[:, :, inner_part : 2 * inner_part]
    grad_x = own_weights[:, :, 2 * inner_part : 3 * inner_part]
    grad_dt = own_weights[:, :, 3 * inner_part + 2 * STATE : 3 * inner_part + 2 * STATE + heads_here]

    dev_grid = jnp.arange(dp_count, dtype=jnp.int32)[:, None, None]
    pos_grid = jnp.arange(pos_here, dtype=jnp.int32)[None, None, :]
    seq_pos = dev_grid * pos_here + pos_grid
    live_slot = (seq_pos < my_lengths[None, :, None]).reshape(-1, 1)
    source = jnp.minimum(my_offsets[None, :, None] + seq_pos, BIN - 1).reshape(-1)
    source = (source % BLK // SHARE) * (BIN // 4) + source // BLK * SHARE + source % SHARE
    rank_of = jnp.zeros_like(packing).at[packing].set(jnp.arange(seq_total, dtype=jnp.int32))

    def from_bins(rows):
        columns = lax.all_to_all(rows, "tensor", split_axis=1, concat_axis=0, tiled=True)
        slots = jnp.where(live_slot, columns[source], 0).reshape(dp_count, 3, pos_here, cols_here)
        returned = lax.all_to_all(slots, "dp", split_axis=0, concat_axis=0, tiled=True)
        return returned.reshape(seq_total, pos_here, cols_here)[rank_of]

    activations = from_bins(final_rows)
    input_grad = from_bins(grad_hidden.astype(BF16))
    return (
        activations, input_grad, shard_pre, grad_z, grad_x, grad_bc, grad_dt,
        grad_convx, grad_convbc, grad_head, grad_norm, grad_out,
    )


def solution(mesh):
    placed = (
        P(None, "dp", "tensor"), P(None, "dp", "tensor"), P(), P(), P(None, "dp"),
        P(None, "dp", "tensor"), P(None, "dp", "tensor"), P(None, "dp", None), P(None, "dp", "tensor"),
        P(None, None, "tensor"), P(), P(None, None, "tensor"), P(None, "tensor"), P(None, "tensor", "dp"),
    )
    results = (
        P(None, "dp", "tensor"), P(None, "dp", "tensor"), P(None, "dp"),
        P(None, "dp", "tensor"), P(None, "dp", "tensor"), P(None, "dp", None), P(None, "dp", "tensor"),
        P(None, None, "tensor"), P(), P(None, None, "tensor"), P(None, "tensor"), P(None, "tensor", "dp"),
    )
    return jax.shard_map(on_device, mesh=mesh, in_specs=placed, out_specs=results, check_vma=False)
```

```python
import functools
import jax
import jax.numpy as jnp
from jax import lax
from jax.experimental import pallas as pl
from jax.experimental.pallas import tpu as pltpu
from jax.sharding import PartitionSpec as P

CONV = 4
INNER = 2048
LAYERS = 2
BIN = 2048
eps = 1e-05
STATE = 128
BLK = 256
LANES = 128
LOG2E = 1.4426950408889634
F32 = jnp.float32
BF16 = jnp.bfloat16


def dot_nn(left, right):
    return lax.dot_general(left, right, (((1,), (0,)), ((), ())), preferred_element_type=F32)


def dot_nt(left, right):
    return lax.dot_general(left, right, (((1,), (1,)), ((), ())), preferred_element_type=F32)


def dot_tn(left, right):
    return lax.dot_general(left, right, (((0,), (0,)), ((), ())), preferred_element_type=F32)


def split_two(values):
    high = values.astype(BF16)
    return high, (values - high.astype(F32)).astype(BF16)


def split_three(values):
    high = values.astype(BF16)
    rest = values - high.astype(F32)
    middle = rest.astype(BF16)
    return high, middle, (rest - middle.astype(F32)).astype(BF16)


def spread_heads(values, spread):
    high, low = split_two(values)
    return dot_nn(jnp.concatenate([high, low], axis=1), spread)


def gather_heads(values, spread):
    high, low = split_two(values)
    half = spread[:LANES]
    return dot_nt(high, half) + dot_nt(low, half)


def sigmoid(values):
    return 0.5 * jnp.tanh(0.5 * values) + 0.5


def softplus(values):
    return jnp.maximum(values, 0.0) + jnp.log1p(jnp.exp(-jnp.abs(values)))


def segment_of(rows, first, second):
    return (rows >= first).astype(jnp.int32) + (rows >= second).astype(jnp.int32)


def block_frame(block, first, second):
    row_col = block * BLK + lax.broadcasted_iota(jnp.int32, (BLK, 1), 0)
    row_row = block * BLK + lax.broadcasted_iota(jnp.int32, (1, BLK), 1)
    return row_col, row_row, segment_of(row_col, first, second), segment_of(row_row, first, second)


def decay_parts(block, dt_raw, head, seg_col, first, second):
    shifted = dt_raw + head[0:1]
    steps = softplus(shifted)
    log_decay = steps * head[1:2]
    above = lax.broadcasted_iota(jnp.int32, (BLK, BLK), 0)
    below = lax.broadcasted_iota(jnp.int32, (BLK, BLK), 1)
    lower = jnp.where(above >= below, 1.0, 0.0).astype(BF16)
    parts = dot_nn(lower, jnp.concatenate(split_three(log_decay), axis=1))
    cumulative = parts[:, :LANES] + parts[:, LANES : 2 * LANES] + parts[:, 2 * LANES :]
    cum2 = cumulative * LOG2E
    final2 = cum2[BLK - 1 : BLK]
    last_seg = segment_of(block * BLK + BLK - 1, first, second)
    prior_seg = jnp.where(block == 0, -1, segment_of(block * BLK - 1, first, second))
    entering = jnp.where(seg_col == prior_seg, jnp.exp2(cum2), 0.0)
    tail = jnp.where(seg_col == last_seg, jnp.exp2(final2 - cum2), 0.0)
    retained = jnp.where(last_seg == prior_seg, jnp.exp2(final2), 0.0)
    return shifted, steps, cum2, entering, tail, retained


def head_half(pair, head):
    lanes = lax.broadcasted_iota(jnp.int32, pair.shape, 1)
    keep = (lanes < LANES // 2) if head % 2 == 0 else (lanes >= LANES // 2)
    return jnp.where(keep, pair, jnp.zeros_like(pair))


SHARE = BLK // 4
AG_OWN, AG_ACROSS, AG_PASS, RS_PAIR, RS_ACROSS, SM_PAIR, SM_ACROSS = range(7)


class Ring:
    def __init__(self, sems):
        me = lax.axis_index("tensor")
        self.low, self.high = me % 2, me // 2
        self.me = me
        self.sibling = self.high * 2 + (1 - self.low)
        self.across = (1 - self.high) * 2 + self.low
        self.beyond = (1 - self.high) * 2 + (1 - self.low)
        self.sems = sems

    def greet(self):
        barrier = pltpu.get_barrier_semaphore()
        for other in (self.sibling, self.across, self.beyond):
            pl.semaphore_signal(barrier, inc=1, device_id={"tensor": other}, device_id_type=pl.DeviceIdType.MESH)
        pl.semaphore_wait(barrier, greet_dp(barrier) + 3)

    def slot(self, owner):
        return ((self.low + owner % 2) % 2) * 2 + (self.high + owner // 2) % 2

    def copy(self, kind, block, source, target, other):
        return pltpu.make_async_remote_copy(
            src_ref=source, dst_ref=target,
            send_sem=self.sems.at[kind, block, 0], recv_sem=self.sems.at[kind, block, 1],
            device_id={"tensor": other}, device_id_type=pl.DeviceIdType.MESH,
        )


def greet_dp(barrier):
    count, me = lax.axis_size("dp"), lax.axis_index("dp")

    @pl.loop(1, count)
    def _(step):
        pl.semaphore_signal(
            barrier, inc=1, device_id={"dp": (me + step) % count}, device_id_type=pl.DeviceIdType.MESH
        )

    return count - 1


class BinExchange:
    def __init__(self, to_bins, source, target, sems):
        self.to_bins, self.source, self.target, self.sems = to_bins, source, target, sems
        self.count, self.me = lax.axis_size("dp"), lax.axis_index("dp")
        self.span = source.shape[2] if to_bins else target.shape[2]

    def pieces(self, other):
        if self.to_bins:
            return self.source.at[other], self.target.at[:, pl.ds(self.me * self.span, self.span), :]
        return self.source.at[:, pl.ds(other * self.span, self.span), :], self.target.at[self.me]

    def remote(self, step, other):
        source, target = self.pieces(other)
        return pltpu.make_async_remote_copy(
            src_ref=source, dst_ref=target, send_sem=self.sems.at[step, 0], recv_sem=self.sems.at[step, 1],
            device_id={"dp": other}, device_id_type=pl.DeviceIdType.MESH,
        )

    def local(self):
        source, target = self.pieces(self.me)
        return pltpu.make_async_copy(source, target, self.sems.at[0, 0])

    def start(self):
        self.local().start()

        @pl.loop(1, self.count)
        def _(step):
            self.remote(step, (self.me + step) % self.count).start()

    def wait(self):
        self.local().wait()

        @pl.loop(1, self.count)
        def _(step):
            self.remote(step, (self.me + step) % self.count).wait()


class RowExchange:
    def __init__(self, to_rows, source, target, sems):
        self.to_rows, self.source, self.target, self.sems = to_rows, source, target, sems
        self.me = lax.axis_index("tensor")
        self.columns = source.shape[2] if to_rows else target.shape[2]

    def pieces(self, other):
        if self.to_rows:
            return (
                self.source.at[:, pl.ds(other * SHARE, SHARE), :],
                self.target.at[:, :, pl.ds(pl.multiple_of(self.me * self.columns, LANES), self.columns)],
            )
        return (
            self.source.at[:, :, pl.ds(pl.multiple_of(other * self.columns, LANES), self.columns)],
            self.target.at[:, pl.ds(self.me * SHARE, SHARE), :],
        )

    def remote(self, step):
        other = (self.me + step) % 4
        source, target = self.pieces(other)
        return pltpu.make_async_remote_copy(
            src_ref=source, dst_ref=target, send_sem=self.sems.at[step, 0], recv_sem=self.sems.at[step, 1],
            device_id={"tensor": other}, device_id_type=pl.DeviceIdType.MESH,
        )

    def local(self):
        source, target = self.pieces(self.me)
        return pltpu.make_async_copy(source, target, self.sems.at[0, 0])

    def start(self):
        self.local().start()
        for step in range(1, 4):
            self.remote(step).start()

    def wait(self):
        self.local().wait()
        for step in range(1, 4):
            self.remote(step).wait()


def row_place(rows, member):
    return rows.at[:, pl.ds(member * SHARE, SHARE), :]


def column_place(rows, member):
    columns = rows.shape[2] // 4
    return rows.at[:, :, pl.ds(pl.multiple_of(member * columns, LANES), columns)]


def gather_copy(ring, kind, block, own, rows, place):
    if kind == AG_PASS:
        passed = place(rows, ring.across).at[block]
        return ring.copy(kind, block, passed, passed, ring.sibling)
    other = ring.sibling if kind == AG_OWN else ring.across
    return ring.copy(kind, block, own.at[block], place(rows, ring.me).at[block], other)


def pair_copy(ring, block, parts, from_pair):
    return ring.copy(RS_PAIR, block, parts.at[block, pl.ds(2 * SHARE, 2 * SHARE), :], from_pair.at[block], ring.sibling)


def across_copy(ring, block, sums, from_across):
    return ring.copy(RS_ACROSS, block, sums.at[block], from_across.at[block], ring.across)


def store_parts(ring, block, part, parts):
    for owner in range(4):
        parts[block, pl.ds(ring.slot(owner) * SHARE, SHARE), :] = part[owner * SHARE : (owner + 1) * SHARE].astype(BF16)


def add_pair(block, parts, from_pair, sums):
    sums[block] = (
        parts[block, pl.ds(SHARE, SHARE), :].astype(F32) + from_pair[block, pl.ds(SHARE, SHARE), :].astype(F32)
    ).astype(BF16)


def add_all(block, parts, from_pair, from_across):
    return (
        parts[block, pl.ds(0, SHARE), :].astype(F32)
        + from_pair[block, pl.ds(0, SHARE), :].astype(F32)
        + from_across[block].astype(F32)
    )


def own_column(line, first_lane):
    lanes = lax.broadcasted_iota(jnp.int32, (SHARE, line.shape[1]), 1)
    rows = lax.broadcasted_iota(jnp.int32, (SHARE, line.shape[1]), 0)
    return jnp.sum(jnp.where(lanes == rows + first_lane, line, 0.0), axis=1, keepdims=True)


def forward_kernel(
    from_columns, make_side,
    off_ref, own_ref, hid_ref, w_ref, taps_ref, head_ref, wide_ref, spread_ref, gains_ref, side_in_ref,
    rows_ref, z_ref, in_ref, pre_ref, dt_ref, y_ref, gg_ref, st_ref, hnext_ref, tot_ref, scale_ref, normed_ref,
    side_out_ref,
    state, padded, rows, parts, from_pair, sums, from_across, sq_own, sq_pair, sq_sums, sq_across, sems, *side_scratch,
):
    place = column_place if from_columns else row_place
    side = make_side(off_ref, side_in_ref, side_out_ref, *side_scratch)
    block = pl.program_id(0)
    inner = y_ref.shape[1]
    mixed = in_ref.shape[1]
    first, second = off_ref[0], off_ref[1]
    blocks = rows.shape[0]
    ring = Ring(sems)

    def sq_pair_copy(at):
        return ring.copy(SM_PAIR, at, sq_own.at[at], sq_pair.at[at], ring.sibling)

    def sq_across_copy(at):
        return ring.copy(SM_ACROSS, at, sq_sums.at[at], sq_across.at[at], ring.across)

    def own_copy():
        return pltpu.make_async_copy(own_ref, place(rows, ring.me), sems.at[SM_PAIR, blocks, 0])

    @pl.when(block == 0)
    def _():
        own_copy().start()
        ring.greet()

        @pl.loop(0, blocks)
        def _(at):
            gather_copy(ring, AG_ACROSS, at, own_ref, rows, place).start()
            gather_copy(ring, AG_OWN, at, own_ref, rows, place).start()

        side.start()

        state[...] = jnp.zeros_like(state)
        padded[pl.ds(0, 8), :] = jnp.zeros((8, mixed), F32)
        own_copy().wait()
        gather_copy(ring, AG_ACROSS, 0, own_ref, rows, place).wait_recv()
        gather_copy(ring, AG_PASS, 0, own_ref, rows, place).start()

    gather_copy(ring, AG_OWN, block, own_ref, rows, place).wait_recv()
    gather_copy(ring, AG_PASS, block, own_ref, rows, place).wait_recv()
    here = rows[block]
    gains = gains_ref[...]
    if from_columns:
        raw = here.astype(F32)
        mean = jnp.sum(raw * raw, axis=1, keepdims=True) / raw.shape[1]
        here = (raw * lax.rsqrt(mean + eps) * gains[1:2]).astype(BF16)
    rows_ref[...] = here
    row_col, row_row, seg_col, seg_row = block_frame(block, first, second)
    seg_start = jnp.where(seg_col == 0, 0, jnp.where(seg_col == 1, first, second))
    within = row_col - seg_start
    product = dot_nn(here, w_ref[:, inner:])
    gate = product[:, :inner]
    mixed_in = product[:, inner : inner + mixed]
    dt_raw = product[:, inner + mixed :]
    z_ref[...] = gate
    in_ref[...] = mixed_in
    dt_ref[...] = dt_raw
    padded[pl.ds(8, BLK), :] = mixed_in
    taps = taps_ref[...]
    conv = taps[CONV : CONV + 1] + taps[CONV - 1 : CONV] * mixed_in
    for delay in range(1, CONV):
        shifted_in = padded[pl.ds(8 - delay, BLK), :]
        conv = conv + taps[CONV - 1 - delay : CONV - delay] * jnp.where(within >= delay, shifted_in, 0.0)
    padded[pl.ds(0, 8), :] = padded[pl.ds(BLK, 8), :]
    pre_ref[...] = conv
    mixed_low = (conv * sigmoid(conv)).astype(BF16)
    x_low = mixed_low[:, :inner]
    b_low = mixed_low[:, inner : inner + STATE]
    c_low = mixed_low[:, inner + STATE :]
    head = head_ref[...]
    spread = spread_ref[...]
    shifted, steps, cum2, entering, tail, retained = decay_parts(block, dt_raw, head, seg_col, first, second)
    cum_row = jnp.transpose(cum2)
    x_in = x_low.astype(F32)
    x_steps = spread_heads(steps, spread) * x_in
    x_steps_low = x_steps.astype(BF16)
    allowed = (seg_col == seg_row) & (row_col >= row_row)
    scores = jnp.where(allowed, dot_nt(c_low, b_low), 0.0)
    old_state = state[...]
    st_ref[0] = old_state
    carried = spread_heads(entering, spread) * dot_nn(c_low, old_state.astype(BF16))
    wide = wide_ref[...]
    pieces = []
    for pair in range(inner // LANES):
        columns = slice(pair * LANES, (pair + 1) * LANES)
        total = None
        for head_index in (2 * pair, 2 * pair + 1):
            gaps = cum2[:, head_index : head_index + 1] - cum_row[head_index : head_index + 1, :]
            coupling = (jnp.exp2(jnp.minimum(gaps, 0.0)) * scores).astype(BF16)
            term = dot_nn(coupling, head_half(x_steps_low[:, columns], head_index))
            total = term if total is None else total + term
        pieces.append(total)
    mixed_out = jnp.concatenate(pieces, axis=1) + carried + wide[0:1] * x_in
    tailed = (spread_heads(tail, spread) * x_steps).astype(BF16)
    keep = spread_heads(jnp.broadcast_to(retained, (8, LANES)), spread)[0:1]
    state[...] = old_state * keep + dot_tn(b_low, tailed)
    y_ref[...] = mixed_out
    gated = mixed_out * (gate * sigmoid(gate))
    gained = (gated * wide[1:2]).astype(BF16)
    gg_ref[...] = gained
    store_parts(ring, block, dot_nt(gained, w_ref[:, :inner]), parts)
    high, low = split_two(gated * gated)
    ones = jnp.ones((8, inner), BF16)
    sq_own[block] = dot_nt(ones, high) + dot_nt(ones, low)
    pair_copy(ring, block, parts, from_pair).start()
    sq_pair_copy(block).start()

    def second_stage(at):
        pair_copy(ring, at, parts, from_pair).wait_recv()
        sq_pair_copy(at).wait_recv()
        add_pair(at, parts, from_pair, sums)
        sq_sums[at] = sq_own[at] + sq_pair[at]
        across_copy(ring, at, sums, from_across).start()
        sq_across_copy(at).start()

    def last_stage(at):
        across_copy(ring, at, sums, from_across).wait_recv()
        sq_across_copy(at).wait_recv()
        total = add_all(at, parts, from_pair, from_across)
        squares = own_column((sq_sums[at] + sq_across[at])[0:1], ring.me * SHARE)
        scale = lax.rsqrt(squares / INNER + eps)
        here = pl.ds(at * SHARE, SHARE)
        if from_columns:
            before = rows[at, pl.ds(ring.me * SHARE, SHARE), :].astype(F32)
            hid_ref[here, :] = before
        else:
            before = hid_ref[here, :]
        hidden = before + total * scale
        hnext_ref[here, :] = hidden
        tot_ref[here, :] = total
        scale_ref[here, :] = scale
        mean = jnp.sum(hidden * hidden, axis=1, keepdims=True) / hidden.shape[1]
        normed_ref[here, :] = (hidden * lax.rsqrt(mean + eps) * gains[0:1]).astype(BF16)

    side.during(block)

    @pl.when(block < blocks - 1)
    def _():
        gather_copy(ring, AG_ACROSS, block + 1, own_ref, rows, place).wait_recv()
        gather_copy(ring, AG_PASS, block + 1, own_ref, rows, place).start()

    @pl.when(block >= 1)
    def _():
        second_stage(block - 1)

    @pl.when(block == blocks - 1)
    def _():
        second_stage(block)

        @pl.loop(0, blocks)
        def _(at):
            last_stage(at)
            for kind in (AG_OWN, AG_ACROSS, AG_PASS):
                gather_copy(ring, kind, at, own_ref, rows, place).wait_send()
            pair_copy(ring, at, parts, from_pair).wait_send()
            across_copy(ring, at, sums, from_across).wait_send()
            sq_pair_copy(at).wait_send()
            sq_across_copy(at).wait_send()

        side.finish()


def backward_kernel(
    make_side,
    off_ref, own_ref, tw_ref, w_ref, taps_ref, head_ref, wide_ref, spread_ref,
    z_ref, in_ref, pre_ref, dt_ref, y_ref, st_ref, side_in_ref,
    rows_ref, gnormed_ref, gproj_ref, gtaps_ref, ghead_ref, gwide_ref, side_out_ref,
    dstate, padded, rows, parts, from_pair, sums, from_across, twice, sems, *side_scratch,
):
    place = row_place
    side = make_side(off_ref, side_in_ref, side_out_ref, *side_scratch)
    step = pl.program_id(0)
    block = pl.num_programs(0) - 1 - step
    inner = y_ref.shape[1]
    mixed = in_ref.shape[1]
    first, second = off_ref[0], off_ref[1]
    blocks = rows.shape[0]
    ring = Ring(sems)

    def twice_copies():
        return (
            ring.copy(SM_PAIR, 0, tw_ref, twice.at[ring.me], ring.sibling),
            ring.copy(SM_ACROSS, 0, tw_ref, twice.at[ring.me], ring.across),
            ring.copy(SM_PAIR, 1, twice.at[ring.across], twice.at[ring.across], ring.sibling),
        )

    def own_copy():
        return pltpu.make_async_copy(own_ref, place(rows, ring.me), sems.at[SM_PAIR, blocks, 0])

    @pl.when(step == 0)
    def _():
        own_copy().start()
        ring.greet()
        to_sibling, to_across, onward = twice_copies()
        to_across.start()
        to_sibling.start()

        @pl.loop(0, blocks)
        def _(at):
            gather_copy(ring, AG_ACROSS, blocks - 1 - at, own_ref, rows, place).start()
            gather_copy(ring, AG_OWN, blocks - 1 - at, own_ref, rows, place).start()

        side.start()
        twice[ring.me] = tw_ref[...]
        own_copy().wait()
        to_across.wait_recv()
        onward.start()
        gather_copy(ring, AG_ACROSS, blocks - 1, own_ref, rows, place).wait_recv()
        gather_copy(ring, AG_PASS, blocks - 1, own_ref, rows, place).start()
        to_sibling.wait_recv()
        onward.wait_recv()
        dstate[...] = jnp.zeros_like(dstate)
        padded[pl.ds(BLK, 8), :] = jnp.zeros((8, mixed), F32)
        gtaps_ref[...] = jnp.zeros_like(gtaps_ref)
        ghead_ref[...] = jnp.zeros_like(ghead_ref)
        gwide_ref[...] = jnp.zeros_like(gwide_ref)

    gather_copy(ring, AG_OWN, block, own_ref, rows, place).wait_recv()
    gather_copy(ring, AG_PASS, block, own_ref, rows, place).wait_recv()
    here = rows[block]
    rows_ref[...] = here
    twice_here = jnp.concatenate([own_column(twice[owner, block][0:1], 0) for owner in range(4)], axis=0)
    row_col, row_row, seg_col, seg_row = block_frame(block, first, second)
    seg_end = jnp.where(seg_col == 0, first, jnp.where(seg_col == 1, second, pl.num_programs(0) * BLK))
    remaining = seg_end - row_col
    head = head_ref[...]
    wide = wide_ref[...]
    spread = spread_ref[...]
    skip, gain = wide[0:1], wide[1:2]
    gate = z_ref[...]
    mixed_out = y_ref[...]
    conv = pre_ref[...]
    gate_sig = sigmoid(gate)
    gate_silu = gate * gate_sig
    gated = mixed_out * gate_silu
    grad_scaled = dot_nn(here, w_ref[:, :inner])
    grad_gated = grad_scaled * gain + twice_here * gated
    grad_out = grad_gated * gate_silu
    grad_gate = grad_gated * mixed_out * (gate_sig * (1.0 + gate * (1.0 - gate_sig)))
    grad_out_low = grad_out.astype(BF16)

    conv_sig = sigmoid(conv)
    mixed_low = (conv * conv_sig).astype(BF16)
    x_low = mixed_low[:, :inner]
    b_low = mixed_low[:, inner : inner + STATE]
    c_low = mixed_low[:, inner + STATE :]
    x_in = x_low.astype(F32)
    shifted, steps, cum2, entering, tail, retained = decay_parts(block, dt_ref[...], head, seg_col, first, second)
    cum_row = jnp.transpose(cum2)
    steps_wide = spread_heads(steps, spread)
    x_steps_low = (steps_wide * x_in).astype(BF16)
    x_steps = x_steps_low.astype(F32)

    allowed = (seg_col == seg_row) & (row_col <= row_row)
    scores = jnp.where(allowed, dot_nt(b_low, c_low), 0.0)
    grad_scores = jnp.zeros((BLK, BLK), F32)
    pieces = []
    for pair in range(inner // LANES):
        columns = slice(pair * LANES, (pair + 1) * LANES)
        total = None
        for head_index in (2 * pair, 2 * pair + 1):
            gaps = cum_row[head_index : head_index + 1, :] - cum2[:, head_index : head_index + 1]
            decays = jnp.exp2(jnp.minimum(gaps, 0.0))
            coupling = (decays * scores).astype(BF16)
            term = dot_nn(coupling, head_half(grad_out_low[:, columns], head_index))
            total = term if total is None else total + term
            grad_scores = grad_scores + decays * dot_nt(
                head_half(x_steps_low[:, columns], head_index), grad_out_low[:, columns]
            )
        pieces.append(total)
    grad_scores_low = jnp.where(allowed, grad_scores, 0.0).astype(BF16)
    old_dstate = dstate[...]
    old_dstate_low = old_dstate.astype(BF16)
    old_state = st_ref[0]
    tail_wide = spread_heads(tail, spread)
    from_state = tail_wide * dot_nn(b_low, old_dstate_low)
    grad_unit = jnp.concatenate(pieces, axis=1) + from_state
    entered = (spread_heads(entering, spread) * grad_out).astype(BF16)
    tailed = (tail_wide * x_steps).astype(BF16)
    grad_c = dot_tn(grad_scores_low, b_low) + dot_nt(entered, old_state.astype(BF16))
    grad_b = dot_nn(grad_scores_low, c_low) + dot_nt(tailed, old_dstate_low)
    keep = spread_heads(jnp.broadcast_to(retained, (8, LANES)), spread)[0:1]
    dstate[...] = old_dstate * keep + dot_tn(c_low, entered)

    balance = gather_heads(grad_out_low.astype(F32) * (mixed_out - skip * x_in) - x_steps * grad_unit, spread)
    direct = gather_heads(x_in * grad_unit, spread)
    final_wide = jnp.sum(x_steps * from_state, axis=0, keepdims=True) + keep * jnp.sum(
        old_dstate * old_state, axis=0, keepdims=True
    )
    final = gather_heads(jnp.broadcast_to(final_wide, (8, inner)), spread)[0:1]
    above = lax.broadcasted_iota(jnp.int32, (BLK, BLK), 0)
    below = lax.broadcasted_iota(jnp.int32, (BLK, BLK), 1)
    upper = jnp.where(above <= below, 1.0, 0.0).astype(BF16)
    thirds = dot_nn(upper, jnp.concatenate(split_three(balance), axis=1))
    grad_log = thirds[:, :LANES] + thirds[:, LANES : 2 * LANES] + thirds[:, 2 * LANES :] + final
    grad_steps = direct + grad_log * head[1:2]
    grad_dt = grad_steps * sigmoid(shifted)
    ghead_ref[0:1, :] += jnp.sum(grad_dt, axis=0, keepdims=True)
    ghead_ref[1:2, :] += jnp.sum(grad_log * steps, axis=0, keepdims=True) * head[1:2]
    gwide_ref[0:1, :] += jnp.sum(grad_out * x_in, axis=0, keepdims=True)
    gwide_ref[1:2, :] += jnp.sum(grad_scaled * gated, axis=0, keepdims=True)

    grad_x = steps_wide * grad_unit + skip * grad_out
    grad_conv = jnp.concatenate([grad_x, grad_b, grad_c], axis=1) * (
        conv_sig * (1.0 + conv * (1.0 - conv_sig))
    )
    padded[pl.ds(0, BLK), :] = grad_conv
    mixed_in = in_ref[...]
    taps = taps_ref[...]
    grad_in = taps[CONV - 1 : CONV] * grad_conv
    gtaps_ref[CONV : CONV + 1, :] += jnp.sum(grad_conv, axis=0, keepdims=True)
    gtaps_ref[CONV - 1 : CONV, :] += jnp.sum(mixed_in * grad_conv, axis=0, keepdims=True)
    for delay in range(1, CONV):
        later = jnp.where(remaining > delay, padded[pl.ds(delay, BLK), :], 0.0)
        grad_in = grad_in + taps[CONV - 1 - delay : CONV - delay] * later
        gtaps_ref[CONV - 1 - delay : CONV - delay, :] += jnp.sum(mixed_in * later, axis=0, keepdims=True)
    padded[pl.ds(BLK, 8), :] = padded[pl.ds(0, 8), :]
    gproj = jnp.concatenate([grad_gate.astype(BF16), grad_in.astype(BF16), grad_dt.astype(BF16)], axis=1)
    gproj_ref[...] = gproj
    store_parts(ring, block, dot_nt(gproj, w_ref[:, inner:]), parts)
    pair_copy(ring, block, parts, from_pair).start()

    def second_stage(at):
        pair_copy(ring, at, parts, from_pair).wait_recv()
        add_pair(at, parts, from_pair, sums)
        across_copy(ring, at, sums, from_across).start()

    def last_stage(at):
        across_copy(ring, at, sums, from_across).wait_recv()
        gnormed_ref[pl.ds(at * SHARE, SHARE), :] = add_all(at, parts, from_pair, from_across)

    side.during(step)

    @pl.when(step < blocks - 1)
    def _():
        gather_copy(ring, AG_ACROSS, block - 1, own_ref, rows, place).wait_recv()
        gather_copy(ring, AG_PASS, block - 1, own_ref, rows, place).start()

    @pl.when(step >= 1)
    def _():
        second_stage(block + 1)

    @pl.when(step == blocks - 1)
    def _():
        second_stage(block)
        for copy in twice_copies():
            copy.wait_send()

        @pl.loop(0, blocks)
        def _(turn):
            at = blocks - 1 - turn
            last_stage(at)
            for kind in (AG_OWN, AG_ACROSS, AG_PASS):
                gather_copy(ring, kind, at, own_ref, rows, place).wait_send()
            pair_copy(ring, at, parts, from_pair).wait_send()
            across_copy(ring, at, sums, from_across).wait_send()

        side.finish()


def whole(shape):
    return pl.BlockSpec(shape, lambda *at: (0,) * len(shape))


def exchange_scratch(blocks, width):
    return [
        pltpu.VMEM((blocks, BLK, width), BF16),
        pltpu.VMEM((blocks, BLK, width), BF16),
        pltpu.VMEM((blocks, 2 * SHARE, width), BF16),
        pltpu.VMEM((blocks, SHARE, width), BF16),
        pltpu.VMEM((blocks, SHARE, width), BF16),
    ]


def layer_forward(offsets, own, hidden, weights, taps, head, wide, spread, gains, side, side_given):
    from_columns = hidden is None
    blocks, width = own.shape[0], gains.shape[1]
    count = blocks * BLK
    own_rows = count // 4
    inner, mixed = wide.shape[1], taps.shape[1]
    total = weights.shape[1]

    def by_block(columns):
        return pl.BlockSpec((BLK, columns), lambda b: (b, 0))

    hidden_specs = [] if from_columns else [whole((own_rows, width))]
    before_specs = [whole((own_rows, width))] if from_columns else []
    before_shapes = [jax.ShapeDtypeStruct((own_rows, width), F32)] if from_columns else []

    def kernel(*refs):
        if from_columns:
            refs = refs[:2] + (refs[9],) + refs[2:9] + refs[10:]
        forward_kernel(from_columns, side.make, *refs)

    return pl.pallas_call(
        kernel,
        grid=(blocks,),
        in_specs=[pl.BlockSpec(memory_space=pltpu.SMEM), whole(own.shape)]
        + hidden_specs
        + [
            whole((width, total)), whole((8, mixed)), whole((8, LANES)), whole((8, inner)),
            whole((2 * LANES, inner)), whole((8, width)), side.given_spec,
        ],
        out_specs=before_specs
        + [
            by_block(width), by_block(inner), by_block(mixed), by_block(mixed),
            by_block(LANES), by_block(inner), by_block(inner),
            pl.BlockSpec((1, STATE, inner), lambda b: (b, 0, 0)),
            whole((own_rows, width)), whole((own_rows, width)), whole((own_rows, 1)), whole((own_rows, width)),
            side.result_spec,
        ],
        out_shape=before_shapes
        + [
            jax.ShapeDtypeStruct((count, width), BF16),
            jax.ShapeDtypeStruct((count, inner), F32),
            jax.ShapeDtypeStruct((count, mixed), F32),
            jax.ShapeDtypeStruct((count, mixed), F32),
            jax.ShapeDtypeStruct((count, LANES), F32),
            jax.ShapeDtypeStruct((count, inner), F32),
            jax.ShapeDtypeStruct((count, inner), BF16),
            jax.ShapeDtypeStruct((blocks, STATE, inner), F32),
            jax.ShapeDtypeStruct((own_rows, width), F32),
            jax.ShapeDtypeStruct((own_rows, width), F32),
            jax.ShapeDtypeStruct((own_rows, 1), F32),
            jax.ShapeDtypeStruct((own_rows, width), BF16),
            side.result,
        ],
        scratch_shapes=[pltpu.VMEM((STATE, inner), F32), pltpu.VMEM((BLK + 8, mixed), F32)]
        + exchange_scratch(blocks, width)
        + [pltpu.VMEM((blocks, 8, BLK), F32)] * 4
        + [pltpu.SemaphoreType.DMA((7, blocks + 1, 2))]
        + side.scratch,
        compiler_params=pltpu.CompilerParams(
            vmem_limit_bytes=56 * 1024 * 1024, collective_id=side.collective_id, has_side_effects=True
        ),
        cost_estimate=pl.CostEstimate(flops=6 * 10**10, bytes_accessed=6 * 10**7, transcendentals=10**7),
        name="layer_forward",
    )(offsets, own, *([] if from_columns else [hidden]), weights, taps, head, wide, spread, gains, side_given)


def layer_backward(offsets, own, twice, weights, taps, head, wide, spread, saved, side, side_given):
    gate, mixed_in, conv, dt_raw, mixed_out, states = saved
    blocks, width = own.shape[0], own.shape[2]
    count = blocks * BLK
    own_rows = count // 4
    inner, mixed = wide.shape[1], taps.shape[1]
    total = weights.shape[1]

    def by_block(columns):
        return pl.BlockSpec((BLK, columns), lambda b: (blocks - 1 - b, 0))

    return pl.pallas_call(
        functools.partial(backward_kernel, side.make),
        grid=(blocks,),
        in_specs=[
            pl.BlockSpec(memory_space=pltpu.SMEM),
            whole(own.shape), whole((blocks, 8, LANES)), whole((width, total)), whole((8, mixed)),
            whole((8, LANES)), whole((8, inner)), whole((2 * LANES, inner)),
            by_block(inner), by_block(mixed), by_block(mixed), by_block(LANES), by_block(inner),
            pl.BlockSpec((1, STATE, inner), lambda b: (blocks - 1 - b, 0, 0)),
            side.given_spec,
        ],
        out_specs=[
            by_block(width), whole((own_rows, width)), by_block(total - inner),
            whole((8, mixed)), whole((8, LANES)), whole((8, inner)), side.result_spec,
        ],
        out_shape=[
            jax.ShapeDtypeStruct((count, width), BF16),
            jax.ShapeDtypeStruct((own_rows, width), F32),
            jax.ShapeDtypeStruct((count, total - inner), BF16),
            jax.ShapeDtypeStruct((8, mixed), F32),
            jax.ShapeDtypeStruct((8, LANES), F32),
            jax.ShapeDtypeStruct((8, inner), F32),
            side.result,
        ],
        scratch_shapes=[pltpu.VMEM((STATE, inner), F32), pltpu.VMEM((BLK + 8, mixed), F32)]
        + exchange_scratch(blocks, width)
        + [pltpu.VMEM((4, blocks, 8, LANES), F32)]
        + [pltpu.SemaphoreType.DMA((7, blocks + 1, 2))]
        + side.scratch,
        compiler_params=pltpu.CompilerParams(
            vmem_limit_bytes=56 * 1024 * 1024, collective_id=side.collective_id, has_side_effects=True
        ),
        cost_estimate=pl.CostEstimate(flops=6 * 10**10, bytes_accessed=6 * 10**7, transcendentals=10**7),
        name="layer_backward",
    )(offsets, own, twice, weights, taps, head, wide, spread, gate, mixed_in, conv, dt_raw, mixed_out, states, side_given)


def spread_matrix(inner, heads):
    lane_head = lax.broadcasted_iota(jnp.int32, (2 * LANES, inner), 1) // (inner // heads)
    row_head = lax.broadcasted_iota(jnp.int32, (2 * LANES, inner), 0) % LANES
    return jnp.where(lane_head == row_head, 1.0, 0.0).astype(BF16)


SEQ_MIN = 512


def choose_rows(wanted, valid, begin, end):
    slots = begin + lax.broadcasted_iota(jnp.int32, (wanted.shape[0], end - begin), 1)
    return jnp.where((slots == wanted) & valid, 1.0, 0.0).astype(BF16)


def pick_all(off_ref, arrived, cols):
    first, second = off_ref[0], off_ref[1]
    length = arrived.shape[1]
    for block in range(cols.shape[0]):
        low, high = block * BLK, (block + 1) * BLK
        row = low + lax.broadcasted_iota(jnp.int32, (BLK, 1), 0)
        total = None
        for member, begin, least, most in ((1, first, SEQ_MIN, length), (2, second, BIN - length, BIN - SEQ_MIN)):
            reach = BIN - SEQ_MIN if member == 1 else BIN
            start, end = max(low - most, 0), min(high - least, length)
            if end <= 0 or start >= length or low >= reach:
                continue
            valid = (row >= first) & (row < second) if member == 1 else row >= second
            term = dot_nn(choose_rows(row - begin, valid, start, end), arrived[member, start:end, :])
            total = term if total is None else total + term
        if high <= length:
            own = arrived[0, low:high, :].astype(F32)
            own = jnp.where(row < first, own, 0.0)
            total = own if total is None else total + own
        cols[block] = total.astype(BF16)


def place_all(off_ref, cols, slots):
    first, second = off_ref[0], off_ref[1]
    length = slots.shape[1]
    for chunk in range(length // BLK):
        low, high = chunk * BLK, (chunk + 1) * BLK
        position = low + lax.broadcasted_iota(jnp.int32, (BLK, 1), 0)
        slots[0, low:high, :] = jnp.where(position < first, cols[low:high, :].astype(F32), 0.0).astype(BF16)
        for member, begin, stop, least, most, reach in (
            (1, first, second, SEQ_MIN, length, BIN - SEQ_MIN),
            (2, second, BIN, BIN - length, BIN - SEQ_MIN, BIN),
        ):
            wanted = begin + position
            start, end = least + low, min(most + high, reach)
            choose = choose_rows(wanted, wanted < stop, start, end)
            slots[member, low:high, :] = dot_nn(choose, cols[start:end, :]).astype(BF16)


class LineGather:
    def __init__(self, own, target, sems):
        self.own, self.target, self.sems = own, target, sems
        me = lax.axis_index("dp")
        self.me, self.low, self.high = me, me % 2, me // 2
        self.line = lax.axis_size("dp") // 2
        self.span = own.shape[0]

    def copy(self, kind, place, other, own):
        here = self.target.at[pl.ds((place * 2 + self.low) * self.span, self.span), :]
        arrival = 2 if kind == 2 else 3
        return pltpu.make_async_remote_copy(
            src_ref=self.own if own else here, dst_ref=here,
            send_sem=self.sems.at[kind, place], recv_sem=self.sems.at[arrival + 1, place],
            device_id={"dp": other}, device_id_type=pl.DeviceIdType.MESH,
        )

    def right(self, place, own=False):
        return self.copy(0, place, (self.high + 1) * 2 + self.low, own)

    def left(self, place, own=False):
        return self.copy(1, place, (self.high - 1) * 2 + self.low, own)

    def pair(self, place, own=False):
        return self.copy(2, place, self.high * 2 + 1 - self.low, own)

    def local(self):
        here = self.target.at[pl.ds(self.me * self.span, self.span), :]
        return pltpu.make_async_copy(self.own, here, self.sems.at[5, 0])

    def start(self):
        self.local().start()

        @pl.when(self.high < self.line - 1)
        def _():
            self.right(self.high, True).start()

        @pl.when(self.high > 0)
        def _():
            self.left(self.high, True).start()

        self.pair(self.high, True).start()

    def stage(self, step):
        @pl.when(self.high - step >= 0)
        def _():
            self.right(self.high - step).wait_recv()

            @pl.when(self.high < self.line - 1)
            def _():
                self.right(self.high - step).start()

            self.pair(self.high - step).start()

        @pl.when(self.high + step < self.line)
        def _():
            self.left(self.high + step).wait_recv()

            @pl.when(self.high > 0)
            def _():
                self.left(self.high + step).start()

            self.pair(self.high + step).start()

    def finish(self):
        self.local().wait()

        @pl.loop(0, self.line)
        def _(place):
            self.pair(place).wait_recv()
            self.pair(place).wait_send()

            @pl.when((self.high < self.line - 1) & (place <= self.high))
            def _():
                self.right(place).wait_send()

            @pl.when((self.high > 0) & (place >= self.high))
            def _():
                self.left(place).wait_send()


class TileGather:
    def __init__(self, own, target, sems):
        self.own, self.target, self.sems = own, target, sems
        self.count, self.me = lax.axis_size("dp"), lax.axis_index("dp")

    def remote(self, step):
        return pltpu.make_async_remote_copy(
            src_ref=self.own, dst_ref=self.target.at[self.me],
            send_sem=self.sems.at[step, 0], recv_sem=self.sems.at[step, 1],
            device_id={"dp": (self.me + step) % self.count}, device_id_type=pl.DeviceIdType.MESH,
        )

    def start(self):
        self.target[self.me] = self.own[...]

        @pl.loop(1, self.count)
        def _(step):
            self.remote(step).start()

    def wait(self):
        @pl.loop(1, self.count)
        def _(step):
            self.remote(step).wait()


def start_kernel(
    off_ref, sorted_ref, own_ref, gain_ref, cols_ref, gains_ref, weights_ref, arrived, bin_sems, line_sems, tile_sems
):
    barrier = pltpu.get_barrier_semaphore()
    pl.semaphore_wait(barrier, greet_dp(barrier))
    line = LineGather(own_ref, weights_ref, line_sems)
    bins = BinExchange(True, sorted_ref, arrived, bin_sems)
    gains = TileGather(gain_ref, gains_ref, tile_sems)
    gains.start()
    line.start()
    bins.start()

    @pl.loop(1, line.line)
    def _(step):
        line.stage(step)

    bins.wait()
    pick_all(off_ref, arrived, cols_ref)
    line.finish()
    gains.wait()


def start_exchange(offsets, given, own, gain):
    count, members, span, columns = given.shape
    return pl.pallas_call(
        start_kernel,
        in_specs=[
            pl.BlockSpec(memory_space=pltpu.SMEM),
            pl.BlockSpec(memory_space=pltpu.VMEM),
            pl.BlockSpec(memory_space=pltpu.VMEM),
            pl.BlockSpec(memory_space=pltpu.VMEM),
        ],
        out_specs=[
            pl.BlockSpec(memory_space=pltpu.VMEM),
            pl.BlockSpec(memory_space=pltpu.VMEM),
            pl.BlockSpec(memory_space=pltpu.HBM),
        ],
        out_shape=[
            jax.ShapeDtypeStruct((BIN // BLK, BLK, columns), BF16),
            jax.ShapeDtypeStruct((count,) + gain.shape, F32),
            jax.ShapeDtypeStruct((count * own.shape[0], own.shape[1]), BF16),
        ],
        scratch_shapes=[
            pltpu.VMEM((members, count * span, columns), BF16),
            pltpu.SemaphoreType.DMA((count, 2)),
            pltpu.SemaphoreType.DMA((6, count // 2)),
            pltpu.SemaphoreType.DMA((count, 2)),
        ],
        compiler_params=pltpu.CompilerParams(
            vmem_limit_bytes=32 * 1024 * 1024, collective_id=5, has_side_effects=True
        ),
        cost_estimate=pl.CostEstimate(flops=6 * 10**10, bytes_accessed=6 * 10**7, transcendentals=0),
        name="start_exchange",
    )(offsets, given, own, gain)


class LineReduce:
    def __init__(self, given, out, pair_buf, from_left, from_right, sems):
        self.given, self.out, self.pair_buf = given, out, pair_buf
        self.from_left, self.from_right, self.sems = from_left, from_right, sems
        me = lax.axis_index("dp")
        self.low, self.high = me % 2, me // 2
        self.line = lax.axis_size("dp") // 2
        self.span = out.shape[0]

    def chunk(self, place, low):
        return pl.ds((place * 2 + low) * self.span, self.span)

    def pair(self, place):
        return pltpu.make_async_remote_copy(
            src_ref=self.given.at[self.chunk(place, 1 - self.low), :], dst_ref=self.pair_buf.at[place],
            send_sem=self.sems.at[0, place], recv_sem=self.sems.at[1, place],
            device_id={"dp": self.high * 2 + 1 - self.low}, device_id_type=pl.DeviceIdType.MESH,
        )

    def onward(self, place, right):
        target = self.from_left if right else self.from_right
        other = (self.high + 1 if right else self.high - 1) * 2 + self.low
        return pltpu.make_async_remote_copy(
            src_ref=self.pair_buf.at[place], dst_ref=target.at[place],
            send_sem=self.sems.at[2, place], recv_sem=self.sems.at[3 if right else 4, place],
            device_id={"dp": other}, device_id_type=pl.DeviceIdType.MESH,
        )

    def by_distance(self, step, act):
        distance = self.line - 1 - step

        @pl.when(self.high + distance < self.line)
        def _():
            act(self.high + distance, True)

        @pl.when(self.high - distance >= 0)
        def _():
            act(self.high - distance, False)

    def send_pairs(self):
        @pl.loop(0, self.line - 1)
        def _(step):
            self.by_distance(step, lambda place, right: self.pair(place).start())

        self.pair(self.high).start()

    def fold(self, place):
        return self.given[self.chunk(place, self.low), :].astype(F32) + self.pair_buf[place].astype(F32)

    def pass_on(self, place, right):
        self.pair(place).wait_recv()
        upstream = (self.high > 0) if right else (self.high < self.line - 1)
        source = self.from_left if right else self.from_right

        @pl.when(upstream)
        def _():
            self.onward(place, right).wait_recv()
            self.pair_buf[place] = (self.fold(place) + source[place].astype(F32)).astype(BF16)

        @pl.when(jnp.logical_not(upstream))
        def _():
            self.pair_buf[place] = self.fold(place).astype(BF16)

        self.onward(place, right).start()

    def stage(self, step):
        self.by_distance(step, self.pass_on)

    def finish(self):
        here = self.high
        self.pair(here).wait_recv()
        self.out[...] = self.fold(here)

        @pl.when(here > 0)
        def _():
            self.onward(here, True).wait_recv()
            self.out[...] += self.from_left[here].astype(F32)

        @pl.when(here < self.line - 1)
        def _():
            self.onward(here, False).wait_recv()
            self.out[...] += self.from_right[here].astype(F32)

        @pl.loop(0, self.line)
        def _(place):
            self.pair(place).wait_send()

            @pl.when(place != here)
            def _():
                self.onward(place, True).wait_send()


def line_scratch(count, span, columns):
    line = count // 2
    return [pltpu.VMEM((line, span, columns), BF16)] * 3 + [pltpu.SemaphoreType.DMA((5, line))]


class WeightsSide:
    collective_id = 1
    given_spec = pl.BlockSpec(memory_space=pltpu.HBM)
    result_spec = pl.BlockSpec(memory_space=pltpu.HBM)

    def __init__(self, own):
        self.count = lax.axis_size("dp")
        self.result = jax.ShapeDtypeStruct((self.count * own.shape[0], own.shape[1]), BF16)
        self.scratch = [pltpu.SemaphoreType.DMA((6, self.count // 2))]

    def make(self, off_ref, given, result, sems):
        line = LineGather(given, result, sems)
        count = line.line

        def during(step):
            if count != 4:
                return
            for stage in (1, 2, 3):

                @pl.when(step == 2 * stage - 1)
                def _(stage=stage):
                    line.stage(stage)

        def finish():
            if count != 4:

                @pl.loop(1, count)
                def _(stage):
                    line.stage(stage)

            line.finish()

        return Side(line.start, during, finish)


class Side:
    def __init__(self, start, during, finish):
        self.start, self.during, self.finish = start, during, finish


class ArriveSide:
    collective_id = 2
    given_spec = pl.BlockSpec(memory_space=pltpu.HBM)
    result_spec = pl.BlockSpec(memory_space=pltpu.HBM)

    def __init__(self, given):
        count, members, span, columns = given.shape
        blocks = BIN // BLK
        self.result = jax.ShapeDtypeStruct((blocks, SHARE, 4 * columns), BF16)
        self.scratch = [
            pltpu.VMEM((members, count * span, columns), BF16),
            pltpu.VMEM((blocks, BLK, columns), BF16),
            pltpu.SemaphoreType.DMA((count, 2)),
            pltpu.SemaphoreType.DMA((4, 2)),
        ]

    def make(self, off_ref, given, result, arrived, cols, bin_sems, row_sems):
        bins = BinExchange(True, given, arrived, bin_sems)
        rows = RowExchange(True, cols, result, row_sems)

        def during(step):
            @pl.when(step == cols.shape[0] - 2)
            def _():
                bins.wait()
                pick_all(off_ref, arrived, cols)
                rows.start()

        return Side(bins.start, during, rows.wait)


class ReturnSide:
    collective_id = 3
    given_spec = pl.BlockSpec(memory_space=pltpu.HBM)
    result_spec = pl.BlockSpec(memory_space=pltpu.HBM)

    def __init__(self, count, span, columns):
        blocks = BIN // BLK
        self.result = jax.ShapeDtypeStruct((count, 3, span, columns), BF16)
        self.scratch = [
            pltpu.VMEM((BIN, columns), BF16),
            pltpu.VMEM((3, count * span, columns), BF16),
            pltpu.SemaphoreType.DMA((4, 2)),
            pltpu.SemaphoreType.DMA((count, 2)),
        ]

    def make(self, off_ref, given, result, cols, slots, row_sems, bin_sems):
        rows = RowExchange(False, given, cols.reshape(BIN // BLK, BLK, cols.shape[1]), row_sems)
        bins = BinExchange(False, slots, result, bin_sems)

        def during(step):
            @pl.when(step == 2)
            def _():
                rows.wait()
                place_all(off_ref, cols, slots)
                bins.start()

        return Side(rows.start, during, bins.wait)


class GradientSide:
    collective_id = 4
    given_spec = pl.BlockSpec(memory_space=pltpu.VMEM)

    def __init__(self, count, given):
        span, columns = given.shape[0] // count, given.shape[1]
        self.result = jax.ShapeDtypeStruct((span, columns), F32)
        self.result_spec = whole((span, columns))
        self.scratch = line_scratch(count, span, columns)

    def make(self, off_ref, given, result, pair_buf, from_left, from_right, sems):
        line = LineReduce(given, result, pair_buf, from_left, from_right, sems)
        count = line.line

        def during(step):
            if count != 4:
                return
            for stage in (0, 1, 2):

                @pl.when(step == 2 * stage + 2)
                def _(stage=stage):
                    line.stage(stage)

        def finish():
            if count != 4:

                @pl.loop(0, count - 1)
                def _(stage):
                    line.stage(stage)

            line.finish()

        return Side(line.send_pairs, during, finish)


class MemberGather:
    def __init__(self, target, sems):
        self.target, self.sems = target, sems
        self.me = lax.axis_index("tensor")

    def remote(self, step):
        return pltpu.make_async_remote_copy(
            src_ref=self.target.at[self.me], dst_ref=self.target.at[self.me],
            send_sem=self.sems.at[step, 0], recv_sem=self.sems.at[step, 1],
            device_id={"tensor": (self.me + step) % 4}, device_id_type=pl.DeviceIdType.MESH,
        )

    def start(self):
        for step in range(1, 4):
            self.remote(step).start()

    def wait(self):
        for step in range(1, 4):
            self.remote(step).wait()


def end_kernel(
    off_ref, grad_ref, rows_ref, gproj_ref, sg_ref, gg_ref, tile_ref, later_ref,
    back_ref, pack_ref, sum_ref, maps_ref,
    cols, slots, packs, pair_buf, from_left, from_right, line_sems, tiles, shared, maps,
    row_sems, bin_sems, tile_sems, shared_sems, maps_sems,
):
    ring = Ring(None)
    ring.greet()
    inner = gg_ref.shape[1]
    first_map = 3 * inner
    rows = RowExchange(False, grad_ref, cols.reshape(BIN // BLK, BLK, cols.shape[1]), row_sems)
    bins = BinExchange(False, slots, back_ref, bin_sems)
    line = LineReduce(packs, pack_ref, pair_buf, from_left, from_right, line_sems)
    dp_tiles = TileGather(tile_ref, tiles, tile_sems)
    shared_tiles = MemberGather(shared, shared_sems)
    shared_maps = MemberGather(maps, maps_sems)
    rows.start()
    dp_tiles.start()

    def compute(place):
        width = 2 * line.span
        lanes = pl.ds(pl.multiple_of(place * width, LANES), width)
        here = pl.ds(place * width, width)
        packs[here, :inner] = dot_tn(sg_ref[:, lanes], gg_ref[...]).astype(BF16)
        packs[here, inner:] = dot_tn(rows_ref[:, lanes], gproj_ref[...]).astype(BF16)

    if 2 * line.span % LANES == 0:

        @pl.loop(0, line.line - 1)
        def _(step):
            def act(place, right):
                compute(place)
                line.pair(place).start()

            line.by_distance(step, act)

        compute(line.high)
        line.pair(line.high).start()
    else:

        @pl.loop(0, packs.shape[0] // BLK)
        def _(turn):
            here = pl.ds(pl.multiple_of(turn * BLK, BLK), BLK)
            packs[here, :inner] = dot_tn(sg_ref[:, here], gg_ref[...]).astype(BF16)
            packs[here, inner:] = dot_tn(rows_ref[:, here], gproj_ref[...]).astype(BF16)

        line.send_pairs()

    rows.wait()
    place_all(off_ref, cols, slots)
    bins.start()

    @pl.loop(0, line.line - 1)
    def _(step):
        line.stage(step)

    dp_tiles.wait()
    sum_ref[...] = tiles[0]

    @pl.loop(1, tiles.shape[0])
    def _(at):
        sum_ref[...] += tiles[at]

    shared[ring.me] = sum_ref[pl.ds(0, shared.shape[1]), :]
    shared_tiles.start()
    line.finish()
    maps[ring.me, 0] = pack_ref[:, first_map : first_map + 2 * STATE].astype(BF16)
    maps[ring.me, 1] = later_ref[...].astype(BF16)
    shared_maps.start()
    shared_tiles.wait()
    sum_ref[pl.ds(0, shared.shape[1]), :] = shared[0] + shared[1] + shared[2] + shared[3]
    shared_maps.wait()
    for layer in range(LAYERS):
        maps_ref[layer] = (maps[0, layer].astype(F32) + maps[1, layer].astype(F32)) + (
            maps[2, layer].astype(F32) + maps[3, layer].astype(F32)
        )
    bins.wait()


def end_exchange(offsets, grad_rows, rows, gproj, spread_grad, gained, tile, shared_rows, later_maps, span):
    count = lax.axis_size("dp")
    width, inner, total = rows.shape[1], gained.shape[1], gained.shape[1] + gproj.shape[1]
    columns = width // 4
    vmem = pl.BlockSpec(memory_space=pltpu.VMEM)
    pack_rows = width // count
    return pl.pallas_call(
        end_kernel,
        in_specs=[pl.BlockSpec(memory_space=pltpu.SMEM)] + [vmem] * 7,
        out_specs=[pl.BlockSpec(memory_space=pltpu.HBM), vmem, vmem, vmem],
        out_shape=[
            jax.ShapeDtypeStruct((count, 3, span, columns), BF16),
            jax.ShapeDtypeStruct((pack_rows, total), F32),
            jax.ShapeDtypeStruct(tile.shape, F32),
            jax.ShapeDtypeStruct((LAYERS, pack_rows, 2 * STATE), F32),
        ],
        scratch_shapes=[
            pltpu.VMEM((BIN, columns), BF16),
            pltpu.VMEM((3, count * span, columns), BF16),
            pltpu.VMEM((width, total), BF16),
        ]
        + line_scratch(count, pack_rows, total)
        + [
            pltpu.VMEM((count,) + tile.shape, F32),
            pltpu.VMEM((4, shared_rows, LANES), F32),
            pltpu.VMEM((4, LAYERS, pack_rows, 2 * STATE), BF16),
            pltpu.SemaphoreType.DMA((4, 2)),
            pltpu.SemaphoreType.DMA((count, 2)),
            pltpu.SemaphoreType.DMA((count, 2)),
            pltpu.SemaphoreType.DMA((4, 2)),
            pltpu.SemaphoreType.DMA((4, 2)),
        ],
        compiler_params=pltpu.CompilerParams(
            vmem_limit_bytes=56 * 1024 * 1024, collective_id=6, has_side_effects=True
        ),
        cost_estimate=pl.CostEstimate(flops=6 * 10**10, bytes_accessed=6 * 10**7, transcendentals=0),
        name="end_exchange",
    )(offsets, grad_rows, rows, gproj, spread_grad, gained, tile, later_maps)


def pre_norm(hidden, gain_full):
    return hidden * lax.rsqrt(jnp.mean(hidden * hidden, axis=-1, keepdims=True) + eps) * gain_full


def pad_to(values, rows, columns):
    return jnp.pad(values, ((0, rows - values.shape[0]), (0, columns - values.shape[1])))


def on_device(
    tokens, cotangent, lengths, packing, pre_gain, w_z, w_x, w_bc, w_dt, conv_x, conv_bc, head_params, norm_gain, w_out,
):
    dp_count = lax.axis_size("dp")
    bin_index = lax.axis_index("dp")
    seq_total, pos_here, cols_here = tokens.shape
    inner_part = conv_x.shape[2]
    heads_here = head_params.shape[2]
    dp_rows = w_z.shape[1]
    mixed = inner_part + 2 * STATE
    triples = lengths[packing].reshape(dp_count, 3)
    offsets = jnp.cumsum(triples, axis=1) - triples
    my_offsets = offsets[bin_index]
    bounds = my_offsets[1:3]
    groups = packing.reshape(dp_count, 3)
    blocks = BIN // BLK

    spread = spread_matrix(inner_part, heads_here)
    packs = []
    for layer in range(LAYERS):
        own = jnp.concatenate(
            [w_out[layer].T, w_z[layer], w_x[layer], w_bc[layer], pad_to(w_dt[layer], dp_rows, LANES)], axis=1
        )
        taps = jnp.concatenate([conv_x[layer], conv_bc[layer]], axis=1).astype(F32)
        head = jnp.stack([head_params[layer, 0], -jnp.exp(head_params[layer, 1])])
        wide = jnp.stack(
            [jnp.repeat(head_params[layer, 2], inner_part // heads_here), norm_gain[layer].astype(F32)]
        )
        packs.append((own, pad_to(taps, 8, mixed), pad_to(head, 8, LANES), pad_to(wide, 8, inner_part)))

    columns, gain_tiles, first_weights = start_exchange(
        bounds, tokens[groups], packs[0][0], pad_to(pre_gain.astype(F32), 8, LANES)
    )
    gains = jnp.swapaxes(gain_tiles[:, :LAYERS, :dp_rows], 0, 1).reshape(LAYERS, dp_count * dp_rows)
    given_cot = cotangent[groups]
    own, hidden, weights = columns, None, first_weights
    records = []
    for layer in range(LAYERS):
        _, taps, head, wide = packs[layer]
        pair = pad_to(jnp.stack([gains[min(layer + 1, LAYERS - 1)], gains[layer]]), 8, gains.shape[1])
        side_given = packs[1][0] if layer == 0 else given_cot
        side = WeightsSide(side_given) if layer == 0 else ArriveSide(side_given)
        results = layer_forward(bounds, own, hidden, weights, taps, head, wide, spread, pair, side, side_given)
        before = results[0] if layer == 0 else hidden
        (
            rows, gate, mixed_in, conv, dt_raw, mixed_out, gained, states, hidden, total, scale, normed, side_out,
        ) = results[1:] if layer == 0 else results
        saved = (gate, mixed_in, conv, dt_raw, mixed_out, states)
        records.append((before, rows, weights, gained, total, scale, saved))
        own = normed.reshape(blocks, SHARE, -1)
        weights = side_out
    grad_hidden = side_out.reshape(BIN // 4, -1).astype(F32)
    side, side_given = ReturnSide(dp_count, pos_here, cols_here), hidden.astype(BF16).reshape(own.shape)
    collected = [None] * LAYERS
    for layer in reversed(range(LAYERS)):
        _, taps, head, wide = packs[layer]
        before, rows, weights, gained, total, scale, saved = records[layer]
        normed, norm_back = jax.vjp(pre_norm, before, gains[layer])
        grad_branch = grad_hidden.astype(BF16).astype(F32)
        twice = 2.0 * (-(scale**3) / (2 * INNER)) * jnp.sum(grad_branch * total, axis=1, keepdims=True)
        twice_rows = jnp.broadcast_to(pad_to(twice.reshape(blocks, SHARE), blocks, LANES)[:, None], (blocks, 8, LANES))
        spread_grad, grad_normed, gproj, gtaps, ghead, gwide, side_out = layer_backward(
            bounds, (grad_branch * scale).astype(BF16).reshape(own.shape), twice_rows, weights, taps, head, wide, spread,
            saved, side, side_given,
        )
        grad_before, grad_gain = norm_back(grad_normed)
        grad_hidden = grad_hidden + grad_before
        collected[layer] = (grad_gain, gtaps, ghead, gwide)
        if layer == LAYERS - 1:
            activations_back = side_out
            side_given = jnp.concatenate(
                [dot_tn(spread_grad, gained).astype(BF16), dot_tn(rows, gproj).astype(BF16)], axis=1
            )
            side = GradientSide(dp_count, side_given)

    pieces = []
    for grad_gain, gtaps, ghead, gwide in collected:
        pieces += [gtaps[: CONV + 1, inner_part:].reshape(-1, LANES), grad_gain.reshape(-1, LANES)]
    shared_rows = sum(piece.shape[0] for piece in pieces)
    gap = -shared_rows % 8
    pieces.append(jnp.zeros((gap, LANES), F32))
    for grad_gain, gtaps, ghead, gwide in collected:
        pieces += [gtaps[: CONV + 1, :inner_part].reshape(-1, LANES), ghead[:2], gwide[:2].reshape(-1, LANES)]
    tile = jnp.concatenate(pieces, axis=0)
    tile = pad_to(tile, tile.shape[0] + -tile.shape[0] % 8, LANES)
    later_pack = side_out
    first_map = 3 * inner_part
    returned, first_pack, sums, maps = end_exchange(
        bounds, grad_hidden.astype(BF16).reshape(own.shape), rows, gproj, spread_grad, gained, tile, shared_rows + gap,
        later_pack[:, first_map : first_map + 2 * STATE], pos_here,
    )
    taken = 0

    def take(shape):
        nonlocal taken
        rows_here = 1
        for size in shape:
            rows_here *= size
        rows_here //= LANES
        piece = sums[taken : taken + rows_here].reshape(shape)
        taken += rows_here
        return piece

    convbc, pre = zip(*[(take((CONV + 1, 2 * STATE)), take((gains.shape[1],))) for _ in range(LAYERS)])
    taken += gap
    convx, heads, wides = zip(
        *[(take((CONV + 1, inner_part)), take((2, LANES)), take((2, inner_part))) for _ in range(LAYERS)]
    )
    grad_convbc, grad_convx = jnp.stack(convbc), jnp.stack(convx)
    shard_pre = lax.dynamic_slice_in_dim(jnp.stack(pre), bin_index * dp_rows, dp_rows, 1)
    grad_head = jnp.stack(
        [
            jnp.concatenate([head[:, :heads_here], jnp.sum(wide[0:1].reshape(1, heads_here, -1), axis=2)], axis=0)
            for head, wide in zip(heads, wides)
        ]
    )
    grad_norm = jnp.stack([wide[1] for wide in wides])
    own_weights = jnp.stack([first_pack, later_pack])
    grad_bc = maps
    grad_out = jnp.swapaxes(own_weights[:, :, :inner_part], 1, 2)
    grad_z = own_weights[:, :, inner_part : 2 * inner_part]
    grad_x = own_weights[:, :, 2 * inner_part : 3 * inner_part]
    grad_dt = own_weights[:, :, 3 * inner_part + 2 * STATE : 3 * inner_part + 2 * STATE + heads_here]

    rank_of = jnp.zeros_like(packing).at[packing].set(jnp.arange(seq_total, dtype=jnp.int32))

    def in_order(returned):
        return returned.reshape(seq_total, pos_here, cols_here)[rank_of]

    activations = in_order(activations_back)
    input_grad = in_order(returned)
    return (
        activations, input_grad, shard_pre, grad_z, grad_x, grad_bc, grad_dt,
        grad_convx, grad_convbc, grad_head, grad_norm, grad_out,
    )


def solution(mesh):
    placed = (
        P(None, "dp", "tensor"), P(None, "dp", "tensor"), P(), P(), P(None, "dp"),
        P(None, "dp", "tensor"), P(None, "dp", "tensor"), P(None, "dp", None), P(None, "dp", "tensor"),
        P(None, None, "tensor"), P(), P(None, None, "tensor"), P(None, "tensor"), P(None, "tensor", "dp"),
    )
    results = (
        P(None, "dp", "tensor"), P(None, "dp", "tensor"), P(None, "dp"),
        P(None, "dp", "tensor"), P(None, "dp", "tensor"), P(None, "dp", None), P(None, "dp", "tensor"),
        P(None, None, "tensor"), P(), P(None, None, "tensor"), P(None, "tensor"), P(None, "tensor", "dp"),
    )
    return jax.shard_map(on_device, mesh=mesh, in_specs=placed, out_specs=results, check_vma=False)
```

```python
import functools
import jax
import jax.numpy as jnp
from jax import lax
from jax.experimental import pallas as pl
from jax.experimental.pallas import tpu as pltpu
from jax.sharding import PartitionSpec as P

CONV = 4
INNER = 2048
LAYERS = 2
BIN = 2048
eps = 1e-05
STATE = 128
BLK = 256
LANES = 128
LOG2E = 1.4426950408889634
F32 = jnp.float32
BF16 = jnp.bfloat16


def dot_nn(left, right):
    return lax.dot_general(left, right, (((1,), (0,)), ((), ())), preferred_element_type=F32)


def dot_nt(left, right):
    return lax.dot_general(left, right, (((1,), (1,)), ((), ())), preferred_element_type=F32)


def dot_tn(left, right):
    return lax.dot_general(left, right, (((0,), (0,)), ((), ())), preferred_element_type=F32)


def split_two(values):
    high = values.astype(BF16)
    return high, (values - high.astype(F32)).astype(BF16)


def split_three(values):
    high = values.astype(BF16)
    rest = values - high.astype(F32)
    middle = rest.astype(BF16)
    return high, middle, (rest - middle.astype(F32)).astype(BF16)


def spread_heads(values, spread):
    high, low = split_two(values)
    return dot_nn(jnp.concatenate([high, low], axis=1), spread)


def gather_heads(values, spread):
    high, low = split_two(values)
    half = spread[:LANES]
    return dot_nt(high, half) + dot_nt(low, half)


def sigmoid(values):
    return 0.5 * jnp.tanh(0.5 * values) + 0.5


def softplus(values):
    return jnp.maximum(values, 0.0) + jnp.log1p(jnp.exp(-jnp.abs(values)))


def segment_of(rows, first, second):
    return (rows >= first).astype(jnp.int32) + (rows >= second).astype(jnp.int32)


def block_frame(block, first, second):
    row_col = block * BLK + lax.broadcasted_iota(jnp.int32, (BLK, 1), 0)
    row_row = block * BLK + lax.broadcasted_iota(jnp.int32, (1, BLK), 1)
    return row_col, row_row, segment_of(row_col, first, second), segment_of(row_row, first, second)


def decay_parts(block, dt_raw, head, seg_col, first, second):
    shifted = dt_raw + head[0:1]
    steps = softplus(shifted)
    log_decay = steps * head[1:2]
    above = lax.broadcasted_iota(jnp.int32, (BLK, BLK), 0)
    below = lax.broadcasted_iota(jnp.int32, (BLK, BLK), 1)
    lower = jnp.where(above >= below, 1.0, 0.0).astype(BF16)
    parts = dot_nn(lower, jnp.concatenate(split_three(log_decay), axis=1))
    cumulative = parts[:, :LANES] + parts[:, LANES : 2 * LANES] + parts[:, 2 * LANES :]
    cum2 = cumulative * LOG2E
    final2 = cum2[BLK - 1 : BLK]
    last_seg = segment_of(block * BLK + BLK - 1, first, second)
    prior_seg = jnp.where(block == 0, -1, segment_of(block * BLK - 1, first, second))
    entering = jnp.where(seg_col == prior_seg, jnp.exp2(cum2), 0.0)
    tail = jnp.where(seg_col == last_seg, jnp.exp2(final2 - cum2), 0.0)
    retained = jnp.where(last_seg == prior_seg, jnp.exp2(final2), 0.0)
    return shifted, steps, cum2, entering, tail, retained


def head_half(pair, head):
    lanes = lax.broadcasted_iota(jnp.int32, pair.shape, 1)
    keep = (lanes < LANES // 2) if head % 2 == 0 else (lanes >= LANES // 2)
    return jnp.where(keep, pair, jnp.zeros_like(pair))


SHARE = BLK // 4
AG_OWN, AG_ACROSS, AG_PASS, RS_PAIR, RS_ACROSS, SM_PAIR, SM_ACROSS = range(7)


class Ring:
    def __init__(self, sems):
        me = lax.axis_index("tensor")
        self.low, self.high = me % 2, me // 2
        self.me = me
        self.sibling = self.high * 2 + (1 - self.low)
        self.across = (1 - self.high) * 2 + self.low
        self.beyond = (1 - self.high) * 2 + (1 - self.low)
        self.sems = sems

    def greet(self):
        barrier = pltpu.get_barrier_semaphore()
        for other in (self.sibling, self.across, self.beyond):
            pl.semaphore_signal(barrier, inc=1, device_id={"tensor": other}, device_id_type=pl.DeviceIdType.MESH)
        pl.semaphore_wait(barrier, greet_dp(barrier) + 3)

    def slot(self, owner):
        return ((self.low + owner % 2) % 2) * 2 + (self.high + owner // 2) % 2

    def copy(self, kind, block, source, target, other):
        return pltpu.make_async_remote_copy(
            src_ref=source, dst_ref=target,
            send_sem=self.sems.at[kind, block, 0], recv_sem=self.sems.at[kind, block, 1],
            device_id={"tensor": other}, device_id_type=pl.DeviceIdType.MESH,
        )


def greet_dp(barrier):
    count, me = lax.axis_size("dp"), lax.axis_index("dp")

    @pl.loop(1, count)
    def _(step):
        pl.semaphore_signal(
            barrier, inc=1, device_id={"dp": (me + step) % count}, device_id_type=pl.DeviceIdType.MESH
        )

    return count - 1


class BinExchange:
    def __init__(self, to_bins, source, target, sems):
        self.to_bins, self.source, self.target, self.sems = to_bins, source, target, sems
        self.count, self.me = lax.axis_size("dp"), lax.axis_index("dp")
        self.span = source.shape[2] if to_bins else target.shape[2]

    def pieces(self, other):
        if self.to_bins:
            return self.source.at[other], self.target.at[:, pl.ds(self.me * self.span, self.span), :]
        return self.source.at[:, pl.ds(other * self.span, self.span), :], self.target.at[self.me]

    def remote(self, step, other):
        source, target = self.pieces(other)
        return pltpu.make_async_remote_copy(
            src_ref=source, dst_ref=target, send_sem=self.sems.at[step, 0], recv_sem=self.sems.at[step, 1],
            device_id={"dp": other}, device_id_type=pl.DeviceIdType.MESH,
        )

    def local(self):
        source, target = self.pieces(self.me)
        return pltpu.make_async_copy(source, target, self.sems.at[0, 0])

    def start(self):
        self.local().start()

        @pl.loop(1, self.count)
        def _(step):
            self.remote(step, (self.me + step) % self.count).start()

    def wait(self):
        self.local().wait()

        @pl.loop(1, self.count)
        def _(step):
            self.remote(step, (self.me + step) % self.count).wait()


class RowExchange:
    def __init__(self, to_rows, source, target, sems):
        self.to_rows, self.source, self.target, self.sems = to_rows, source, target, sems
        self.me = lax.axis_index("tensor")
        self.columns = source.shape[2] if to_rows else target.shape[2]

    def pieces(self, other):
        if self.to_rows:
            return (
                self.source.at[:, pl.ds(other * SHARE, SHARE), :],
                self.target.at[:, :, pl.ds(pl.multiple_of(self.me * self.columns, LANES), self.columns)],
            )
        return (
            self.source.at[:, :, pl.ds(pl.multiple_of(other * self.columns, LANES), self.columns)],
            self.target.at[:, pl.ds(self.me * SHARE, SHARE), :],
        )

    def remote(self, step):
        other = (self.me + step) % 4
        source, target = self.pieces(other)
        return pltpu.make_async_remote_copy(
            src_ref=source, dst_ref=target, send_sem=self.sems.at[step, 0], recv_sem=self.sems.at[step, 1],
            device_id={"tensor": other}, device_id_type=pl.DeviceIdType.MESH,
        )

    def local(self):
        source, target = self.pieces(self.me)
        return pltpu.make_async_copy(source, target, self.sems.at[0, 0])

    def start(self):
        self.local().start()
        for step in range(1, 4):
            self.remote(step).start()

    def wait(self):
        self.local().wait()
        for step in range(1, 4):
            self.remote(step).wait()


def row_place(rows, member):
    return rows.at[:, pl.ds(member * SHARE, SHARE), :]


def column_place(rows, member):
    columns = rows.shape[2] // 4
    return rows.at[:, :, pl.ds(pl.multiple_of(member * columns, LANES), columns)]


def gather_copy(ring, kind, block, own, rows, place):
    if kind == AG_PASS:
        passed = place(rows, ring.across).at[block]
        return ring.copy(kind, block, passed, passed, ring.sibling)
    other = ring.sibling if kind == AG_OWN else ring.across
    target = place(rows, ring.me).at[block]
    return ring.copy(kind, block, target if own is None else own.at[block], target, other)


def pair_copy(ring, block, parts, from_pair):
    return ring.copy(RS_PAIR, block, parts.at[block, pl.ds(2 * SHARE, 2 * SHARE), :], from_pair.at[block], ring.sibling)


def across_copy(ring, block, parts, from_across):
    return ring.copy(RS_ACROSS, block, parts.at[block, pl.ds(SHARE, SHARE), :], from_across.at[block], ring.across)


def store_parts(ring, block, part, parts):
    for owner in range(4):
        parts[block, pl.ds(ring.slot(owner) * SHARE, SHARE), :] = part[owner * SHARE : (owner + 1) * SHARE].astype(BF16)


def add_pair(block, parts, from_pair):
    parts[block, pl.ds(SHARE, SHARE), :] = (
        parts[block, pl.ds(SHARE, SHARE), :].astype(F32) + from_pair[block, pl.ds(SHARE, SHARE), :].astype(F32)
    ).astype(BF16)


def add_all(block, parts, from_pair, from_across):
    return (
        parts[block, pl.ds(0, SHARE), :].astype(F32)
        + from_pair[block, pl.ds(0, SHARE), :].astype(F32)
        + from_across[block].astype(F32)
    )


def own_column(line, first_lane):
    lanes = lax.broadcasted_iota(jnp.int32, (SHARE, line.shape[1]), 1)
    rows = lax.broadcasted_iota(jnp.int32, (SHARE, line.shape[1]), 0)
    return jnp.sum(jnp.where(lanes == rows + first_lane, line, 0.0), axis=1, keepdims=True)


LAG = 4
DEFER = 2
PASS_AHEAD = 2


def forward_kernel(
    off_ref, tok_ref, packs_ref, own_gains_ref, cot_ref, taps_ref, head_ref, wide_ref, spread_ref,
    rows_ref, z_ref, in_ref, pre_ref, dt_ref, y_ref, gg_ref, st_ref,
    before_ref, middle_ref, tot_ref, scale_ref, final_ref, gains_ref, cot_cols_ref, weights_ref,
    state, padded, rows, parts, from_pair, from_across, sq_own, sq_pair, sq_sums, sq_across,
    weights, arrived, cols, cot_arrived, all_gains, middle, kept,
    sems, copy_sems, line_sems, bin_sems, cot_sems, gain_sems,
):
    step = pl.program_id(0)
    inner = y_ref.shape[1]
    mixed = in_ref.shape[1]
    first, second = off_ref[0], off_ref[1]
    blocks = rows.shape[0]
    layer, block = step // blocks, step % blocks
    rings = (Ring(sems.at[0]), Ring(sems.at[1]))
    ring = rings[0]
    total_columns = weights.shape[2]
    out_part, in_part = pl.ds(0, inner), pl.ds(inner, total_columns - inner)
    line = LineGather(packs_ref.at[1], weights.at[1], line_sems.at[1])
    in_line = LineGather(packs_ref.at[0, :, in_part], weights.at[0, :, in_part], line_sems.at[0])
    out_line = LineGather(packs_ref.at[0, :, out_part], weights.at[0, :, out_part], line_sems.at[2])
    bins = BinExchange(True, tok_ref, arrived, bin_sems)
    cot_bins = BinExchange(True, cot_ref, cot_arrived, cot_sems)
    gain_tiles = TileGather(own_gains_ref, all_gains, gain_sems)
    four = line.line == 4

    def gather(at_layer, kind, at):
        own, place = ((cols, column_place), (None, row_place))[at_layer]
        return gather_copy(rings[at_layer], kind, at, own, rows, place)

    def sq_pair_copy(at_ring, slot):
        return at_ring.copy(SM_PAIR, slot % blocks, sq_own.at[slot], sq_pair.at[slot], at_ring.sibling)

    def sq_across_copy(at_ring, slot):
        return at_ring.copy(SM_ACROSS, slot % blocks, sq_sums.at[slot], sq_across.at[slot], at_ring.across)

    def own_copy():
        return pltpu.make_async_copy(cols, column_place(rows, ring.me), copy_sems.at[LAYERS])

    def keep_weights(at):
        return pltpu.make_async_copy(weights.at[at], weights_ref.at[at], copy_sems.at[at])

    def clear():
        state[...] = jnp.zeros_like(state)
        padded[pl.ds(0, 8), :] = jnp.zeros((8, mixed), F32)

    @pl.when(step == 0)
    def _():
        ring.greet()
        bins.start()
        in_line.start_pair()
        gain_tiles.start()
        clear()
        bins.wait()
        in_line.start_line()
        pick_all(off_ref, arrived, cols)
        own_copy().start()

        @pl.loop(0, blocks)
        def _(at):
            gather(0, AG_ACROSS, at).start()
            gather(0, AG_OWN, at).start()

        gain_tiles.wait()
        gains_ref[...] = all_gains[0]

        @pl.loop(1, all_gains.shape[0])
        def _(at):
            gains_ref[...] += all_gains[at]

        own_copy().wait()

        def pass_rows(begin, end):
            @pl.loop(begin, end)
            def _(at):
                gather(0, AG_ACROSS, at).wait_recv()
                gather(0, AG_PASS, at).start()

        if four:
            in_line.stage(1)
            pass_rows(0, blocks // 2)
            in_line.stage(2)
            pass_rows(blocks // 2, blocks)
            in_line.stage(3)
            out_line.start()
            line.start()
        else:
            pass_rows(0, blocks)

            @pl.loop(1, line.line)
            def _(stage):
                in_line.stage(stage)

        in_line.finish()
        if not four:
            out_line.start()
            line.start()

    @pl.when(step == blocks)
    def _():
        clear()

    for at_layer in range(LAYERS):

        @pl.when(layer == at_layer)
        def _(at_layer=at_layer):
            gather(at_layer, AG_OWN, block).wait_recv()
            gather(at_layer, AG_PASS, block).wait_recv()

    gains = gains_ref[...]
    raw = rows[block].astype(F32)
    mean = jnp.sum(raw * raw, axis=1, keepdims=True) / raw.shape[1]
    normed = raw * lax.rsqrt(mean + eps) * gains[0:1]
    here = jnp.where(layer == 0, normed, raw).astype(BF16)
    rows_ref[...] = here
    row_col, row_row, seg_col, seg_row = block_frame(block, first, second)
    seg_start = jnp.where(seg_col == 0, 0, jnp.where(seg_col == 1, first, second))
    within = row_col - seg_start
    product = dot_nn(here, weights[layer, :, inner:])
    gate = product[:, :inner]
    mixed_in = product[:, inner : inner + mixed]
    dt_raw = product[:, inner + mixed :]
    z_ref[...] = gate.astype(BF16)
    in_ref[...] = mixed_in.astype(BF16)
    dt_ref[...] = dt_raw
    padded[pl.ds(8, BLK), :] = mixed_in
    taps = taps_ref[layer]
    conv = taps[CONV : CONV + 1] + taps[CONV - 1 : CONV] * mixed_in
    for delay in range(1, CONV):
        shifted_in = padded[pl.ds(8 - delay, BLK), :]
        conv = conv + taps[CONV - 1 - delay : CONV - delay] * jnp.where(within >= delay, shifted_in, 0.0)
    padded[pl.ds(0, 8), :] = padded[pl.ds(BLK, 8), :]
    pre_ref[...] = conv
    mixed_low = (conv * sigmoid(conv)).astype(BF16)
    x_low = mixed_low[:, :inner]
    b_low = mixed_low[:, inner : inner + STATE]
    c_low = mixed_low[:, inner + STATE :]
    head = head_ref[layer]
    spread = spread_ref[...]
    shifted, steps, cum2, entering, tail, retained = decay_parts(block, dt_raw, head, seg_col, first, second)
    cum_row = jnp.transpose(cum2)
    x_in = x_low.astype(F32)
    x_steps = spread_heads(steps, spread) * x_in
    x_steps_low = x_steps.astype(BF16)
    allowed = (seg_col == seg_row) & (row_col >= row_row)
    scores = jnp.where(allowed, dot_nt(c_low, b_low), 0.0)
    old_state = state[...]
    st_ref[0] = old_state
    carried = spread_heads(entering, spread) * dot_nn(c_low, old_state.astype(BF16))
    wide = wide_ref[layer]
    pieces = []
    for pair in range(inner // LANES):
        columns = slice(pair * LANES, (pair + 1) * LANES)
        total = None
        for head_index in (2 * pair, 2 * pair + 1):
            gaps = cum2[:, head_index : head_index + 1] - cum_row[head_index : head_index + 1, :]
            coupling = (jnp.exp2(jnp.minimum(gaps, 0.0)) * scores).astype(BF16)
            term = dot_nn(coupling, head_half(x_steps_low[:, columns], head_index))
            total = term if total is None else total + term
        pieces.append(total)
    mixed_out = jnp.concatenate(pieces, axis=1) + carried + wide[0:1] * x_in
    tailed = (spread_heads(tail, spread) * x_steps).astype(BF16)
    keep = spread_heads(jnp.broadcast_to(retained, (8, LANES)), spread)[0:1]
    state[...] = old_state * keep + dot_tn(b_low, tailed)
    y_ref[...] = mixed_out
    gated = mixed_out * (gate * sigmoid(gate))
    gained = (gated * wide[1:2]).astype(BF16)
    gg_ref[...] = gained
    now = Ring(sems.at[layer])
    high, low = split_two(gated * gated)
    ones = jnp.ones((8, inner), BF16)
    sq_own[step] = dot_nt(ones, high) + dot_nt(ones, low)
    sq_pair_copy(now, step).start()

    def send_parts(at_ring, at, values, out_weights):
        store_parts(at_ring, at, dot_nt(values, out_weights), parts)
        pair_copy(at_ring, at, parts, from_pair).start()

    @pl.when(step < DEFER)
    def _():
        kept[step] = gained

    if four:
        for stage in (1, 2, 3):

            @pl.when(step == min(stage - 1, DEFER))
            def _(stage=stage):
                out_line.stage(stage)

    @pl.when(step == DEFER)
    def _():
        if not four:

            @pl.loop(1, line.line)
            def _(stage):
                out_line.stage(stage)

        out_line.finish()
        keep_weights(0).start()

        @pl.loop(0, DEFER)
        def _(at):
            gather(0, AG_PASS, at).wait_send()
            send_parts(ring, at, kept[at], weights[0, :, :inner])

    @pl.when(layer > 0)
    def _():
        pair_copy(ring, block, parts, from_pair).wait_send()
        across_copy(ring, block, parts, from_across).wait_send()

    @pl.when((step >= DEFER) & (layer == 0))
    def _():
        gather(0, AG_PASS, block).wait_send()

    @pl.when(step >= DEFER)
    def _():
        send_parts(now, block, gained, weights[layer, :, :inner])

    def second_stage(slot):
        at_layer, at = slot // blocks, slot % blocks
        at_ring = Ring(sems.at[at_layer])
        pair_copy(at_ring, at, parts, from_pair).wait_recv()
        sq_pair_copy(at_ring, slot).wait_recv()

        add_pair(at, parts, from_pair)
        sq_sums[slot] = sq_own[slot] + sq_pair[slot]
        across_copy(at_ring, at, parts, from_across).start()
        sq_across_copy(at_ring, slot).start()

    def last_stage(at_layer, at):
        at_ring, slot = rings[at_layer], at_layer * blocks + at
        across_copy(at_ring, at, parts, from_across).wait_recv()
        sq_across_copy(at_ring, slot).wait_recv()
        total = add_all(at, parts, from_pair, from_across)
        squares = own_column((sq_sums[slot] + sq_across[slot])[0:1], ring.me * SHARE)
        scale = lax.rsqrt(squares / INNER + eps)
        here = pl.ds(at * SHARE, SHARE)
        mine = pl.ds(ring.me * SHARE, SHARE)
        tot_ref[slot] = total.astype(BF16)
        scale_ref[slot] = scale
        if at_layer == 0:
            before = rows[at, mine, :]
            before_ref[at] = before
            hidden = before.astype(F32) + total * scale
            middle[at] = hidden
            middle_ref[at] = hidden.astype(BF16)
            mean = jnp.sum(hidden * hidden, axis=1, keepdims=True) / hidden.shape[1]
            later = (hidden * lax.rsqrt(mean + eps) * gains[1:2]).astype(BF16)
            rows[at, mine, :] = later
            gather(1, AG_ACROSS, at).start()
            gather(1, AG_OWN, at).start()
        else:
            final_ref[at] = (middle[at] + total * scale).astype(BF16)

    @pl.when((step >= LAG) & (step < blocks + LAG))
    def _():
        last_stage(0, step - LAG)

    @pl.when(step >= blocks + LAG)
    def _():
        last_stage(1, step - LAG - blocks)

    if four:
        for stage, when in ((1, 0), (2, 2), (3, 4)):

            @pl.when(step == when)
            def _(stage=stage):
                line.stage(stage)

    @pl.when(step == 2)
    def _():
        cot_bins.start()

    @pl.when((step >= blocks - PASS_AHEAD) & (step < 2 * blocks - PASS_AHEAD))
    def _():
        gather(1, AG_ACROSS, (step + PASS_AHEAD) % blocks).wait_recv()
        gather(1, AG_PASS, (step + PASS_AHEAD) % blocks).start()

    @pl.when(step == DEFER + 1)
    def _():
        @pl.loop(0, DEFER)
        def _(at):
            second_stage(at)

    @pl.when(step > DEFER)
    def _():
        second_stage(step - 1)

    @pl.when(step == blocks - 1)
    def _():
        if not four:

            @pl.loop(1, line.line)
            def _(stage):
                line.stage(stage)

        line.finish()
        keep_weights(1).start()

    @pl.when(step == 2 * blocks - 1)
    def _():
        second_stage(step)
        cot_bins.wait()
        pick_all(off_ref, cot_arrived, cot_cols_ref)

        @pl.loop(blocks - LAG, blocks)
        def _(at):
            last_stage(1, at)

        @pl.loop(0, blocks)
        def _(at):
            gather(0, AG_OWN, at).wait_send()
            gather(0, AG_ACROSS, at).wait_send()
            for kind in (AG_OWN, AG_ACROSS, AG_PASS):
                gather(1, kind, at).wait_send()
            pair_copy(rings[1], at, parts, from_pair).wait_send()
            across_copy(rings[1], at, parts, from_across).wait_send()
            for at_layer in range(LAYERS):
                sq_pair_copy(rings[at_layer], at_layer * blocks + at).wait_send()
                sq_across_copy(rings[at_layer], at_layer * blocks + at).wait_send()

        for at in range(LAYERS):
            keep_weights(at).wait()


def own_line(column):
    lanes = lax.broadcasted_iota(jnp.int32, (SHARE, LANES), 1)
    rows = lax.broadcasted_iota(jnp.int32, (SHARE, LANES), 0)
    return jnp.sum(jnp.where(lanes == rows, column, 0.0), axis=0, keepdims=True)


TILE_KINDS = (5, 6, 7)
AHEAD = 2
QUEUED = 4
BACK_LAG = 4


def backward_kernel(
    off_ref, cot_ref, tot_ref, scale_ref, before_ref, middle_ref, gains_ref, taps_ref, head_ref, wide_ref, spread_ref,
    weights_ref, final_ref,
    z_ref, in_ref, pre_ref, dt_ref, y_ref, st_ref, normed_ref, gg_ref,
    ginput_ref, small_ref, pack_ref, packs_ref, back_ref,
    dstate, padded, rows, parts, from_pair, from_across, tiles, held, running, weights, acc_out, acc_in,
    packs, pair_buf, arrivals, cols, slots,
    sems, copy_sems, line_sems, row_sems, bin_sems,
):
    step = pl.program_id(0)
    inner = y_ref.shape[1]
    mixed = in_ref.shape[1]
    first, second = off_ref[0], off_ref[1]
    blocks = rows.shape[0]
    phase, block = step // blocks, blocks - 1 - step % blocks
    layer = LAYERS - 1 - phase
    rings = (Ring(sems.at[0]), Ring(sems.at[1]))
    ring = rings[0]
    line = LineReduce(packs, pack_ref, pair_buf, arrivals, line_sems)
    four = line.line == 4
    final_rows = RowExchange(False, final_ref, cols.reshape(blocks, BLK, cols.shape[1]), row_sems)
    bins = BinExchange(False, slots, back_ref, bin_sems)
    mine = pl.ds(ring.me * SHARE, SHARE)

    def gather(at_phase, kind, at):
        own, place = ((cot_ref, column_place), (None, row_place))[at_phase]
        return gather_copy(rings[at_phase], kind, at, own, rows, place)

    def tile_copies(at_phase, at):
        at_ring = rings[at_phase]
        here = tiles.at[at_phase, ring.me, at]
        return [
            at_ring.copy(kind, at, here, here, other)
            for kind, other in zip(TILE_KINDS, (ring.sibling, ring.across, ring.beyond))
        ]

    def make_tile(at_phase, at, grad_low):
        slot = (LAYERS - 1 - at_phase) * blocks + at
        scale = scale_ref[slot]
        weighted = jnp.sum(grad_low.astype(F32) * tot_ref[slot].astype(F32), axis=1, keepdims=True)
        twice = -(scale * scale * scale) / INNER * weighted
        row = lax.broadcasted_iota(jnp.int32, (8, LANES), 0)
        tiles[at_phase, ring.me, at] = jnp.where(row == 0, own_line(twice), own_line(scale))
        for copy in tile_copies(at_phase, at):
            copy.start()

    def prepare(at):
        gather(0, AG_OWN, at).wait_recv()
        gather(0, AG_PASS, at).wait_recv()
        make_tile(0, at, rows[at, mine, :])

    def pass_rows(at_phase, at):
        gather(at_phase, AG_ACROSS, at).wait_recv()
        gather(at_phase, AG_PASS, at).start()

    def send_rows(at):
        gather(0, AG_ACROSS, at).start()
        gather(0, AG_OWN, at).start()

    def own_copy():
        return pltpu.make_async_copy(cot_ref, column_place(rows, ring.me), copy_sems.at[0])

    def load_weights(at_layer):
        return pltpu.make_async_copy(weights_ref.at[at_layer], weights, copy_sems.at[1])

    def load_held(at_phase):
        return pltpu.make_async_copy((middle_ref, before_ref)[at_phase], held, copy_sems.at[3 + at_phase])

    def store_packs():
        return pltpu.make_async_copy(packs, packs_ref, copy_sems.at[2])

    def clear():
        dstate[...] = jnp.zeros_like(dstate)
        padded[pl.ds(BLK, 8), :] = jnp.zeros((8, mixed), F32)
        acc_out[...] = jnp.zeros_like(acc_out)
        acc_in[...] = jnp.zeros_like(acc_in)

    @pl.when(step == 0)
    def _():
        own_copy().start()
        load_weights(LAYERS - 1).start()
        load_held(0).start()
        ring.greet()

        send_rows(blocks - 1)
        clear()
        small_ref[...] = jnp.zeros_like(small_ref)
        own_copy().wait()
        pass_rows(0, blocks - 1)
        for at in range(1, QUEUED):
            send_rows(blocks - 1 - at)
        prepare(blocks - 1)
        for at in range(1, AHEAD + 1):
            pass_rows(0, blocks - 1 - at)
        for at in range(1, AHEAD):
            prepare(blocks - 1 - at)
        load_weights(LAYERS - 1).wait()

    @pl.when(step == blocks)
    def _():
        load_weights(0).start()
        clear()
        load_weights(0).wait()

    @pl.when(phase > 0)
    def _():
        gather(1, AG_OWN, block).wait_recv()
        gather(1, AG_PASS, block).wait_recv()

    for at_phase in range(LAYERS):

        @pl.when(phase == at_phase)
        def _(at_phase=at_phase):
            for copy in tile_copies(at_phase, block):
                copy.wait_recv()

    here = rows[block]
    tile_rows = [tiles[phase, owner, block] for owner in range(4)]
    twice_here = jnp.concatenate([own_column(tile[0:1], 0) for tile in tile_rows], axis=0)
    scale_here = jnp.concatenate([own_column(tile[1:2], 0) for tile in tile_rows], axis=0)
    row_col, row_row, seg_col, seg_row = block_frame(block, first, second)
    seg_end = jnp.where(seg_col == 0, first, jnp.where(seg_col == 1, second, BIN))
    remaining = seg_end - row_col
    head = head_ref[layer]
    wide = wide_ref[layer]
    spread = spread_ref[...]
    skip, gain = wide[0:1], wide[1:2]
    gate = z_ref[...].astype(F32)
    mixed_out = y_ref[...]
    conv = pre_ref[...]
    gate_sig = sigmoid(gate)
    gate_silu = gate * gate_sig
    gated = mixed_out * gate_silu
    grad_scaled = dot_nn(here, weights[:, :inner]) * scale_here
    grad_gated = grad_scaled * gain + twice_here * gated
    grad_out = grad_gated * gate_silu
    grad_gate = grad_gated * mixed_out * (gate_sig * (1.0 + gate * (1.0 - gate_sig)))
    grad_out_low = grad_out.astype(BF16)

    conv_sig = sigmoid(conv)
    mixed_low = (conv * conv_sig).astype(BF16)
    x_low = mixed_low[:, :inner]
    b_low = mixed_low[:, inner : inner + STATE]
    c_low = mixed_low[:, inner + STATE :]
    x_in = x_low.astype(F32)
    shifted, steps, cum2, entering, tail, retained = decay_parts(block, dt_ref[...], head, seg_col, first, second)
    cum_row = jnp.transpose(cum2)
    steps_wide = spread_heads(steps, spread)
    x_steps_low = (steps_wide * x_in).astype(BF16)
    x_steps = x_steps_low.astype(F32)

    allowed = (seg_col == seg_row) & (row_col <= row_row)
    scores = jnp.where(allowed, dot_nt(b_low, c_low), 0.0)
    grad_scores = jnp.zeros((BLK, BLK), F32)
    pieces = []
    for pair in range(inner // LANES):
        columns = slice(pair * LANES, (pair + 1) * LANES)
        total = None
        for head_index in (2 * pair, 2 * pair + 1):
            gaps = cum_row[head_index : head_index + 1, :] - cum2[:, head_index : head_index + 1]
            decays = jnp.exp2(jnp.minimum(gaps, 0.0))
            coupling = (decays * scores).astype(BF16)
            term = dot_nn(coupling, head_half(grad_out_low[:, columns], head_index))
            total = term if total is None else total + term
            grad_scores = grad_scores + decays * dot_nt(
                head_half(x_steps_low[:, columns], head_index), grad_out_low[:, columns]
            )
        pieces.append(total)
    grad_scores_low = jnp.where(allowed, grad_scores, 0.0).astype(BF16)
    old_dstate = dstate[...]
    old_dstate_low = old_dstate.astype(BF16)
    old_state = st_ref[0]
    tail_wide = spread_heads(tail, spread)
    from_state = tail_wide * dot_nn(b_low, old_dstate_low)
    grad_unit = jnp.concatenate(pieces, axis=1) + from_state
    entered = (spread_heads(entering, spread) * grad_out).astype(BF16)
    tailed = (tail_wide * x_steps).astype(BF16)
    grad_c = dot_tn(grad_scores_low, b_low) + dot_nt(entered, old_state.astype(BF16))
    grad_b = dot_nn(grad_scores_low, c_low) + dot_nt(tailed, old_dstate_low)
    keep = spread_heads(jnp.broadcast_to(retained, (8, LANES)), spread)[0:1]
    dstate[...] = old_dstate * keep + dot_tn(c_low, entered)

    balance = gather_heads(grad_out_low.astype(F32) * (mixed_out - skip * x_in) - x_steps * grad_unit, spread)
    direct = gather_heads(x_in * grad_unit, spread)
    final_wide = jnp.sum(x_steps * from_state, axis=0, keepdims=True) + keep * jnp.sum(
        old_dstate * old_state, axis=0, keepdims=True
    )
    final = gather_heads(jnp.broadcast_to(final_wide, (8, inner)), spread)[0:1]
    above = lax.broadcasted_iota(jnp.int32, (BLK, BLK), 0)
    below = lax.broadcasted_iota(jnp.int32, (BLK, BLK), 1)
    upper = jnp.where(above <= below, 1.0, 0.0).astype(BF16)
    thirds = dot_nn(upper, jnp.concatenate(split_three(balance), axis=1))
    grad_log = thirds[:, :LANES] + thirds[:, LANES : 2 * LANES] + thirds[:, 2 * LANES :] + final
    grad_steps = direct + grad_log * head[1:2]
    grad_dt = grad_steps * sigmoid(shifted)
    small_ref[layer, 7:8, :LANES] += jnp.sum(grad_dt, axis=0, keepdims=True)
    small_ref[layer, 7:8, LANES : 2 * LANES] += jnp.sum(grad_log * steps, axis=0, keepdims=True) * head[1:2]
    small_ref[layer, 6:7, :inner] += jnp.sum(grad_out * x_in, axis=0, keepdims=True)
    small_ref[layer, 6:7, inner : 2 * inner] += jnp.sum(grad_scaled * gated, axis=0, keepdims=True)

    grad_x = steps_wide * grad_unit + skip * grad_out
    grad_conv = jnp.concatenate([grad_x, grad_b, grad_c], axis=1) * (
        conv_sig * (1.0 + conv * (1.0 - conv_sig))
    )
    padded[pl.ds(0, BLK), :] = grad_conv
    mixed_in = in_ref[...].astype(F32)
    taps = taps_ref[layer]
    grad_in = taps[CONV - 1 : CONV] * grad_conv
    small_ref[layer, CONV : CONV + 1, :mixed] += jnp.sum(grad_conv, axis=0, keepdims=True)
    small_ref[layer, CONV - 1 : CONV, :mixed] += jnp.sum(mixed_in * grad_conv, axis=0, keepdims=True)
    for delay in range(1, CONV):
        later = jnp.where(remaining > delay, padded[pl.ds(delay, BLK), :], 0.0)
        grad_in = grad_in + taps[CONV - 1 - delay : CONV - delay] * later
        small_ref[layer, CONV - 1 - delay : CONV - delay, :mixed] += jnp.sum(mixed_in * later, axis=0, keepdims=True)
    padded[pl.ds(BLK, 8), :] = padded[pl.ds(0, 8), :]
    gproj = jnp.concatenate([grad_gate.astype(BF16), grad_in.astype(BF16), grad_dt.astype(BF16)], axis=1)
    acc_out[...] += dot_tn(here, (gg_ref[...].astype(F32) * scale_here).astype(BF16))
    acc_in[...] += dot_tn(normed_ref[...], gproj)
    part = dot_nt(gproj, weights[:, inner:])

    @pl.when(phase > 0)
    def _():
        pair_copy(ring, block, parts, from_pair).wait_send()
        across_copy(ring, block, parts, from_across).wait_send()

    @pl.when(phase == 0)
    def _():
        gather(0, AG_PASS, block).wait_send()

    now = Ring(sems.at[phase])
    store_parts(now, block, part, parts)
    pair_copy(now, block, parts, from_pair).start()

    def second_stage(turn):
        at_phase, at = turn // blocks, blocks - 1 - turn % blocks
        at_ring = Ring(sems.at[at_phase])
        pair_copy(at_ring, at, parts, from_pair).wait_recv()

        add_pair(at, parts, from_pair)
        across_copy(at_ring, at, parts, from_across).start()

    def last_stage(at_phase, at):
        at_layer = LAYERS - 1 - at_phase
        across_copy(rings[at_phase], at, parts, from_across).wait_recv()
        grad_normed = add_all(at, parts, from_pair, from_across)
        hidden = held[at].astype(F32)
        width = hidden.shape[1]
        root = lax.rsqrt(jnp.sum(hidden * hidden, axis=1, keepdims=True) / width + eps)
        gained = grad_normed * gains_ref[at_layer : at_layer + 1, :]
        small_ref[at_layer, 5:6, :] += jnp.sum(grad_normed * hidden * root, axis=0, keepdims=True)
        along = jnp.sum(gained * hidden, axis=1, keepdims=True) * (root * root * root) / width
        change = gained * root - hidden * along
        if at_phase == 0:
            grad = rows[at, mine, :].astype(F32) + change
            running[at] = grad
            grad_low = grad.astype(BF16)
            rows[at, mine, :] = grad_low
            gather(1, AG_ACROSS, at).start()
            gather(1, AG_OWN, at).start()
            make_tile(1, at, grad_low)
        else:
            ginput_ref[at] = (running[at] + change).astype(BF16)

    @pl.when(step == BACK_LAG)
    def _():
        load_held(0).wait()

    @pl.when(step == blocks + BACK_LAG)
    def _():
        load_held(1).start()
        load_held(1).wait()

    @pl.when((step >= BACK_LAG) & (step < blocks + BACK_LAG))
    def _():
        last_stage(0, blocks - 1 - (step - BACK_LAG))

    @pl.when(step >= blocks + BACK_LAG)
    def _():
        last_stage(1, blocks - 1 - (step - BACK_LAG - blocks))

    @pl.when(step + QUEUED < blocks)
    def _():
        send_rows(blocks - 1 - (step + QUEUED))

    @pl.when(step + AHEAD + 1 < blocks)
    def _():
        pass_rows(0, blocks - 1 - (step + AHEAD + 1))

    @pl.when(step + AHEAD < blocks)
    def _():
        prepare(blocks - 1 - (step + AHEAD))

    @pl.when((step >= blocks - PASS_AHEAD) & (step < 2 * blocks - PASS_AHEAD))
    def _():
        pass_rows(1, blocks - 1 - (step + PASS_AHEAD) % blocks)

    @pl.when(step >= 1)
    def _():
        second_stage(step - 1)

    @pl.when(step == 1)
    def _():
        final_rows.start()

    @pl.when(step == 4)
    def _():
        final_rows.wait()
        place_all(off_ref, cols, slots)
        bins.start()

    @pl.when(step == blocks - 1)
    def _():
        packs[:, :inner] = acc_out[...].astype(BF16)
        packs[:, inner:] = acc_in[...].astype(BF16)
        line.send_pairs()

    if four:
        for stage in (0, 1, 2):

            @pl.when(step == blocks + 1 + 2 * stage)
            def _(stage=stage):
                line.stage(stage)

    @pl.when(step == 2 * blocks - 1)
    def _():
        second_stage(step)
        if not four:

            @pl.loop(0, line.line - 1)
            def _(stage):
                line.stage(stage)

        line.finish()
        packs[:, :inner] = acc_out[...].astype(BF16)
        packs[:, inner:] = acc_in[...].astype(BF16)
        store_packs().start()

        @pl.loop(0, BACK_LAG)
        def _(turn):
            last_stage(1, BACK_LAG - 1 - turn)

        @pl.loop(0, blocks)
        def _(at):
            gather(0, AG_OWN, at).wait_send()
            gather(0, AG_ACROSS, at).wait_send()
            for kind in (AG_OWN, AG_ACROSS, AG_PASS):
                gather(1, kind, at).wait_send()
            pair_copy(rings[1], at, parts, from_pair).wait_send()
            across_copy(rings[1], at, parts, from_across).wait_send()
            for at_phase in range(LAYERS):
                for copy in tile_copies(at_phase, at):
                    copy.wait_send()

        store_packs().wait()
        bins.wait()


def whole(shape):
    return pl.BlockSpec(shape, lambda *at: (0,) * len(shape))


def exchange_scratch(blocks, width):
    return [
        pltpu.VMEM((blocks, BLK, width), BF16),
        pltpu.VMEM((blocks, BLK, width), BF16),
        pltpu.VMEM((blocks, 2 * SHARE, width), BF16),
        pltpu.VMEM((blocks, SHARE, width), BF16),
    ]


def layers_forward(offsets, given, packs, own_gains, given_cot, taps, head, wide, spread):
    blocks, width = BIN // BLK, own_gains.shape[1]
    inner, mixed = wide.shape[2], taps.shape[2]
    dp_count, members, span, columns = given_cot.shape
    total = packs.shape[2]
    steps = LAYERS * blocks
    vmem, hbm = pl.BlockSpec(memory_space=pltpu.VMEM), pl.BlockSpec(memory_space=pltpu.HBM)

    def by_block(size):
        return pl.BlockSpec((BLK, size), lambda s: (s, 0))

    return pl.pallas_call(
        forward_kernel,
        grid=(steps,),
        in_specs=[pl.BlockSpec(memory_space=pltpu.SMEM), hbm, vmem, vmem, hbm] + [vmem] * 4,
        out_specs=[
            by_block(width), by_block(inner), by_block(mixed), by_block(mixed),
            by_block(LANES), by_block(inner), by_block(inner),
            pl.BlockSpec((1, STATE, inner), lambda s: (s, 0, 0)),
            vmem, vmem, vmem, vmem, vmem, vmem, vmem, hbm,
        ],
        out_shape=[
            jax.ShapeDtypeStruct((steps * BLK, width), BF16),
            jax.ShapeDtypeStruct((steps * BLK, inner), BF16),
            jax.ShapeDtypeStruct((steps * BLK, mixed), BF16),
            jax.ShapeDtypeStruct((steps * BLK, mixed), F32),
            jax.ShapeDtypeStruct((steps * BLK, LANES), F32),
            jax.ShapeDtypeStruct((steps * BLK, inner), F32),
            jax.ShapeDtypeStruct((steps * BLK, inner), BF16),
            jax.ShapeDtypeStruct((steps, STATE, inner), F32),
            jax.ShapeDtypeStruct((blocks, SHARE, width), BF16),
            jax.ShapeDtypeStruct((blocks, SHARE, width), BF16),
            jax.ShapeDtypeStruct((steps, SHARE, width), BF16),
            jax.ShapeDtypeStruct((steps, SHARE, 1), F32),
            jax.ShapeDtypeStruct((blocks, SHARE, width), BF16),
            jax.ShapeDtypeStruct(own_gains.shape, F32),
            jax.ShapeDtypeStruct((blocks, BLK, columns), BF16),
            jax.ShapeDtypeStruct((LAYERS, width, total), BF16),
        ],
        scratch_shapes=[pltpu.VMEM((STATE, inner), F32), pltpu.VMEM((BLK + 8, mixed), F32)]
        + exchange_scratch(blocks, width)
        + [pltpu.VMEM((steps, 8, BLK), F32)] * 4
        + [
            pltpu.VMEM((LAYERS, width, total), BF16),
            pltpu.VMEM((members, dp_count * span, columns), BF16),
            pltpu.VMEM((blocks, BLK, columns), BF16),
            pltpu.VMEM((members, dp_count * span, columns), BF16),
            pltpu.VMEM((dp_count,) + own_gains.shape, F32),
            pltpu.VMEM((blocks, SHARE, width), F32),
            pltpu.VMEM((DEFER, BLK, inner), BF16),
            pltpu.SemaphoreType.DMA((LAYERS, 7, blocks, 2)),
            pltpu.SemaphoreType.DMA((LAYERS + 1,)),
            pltpu.SemaphoreType.DMA((LAYERS + 1, 6, dp_count // 2)),
            pltpu.SemaphoreType.DMA((dp_count, 2)),
            pltpu.SemaphoreType.DMA((dp_count, 2)),
            pltpu.SemaphoreType.DMA((dp_count, 2)),
        ],
        compiler_params=pltpu.CompilerParams(
            vmem_limit_bytes=48 * 1024 * 1024, collective_id=1, has_side_effects=True
        ),
        cost_estimate=pl.CostEstimate(flops=6 * 10**10, bytes_accessed=6 * 10**7, transcendentals=10**7),
        name="layers_forward",
    )(offsets, given, packs, own_gains, given_cot, taps, head, wide, spread)


def layers_backward(offsets, cot, totals, scales, before, middle, gains, taps, head, wide, spread, weights, final, saved, span):
    gate, mixed_in, conv, dt_raw, mixed_out, states, normed, gained = saved
    blocks, _, columns = cot.shape
    width = gains.shape[1]
    inner, mixed = wide.shape[2], taps.shape[2]
    total = weights.shape[2]
    steps = LAYERS * blocks
    count = lax.axis_size("dp")
    vmem, hbm = pl.BlockSpec(memory_space=pltpu.VMEM), pl.BlockSpec(memory_space=pltpu.HBM)

    def by_block(size):
        return pl.BlockSpec((BLK, size), lambda s: (steps - 1 - s, 0))

    return pl.pallas_call(
        backward_kernel,
        grid=(steps,),
        in_specs=[pl.BlockSpec(memory_space=pltpu.SMEM)]
        + [vmem] * 3
        + [hbm, hbm]
        + [vmem] * 5
        + [hbm, hbm]
        + [
            by_block(inner), by_block(mixed), by_block(mixed), by_block(LANES), by_block(inner),
            pl.BlockSpec((1, STATE, inner), lambda s: (steps - 1 - s, 0, 0)),
            by_block(width), by_block(inner),
        ],
        out_specs=[vmem, vmem, vmem, hbm, hbm],
        out_shape=[
            jax.ShapeDtypeStruct((blocks, SHARE, width), BF16),
            jax.ShapeDtypeStruct((LAYERS, 8, width), F32),
            jax.ShapeDtypeStruct((width // count, total), F32),
            jax.ShapeDtypeStruct((width, total), BF16),
            jax.ShapeDtypeStruct((count, 3, span, columns), BF16),
        ],
        scratch_shapes=[pltpu.VMEM((STATE, inner), F32), pltpu.VMEM((BLK + 8, mixed), F32)]
        + exchange_scratch(blocks, width)
        + [
            pltpu.VMEM((LAYERS, 4, blocks, 8, LANES), F32),
            pltpu.VMEM((blocks, SHARE, width), BF16),
            pltpu.VMEM((blocks, SHARE, width), F32),
            pltpu.VMEM((width, total), BF16),
            pltpu.VMEM((width, inner), F32),
            pltpu.VMEM((width, total - inner), F32),
            pltpu.VMEM((width, total), BF16),
        ]
        + [
            pltpu.VMEM((count // 2, width // count, total), BF16),
            pltpu.VMEM((count // 2 + 1, width // count, total), BF16),
            pltpu.VMEM((BIN, columns), BF16),
            pltpu.VMEM((3, count * span, columns), BF16),
            pltpu.SemaphoreType.DMA((LAYERS, 8, blocks, 2)),
            pltpu.SemaphoreType.DMA((3 + LAYERS,)),
            pltpu.SemaphoreType.DMA((5, count // 2)),
            pltpu.SemaphoreType.DMA((4, 2)),
            pltpu.SemaphoreType.DMA((count, 2)),
        ],
        compiler_params=pltpu.CompilerParams(
            vmem_limit_bytes=61 * 1024 * 1024, collective_id=2, has_side_effects=True
        ),
        cost_estimate=pl.CostEstimate(flops=6 * 10**10, bytes_accessed=6 * 10**7, transcendentals=10**7),
        name="layers_backward",
    )(
        offsets, cot, totals, scales, before, middle, gains, taps, head, wide, spread, weights, final,
        gate, mixed_in, conv, dt_raw, mixed_out, states, normed, gained,
    )


def spread_matrix(inner, heads):
    lane_head = lax.broadcasted_iota(jnp.int32, (2 * LANES, inner), 1) // (inner // heads)
    row_head = lax.broadcasted_iota(jnp.int32, (2 * LANES, inner), 0) % LANES
    return jnp.where(lane_head == row_head, 1.0, 0.0).astype(BF16)


SEQ_MIN = 512


def choose_rows(wanted, valid, begin, end):
    slots = begin + lax.broadcasted_iota(jnp.int32, (wanted.shape[0], end - begin), 1)
    return jnp.where((slots == wanted) & valid, 1.0, 0.0).astype(BF16)


def pick_all(off_ref, arrived, cols):
    first, second = off_ref[0], off_ref[1]
    length = arrived.shape[1]
    for block in range(cols.shape[0]):
        low, high = block * BLK, (block + 1) * BLK
        row = low + lax.broadcasted_iota(jnp.int32, (BLK, 1), 0)
        total = None
        for member, begin, least, most in ((1, first, SEQ_MIN, length), (2, second, BIN - length, BIN - SEQ_MIN)):
            reach = BIN - SEQ_MIN if member == 1 else BIN
            start, end = max(low - most, 0), min(high - least, length)
            if end <= 0 or start >= length or low >= reach:
                continue
            valid = (row >= first) & (row < second) if member == 1 else row >= second
            term = dot_nn(choose_rows(row - begin, valid, start, end), arrived[member, start:end, :])
            total = term if total is None else total + term
        if high <= length:
            own = arrived[0, low:high, :].astype(F32)
            own = jnp.where(row < first, own, 0.0)
            total = own if total is None else total + own
        cols[block] = total.astype(BF16)


def place_all(off_ref, cols, slots):
    first, second = off_ref[0], off_ref[1]
    length = slots.shape[1]
    for chunk in range(length // BLK):
        low, high = chunk * BLK, (chunk + 1) * BLK
        position = low + lax.broadcasted_iota(jnp.int32, (BLK, 1), 0)
        slots[0, low:high, :] = jnp.where(position < first, cols[low:high, :].astype(F32), 0.0).astype(BF16)
        for member, begin, stop, least, most, reach in (
            (1, first, second, SEQ_MIN, length, BIN - SEQ_MIN),
            (2, second, BIN, BIN - length, BIN - SEQ_MIN, BIN),
        ):
            wanted = begin + position
            start, end = least + low, min(most + high, reach)
            choose = choose_rows(wanted, wanted < stop, start, end)
            slots[member, low:high, :] = dot_nn(choose, cols[start:end, :]).astype(BF16)


class LineGather:
    def __init__(self, own, target, sems):
        self.own, self.target, self.sems = own, target, sems
        me = lax.axis_index("dp")
        self.me, self.low, self.high = me, me % 2, me // 2
        self.line = lax.axis_size("dp") // 2
        self.span = own.shape[0]

    def copy(self, kind, place, other, own):
        here = self.target.at[pl.ds((place * 2 + self.low) * self.span, self.span), :]
        arrival = 2 if kind == 2 else 3
        return pltpu.make_async_remote_copy(
            src_ref=self.own if own else here, dst_ref=here,
            send_sem=self.sems.at[kind, place], recv_sem=self.sems.at[arrival + 1, place],
            device_id={"dp": other}, device_id_type=pl.DeviceIdType.MESH,
        )

    def right(self, place, own=False):
        return self.copy(0, place, (self.high + 1) * 2 + self.low, own)

    def left(self, place, own=False):
        return self.copy(1, place, (self.high - 1) * 2 + self.low, own)

    def pair(self, place, own=False):
        return self.copy(2, place, self.high * 2 + 1 - self.low, own)

    def local(self):
        here = self.target.at[pl.ds(self.me * self.span, self.span), :]
        return pltpu.make_async_copy(self.own, here, self.sems.at[5, 0])

    def start_pair(self):
        self.local().start()
        self.pair(self.high, True).start()

    def start_line(self):
        @pl.when(self.high < self.line - 1)
        def _():
            self.right(self.high, True).start()

        @pl.when(self.high > 0)
        def _():
            self.left(self.high, True).start()

    def start(self):
        self.start_line()
        self.start_pair()

    def stage(self, step):
        @pl.when(self.high - step >= 0)
        def _():
            self.right(self.high - step).wait_recv()

            @pl.when(self.high < self.line - 1)
            def _():
                self.right(self.high - step).start()

            self.pair(self.high - step).start()

        @pl.when(self.high + step < self.line)
        def _():
            self.left(self.high + step).wait_recv()

            @pl.when(self.high > 0)
            def _():
                self.left(self.high + step).start()

            self.pair(self.high + step).start()

    def finish(self):
        self.local().wait()

        @pl.loop(0, self.line)
        def _(place):
            self.pair(place).wait_recv()
            self.pair(place).wait_send()

            @pl.when((self.high < self.line - 1) & (place <= self.high))
            def _():
                self.right(place).wait_send()

            @pl.when((self.high > 0) & (place >= self.high))
            def _():
                self.left(place).wait_send()


class TileGather:
    def __init__(self, own, target, sems):
        self.own, self.target, self.sems = own, target, sems
        self.count, self.me = lax.axis_size("dp"), lax.axis_index("dp")

    def remote(self, step):
        return pltpu.make_async_remote_copy(
            src_ref=self.own, dst_ref=self.target.at[self.me],
            send_sem=self.sems.at[step, 0], recv_sem=self.sems.at[step, 1],
            device_id={"dp": (self.me + step) % self.count}, device_id_type=pl.DeviceIdType.MESH,
        )

    def start(self):
        self.target[self.me] = self.own[...]

        @pl.loop(1, self.count)
        def _(step):
            self.remote(step).start()

    def wait(self):
        @pl.loop(1, self.count)
        def _(step):
            self.remote(step).wait()


class LineReduce:
    def __init__(self, given, out, pair_buf, arrivals, sems):
        self.given, self.out, self.pair_buf = given, out, pair_buf
        self.arrivals, self.sems = arrivals, sems
        me = lax.axis_index("dp")
        self.low, self.high = me % 2, me // 2
        self.line = lax.axis_size("dp") // 2
        self.span = out.shape[0]

    def chunk(self, place, low):
        return pl.ds((place * 2 + low) * self.span, self.span)

    def pair(self, place):
        return pltpu.make_async_remote_copy(
            src_ref=self.given.at[self.chunk(place, 1 - self.low), :], dst_ref=self.pair_buf.at[place],
            send_sem=self.sems.at[0, place], recv_sem=self.sems.at[1, place],
            device_id={"dp": self.high * 2 + 1 - self.low}, device_id_type=pl.DeviceIdType.MESH,
        )

    def onward(self, place, right):
        slot = place + 1 if right else place
        other = (self.high + 1 if right else self.high - 1) * 2 + self.low
        return pltpu.make_async_remote_copy(
            src_ref=self.pair_buf.at[place], dst_ref=self.arrivals.at[slot],
            send_sem=self.sems.at[2, place], recv_sem=self.sems.at[3 if right else 4, place],
            device_id={"dp": other}, device_id_type=pl.DeviceIdType.MESH,
        )

    def by_distance(self, step, act):
        distance = self.line - 1 - step

        @pl.when(self.high + distance < self.line)
        def _():
            act(self.high + distance, True)

        @pl.when(self.high - distance >= 0)
        def _():
            act(self.high - distance, False)

    def send_pairs(self):
        @pl.loop(0, self.line - 1)
        def _(step):
            self.by_distance(step, lambda place, right: self.pair(place).start())

        self.pair(self.high).start()

    def fold(self, place):
        return self.given[self.chunk(place, self.low), :].astype(F32) + self.pair_buf[place].astype(F32)

    def pass_on(self, place, right):
        self.pair(place).wait_recv()
        upstream = (self.high > 0) if right else (self.high < self.line - 1)
        slot = place + 1 if right else place

        @pl.when(upstream)
        def _():
            self.onward(place, right).wait_recv()
            self.pair_buf[place] = (self.fold(place) + self.arrivals[slot].astype(F32)).astype(BF16)

        @pl.when(jnp.logical_not(upstream))
        def _():
            self.pair_buf[place] = self.fold(place).astype(BF16)

        self.onward(place, right).start()

    def stage(self, step):
        self.by_distance(step, self.pass_on)

    def finish(self):
        here = self.high
        self.pair(here).wait_recv()
        self.out[...] = self.fold(here)

        @pl.when(here > 0)
        def _():
            self.onward(here, True).wait_recv()
            self.out[...] += self.arrivals[here + 1].astype(F32)

        @pl.when(here < self.line - 1)
        def _():
            self.onward(here, False).wait_recv()
            self.out[...] += self.arrivals[here].astype(F32)

        @pl.loop(0, self.line)
        def _(place):
            self.pair(place).wait_send()

            @pl.when(place != here)
            def _():
                self.onward(place, True).wait_send()


def line_scratch(count, span, columns):
    line = count // 2
    return [
        pltpu.VMEM((line, span, columns), BF16),
        pltpu.VMEM((line + 1, span, columns), BF16),
        pltpu.SemaphoreType.DMA((5, line)),
    ]


class MemberGather:
    def __init__(self, target, sems):
        self.target, self.sems = target, sems
        self.me = lax.axis_index("tensor")

    def remote(self, step):
        return pltpu.make_async_remote_copy(
            src_ref=self.target.at[self.me], dst_ref=self.target.at[self.me],
            send_sem=self.sems.at[step, 0], recv_sem=self.sems.at[step, 1],
            device_id={"tensor": (self.me + step) % 4}, device_id_type=pl.DeviceIdType.MESH,
        )

    def start(self):
        for step in range(1, 4):
            self.remote(step).start()

    def wait(self):
        for step in range(1, 4):
            self.remote(step).wait()


def end_kernel(
    off_ref, grad_ref, packs_ref, small_ref, later_ref,
    back_ref, pack_ref, sum_ref, shared_ref, maps_ref,
    cols, slots, pair_buf, arrivals, line_sems, smalls, shared, maps,
    row_sems, bin_sems, small_sems, shared_sems, maps_sems,
):
    ring = Ring(None)
    ring.greet()
    inner = (pack_ref.shape[1] - 2 * STATE - LANES) // 3
    first_map = 3 * inner
    rows = RowExchange(False, grad_ref, cols.reshape(BIN // BLK, BLK, cols.shape[1]), row_sems)
    bins = BinExchange(False, slots, back_ref, bin_sems)
    line = LineReduce(packs_ref, pack_ref, pair_buf, arrivals, line_sems)
    dp_smalls = TileGather(small_ref, smalls, small_sems)
    shared_smalls = MemberGather(shared, shared_sems)
    shared_maps = MemberGather(maps, maps_sems)
    rows.start()
    line.send_pairs()
    dp_smalls.start()
    rows.wait()
    place_all(off_ref, cols, slots)
    bins.start()

    @pl.loop(0, line.line - 1)
    def _(step):
        line.stage(step)

    dp_smalls.wait()
    sum_ref[...] = smalls[0]

    @pl.loop(1, smalls.shape[0])
    def _(at):
        sum_ref[...] += smalls[at]

    shared[ring.me] = sum_ref[...]
    shared_smalls.start()
    line.finish()
    maps[ring.me, 0] = pack_ref[:, first_map : first_map + 2 * STATE].astype(BF16)
    maps[ring.me, 1] = later_ref[:, first_map : first_map + 2 * STATE].astype(BF16)
    shared_maps.start()
    shared_smalls.wait()
    shared_ref[...] = (shared[0] + shared[1]) + (shared[2] + shared[3])
    shared_maps.wait()
    for layer in range(LAYERS):
        maps_ref[layer] = (maps[0, layer].astype(F32) + maps[1, layer].astype(F32)) + (
            maps[2, layer].astype(F32) + maps[3, layer].astype(F32)
        )
    bins.wait()


def end_exchange(offsets, grad_rows, packs, small, later_pack, span):
    count = lax.axis_size("dp")
    width, total = packs.shape
    columns = width // 4
    vmem = pl.BlockSpec(memory_space=pltpu.VMEM)
    pack_rows = width // count
    return pl.pallas_call(
        end_kernel,
        in_specs=[pl.BlockSpec(memory_space=pltpu.SMEM)] + [vmem] * 4,
        out_specs=[pl.BlockSpec(memory_space=pltpu.HBM), vmem, vmem, vmem, vmem],
        out_shape=[
            jax.ShapeDtypeStruct((count, 3, span, columns), BF16),
            jax.ShapeDtypeStruct((pack_rows, total), F32),
            jax.ShapeDtypeStruct(small.shape, F32),
            jax.ShapeDtypeStruct(small.shape, F32),
            jax.ShapeDtypeStruct((LAYERS, pack_rows, 2 * STATE), F32),
        ],
        scratch_shapes=[
            pltpu.VMEM((BIN, columns), BF16),
            pltpu.VMEM((3, count * span, columns), BF16),
        ]
        + line_scratch(count, pack_rows, total)
        + [
            pltpu.VMEM((count,) + small.shape, F32),
            pltpu.VMEM((4,) + small.shape, F32),
            pltpu.VMEM((4, LAYERS, pack_rows, 2 * STATE), BF16),
            pltpu.SemaphoreType.DMA((4, 2)),
            pltpu.SemaphoreType.DMA((count, 2)),
            pltpu.SemaphoreType.DMA((count, 2)),
            pltpu.SemaphoreType.DMA((4, 2)),
            pltpu.SemaphoreType.DMA((4, 2)),
        ],
        compiler_params=pltpu.CompilerParams(
            vmem_limit_bytes=56 * 1024 * 1024, collective_id=3, has_side_effects=True
        ),
        cost_estimate=pl.CostEstimate(flops=6 * 10**10, bytes_accessed=6 * 10**7, transcendentals=0),
        name="end_exchange",
    )(offsets, grad_rows, packs, small, later_pack)


def pad_to(values, rows, columns):
    return jnp.pad(values, ((0, rows - values.shape[0]), (0, columns - values.shape[1])))


def on_device(
    tokens, cotangent, lengths, packing, pre_gain, w_z, w_x, w_bc, w_dt, conv_x, conv_bc, head_params, norm_gain, w_out,
):
    dp_count = lax.axis_size("dp")
    bin_index = lax.axis_index("dp")
    seq_total, pos_here, cols_here = tokens.shape
    inner_part = conv_x.shape[2]
    heads_here = head_params.shape[2]
    dp_rows = w_z.shape[1]
    mixed = inner_part + 2 * STATE
    triples = lengths[packing].reshape(dp_count, 3)
    offsets = jnp.cumsum(triples, axis=1) - triples
    my_offsets = offsets[bin_index]
    bounds = my_offsets[1:3]
    groups = packing.reshape(dp_count, 3)

    spread = spread_matrix(inner_part, heads_here)
    packs = []
    for layer in range(LAYERS):
        own = jnp.concatenate(
            [w_out[layer].T, w_z[layer], w_x[layer], w_bc[layer], pad_to(w_dt[layer], dp_rows, LANES)], axis=1
        )
        taps = jnp.concatenate([conv_x[layer], conv_bc[layer]], axis=1).astype(F32)
        head = jnp.stack([head_params[layer, 0], -jnp.exp(head_params[layer, 1])])
        wide = jnp.stack(
            [jnp.repeat(head_params[layer, 2], inner_part // heads_here), norm_gain[layer].astype(F32)]
        )
        packs.append((own, pad_to(taps, 8, mixed), pad_to(head, 8, LANES), pad_to(wide, 8, inner_part)))

    own_gains = lax.dynamic_update_slice(
        jnp.zeros((8, dp_count * dp_rows), F32), pre_gain.astype(F32), (0, bin_index * dp_rows)
    )
    taps_all, head_all, wide_all = (jnp.stack([pack[at] for pack in packs]) for at in (1, 2, 3))
    (
        rows_all, gate, mixed_in, conv, dt_raw, mixed_out, gained_all, states, first_before, middle, totals, scales,
        final_rows, gains, cot_columns, all_weights,
    ) = layers_forward(
        bounds, tokens[groups], jnp.stack([pack[0] for pack in packs]), own_gains, cotangent[groups],
        taps_all, head_all, wide_all, spread,
    )
    grad_rows, small, later_pack, first_packs, activations_back = layers_backward(
        bounds, cot_columns, totals, scales, first_before, middle, gains, taps_all, head_all, wide_all, spread,
        all_weights, final_rows, (gate, mixed_in, conv, dt_raw, mixed_out, states, rows_all, gained_all), pos_here,
    )
    returned, first_pack, sums, shared, maps = end_exchange(bounds, grad_rows, first_packs, small, later_pack, pos_here)
    grad_convx = sums[:, : CONV + 1, :inner_part]
    grad_convbc = shared[:, : CONV + 1, inner_part:mixed]
    shard_pre = lax.dynamic_slice_in_dim(shared[:, 5], bin_index * dp_rows, dp_rows, 1)
    skips = jnp.sum(sums[:, 6, :inner_part].reshape(LAYERS, heads_here, -1), axis=2)
    grad_head = jnp.stack([sums[:, 7, :heads_here], sums[:, 7, LANES : LANES + heads_here], skips], axis=1)
    grad_norm = sums[:, 6, inner_part : 2 * inner_part]
    own_weights = jnp.stack([first_pack, later_pack])
    grad_bc = maps
    grad_out = jnp.swapaxes(own_weights[:, :, :inner_part], 1, 2)
    grad_z = own_weights[:, :, inner_part : 2 * inner_part]
    grad_x = own_weights[:, :, 2 * inner_part : 3 * inner_part]
    grad_dt = own_weights[:, :, 3 * inner_part + 2 * STATE : 3 * inner_part + 2 * STATE + heads_here]

    rank_of = jnp.zeros_like(packing).at[packing].set(jnp.arange(seq_total, dtype=jnp.int32))

    def in_order(returned):
        return returned.reshape(seq_total, pos_here, cols_here)[rank_of]

    activations = in_order(activations_back)
    input_grad = in_order(returned)
    return (
        activations, input_grad, shard_pre, grad_z, grad_x, grad_bc, grad_dt,
        grad_convx, grad_convbc, grad_head, grad_norm, grad_out,
    )


def solution(mesh):
    placed = (
        P(None, "dp", "tensor"), P(None, "dp", "tensor"), P(), P(), P(None, "dp"),
        P(None, "dp", "tensor"), P(None, "dp", "tensor"), P(None, "dp", None), P(None, "dp", "tensor"),
        P(None, None, "tensor"), P(), P(None, None, "tensor"), P(None, "tensor"), P(None, "tensor", "dp"),
    )
    results = (
        P(None, "dp", "tensor"), P(None, "dp", "tensor"), P(None, "dp"),
        P(None, "dp", "tensor"), P(None, "dp", "tensor"), P(None, "dp", None), P(None, "dp", "tensor"),
        P(None, None, "tensor"), P(), P(None, None, "tensor"), P(None, "tensor"), P(None, "tensor", "dp"),
    )
    return jax.shard_map(on_device, mesh=mesh, in_specs=placed, out_specs=results, check_vma=False)
```

```python
import functools
import jax
import jax.numpy as jnp
from jax import lax
from jax.experimental import pallas as pl
from jax.experimental.pallas import tpu as pltpu
from jax.sharding import PartitionSpec as P

CONV = 4
INNER = 2048
LAYERS = 2
BIN = 2048
eps = 1e-05
STATE = 128
BLK = 256
LANES = 128
LOG2E = 1.4426950408889634
F32 = jnp.float32
BF16 = jnp.bfloat16


def dot_nn(left, right):
    return lax.dot_general(left, right, (((1,), (0,)), ((), ())), preferred_element_type=F32)


def dot_nt(left, right):
    return lax.dot_general(left, right, (((1,), (1,)), ((), ())), preferred_element_type=F32)


def dot_tn(left, right):
    return lax.dot_general(left, right, (((0,), (0,)), ((), ())), preferred_element_type=F32)


def split_two(values):
    high = values.astype(BF16)
    return high, (values - high.astype(F32)).astype(BF16)


def split_three(values):
    high = values.astype(BF16)
    rest = values - high.astype(F32)
    middle = rest.astype(BF16)
    return high, middle, (rest - middle.astype(F32)).astype(BF16)


def spread_heads(values, spread):
    high, low = split_two(values)
    return dot_nn(jnp.concatenate([high, low], axis=1), spread)


def gather_heads(values, spread):
    high, low = split_two(values)
    half = spread[:LANES]
    return dot_nt(high, half) + dot_nt(low, half)


def sigmoid(values):
    return 0.5 * jnp.tanh(0.5 * values) + 0.5


def softplus(values):
    return jnp.maximum(values, 0.0) + jnp.log1p(jnp.exp(-jnp.abs(values)))


def segment_of(rows, first, second):
    return (rows >= first).astype(jnp.int32) + (rows >= second).astype(jnp.int32)


def block_frame(block, first, second):
    row_col = block * BLK + lax.broadcasted_iota(jnp.int32, (BLK, 1), 0)
    row_row = block * BLK + lax.broadcasted_iota(jnp.int32, (1, BLK), 1)
    return row_col, row_row, segment_of(row_col, first, second), segment_of(row_row, first, second)


def decay_parts(block, dt_raw, head, seg_col, first, second):
    shifted = dt_raw + head[0:1]
    steps = softplus(shifted)
    log_decay = steps * head[1:2]
    above = lax.broadcasted_iota(jnp.int32, (BLK, BLK), 0)
    below = lax.broadcasted_iota(jnp.int32, (BLK, BLK), 1)
    lower = jnp.where(above >= below, 1.0, 0.0).astype(BF16)
    parts = dot_nn(lower, jnp.concatenate(split_three(log_decay), axis=1))
    cumulative = parts[:, :LANES] + parts[:, LANES : 2 * LANES] + parts[:, 2 * LANES :]
    cum2 = cumulative * LOG2E
    final2 = cum2[BLK - 1 : BLK]
    last_seg = segment_of(block * BLK + BLK - 1, first, second)
    prior_seg = jnp.where(block == 0, -1, segment_of(block * BLK - 1, first, second))
    entering = jnp.where(seg_col == prior_seg, jnp.exp2(cum2), 0.0)
    tail = jnp.where(seg_col == last_seg, jnp.exp2(final2 - cum2), 0.0)
    retained = jnp.where(last_seg == prior_seg, jnp.exp2(final2), 0.0)
    return shifted, steps, cum2, entering, tail, retained


def head_half(pair, head):
    lanes = lax.broadcasted_iota(jnp.int32, pair.shape, 1)
    keep = (lanes < LANES // 2) if head % 2 == 0 else (lanes >= LANES // 2)
    return jnp.where(keep, pair, jnp.zeros_like(pair))


SHARE = BLK // 4
AG_OWN, AG_ACROSS, AG_PASS, RS_PAIR, RS_ACROSS, SM_PAIR, SM_ACROSS = range(7)


class Ring:
    def __init__(self, sems):
        me = lax.axis_index("tensor")
        self.low, self.high = me % 2, me // 2
        self.me = me
        self.sibling = self.high * 2 + (1 - self.low)
        self.across = (1 - self.high) * 2 + self.low
        self.beyond = (1 - self.high) * 2 + (1 - self.low)
        self.sems = sems

    def greet(self):
        barrier = pltpu.get_barrier_semaphore()
        for other in (self.sibling, self.across, self.beyond):
            pl.semaphore_signal(barrier, inc=1, device_id={"tensor": other}, device_id_type=pl.DeviceIdType.MESH)
        pl.semaphore_wait(barrier, greet_dp(barrier) + 3)

    def slot(self, owner):
        return ((self.low + owner % 2) % 2) * 2 + (self.high + owner // 2) % 2

    def copy(self, kind, block, source, target, other):
        return pltpu.make_async_remote_copy(
            src_ref=source, dst_ref=target,
            send_sem=self.sems.at[kind, block, 0], recv_sem=self.sems.at[kind, block, 1],
            device_id={"tensor": other}, device_id_type=pl.DeviceIdType.MESH,
        )


def greet_dp(barrier):
    count, me = lax.axis_size("dp"), lax.axis_index("dp")

    @pl.loop(1, count)
    def _(step):
        pl.semaphore_signal(
            barrier, inc=1, device_id={"dp": (me + step) % count}, device_id_type=pl.DeviceIdType.MESH
        )

    return count - 1


class BinExchange:
    def __init__(self, to_bins, source, target, sems):
        self.to_bins, self.source, self.target, self.sems = to_bins, source, target, sems
        self.count, self.me = lax.axis_size("dp"), lax.axis_index("dp")
        self.span = source.shape[2] if to_bins else target.shape[2]

    def pieces(self, other):
        if self.to_bins:
            return self.source.at[other], self.target.at[:, pl.ds(self.me * self.span, self.span), :]
        return self.source.at[:, pl.ds(other * self.span, self.span), :], self.target.at[self.me]

    def remote(self, step, other):
        source, target = self.pieces(other)
        return pltpu.make_async_remote_copy(
            src_ref=source, dst_ref=target, send_sem=self.sems.at[step, 0], recv_sem=self.sems.at[step, 1],
            device_id={"dp": other}, device_id_type=pl.DeviceIdType.MESH,
        )

    def local(self):
        source, target = self.pieces(self.me)
        return pltpu.make_async_copy(source, target, self.sems.at[0, 0])

    def start(self):
        self.local().start()
        self.start_steps(1, self.count)

    def wait(self):
        self.local().wait()
        self.wait_steps(1, self.count)

    def start_steps(self, begin, end):
        @pl.loop(begin, end)
        def _(step):
            self.remote(step, (self.me + step) % self.count).start()

    def wait_steps(self, begin, end):
        @pl.loop(begin, end)
        def _(step):
            self.remote(step, (self.me + step) % self.count).wait()


class RowExchange:
    def __init__(self, to_rows, source, target, sems):
        self.to_rows, self.source, self.target, self.sems = to_rows, source, target, sems
        self.me = lax.axis_index("tensor")
        self.columns = source.shape[2] if to_rows else target.shape[2]

    def pieces(self, other):
        if self.to_rows:
            return (
                self.source.at[:, pl.ds(other * SHARE, SHARE), :],
                self.target.at[:, :, pl.ds(pl.multiple_of(self.me * self.columns, LANES), self.columns)],
            )
        return (
            self.source.at[:, :, pl.ds(pl.multiple_of(other * self.columns, LANES), self.columns)],
            self.target.at[:, pl.ds(self.me * SHARE, SHARE), :],
        )

    def remote(self, step):
        other = (self.me + step) % 4
        source, target = self.pieces(other)
        return pltpu.make_async_remote_copy(
            src_ref=source, dst_ref=target, send_sem=self.sems.at[step, 0], recv_sem=self.sems.at[step, 1],
            device_id={"tensor": other}, device_id_type=pl.DeviceIdType.MESH,
        )

    def local(self):
        source, target = self.pieces(self.me)
        return pltpu.make_async_copy(source, target, self.sems.at[0, 0])

    def start(self):
        self.local().start()
        for step in range(1, 4):
            self.remote(step).start()

    def wait(self):
        self.local().wait()
        for step in range(1, 4):
            self.remote(step).wait()


def row_place(rows, member):
    return rows.at[:, pl.ds(member * SHARE, SHARE), :]


def column_place(rows, member):
    columns = rows.shape[2] // 4
    return rows.at[:, :, pl.ds(pl.multiple_of(member * columns, LANES), columns)]


def gather_copy(ring, kind, block, own, rows, place):
    if kind == AG_PASS:
        passed = place(rows, ring.across).at[block]
        return ring.copy(kind, block, passed, passed, ring.sibling)
    other = ring.sibling if kind == AG_OWN else ring.across
    target = place(rows, ring.me).at[block]
    return ring.copy(kind, block, target if own is None else own.at[block], target, other)


def pair_copy(ring, block, parts, from_pair):
    return ring.copy(RS_PAIR, block, parts.at[block, pl.ds(2 * SHARE, 2 * SHARE), :], from_pair.at[block], ring.sibling)


def across_copy(ring, block, parts, from_across):
    return ring.copy(RS_ACROSS, block, parts.at[block, pl.ds(SHARE, SHARE), :], from_across.at[block], ring.across)


def store_parts(ring, block, part, parts):
    for owner in range(4):
        parts[block, pl.ds(ring.slot(owner) * SHARE, SHARE), :] = part[owner * SHARE : (owner + 1) * SHARE].astype(BF16)


def add_pair(block, parts, from_pair):
    parts[block, pl.ds(SHARE, SHARE), :] = (
        parts[block, pl.ds(SHARE, SHARE), :].astype(F32) + from_pair[block, pl.ds(SHARE, SHARE), :].astype(F32)
    ).astype(BF16)


def add_all(block, parts, from_pair, from_across):
    return (
        parts[block, pl.ds(0, SHARE), :].astype(F32)
        + from_pair[block, pl.ds(0, SHARE), :].astype(F32)
        + from_across[block].astype(F32)
    )


def own_column(line, first_lane):
    lanes = lax.broadcasted_iota(jnp.int32, (SHARE, line.shape[1]), 1)
    rows = lax.broadcasted_iota(jnp.int32, (SHARE, line.shape[1]), 0)
    return jnp.sum(jnp.where(lanes == rows + first_lane, line, 0.0), axis=1, keepdims=True)


LAG = 4
DEFER = 2
PASS_AHEAD = 2


def forward_kernel(
    off_ref, tok_ref, packs_ref, own_gains_ref, cot_ref, taps_ref, head_ref, wide_ref, spread_ref,
    rows_ref, z_ref, in_ref, pre_ref, dt_ref, y_ref, gg_ref, st_ref,
    before_ref, middle_ref, tot_ref, scale_ref, final_ref, gains_ref, cot_cols_ref, weights_ref,
    state, padded, rows, parts, from_pair, from_across, sq_own, sq_pair, sq_sums, sq_across,
    weights, arrived, cols, cot_arrived, all_gains, middle, kept,
    before_buf, middle_buf, tot_buf, scale_buf, final_buf, cot_cols, keep_sems,
    sems, copy_sems, line_sems, bin_sems, cot_sems, gain_sems,
):
    step = pl.program_id(0)
    inner = y_ref.shape[1]
    mixed = in_ref.shape[1]
    first, second = off_ref[0], off_ref[1]
    blocks = rows.shape[0]
    layer, block = step // blocks, step % blocks
    rings = (Ring(sems.at[0]), Ring(sems.at[1]))
    ring = rings[0]
    total_columns = weights.shape[2]

    def line_of(at_layer, begin, end, slot):
        part = pl.ds(begin, end - begin)
        return LineGather(packs_ref.at[at_layer, :, part], weights.at[at_layer, :, part], line_sems.at[slot])

    cut = inner + (total_columns - inner) // (2 * LANES) * LANES
    in_lines = [Lines([line_of(at, inner, cut, 3 * at), line_of(at, cut, total_columns, 3 * at + 1)]) for at in range(LAYERS)]
    out_lines = [line_of(at, 0, inner, 3 * at + 2) for at in range(LAYERS)]
    in_line, line = in_lines
    bins = BinExchange(True, tok_ref, arrived, bin_sems)
    cot_bins = BinExchange(True, cot_ref, cot_arrived, cot_sems)
    gain_tiles = TileGather(own_gains_ref, all_gains, gain_sems)
    four = line.line == 4

    def gather(at_layer, kind, at):
        own, place = ((cols, column_place), (None, row_place))[at_layer]
        return gather_copy(rings[at_layer], kind, at, own, rows, place)

    def sq_pair_copy(at_ring, slot):
        return at_ring.copy(SM_PAIR, slot % blocks, sq_own.at[slot], sq_pair.at[slot], at_ring.sibling)

    def sq_across_copy(at_ring, slot):
        return at_ring.copy(SM_ACROSS, slot % blocks, sq_sums.at[slot], sq_across.at[slot], at_ring.across)

    def own_copy():
        return pltpu.make_async_copy(cols, column_place(rows, ring.me), copy_sems.at[LAYERS])

    def keep_weights(at):
        return pltpu.make_async_copy(weights.at[at], weights_ref.at[at], copy_sems.at[at])

    def keep_copies():
        kept_pairs = (
            (before_buf, before_ref), (middle_buf, middle_ref), (tot_buf, tot_ref),
            (scale_buf, scale_ref), (final_buf, final_ref), (cot_cols, cot_cols_ref),
        )
        return [pltpu.make_async_copy(a, b, keep_sems.at[at]) for at, (a, b) in enumerate(kept_pairs)]

    def clear():
        state[...] = jnp.zeros_like(state)
        padded[pl.ds(0, 8), :] = jnp.zeros((8, mixed), F32)

    @pl.when(step == 0)
    def _():
        ring.greet()
        half = bins.count // 2
        bins.local().start()
        bins.start_steps(half - 1, half + 2)
        in_line.start_pair()
        for part in (out_lines[0], line, out_lines[1]):
            part.start_pair()
        gain_tiles.start()
        clear()
        bins.wait_steps(half - 1, half + 2)
        in_line.start_line()
        bins.start_steps(1, half - 1)
        bins.start_steps(half + 2, bins.count)
        bins.local().wait()
        bins.wait_steps(1, half - 1)
        bins.wait_steps(half + 2, bins.count)
        pick_all(off_ref, arrived, cols)
        own_copy().start()

        @pl.loop(0, blocks)
        def _(at):
            gather(0, AG_ACROSS, at).start()
            gather(0, AG_OWN, at).start()

        gain_tiles.wait()
        gains_ref[...] = all_gains[0]

        @pl.loop(1, all_gains.shape[0])
        def _(at):
            gains_ref[...] += all_gains[at]

        own_copy().wait()

        def pass_rows(begin, end):
            @pl.loop(begin, end)
            def _(at):
                gather(0, AG_ACROSS, at).wait_recv()
                gather(0, AG_PASS, at).start()

        if four:
            in_line.stage(1)
            pass_rows(0, blocks // 2)
            in_line.stage(2)
            pass_rows(blocks // 2, blocks)
            in_line.stage(3)
            for part in (out_lines[0], line, out_lines[1]):
                part.start_line()
        else:
            pass_rows(0, blocks)

            @pl.loop(1, line.line)
            def _(stage):
                in_line.stage(stage)

        in_line.finish()
        if not four:
            for part in (out_lines[0], line, out_lines[1]):
                part.start_line()

    @pl.when(step == blocks)
    def _():
        clear()

    for at_layer in range(LAYERS):

        @pl.when(layer == at_layer)
        def _(at_layer=at_layer):
            gather(at_layer, AG_OWN, block).wait_recv()
            gather(at_layer, AG_PASS, block).wait_recv()

    gains = gains_ref[...]
    raw = rows[block].astype(F32)
    mean = jnp.sum(raw * raw, axis=1, keepdims=True) / raw.shape[1]
    normed = raw * lax.rsqrt(mean + eps) * gains[0:1]
    here = jnp.where(layer == 0, normed, raw).astype(BF16)
    rows_ref[...] = here
    row_col, row_row, seg_col, seg_row = block_frame(block, first, second)
    seg_start = jnp.where(seg_col == 0, 0, jnp.where(seg_col == 1, first, second))
    within = row_col - seg_start
    product = dot_nn(here, weights[layer, :, inner:])
    gate = product[:, :inner]
    mixed_in = product[:, inner : inner + mixed]
    dt_raw = product[:, inner + mixed :]
    z_ref[...] = gate.astype(BF16)
    in_ref[...] = mixed_in.astype(BF16)
    dt_ref[...] = dt_raw
    padded[pl.ds(8, BLK), :] = mixed_in
    taps = taps_ref[layer]
    conv = taps[CONV : CONV + 1] + taps[CONV - 1 : CONV] * mixed_in
    for delay in range(1, CONV):
        shifted_in = padded[pl.ds(8 - delay, BLK), :]
        conv = conv + taps[CONV - 1 - delay : CONV - delay] * jnp.where(within >= delay, shifted_in, 0.0)
    padded[pl.ds(0, 8), :] = padded[pl.ds(BLK, 8), :]
    pre_ref[...] = conv
    mixed_low = (conv * sigmoid(conv)).astype(BF16)
    x_low = mixed_low[:, :inner]
    b_low = mixed_low[:, inner : inner + STATE]
    c_low = mixed_low[:, inner + STATE :]
    head = head_ref[layer]
    spread = spread_ref[...]
    shifted, steps, cum2, entering, tail, retained = decay_parts(block, dt_raw, head, seg_col, first, second)
    cum_row = jnp.transpose(cum2)
    x_in = x_low.astype(F32)
    x_steps = spread_heads(steps, spread) * x_in
    x_steps_low = x_steps.astype(BF16)
    allowed = (seg_col == seg_row) & (row_col >= row_row)
    scores = jnp.where(allowed, dot_nt(c_low, b_low), 0.0)
    old_state = state[...]
    st_ref[0] = old_state
    carried = spread_heads(entering, spread) * dot_nn(c_low, old_state.astype(BF16))
    wide = wide_ref[layer]
    pieces = []
    for pair in range(inner // LANES):
        columns = slice(pair * LANES, (pair + 1) * LANES)
        total = None
        for head_index in (2 * pair, 2 * pair + 1):
            gaps = cum2[:, head_index : head_index + 1] - cum_row[head_index : head_index + 1, :]
            coupling = (jnp.exp2(jnp.minimum(gaps, 0.0)) * scores).astype(BF16)
            term = dot_nn(coupling, head_half(x_steps_low[:, columns], head_index))
            total = term if total is None else total + term
        pieces.append(total)
    mixed_out = jnp.concatenate(pieces, axis=1) + carried + wide[0:1] * x_in
    tailed = (spread_heads(tail, spread) * x_steps).astype(BF16)
    keep = spread_heads(jnp.broadcast_to(retained, (8, LANES)), spread)[0:1]
    state[...] = old_state * keep + dot_tn(b_low, tailed)
    y_ref[...] = mixed_out
    gated = mixed_out * (gate * sigmoid(gate))
    gained = (gated * wide[1:2]).astype(BF16)
    gg_ref[...] = gained
    now = Ring(sems.at[layer])
    high, low = split_two(gated * gated)
    ones = jnp.ones((8, inner), BF16)
    sq_own[step] = dot_nt(ones, high) + dot_nt(ones, low)
    sq_pair_copy(now, step).start()

    def free_parts(at_layer, at):
        if at_layer == 0:
            gather(0, AG_PASS, at).wait_send()
        else:
            pair_copy(ring, at, parts, from_pair).wait_send()
            across_copy(ring, at, parts, from_across).wait_send()

    def send_parts(at_ring, at, values, out_weights):
        store_parts(at_ring, at, dot_nt(values, out_weights), parts)
        pair_copy(at_ring, at, parts, from_pair).start()

    @pl.when(block < DEFER)
    def _():
        kept[block] = gained

    for at_layer in range(LAYERS):
        first_step = at_layer * blocks
        if four:
            for stage in (1, 2, 3):
                when = min(stage - 1, DEFER) if at_layer == 0 else 2 * stage + 2

                @pl.when(step == when)
                def _(at_layer=at_layer, stage=stage):
                    out_lines[at_layer].stage(stage)

        @pl.when(step == first_step + DEFER)
        def _(at_layer=at_layer):
            if not four:

                @pl.loop(1, line.line)
                def _(stage):
                    out_lines[at_layer].stage(stage)

            out_lines[at_layer].finish()
            keep_weights(at_layer).start()

            @pl.loop(0, DEFER)
            def _(at):
                free_parts(at_layer, at)
                send_parts(rings[at_layer], at, kept[at], weights[at_layer, :, :inner])

    @pl.when(block >= DEFER)
    def _():
        for at_layer in range(LAYERS):

            @pl.when(layer == at_layer)
            def _(at_layer=at_layer):
                free_parts(at_layer, block)

        send_parts(now, block, gained, weights[layer, :, :inner])

    def second_stage(slot):
        at_layer, at = slot // blocks, slot % blocks
        at_ring = Ring(sems.at[at_layer])
        pair_copy(at_ring, at, parts, from_pair).wait_recv()
        sq_pair_copy(at_ring, slot).wait_recv()

        add_pair(at, parts, from_pair)
        sq_sums[slot] = sq_own[slot] + sq_pair[slot]
        across_copy(at_ring, at, parts, from_across).start()
        sq_across_copy(at_ring, slot).start()

    def last_stage(at_layer, at):
        at_ring, slot = rings[at_layer], at_layer * blocks + at
        across_copy(at_ring, at, parts, from_across).wait_recv()
        sq_across_copy(at_ring, slot).wait_recv()
        total = add_all(at, parts, from_pair, from_across)
        squares = own_column((sq_sums[slot] + sq_across[slot])[0:1], ring.me * SHARE)
        scale = lax.rsqrt(squares / INNER + eps)
        here = pl.ds(at * SHARE, SHARE)
        mine = pl.ds(ring.me * SHARE, SHARE)
        tot_buf[slot] = total.astype(BF16)
        scale_buf[slot] = scale
        if at_layer == 0:
            before = rows[at, mine, :]
            before_buf[at] = before
            hidden = before.astype(F32) + total * scale
            middle[at] = hidden
            middle_buf[at] = hidden.astype(BF16)
            mean = jnp.sum(hidden * hidden, axis=1, keepdims=True) / hidden.shape[1]
            later = (hidden * lax.rsqrt(mean + eps) * gains[1:2]).astype(BF16)
            rows[at, mine, :] = later
            gather(1, AG_ACROSS, at).start()
            gather(1, AG_OWN, at).start()
        else:
            final_buf[at] = (middle[at] + total * scale).astype(BF16)

    @pl.when((step >= LAG) & (step < blocks + LAG))
    def _():
        last_stage(0, step - LAG)

    @pl.when(step >= blocks + LAG)
    def _():
        last_stage(1, step - LAG - blocks)

    if four:
        for stage, when in ((1, 1), (2, 3), (3, 5)):

            @pl.when(step == when)
            def _(stage=stage):
                line.stage(stage)

    @pl.when(step == blocks)
    def _():
        cot_bins.start()

    @pl.when((step >= blocks - PASS_AHEAD) & (step < 2 * blocks - PASS_AHEAD))
    def _():
        gather(1, AG_ACROSS, (step + PASS_AHEAD) % blocks).wait_recv()
        gather(1, AG_PASS, (step + PASS_AHEAD) % blocks).start()

    @pl.when((step % blocks == DEFER + 1) & (step > 0))
    def _():
        @pl.loop(0, DEFER)
        def _(at):
            second_stage(layer * blocks + at)

    @pl.when((step > 0) & ((step - 1 + blocks) % blocks >= DEFER))
    def _():
        second_stage(step - 1)

    @pl.when(step == blocks - 1)
    def _():
        if not four:

            @pl.loop(1, line.line)
            def _(stage):
                line.stage(stage)

        line.finish()

    @pl.when(step == 2 * blocks - 1)
    def _():
        second_stage(step)
        cot_bins.wait()
        pick_all(off_ref, cot_arrived, cot_cols)

        before_keep, middle_keep, *late_keep, cot_keep = keep_copies()
        for copy in (before_keep, middle_keep, cot_keep):
            copy.start()

        @pl.loop(blocks - LAG, blocks)
        def _(at):
            last_stage(1, at)

        for copy in late_keep:
            copy.start()

        @pl.loop(0, blocks)
        def _(at):
            gather(0, AG_OWN, at).wait_send()
            gather(0, AG_ACROSS, at).wait_send()
            for kind in (AG_OWN, AG_ACROSS, AG_PASS):
                gather(1, kind, at).wait_send()
            pair_copy(rings[1], at, parts, from_pair).wait_send()
            across_copy(rings[1], at, parts, from_across).wait_send()
            for at_layer in range(LAYERS):
                sq_pair_copy(rings[at_layer], at_layer * blocks + at).wait_send()
                sq_across_copy(rings[at_layer], at_layer * blocks + at).wait_send()

        for at in range(LAYERS):
            keep_weights(at).wait()
        for copy in (before_keep, middle_keep, *late_keep, cot_keep):
            copy.wait()


def own_line(column):
    lanes = lax.broadcasted_iota(jnp.int32, (SHARE, LANES), 1)
    rows = lax.broadcasted_iota(jnp.int32, (SHARE, LANES), 0)
    return jnp.sum(jnp.where(lanes == rows, column, 0.0), axis=0, keepdims=True)


TILE_KINDS = (5, 6, 7)
AHEAD = 2
QUEUED = 4
BACK_LAG = 4


def backward_kernel(
    off_ref, cot_in, tot_in, scale_in, before_ref, middle_ref, gains_ref, taps_ref, head_ref, wide_ref, spread_ref,
    weights_ref, final_ref,
    z_ref, in_ref, pre_ref, dt_ref, y_ref, st_ref, normed_ref, gg_ref,
    gcols_out, small_ref, pack_ref, packs_ref, back_ref,
    dstate, padded, rows, parts, from_pair, from_across, tiles, held, running, weights, acc_out, acc_in,
    packs, pair_buf, arrivals, cols, slots,
    cot_ref, tot_ref, scale_ref, ginput, gcols_ref, sems, copy_sems, line_sems, row_sems, bin_sems, load_sems, col_sems,
):
    step = pl.program_id(0)
    inner = y_ref.shape[1]
    mixed = in_ref.shape[1]
    first, second = off_ref[0], off_ref[1]
    blocks = rows.shape[0]
    phase, block = step // blocks, blocks - 1 - step % blocks
    layer = LAYERS - 1 - phase
    rings = (Ring(sems.at[0]), Ring(sems.at[1]))
    ring = rings[0]
    line = LineReduce(packs, pack_ref, pair_buf, arrivals, line_sems)
    four = line.line == 4
    final_rows = RowExchange(False, final_ref, cols.reshape(blocks, BLK, cols.shape[1]), row_sems)
    bins = BinExchange(False, slots, back_ref, bin_sems)
    mine = pl.ds(ring.me * SHARE, SHARE)

    def gather(at_phase, kind, at):
        own, place = ((cot_ref, column_place), (None, row_place))[at_phase]
        return gather_copy(rings[at_phase], kind, at, own, rows, place)

    def tile_copies(at_phase, at):
        at_ring = rings[at_phase]
        here = tiles.at[at_phase, ring.me, at]
        return [
            at_ring.copy(kind, at, here, here, other)
            for kind, other in zip(TILE_KINDS, (ring.sibling, ring.across, ring.beyond))
        ]

    def make_tile(at_phase, at, grad_low):
        slot = (LAYERS - 1 - at_phase) * blocks + at
        scale = scale_ref[slot]
        weighted = jnp.sum(grad_low.astype(F32) * tot_ref[slot].astype(F32), axis=1, keepdims=True)
        twice = -(scale * scale * scale) / INNER * weighted
        row = lax.broadcasted_iota(jnp.int32, (8, LANES), 0)
        tiles[at_phase, ring.me, at] = jnp.where(row == 0, own_line(twice), own_line(scale))
        for copy in tile_copies(at_phase, at):
            copy.start()

    def prepare(at):
        gather(0, AG_OWN, at).wait_recv()
        gather(0, AG_PASS, at).wait_recv()
        make_tile(0, at, rows[at, mine, :])

    def pass_rows(at_phase, at):
        gather(at_phase, AG_ACROSS, at).wait_recv()
        gather(at_phase, AG_PASS, at).start()

    def load_inputs():
        pairs = ((cot_in, cot_ref), (tot_in, tot_ref), (scale_in, scale_ref))
        return [pltpu.make_async_copy(a, b, load_sems.at[at]) for at, (a, b) in enumerate(pairs)]

    def column_copy(at, hop):
        other = (ring.me + hop) % 4
        columns = gcols_ref.shape[2]
        source = ginput.at[at, :, pl.ds(pl.multiple_of(other * columns, LANES), columns)]
        target = gcols_ref.at[at, mine, :]
        if hop == 0:
            return pltpu.make_async_copy(source, target, col_sems.at[at, 0, 0])
        return pltpu.make_async_remote_copy(
            src_ref=source, dst_ref=target, send_sem=col_sems.at[at, hop, 0], recv_sem=col_sems.at[at, hop, 1],
            device_id={"tensor": other}, device_id_type=pl.DeviceIdType.MESH,
        )

    def send_rows(at):
        gather(0, AG_ACROSS, at).start()
        gather(0, AG_OWN, at).start()

    def own_copy():
        return pltpu.make_async_copy(cot_ref, column_place(rows, ring.me), copy_sems.at[0])

    def load_weights(at_layer):
        return pltpu.make_async_copy(weights_ref.at[at_layer], weights, copy_sems.at[1])

    def load_held(at_phase):
        return pltpu.make_async_copy((middle_ref, before_ref)[at_phase], held, copy_sems.at[3 + at_phase])

    def store_packs():
        return pltpu.make_async_copy(packs, packs_ref, copy_sems.at[2])

    def clear():
        dstate[...] = jnp.zeros_like(dstate)
        padded[pl.ds(BLK, 8), :] = jnp.zeros((8, mixed), F32)
        acc_out[...] = jnp.zeros_like(acc_out)
        acc_in[...] = jnp.zeros_like(acc_in)

    @pl.when(step == 0)
    def _():
        cot_load, *loads = load_inputs()
        for copy in (cot_load, *loads):
            copy.start()
        load_weights(LAYERS - 1).start()
        load_held(0).start()
        cot_load.wait()
        own_copy().start()
        ring.greet()

        send_rows(blocks - 1)
        clear()
        small_ref[...] = jnp.zeros_like(small_ref)
        own_copy().wait()
        pass_rows(0, blocks - 1)
        for at in range(1, QUEUED):
            send_rows(blocks - 1 - at)
        for copy in loads:
            copy.wait()
        prepare(blocks - 1)
        for at in range(1, AHEAD + 1):
            pass_rows(0, blocks - 1 - at)
        for at in range(1, AHEAD):
            prepare(blocks - 1 - at)
        load_weights(LAYERS - 1).wait()

    @pl.when(step == blocks)
    def _():
        load_weights(0).start()
        clear()
        load_weights(0).wait()

    @pl.when(phase > 0)
    def _():
        gather(1, AG_OWN, block).wait_recv()
        gather(1, AG_PASS, block).wait_recv()

    for at_phase in range(LAYERS):

        @pl.when(phase == at_phase)
        def _(at_phase=at_phase):
            for copy in tile_copies(at_phase, block):
                copy.wait_recv()

    here = rows[block]
    tile_rows = [tiles[phase, owner, block] for owner in range(4)]
    twice_here = jnp.concatenate([own_column(tile[0:1], 0) for tile in tile_rows], axis=0)
    scale_here = jnp.concatenate([own_column(tile[1:2], 0) for tile in tile_rows], axis=0)
    row_col, row_row, seg_col, seg_row = block_frame(block, first, second)
    seg_end = jnp.where(seg_col == 0, first, jnp.where(seg_col == 1, second, BIN))
    remaining = seg_end - row_col
    head = head_ref[layer]
    wide = wide_ref[layer]
    spread = spread_ref[...]
    skip, gain = wide[0:1], wide[1:2]
    gate = z_ref[...].astype(F32)
    mixed_out = y_ref[...]
    conv = pre_ref[...]
    gate_sig = sigmoid(gate)
    gate_silu = gate * gate_sig
    gated = mixed_out * gate_silu
    grad_scaled = dot_nn(here, weights[:, :inner]) * scale_here
    grad_gated = grad_scaled * gain + twice_here * gated
    grad_out = grad_gated * gate_silu
    grad_gate = grad_gated * mixed_out * (gate_sig * (1.0 + gate * (1.0 - gate_sig)))
    grad_out_low = grad_out.astype(BF16)

    conv_sig = sigmoid(conv)
    mixed_low = (conv * conv_sig).astype(BF16)
    x_low = mixed_low[:, :inner]
    b_low = mixed_low[:, inner : inner + STATE]
    c_low = mixed_low[:, inner + STATE :]
    x_in = x_low.astype(F32)
    shifted, steps, cum2, entering, tail, retained = decay_parts(block, dt_ref[...], head, seg_col, first, second)
    cum_row = jnp.transpose(cum2)
    steps_wide = spread_heads(steps, spread)
    x_steps_low = (steps_wide * x_in).astype(BF16)
    x_steps = x_steps_low.astype(F32)

    allowed = (seg_col == seg_row) & (row_col <= row_row)
    scores = jnp.where(allowed, dot_nt(b_low, c_low), 0.0)
    grad_scores = jnp.zeros((BLK, BLK), F32)
    pieces = []
    for pair in range(inner // LANES):
        columns = slice(pair * LANES, (pair + 1) * LANES)
        total = None
        for head_index in (2 * pair, 2 * pair + 1):
            gaps = cum_row[head_index : head_index + 1, :] - cum2[:, head_index : head_index + 1]
            decays = jnp.exp2(jnp.minimum(gaps, 0.0))
            coupling = (decays * scores).astype(BF16)
            term = dot_nn(coupling, head_half(grad_out_low[:, columns], head_index))
            total = term if total is None else total + term
            grad_scores = grad_scores + decays * dot_nt(
                head_half(x_steps_low[:, columns], head_index), grad_out_low[:, columns]
            )
        pieces.append(total)
    grad_scores_low = jnp.where(allowed, grad_scores, 0.0).astype(BF16)
    old_dstate = dstate[...]
    old_dstate_low = old_dstate.astype(BF16)
    old_state = st_ref[0]
    tail_wide = spread_heads(tail, spread)
    from_state = tail_wide * dot_nn(b_low, old_dstate_low)
    grad_unit = jnp.concatenate(pieces, axis=1) + from_state
    entered = (spread_heads(entering, spread) * grad_out).astype(BF16)
    tailed = (tail_wide * x_steps).astype(BF16)
    grad_c = dot_tn(grad_scores_low, b_low) + dot_nt(entered, old_state.astype(BF16))
    grad_b = dot_nn(grad_scores_low, c_low) + dot_nt(tailed, old_dstate_low)
    keep = spread_heads(jnp.broadcast_to(retained, (8, LANES)), spread)[0:1]
    dstate[...] = old_dstate * keep + dot_tn(c_low, entered)

    balance = gather_heads(grad_out_low.astype(F32) * (mixed_out - skip * x_in) - x_steps * grad_unit, spread)
    direct = gather_heads(x_in * grad_unit, spread)
    final_wide = jnp.sum(x_steps * from_state, axis=0, keepdims=True) + keep * jnp.sum(
        old_dstate * old_state, axis=0, keepdims=True
    )
    final = gather_heads(jnp.broadcast_to(final_wide, (8, inner)), spread)[0:1]
    above = lax.broadcasted_iota(jnp.int32, (BLK, BLK), 0)
    below = lax.broadcasted_iota(jnp.int32, (BLK, BLK), 1)
    upper = jnp.where(above <= below, 1.0, 0.0).astype(BF16)
    thirds = dot_nn(upper, jnp.concatenate(split_three(balance), axis=1))
    grad_log = thirds[:, :LANES] + thirds[:, LANES : 2 * LANES] + thirds[:, 2 * LANES :] + final
    grad_steps = direct + grad_log * head[1:2]
    grad_dt = grad_steps * sigmoid(shifted)
    small_ref[layer, 7:8, :LANES] += jnp.sum(grad_dt, axis=0, keepdims=True)
    small_ref[layer, 7:8, LANES : 2 * LANES] += jnp.sum(grad_log * steps, axis=0, keepdims=True) * head[1:2]
    small_ref[layer, 6:7, :inner] += jnp.sum(grad_out * x_in, axis=0, keepdims=True)
    small_ref[layer, 6:7, inner : 2 * inner] += jnp.sum(grad_scaled * gated, axis=0, keepdims=True)

    grad_x = steps_wide * grad_unit + skip * grad_out
    grad_conv = jnp.concatenate([grad_x, grad_b, grad_c], axis=1) * (
        conv_sig * (1.0 + conv * (1.0 - conv_sig))
    )
    padded[pl.ds(0, BLK), :] = grad_conv
    mixed_in = in_ref[...].astype(F32)
    taps = taps_ref[layer]
    grad_in = taps[CONV - 1 : CONV] * grad_conv
    small_ref[layer, CONV : CONV + 1, :mixed] += jnp.sum(grad_conv, axis=0, keepdims=True)
    small_ref[layer, CONV - 1 : CONV, :mixed] += jnp.sum(mixed_in * grad_conv, axis=0, keepdims=True)
    for delay in range(1, CONV):
        later = jnp.where(remaining > delay, padded[pl.ds(delay, BLK), :], 0.0)
        grad_in = grad_in + taps[CONV - 1 - delay : CONV - delay] * later
        small_ref[layer, CONV - 1 - delay : CONV - delay, :mixed] += jnp.sum(mixed_in * later, axis=0, keepdims=True)
    padded[pl.ds(BLK, 8), :] = padded[pl.ds(0, 8), :]
    gproj = jnp.concatenate([grad_gate.astype(BF16), grad_in.astype(BF16), grad_dt.astype(BF16)], axis=1)
    acc_out[...] += dot_tn(here, (gg_ref[...].astype(F32) * scale_here).astype(BF16))
    acc_in[...] += dot_tn(normed_ref[...], gproj)
    part = dot_nt(gproj, weights[:, inner:])

    @pl.when(phase > 0)
    def _():
        pair_copy(ring, block, parts, from_pair).wait_send()
        across_copy(ring, block, parts, from_across).wait_send()

    @pl.when(phase == 0)
    def _():
        gather(0, AG_PASS, block).wait_send()

    now = Ring(sems.at[phase])
    store_parts(now, block, part, parts)
    pair_copy(now, block, parts, from_pair).start()

    def second_stage(turn):
        at_phase, at = turn // blocks, blocks - 1 - turn % blocks
        at_ring = Ring(sems.at[at_phase])
        pair_copy(at_ring, at, parts, from_pair).wait_recv()

        add_pair(at, parts, from_pair)
        across_copy(at_ring, at, parts, from_across).start()

    def last_stage(at_phase, at):
        at_layer = LAYERS - 1 - at_phase
        across_copy(rings[at_phase], at, parts, from_across).wait_recv()
        grad_normed = add_all(at, parts, from_pair, from_across)
        hidden = held[at].astype(F32)
        width = hidden.shape[1]
        root = lax.rsqrt(jnp.sum(hidden * hidden, axis=1, keepdims=True) / width + eps)
        gained = grad_normed * gains_ref[at_layer : at_layer + 1, :]
        small_ref[at_layer, 5:6, :] += jnp.sum(grad_normed * hidden * root, axis=0, keepdims=True)
        along = jnp.sum(gained * hidden, axis=1, keepdims=True) * (root * root * root) / width
        change = gained * root - hidden * along
        if at_phase == 0:
            grad = rows[at, mine, :].astype(F32) + change
            running[at] = grad
            grad_low = grad.astype(BF16)
            rows[at, mine, :] = grad_low
            gather(1, AG_ACROSS, at).start()
            gather(1, AG_OWN, at).start()
            make_tile(1, at, grad_low)
        else:
            ginput[at] = (running[at] + change).astype(BF16)
            for hop in range(4):
                column_copy(at, hop).start()

    @pl.when(step == BACK_LAG)
    def _():
        load_held(0).wait()

    @pl.when(step == blocks + BACK_LAG)
    def _():
        load_held(1).start()
        load_held(1).wait()

    @pl.when((step >= BACK_LAG) & (step < blocks + BACK_LAG))
    def _():
        last_stage(0, blocks - 1 - (step - BACK_LAG))

    @pl.when(step >= blocks + BACK_LAG)
    def _():
        last_stage(1, blocks - 1 - (step - BACK_LAG - blocks))

    @pl.when(step + QUEUED < blocks)
    def _():
        send_rows(blocks - 1 - (step + QUEUED))

    @pl.when(step + AHEAD + 1 < blocks)
    def _():
        pass_rows(0, blocks - 1 - (step + AHEAD + 1))

    @pl.when(step + AHEAD < blocks)
    def _():
        prepare(blocks - 1 - (step + AHEAD))

    @pl.when((step >= blocks - PASS_AHEAD) & (step < 2 * blocks - PASS_AHEAD))
    def _():
        pass_rows(1, blocks - 1 - (step + PASS_AHEAD) % blocks)

    @pl.when(step >= 1)
    def _():
        second_stage(step - 1)

    @pl.when(step == 1)
    def _():
        final_rows.start()

    @pl.when(step == 4)
    def _():
        final_rows.wait()
        place_all(off_ref, cols, slots)
        bins.start()

    @pl.when(step == blocks - 1)
    def _():
        packs[:, :inner] = acc_out[...].astype(BF16)
        packs[:, inner:] = acc_in[...].astype(BF16)
        line.send_pairs()

    if four:
        for stage in (0, 1, 2):

            @pl.when(step == blocks + 1 + 2 * stage)
            def _(stage=stage):
                line.stage(stage)

    @pl.when(step == 2 * blocks - 1)
    def _():
        second_stage(step)
        if not four:

            @pl.loop(0, line.line - 1)
            def _(stage):
                line.stage(stage)

        line.finish()
        packs[:, :inner] = acc_out[...].astype(BF16)
        packs[:, inner:] = acc_in[...].astype(BF16)
        store_packs().start()

        @pl.loop(0, BACK_LAG)
        def _(turn):
            last_stage(1, BACK_LAG - 1 - turn)

        @pl.loop(0, blocks)
        def _(at):
            gather(0, AG_OWN, at).wait_send()
            gather(0, AG_ACROSS, at).wait_send()
            for kind in (AG_OWN, AG_ACROSS, AG_PASS):
                gather(1, kind, at).wait_send()
            pair_copy(rings[1], at, parts, from_pair).wait_send()
            across_copy(rings[1], at, parts, from_across).wait_send()
            for at_phase in range(LAYERS):
                for copy in tile_copies(at_phase, at):
                    copy.wait_send()

        @pl.loop(0, blocks)
        def _(at):
            for hop in range(4):
                column_copy(at, hop).wait()

        keep_columns = pltpu.make_async_copy(gcols_ref, gcols_out, load_sems.at[0])
        keep_columns.start()
        keep_columns.wait()
        store_packs().wait()
        bins.wait()


def whole(shape):
    return pl.BlockSpec(shape, lambda *at: (0,) * len(shape))


def exchange_scratch(blocks, width):
    return [
        pltpu.VMEM((blocks, BLK, width), BF16),
        pltpu.VMEM((blocks, BLK, width), BF16),
        pltpu.VMEM((blocks, 2 * SHARE, width), BF16),
        pltpu.VMEM((blocks, SHARE, width), BF16),
    ]


def layers_forward(offsets, given, packs, own_gains, given_cot, taps, head, wide, spread):
    blocks, width = BIN // BLK, own_gains.shape[1]
    inner, mixed = wide.shape[2], taps.shape[2]
    dp_count, members, span, columns = given_cot.shape
    total = packs.shape[2]
    steps = LAYERS * blocks
    vmem, hbm = pl.BlockSpec(memory_space=pltpu.VMEM), pl.BlockSpec(memory_space=pltpu.HBM)

    def by_block(size):
        return pl.BlockSpec((BLK, size), lambda s: (s, 0))

    return pl.pallas_call(
        forward_kernel,
        grid=(steps,),
        in_specs=[pl.BlockSpec(memory_space=pltpu.SMEM), hbm, vmem, vmem, hbm] + [vmem] * 4,
        out_specs=[
            by_block(width), by_block(inner), by_block(mixed), by_block(mixed),
            by_block(LANES), by_block(inner), by_block(inner),
            pl.BlockSpec((1, STATE, inner), lambda s: (s, 0, 0)),
            hbm, hbm, hbm, hbm, hbm, vmem, hbm, hbm,
        ],
        out_shape=[
            jax.ShapeDtypeStruct((steps * BLK, width), BF16),
            jax.ShapeDtypeStruct((steps * BLK, inner), BF16),
            jax.ShapeDtypeStruct((steps * BLK, mixed), BF16),
            jax.ShapeDtypeStruct((steps * BLK, mixed), F32),
            jax.ShapeDtypeStruct((steps * BLK, LANES), F32),
            jax.ShapeDtypeStruct((steps * BLK, inner), F32),
            jax.ShapeDtypeStruct((steps * BLK, inner), BF16),
            jax.ShapeDtypeStruct((steps, STATE, inner), F32),
            jax.ShapeDtypeStruct((blocks, SHARE, width), BF16),
            jax.ShapeDtypeStruct((blocks, SHARE, width), BF16),
            jax.ShapeDtypeStruct((steps, SHARE, width), BF16),
            jax.ShapeDtypeStruct((steps, SHARE, 1), F32),
            jax.ShapeDtypeStruct((blocks, SHARE, width), BF16),
            jax.ShapeDtypeStruct(own_gains.shape, F32),
            jax.ShapeDtypeStruct((blocks, BLK, columns), BF16),
            jax.ShapeDtypeStruct((LAYERS, width, total), BF16),
        ],
        scratch_shapes=[pltpu.VMEM((STATE, inner), F32), pltpu.VMEM((BLK + 8, mixed), F32)]
        + exchange_scratch(blocks, width)
        + [pltpu.VMEM((steps, 8, BLK), F32)] * 4
        + [
            pltpu.VMEM((LAYERS, width, total), BF16),
            pltpu.VMEM((members, dp_count * span, columns), BF16),
            pltpu.VMEM((blocks, BLK, columns), BF16),
            pltpu.VMEM((members, dp_count * span, columns), BF16),
            pltpu.VMEM((dp_count,) + own_gains.shape, F32),
            pltpu.VMEM((blocks, SHARE, width), F32),
            pltpu.VMEM((DEFER, BLK, inner), BF16),
            pltpu.VMEM((blocks, SHARE, width), BF16),
            pltpu.VMEM((blocks, SHARE, width), BF16),
            pltpu.VMEM((steps, SHARE, width), BF16),
            pltpu.VMEM((steps, SHARE, 1), F32),
            pltpu.VMEM((blocks, SHARE, width), BF16),
            pltpu.VMEM((blocks, BLK, columns), BF16),
            pltpu.SemaphoreType.DMA((6,)),
            pltpu.SemaphoreType.DMA((LAYERS, 7, blocks, 2)),
            pltpu.SemaphoreType.DMA((LAYERS + 1,)),
            pltpu.SemaphoreType.DMA((3 * LAYERS, 6, dp_count // 2)),
            pltpu.SemaphoreType.DMA((dp_count, 2)),
            pltpu.SemaphoreType.DMA((dp_count, 2)),
            pltpu.SemaphoreType.DMA((dp_count, 2)),
        ],
        compiler_params=pltpu.CompilerParams(
            vmem_limit_bytes=48 * 1024 * 1024, collective_id=1, has_side_effects=True
        ),
        cost_estimate=pl.CostEstimate(flops=6 * 10**10, bytes_accessed=6 * 10**7, transcendentals=10**7),
        name="layers_forward",
    )(offsets, given, packs, own_gains, given_cot, taps, head, wide, spread)


def layers_backward(offsets, cot, totals, scales, before, middle, gains, taps, head, wide, spread, weights, final, saved, span):
    gate, mixed_in, conv, dt_raw, mixed_out, states, normed, gained = saved
    blocks, _, columns = cot.shape
    width = gains.shape[1]
    inner, mixed = wide.shape[2], taps.shape[2]
    total = weights.shape[2]
    steps = LAYERS * blocks
    count = lax.axis_size("dp")
    vmem, hbm = pl.BlockSpec(memory_space=pltpu.VMEM), pl.BlockSpec(memory_space=pltpu.HBM)

    def by_block(size):
        return pl.BlockSpec((BLK, size), lambda s: (steps - 1 - s, 0))

    return pl.pallas_call(
        backward_kernel,
        grid=(steps,),
        in_specs=[pl.BlockSpec(memory_space=pltpu.SMEM)]
        + [hbm] * 5
        + [vmem] * 5
        + [hbm, hbm]
        + [
            by_block(inner), by_block(mixed), by_block(mixed), by_block(LANES), by_block(inner),
            pl.BlockSpec((1, STATE, inner), lambda s: (steps - 1 - s, 0, 0)),
            by_block(width), by_block(inner),
        ],
        out_specs=[hbm, vmem, vmem, hbm, hbm],
        out_shape=[
            jax.ShapeDtypeStruct((blocks, BLK, columns), BF16),
            jax.ShapeDtypeStruct((LAYERS, 8, width), F32),
            jax.ShapeDtypeStruct((width // count, total), F32),
            jax.ShapeDtypeStruct((width, total), BF16),
            jax.ShapeDtypeStruct((count, 3, span, columns), BF16),
        ],
        scratch_shapes=[pltpu.VMEM((STATE, inner), F32), pltpu.VMEM((BLK + 8, mixed), F32)]
        + exchange_scratch(blocks, width)
        + [
            pltpu.VMEM((LAYERS, 4, blocks, 8, LANES), F32),
            pltpu.VMEM((blocks, SHARE, width), BF16),
            pltpu.VMEM((blocks, SHARE, width), F32),
            pltpu.VMEM((width, total), BF16),
            pltpu.VMEM((width, inner), F32),
            pltpu.VMEM((width, total - inner), F32),
            pltpu.VMEM((width, total), BF16),
        ]
        + [
            pltpu.VMEM((count // 2, width // count, total), BF16),
            pltpu.VMEM((count // 2 + 1, width // count, total), BF16),
            pltpu.VMEM((BIN, columns), BF16),
            pltpu.VMEM((3, count * span, columns), BF16),
            pltpu.VMEM(cot.shape, BF16),
            pltpu.VMEM(totals.shape, BF16),
            pltpu.VMEM(scales.shape, F32),
            pltpu.VMEM((blocks, SHARE, width), BF16),
            pltpu.VMEM((blocks, BLK, columns), BF16),
            pltpu.SemaphoreType.DMA((LAYERS, 8, blocks, 2)),
            pltpu.SemaphoreType.DMA((3 + LAYERS,)),
            pltpu.SemaphoreType.DMA((5, count // 2)),
            pltpu.SemaphoreType.DMA((4, 2)),
            pltpu.SemaphoreType.DMA((count, 2)),
            pltpu.SemaphoreType.DMA((3,)),
            pltpu.SemaphoreType.DMA((blocks, 4, 2)),
        ],
        compiler_params=pltpu.CompilerParams(
            vmem_limit_bytes=61 * 1024 * 1024, collective_id=2, has_side_effects=True
        ),
        cost_estimate=pl.CostEstimate(flops=6 * 10**10, bytes_accessed=6 * 10**7, transcendentals=10**7),
        name="layers_backward",
    )(
        offsets, cot, totals, scales, before, middle, gains, taps, head, wide, spread, weights, final,
        gate, mixed_in, conv, dt_raw, mixed_out, states, normed, gained,
    )


def spread_matrix(inner, heads):
    lane_head = lax.broadcasted_iota(jnp.int32, (2 * LANES, inner), 1) // (inner // heads)
    row_head = lax.broadcasted_iota(jnp.int32, (2 * LANES, inner), 0) % LANES
    return jnp.where(lane_head == row_head, 1.0, 0.0).astype(BF16)


SEQ_MIN = 512


def choose_rows(wanted, valid, begin, end):
    slots = begin + lax.broadcasted_iota(jnp.int32, (wanted.shape[0], end - begin), 1)
    return jnp.where((slots == wanted) & valid, 1.0, 0.0).astype(BF16)


def pick_all(off_ref, arrived, cols):
    first, second = off_ref[0], off_ref[1]
    length = arrived.shape[1]
    for block in range(cols.shape[0]):
        low, high = block * BLK, (block + 1) * BLK
        row = low + lax.broadcasted_iota(jnp.int32, (BLK, 1), 0)
        total = None
        for member, begin, least, most in ((1, first, SEQ_MIN, length), (2, second, BIN - length, BIN - SEQ_MIN)):
            reach = BIN - SEQ_MIN if member == 1 else BIN
            start, end = max(low - most, 0), min(high - least, length)
            if end <= 0 or start >= length or low >= reach:
                continue
            valid = (row >= first) & (row < second) if member == 1 else row >= second
            term = dot_nn(choose_rows(row - begin, valid, start, end), arrived[member, start:end, :])
            total = term if total is None else total + term
        if high <= length:
            own = arrived[0, low:high, :].astype(F32)
            own = jnp.where(row < first, own, 0.0)
            total = own if total is None else total + own
        cols[block] = total.astype(BF16)


def place_all(off_ref, cols, slots):
    first, second = off_ref[0], off_ref[1]
    length = slots.shape[1]
    for chunk in range(length // BLK):
        low, high = chunk * BLK, (chunk + 1) * BLK
        position = low + lax.broadcasted_iota(jnp.int32, (BLK, 1), 0)
        slots[0, low:high, :] = jnp.where(position < first, cols[low:high, :].astype(F32), 0.0).astype(BF16)
        for member, begin, stop, least, most, reach in (
            (1, first, second, SEQ_MIN, length, BIN - SEQ_MIN),
            (2, second, BIN, BIN - length, BIN - SEQ_MIN, BIN),
        ):
            wanted = begin + position
            start, end = least + low, min(most + high, reach)
            choose = choose_rows(wanted, wanted < stop, start, end)
            slots[member, low:high, :] = dot_nn(choose, cols[start:end, :]).astype(BF16)


class LineGather:
    def __init__(self, own, target, sems):
        self.own, self.target, self.sems = own, target, sems
        me = lax.axis_index("dp")
        self.me, self.low, self.high = me, me % 2, me // 2
        self.line = lax.axis_size("dp") // 2
        self.span = own.shape[0]

    def copy(self, kind, place, other, own):
        here = self.target.at[pl.ds((place * 2 + self.low) * self.span, self.span), :]
        arrival = 2 if kind == 2 else 3
        return pltpu.make_async_remote_copy(
            src_ref=self.own if own else here, dst_ref=here,
            send_sem=self.sems.at[kind, place], recv_sem=self.sems.at[arrival + 1, place],
            device_id={"dp": other}, device_id_type=pl.DeviceIdType.MESH,
        )

    def right(self, place, own=False):
        return self.copy(0, place, (self.high + 1) * 2 + self.low, own)

    def left(self, place, own=False):
        return self.copy(1, place, (self.high - 1) * 2 + self.low, own)

    def pair(self, place, own=False):
        return self.copy(2, place, self.high * 2 + 1 - self.low, own)

    def local(self):
        here = self.target.at[pl.ds(self.me * self.span, self.span), :]
        return pltpu.make_async_copy(self.own, here, self.sems.at[5, 0])

    def start_pair(self):
        self.local().start()
        self.pair(self.high, True).start()

    def start_line(self):
        @pl.when(self.high < self.line - 1)
        def _():
            self.right(self.high, True).start()

        @pl.when(self.high > 0)
        def _():
            self.left(self.high, True).start()

    def start(self):
        self.start_line()
        self.start_pair()

    def stage(self, step):
        @pl.when(self.high - step >= 0)
        def _():
            self.right(self.high - step).wait_recv()

            @pl.when(self.high < self.line - 1)
            def _():
                self.right(self.high - step).start()

            self.pair(self.high - step).start()

        @pl.when(self.high + step < self.line)
        def _():
            self.left(self.high + step).wait_recv()

            @pl.when(self.high > 0)
            def _():
                self.left(self.high + step).start()

            self.pair(self.high + step).start()

    def finish(self):
        self.local().wait()

        @pl.loop(0, self.line)
        def _(place):
            self.pair(place).wait_recv()
            self.pair(place).wait_send()

            @pl.when((self.high < self.line - 1) & (place <= self.high))
            def _():
                self.right(place).wait_send()

            @pl.when((self.high > 0) & (place >= self.high))
            def _():
                self.left(place).wait_send()


class Lines:
    def __init__(self, parts):
        self.parts, self.line = parts, parts[0].line

    def each(self, name, *given):
        for part in self.parts:
            getattr(part, name)(*given)

    def start(self):
        self.each("start")

    def start_pair(self):
        self.each("start_pair")

    def start_line(self):
        self.each("start_line")

    def stage(self, step):
        self.each("stage", step)

    def finish(self):
        self.each("finish")


class TileGather:
    def __init__(self, own, target, sems):
        self.own, self.target, self.sems = own, target, sems
        self.count, self.me = lax.axis_size("dp"), lax.axis_index("dp")

    def remote(self, step):
        return pltpu.make_async_remote_copy(
            src_ref=self.own, dst_ref=self.target.at[self.me],
            send_sem=self.sems.at[step, 0], recv_sem=self.sems.at[step, 1],
            device_id={"dp": (self.me + step) % self.count}, device_id_type=pl.DeviceIdType.MESH,
        )

    def start(self):
        self.target[self.me] = self.own[...]

        @pl.loop(1, self.count)
        def _(step):
            self.remote(step).start()

    def wait(self):
        @pl.loop(1, self.count)
        def _(step):
            self.remote(step).wait()


class LineReduce:
    def __init__(self, given, out, pair_buf, arrivals, sems):
        self.given, self.out, self.pair_buf = given, out, pair_buf
        self.arrivals, self.sems = arrivals, sems
        me = lax.axis_index("dp")
        self.low, self.high = me % 2, me // 2
        self.line = lax.axis_size("dp") // 2
        self.span = out.shape[0]

    def chunk(self, place, low):
        return pl.ds((place * 2 + low) * self.span, self.span)

    def pair(self, place):
        return pltpu.make_async_remote_copy(
            src_ref=self.given.at[self.chunk(place, 1 - self.low), :], dst_ref=self.pair_buf.at[place],
            send_sem=self.sems.at[0, place], recv_sem=self.sems.at[1, place],
            device_id={"dp": self.high * 2 + 1 - self.low}, device_id_type=pl.DeviceIdType.MESH,
        )

    def onward(self, place, right):
        slot = place + 1 if right else place
        other = (self.high + 1 if right else self.high - 1) * 2 + self.low
        return pltpu.make_async_remote_copy(
            src_ref=self.pair_buf.at[place], dst_ref=self.arrivals.at[slot],
            send_sem=self.sems.at[2, place], recv_sem=self.sems.at[3 if right else 4, place],
            device_id={"dp": other}, device_id_type=pl.DeviceIdType.MESH,
        )

    def by_distance(self, step, act):
        distance = self.line - 1 - step

        @pl.when(self.high + distance < self.line)
        def _():
            act(self.high + distance, True)

        @pl.when(self.high - distance >= 0)
        def _():
            act(self.high - distance, False)

    def send_pairs(self):
        @pl.loop(0, self.line - 1)
        def _(step):
            self.by_distance(step, lambda place, right: self.pair(place).start())

        self.pair(self.high).start()

    def fold(self, place):
        return self.given[self.chunk(place, self.low), :].astype(F32) + self.pair_buf[place].astype(F32)

    def pass_on(self, place, right):
        self.pair(place).wait_recv()
        upstream = (self.high > 0) if right else (self.high < self.line - 1)
        slot = place + 1 if right else place

        @pl.when(upstream)
        def _():
            self.onward(place, right).wait_recv()
            self.pair_buf[place] = (self.fold(place) + self.arrivals[slot].astype(F32)).astype(BF16)

        @pl.when(jnp.logical_not(upstream))
        def _():
            self.pair_buf[place] = self.fold(place).astype(BF16)

        self.onward(place, right).start()

    def stage(self, step):
        self.by_distance(step, self.pass_on)

    def finish(self):
        here = self.high
        self.pair(here).wait_recv()
        self.out[...] = self.fold(here)

        @pl.when(here > 0)
        def _():
            self.onward(here, True).wait_recv()
            self.out[...] += self.arrivals[here + 1].astype(F32)

        @pl.when(here < self.line - 1)
        def _():
            self.onward(here, False).wait_recv()
            self.out[...] += self.arrivals[here].astype(F32)

        @pl.loop(0, self.line)
        def _(place):
            self.pair(place).wait_send()

            @pl.when(place != here)
            def _():
                self.onward(place, True).wait_send()


def line_scratch(count, span, columns):
    line = count // 2
    return [
        pltpu.VMEM((line, span, columns), BF16),
        pltpu.VMEM((line + 1, span, columns), BF16),
        pltpu.SemaphoreType.DMA((5, line)),
    ]


class MemberGather:
    def __init__(self, target, sems):
        self.target, self.sems = target, sems
        self.me = lax.axis_index("tensor")

    def remote(self, step):
        return pltpu.make_async_remote_copy(
            src_ref=self.target.at[self.me], dst_ref=self.target.at[self.me],
            send_sem=self.sems.at[step, 0], recv_sem=self.sems.at[step, 1],
            device_id={"tensor": (self.me + step) % 4}, device_id_type=pl.DeviceIdType.MESH,
        )

    def start(self):
        for step in range(1, 4):
            self.remote(step).start()

    def wait(self):
        for step in range(1, 4):
            self.remote(step).wait()


def end_kernel(
    off_ref, cols_ref, packs_ref, small_ref, later_ref,
    back_ref, pack_ref, sum_ref, shared_ref, maps_ref,
    slots, pair_buf, arrivals, line_sems, smalls, shared, maps,
    bin_sems, small_sems, shared_sems, maps_sems,
):
    ring = Ring(None)
    ring.greet()
    inner = (pack_ref.shape[1] - 2 * STATE - LANES) // 3
    first_map = 3 * inner
    bins = BinExchange(False, slots, back_ref, bin_sems)
    cut = pack_ref.shape[1] // (2 * LANES) * LANES
    line = Lines(
        [
            LineReduce(
                packs_ref.at[:, part], pack_ref.at[:, part], pair_buf.at[:, :, part], arrivals.at[:, :, part], line_sems.at[at]
            )
            for at, part in enumerate((pl.ds(0, cut), pl.ds(cut, pack_ref.shape[1] - cut)))
        ]
    )
    dp_smalls = TileGather(small_ref, smalls, small_sems)
    shared_smalls = MemberGather(shared, shared_sems)
    shared_maps = MemberGather(maps, maps_sems)
    line.each("send_pairs")
    place_all(off_ref, cols_ref, slots)
    bins.start()
    dp_smalls.start()

    @pl.loop(0, line.line - 1)
    def _(step):
        line.stage(step)

    dp_smalls.wait()
    sum_ref[...] = smalls[0]

    @pl.loop(1, smalls.shape[0])
    def _(at):
        sum_ref[...] += smalls[at]

    shared[ring.me] = sum_ref[...]
    shared_smalls.start()
    line.finish()
    maps[ring.me, 0] = pack_ref[:, first_map : first_map + 2 * STATE].astype(BF16)
    maps[ring.me, 1] = later_ref[:, first_map : first_map + 2 * STATE].astype(BF16)
    shared_maps.start()
    shared_smalls.wait()
    shared_ref[...] = (shared[0] + shared[1]) + (shared[2] + shared[3])
    shared_maps.wait()
    for layer in range(LAYERS):
        maps_ref[layer] = (maps[0, layer].astype(F32) + maps[1, layer].astype(F32)) + (
            maps[2, layer].astype(F32) + maps[3, layer].astype(F32)
        )
    bins.wait()


def end_exchange(offsets, grad_columns, packs, small, later_pack, span):
    count = lax.axis_size("dp")
    width, total = packs.shape
    columns = width // 4
    vmem = pl.BlockSpec(memory_space=pltpu.VMEM)
    pack_rows = width // count
    return pl.pallas_call(
        end_kernel,
        in_specs=[pl.BlockSpec(memory_space=pltpu.SMEM)] + [vmem] * 4,
        out_specs=[pl.BlockSpec(memory_space=pltpu.HBM), vmem, vmem, vmem, vmem],
        out_shape=[
            jax.ShapeDtypeStruct((count, 3, span, columns), BF16),
            jax.ShapeDtypeStruct((pack_rows, total), F32),
            jax.ShapeDtypeStruct(small.shape, F32),
            jax.ShapeDtypeStruct(small.shape, F32),
            jax.ShapeDtypeStruct((LAYERS, pack_rows, 2 * STATE), F32),
        ],
        scratch_shapes=[pltpu.VMEM((3, count * span, columns), BF16)]
        + line_scratch(count, pack_rows, total)[:2]
        + [
            pltpu.SemaphoreType.DMA((2, 5, count // 2)),
            pltpu.VMEM((count,) + small.shape, F32),
            pltpu.VMEM((4,) + small.shape, F32),
            pltpu.VMEM((4, LAYERS, pack_rows, 2 * STATE), BF16),
            pltpu.SemaphoreType.DMA((count, 2)),
            pltpu.SemaphoreType.DMA((count, 2)),
            pltpu.SemaphoreType.DMA((4, 2)),
            pltpu.SemaphoreType.DMA((4, 2)),
        ],
        compiler_params=pltpu.CompilerParams(
            vmem_limit_bytes=56 * 1024 * 1024, collective_id=3, has_side_effects=True
        ),
        cost_estimate=pl.CostEstimate(flops=6 * 10**10, bytes_accessed=6 * 10**7, transcendentals=0),
        name="end_exchange",
    )(offsets, grad_columns.reshape(BIN, columns), packs, small, later_pack)


def pad_to(values, rows, columns):
    return jnp.pad(values, ((0, rows - values.shape[0]), (0, columns - values.shape[1])))


def on_device(
    tokens, cotangent, lengths, packing, pre_gain, w_z, w_x, w_bc, w_dt, conv_x, conv_bc, head_params, norm_gain, w_out,
):
    dp_count = lax.axis_size("dp")
    bin_index = lax.axis_index("dp")
    seq_total, pos_here, cols_here = tokens.shape
    inner_part = conv_x.shape[2]
    heads_here = head_params.shape[2]
    dp_rows = w_z.shape[1]
    mixed = inner_part + 2 * STATE
    triples = lengths[packing].reshape(dp_count, 3)
    offsets = jnp.cumsum(triples, axis=1) - triples
    my_offsets = offsets[bin_index]
    bounds = my_offsets[1:3]
    by_bin = (dp_count, 3, pos_here, cols_here)
    given_tokens, given_cot = (array[packing].reshape(by_bin) for array in (tokens, cotangent))

    spread = spread_matrix(inner_part, heads_here)
    packs = []
    for layer in range(LAYERS):
        own = jnp.concatenate(
            [w_out[layer].T, w_z[layer], w_x[layer], w_bc[layer], pad_to(w_dt[layer], dp_rows, LANES)], axis=1
        )
        taps = jnp.concatenate([conv_x[layer], conv_bc[layer]], axis=1).astype(F32)
        head = jnp.stack([head_params[layer, 0], -jnp.exp(head_params[layer, 1])])
        wide = jnp.stack(
            [jnp.repeat(head_params[layer, 2], inner_part // heads_here), norm_gain[layer].astype(F32)]
        )
        packs.append((own, pad_to(taps, 8, mixed), pad_to(head, 8, LANES), pad_to(wide, 8, inner_part)))

    own_gains = lax.dynamic_update_slice(
        jnp.zeros((8, dp_count * dp_rows), F32), pre_gain.astype(F32), (0, bin_index * dp_rows)
    )
    taps_all, head_all, wide_all = (jnp.stack([pack[at] for pack in packs]) for at in (1, 2, 3))
    (
        rows_all, gate, mixed_in, conv, dt_raw, mixed_out, gained_all, states, first_before, middle, totals, scales,
        final_rows, gains, cot_columns, all_weights,
    ) = layers_forward(
        bounds, given_tokens, jnp.stack([pack[0] for pack in packs]), own_gains, given_cot,
        taps_all, head_all, wide_all, spread,
    )
    grad_columns, small, later_pack, first_packs, activations_back = layers_backward(
        bounds, cot_columns, totals, scales, first_before, middle, gains, taps_all, head_all, wide_all, spread,
        all_weights, final_rows, (gate, mixed_in, conv, dt_raw, mixed_out, states, rows_all, gained_all), pos_here,
    )
    returned, first_pack, sums, shared, maps = end_exchange(bounds, grad_columns, first_packs, small, later_pack, pos_here)
    grad_convx = sums[:, : CONV + 1, :inner_part]
    grad_convbc = shared[:, : CONV + 1, inner_part:mixed]
    shard_pre = lax.dynamic_slice_in_dim(shared[:, 5], bin_index * dp_rows, dp_rows, 1)
    skips = jnp.sum(sums[:, 6, :inner_part].reshape(LAYERS, heads_here, -1), axis=2)
    grad_head = jnp.stack([sums[:, 7, :heads_here], sums[:, 7, LANES : LANES + heads_here], skips], axis=1)
    grad_norm = sums[:, 6, inner_part : 2 * inner_part]
    own_weights = jnp.stack([first_pack, later_pack])
    grad_bc = maps
    grad_out = jnp.swapaxes(own_weights[:, :, :inner_part], 1, 2)
    grad_z = own_weights[:, :, inner_part : 2 * inner_part]
    grad_x = own_weights[:, :, 2 * inner_part : 3 * inner_part]
    grad_dt = own_weights[:, :, 3 * inner_part + 2 * STATE : 3 * inner_part + 2 * STATE + heads_here]

    rank_of = jnp.zeros_like(packing).at[packing].set(jnp.arange(seq_total, dtype=jnp.int32))

    def in_order(returned):
        return returned.reshape(seq_total, pos_here, cols_here)[rank_of]

    activations = in_order(activations_back)
    input_grad = in_order(returned)
    return (
        activations, input_grad, shard_pre, grad_z, grad_x, grad_bc, grad_dt,
        grad_convx, grad_convbc, grad_head, grad_norm, grad_out,
    )


def solution(mesh):
    placed = (
        P(None, "dp", "tensor"), P(None, "dp", "tensor"), P(), P(), P(None, "dp"),
        P(None, "dp", "tensor"), P(None, "dp", "tensor"), P(None, "dp", None), P(None, "dp", "tensor"),
        P(None, None, "tensor"), P(), P(None, None, "tensor"), P(None, "tensor"), P(None, "tensor", "dp"),
    )
    results = (
        P(None, "dp", "tensor"), P(None, "dp", "tensor"), P(None, "dp"),
        P(None, "dp", "tensor"), P(None, "dp", "tensor"), P(None, "dp", None), P(None, "dp", "tensor"),
        P(None, None, "tensor"), P(), P(None, None, "tensor"), P(None, "tensor"), P(None, "tensor", "dp"),
    )
    return jax.shard_map(on_device, mesh=mesh, in_specs=placed, out_specs=results, check_vma=False)
```

```python
import functools
import jax
import jax.numpy as jnp
from jax import lax
from jax.experimental import pallas as pl
from jax.experimental.pallas import tpu as pltpu
from jax.sharding import PartitionSpec as P

CONV = 4
INNER = 2048
LAYERS = 2
BIN = 2048
eps = 1e-05
STATE = 128
BLK = 256
LANES = 128
LOG2E = 1.4426950408889634
F32 = jnp.float32
BF16 = jnp.bfloat16


def dot_nn(left, right):
    return lax.dot_general(left, right, (((1,), (0,)), ((), ())), preferred_element_type=F32)


def dot_nt(left, right):
    return lax.dot_general(left, right, (((1,), (1,)), ((), ())), preferred_element_type=F32)


def dot_tn(left, right):
    return lax.dot_general(left, right, (((0,), (0,)), ((), ())), preferred_element_type=F32)


def split_two(values):
    high = values.astype(BF16)
    return high, (values - high.astype(F32)).astype(BF16)


def split_three(values):
    high = values.astype(BF16)
    rest = values - high.astype(F32)
    middle = rest.astype(BF16)
    return high, middle, (rest - middle.astype(F32)).astype(BF16)


def spread_heads(values, spread):
    high, low = split_two(values)
    return dot_nn(jnp.concatenate([high, low], axis=1), spread)


def gather_heads(values, spread):
    high, low = split_two(values)
    half = spread[:LANES]
    return dot_nt(high, half) + dot_nt(low, half)


def sigmoid(values):
    return 0.5 * jnp.tanh(0.5 * values) + 0.5


def softplus(values):
    return jnp.maximum(values, 0.0) + jnp.log1p(jnp.exp(-jnp.abs(values)))


def segment_of(rows, first, second):
    return (rows >= first).astype(jnp.int32) + (rows >= second).astype(jnp.int32)


def block_frame(block, first, second):
    row_col = block * BLK + lax.broadcasted_iota(jnp.int32, (BLK, 1), 0)
    row_row = block * BLK + lax.broadcasted_iota(jnp.int32, (1, BLK), 1)
    return row_col, row_row, segment_of(row_col, first, second), segment_of(row_row, first, second)


def decay_parts(block, dt_raw, head, seg_col, first, second):
    shifted = dt_raw + head[0:1]
    steps = softplus(shifted)
    log_decay = steps * head[1:2]
    above = lax.broadcasted_iota(jnp.int32, (BLK, BLK), 0)
    below = lax.broadcasted_iota(jnp.int32, (BLK, BLK), 1)
    lower = jnp.where(above >= below, 1.0, 0.0).astype(BF16)
    parts = dot_nn(lower, jnp.concatenate(split_three(log_decay), axis=1))
    cumulative = parts[:, :LANES] + parts[:, LANES : 2 * LANES] + parts[:, 2 * LANES :]
    cum2 = cumulative * LOG2E
    final2 = cum2[BLK - 1 : BLK]
    last_seg = segment_of(block * BLK + BLK - 1, first, second)
    prior_seg = jnp.where(block == 0, -1, segment_of(block * BLK - 1, first, second))
    entering = jnp.where(seg_col == prior_seg, jnp.exp2(cum2), 0.0)
    tail = jnp.where(seg_col == last_seg, jnp.exp2(final2 - cum2), 0.0)
    retained = jnp.where(last_seg == prior_seg, jnp.exp2(final2), 0.0)
    return shifted, steps, cum2, entering, tail, retained


def head_half(pair, head):
    lanes = lax.broadcasted_iota(jnp.int32, pair.shape, 1)
    keep = (lanes < LANES // 2) if head % 2 == 0 else (lanes >= LANES // 2)
    return jnp.where(keep, pair, jnp.zeros_like(pair))


SHARE = BLK // 4
AG_OWN, AG_ACROSS, AG_PASS, RS_PAIR, RS_ACROSS, SM_PAIR, SM_ACROSS = range(7)


class Ring:
    def __init__(self, sems):
        me = lax.axis_index("tensor")
        self.low, self.high = me % 2, me // 2
        self.me = me
        self.sibling = self.high * 2 + (1 - self.low)
        self.across = (1 - self.high) * 2 + self.low
        self.beyond = (1 - self.high) * 2 + (1 - self.low)
        self.sems = sems

    def greet(self):
        barrier = pltpu.get_barrier_semaphore()
        for other in (self.sibling, self.across, self.beyond):
            pl.semaphore_signal(barrier, inc=1, device_id={"tensor": other}, device_id_type=pl.DeviceIdType.MESH)
        pl.semaphore_wait(barrier, greet_dp(barrier) + 3)

    def slot(self, owner):
        return ((self.low + owner % 2) % 2) * 2 + (self.high + owner // 2) % 2

    def copy(self, kind, block, source, target, other):
        return pltpu.make_async_remote_copy(
            src_ref=source, dst_ref=target,
            send_sem=self.sems.at[kind, block, 0], recv_sem=self.sems.at[kind, block, 1],
            device_id={"tensor": other}, device_id_type=pl.DeviceIdType.MESH,
        )


def greet_dp(barrier):
    count, me = lax.axis_size("dp"), lax.axis_index("dp")

    @pl.loop(1, count)
    def _(step):
        pl.semaphore_signal(
            barrier, inc=1, device_id={"dp": (me + step) % count}, device_id_type=pl.DeviceIdType.MESH
        )

    return count - 1


class BinExchange:
    def __init__(self, to_bins, source, target, sems):
        self.to_bins, self.source, self.target, self.sems = to_bins, source, target, sems
        self.count, self.me = lax.axis_size("dp"), lax.axis_index("dp")
        self.span = source.shape[2] if to_bins else target.shape[2]

    def pieces(self, other):
        if self.to_bins:
            return self.source.at[other], self.target.at[:, pl.ds(self.me * self.span, self.span), :]
        return self.source.at[:, pl.ds(other * self.span, self.span), :], self.target.at[self.me]

    def remote(self, step, other):
        source, target = self.pieces(other)
        return pltpu.make_async_remote_copy(
            src_ref=source, dst_ref=target, send_sem=self.sems.at[step, 0], recv_sem=self.sems.at[step, 1],
            device_id={"dp": other}, device_id_type=pl.DeviceIdType.MESH,
        )

    def local(self):
        source, target = self.pieces(self.me)
        return pltpu.make_async_copy(source, target, self.sems.at[0, 0])

    def start(self):
        self.local().start()
        self.start_steps(1, self.count)

    def wait(self):
        self.local().wait()
        self.wait_steps(1, self.count)

    def start_steps(self, begin, end):
        @pl.loop(begin, end)
        def _(step):
            self.remote(step, (self.me + step) % self.count).start()

    def wait_steps(self, begin, end):
        @pl.loop(begin, end)
        def _(step):
            self.remote(step, (self.me + step) % self.count).wait()


class RowExchange:
    def __init__(self, to_rows, source, target, sems):
        self.to_rows, self.source, self.target, self.sems = to_rows, source, target, sems
        self.me = lax.axis_index("tensor")
        self.columns = source.shape[2] if to_rows else target.shape[2]

    def pieces(self, other):
        if self.to_rows:
            return (
                self.source.at[:, pl.ds(other * SHARE, SHARE), :],
                self.target.at[:, :, pl.ds(pl.multiple_of(self.me * self.columns, LANES), self.columns)],
            )
        return (
            self.source.at[:, :, pl.ds(pl.multiple_of(other * self.columns, LANES), self.columns)],
            self.target.at[:, pl.ds(self.me * SHARE, SHARE), :],
        )

    def remote(self, step):
        other = (self.me + step) % 4
        source, target = self.pieces(other)
        return pltpu.make_async_remote_copy(
            src_ref=source, dst_ref=target, send_sem=self.sems.at[step, 0], recv_sem=self.sems.at[step, 1],
            device_id={"tensor": other}, device_id_type=pl.DeviceIdType.MESH,
        )

    def local(self):
        source, target = self.pieces(self.me)
        return pltpu.make_async_copy(source, target, self.sems.at[0, 0])

    def start(self):
        self.local().start()
        for step in range(1, 4):
            self.remote(step).start()

    def wait(self):
        self.local().wait()
        for step in range(1, 4):
            self.remote(step).wait()


def row_place(rows, member):
    return rows.at[:, pl.ds(member * SHARE, SHARE), :]


def column_place(rows, member):
    columns = rows.shape[2] // 4
    return rows.at[:, :, pl.ds(pl.multiple_of(member * columns, LANES), columns)]


def gather_copy(ring, kind, block, own, rows, place):
    if kind == AG_PASS:
        passed = place(rows, ring.across).at[block]
        return ring.copy(kind, block, passed, passed, ring.sibling)
    other = ring.sibling if kind == AG_OWN else ring.across
    target = place(rows, ring.me).at[block]
    return ring.copy(kind, block, target if own is None else own.at[block], target, other)


def pair_copy(ring, block, parts, from_pair):
    return ring.copy(RS_PAIR, block, parts.at[block, pl.ds(2 * SHARE, 2 * SHARE), :], from_pair.at[block], ring.sibling)


def across_copy(ring, block, parts, from_across):
    return ring.copy(RS_ACROSS, block, parts.at[block, pl.ds(SHARE, SHARE), :], from_across.at[block], ring.across)


def store_parts(ring, block, part, parts):
    for owner in range(4):
        parts[block, pl.ds(ring.slot(owner) * SHARE, SHARE), :] = part[owner * SHARE : (owner + 1) * SHARE].astype(BF16)


def add_pair(block, parts, from_pair):
    parts[block, pl.ds(SHARE, SHARE), :] = (
        parts[block, pl.ds(SHARE, SHARE), :].astype(F32) + from_pair[block, pl.ds(SHARE, SHARE), :].astype(F32)
    ).astype(BF16)


def add_all(block, parts, from_pair, from_across):
    return (
        parts[block, pl.ds(0, SHARE), :].astype(F32)
        + from_pair[block, pl.ds(0, SHARE), :].astype(F32)
        + from_across[block].astype(F32)
    )


def own_column(line, first_lane):
    lanes = lax.broadcasted_iota(jnp.int32, (SHARE, line.shape[1]), 1)
    rows = lax.broadcasted_iota(jnp.int32, (SHARE, line.shape[1]), 0)
    return jnp.sum(jnp.where(lanes == rows + first_lane, line, 0.0), axis=1, keepdims=True)


LAG = 4
DEFER = 2
PASS_AHEAD = 2


def forward_kernel(
    off_ref, tok_ref, packs_ref, cot_ref, taps_ref, head_ref, wide_ref, spread_ref,
    rows_ref, z_ref, in_ref, pre_ref, dt_ref, y_ref, gg_ref, st_ref,
    before_ref, middle_ref, tot_ref, scale_ref, final_ref, gains_ref, cot_cols_ref, weights_ref,
    state, padded, rows, parts, from_pair, from_across, sq_own, sq_pair, sq_sums, sq_across,
    weights, arrived, cols, cot_arrived, middle, kept,
    before_buf, middle_buf, tot_buf, scale_buf, final_buf, cot_cols, keep_sems,
    sems, copy_sems, line_sems, bin_sems, cot_sems,
):
    step = pl.program_id(0)
    inner = y_ref.shape[1]
    mixed = in_ref.shape[1]
    first, second = off_ref[0], off_ref[1]
    blocks = rows.shape[0]
    layer, block = step // blocks, step % blocks
    rings = (Ring(sems.at[0]), Ring(sems.at[1]))
    ring = rings[0]
    total_columns = weights.shape[2]

    def line_of(at_layer, begin, end, slot):
        part = pl.ds(begin, end - begin)
        return LineGather(packs_ref.at[at_layer, :, part], weights.at[at_layer, :, part], line_sems.at[slot])

    cut = inner + (total_columns - inner) // (2 * LANES) * LANES
    in_lines = [Lines([line_of(at, inner, cut, 3 * at), line_of(at, cut, total_columns, 3 * at + 1)]) for at in range(LAYERS)]
    out_lines = [line_of(at, 0, inner, 3 * at + 2) for at in range(LAYERS)]
    in_line, line = in_lines
    bins = BinExchange(True, tok_ref, arrived, bin_sems)
    cot_bins = BinExchange(True, cot_ref, cot_arrived, cot_sems)
    four = line.line == 4

    def gather(at_layer, kind, at):
        own, place = ((cols, column_place), (None, row_place))[at_layer]
        return gather_copy(rings[at_layer], kind, at, own, rows, place)

    def sq_pair_copy(at_ring, slot):
        return at_ring.copy(SM_PAIR, slot % blocks, sq_own.at[slot], sq_pair.at[slot], at_ring.sibling)

    def sq_across_copy(at_ring, slot):
        return at_ring.copy(SM_ACROSS, slot % blocks, sq_sums.at[slot], sq_across.at[slot], at_ring.across)

    def own_copy():
        return pltpu.make_async_copy(cols, column_place(rows, ring.me), copy_sems.at[LAYERS])

    def keep_weights(at):
        return pltpu.make_async_copy(weights.at[at], weights_ref.at[at], copy_sems.at[at])

    def keep_copies():
        kept_pairs = (
            (before_buf, before_ref), (middle_buf, middle_ref), (tot_buf, tot_ref),
            (scale_buf, scale_ref), (final_buf, final_ref), (cot_cols, cot_cols_ref),
        )
        return [pltpu.make_async_copy(a, b, keep_sems.at[at]) for at, (a, b) in enumerate(kept_pairs)]

    def clear():
        state[...] = jnp.zeros_like(state)
        padded[pl.ds(0, 8), :] = jnp.zeros((8, mixed), F32)

    @pl.when(step == 0)
    def _():
        ring.greet()
        half = bins.count // 2
        bins.local().start()
        bins.start_steps(half - 1, half + 2)
        in_line.start_pair()
        for part in (out_lines[0], line, out_lines[1]):
            part.start_pair()
        clear()
        bins.wait_steps(half - 1, half + 2)
        in_line.start_line()
        bins.start_steps(1, half - 1)
        bins.start_steps(half + 2, bins.count)
        bins.local().wait()
        bins.wait_steps(1, half - 1)
        bins.wait_steps(half + 2, bins.count)
        pick_all(off_ref, arrived, cols)
        own_copy().start()

        @pl.loop(0, blocks)
        def _(at):
            gather(0, AG_ACROSS, at).start()
            gather(0, AG_OWN, at).start()

        own_copy().wait()

        def pass_rows(begin, end):
            @pl.loop(begin, end)
            def _(at):
                gather(0, AG_ACROSS, at).wait_recv()
                gather(0, AG_PASS, at).start()

        if four:
            in_line.stage(1)
            pass_rows(0, blocks // 2)
            in_line.stage(2)
            pass_rows(blocks // 2, blocks)
            in_line.stage(3)
            for part in (out_lines[0], line, out_lines[1]):
                part.start_line()
        else:
            pass_rows(0, blocks)

            @pl.loop(1, line.line)
            def _(stage):
                in_line.stage(stage)

        in_line.finish()
        last_columns = weights[0, :, total_columns - LANES :].astype(F32)
        gains_ref[...] = jnp.transpose(last_columns)[8:16]
        if not four:
            for part in (out_lines[0], line, out_lines[1]):
                part.start_line()

    @pl.when(step == blocks)
    def _():
        clear()

    for at_layer in range(LAYERS):

        @pl.when(layer == at_layer)
        def _(at_layer=at_layer):
            gather(at_layer, AG_OWN, block).wait_recv()
            gather(at_layer, AG_PASS, block).wait_recv()

    gains = gains_ref[...]
    raw = rows[block].astype(F32)
    mean = jnp.sum(raw * raw, axis=1, keepdims=True) / raw.shape[1]
    normed = raw * lax.rsqrt(mean + eps) * gains[0:1]
    here = jnp.where(layer == 0, normed, raw).astype(BF16)
    rows_ref[...] = here
    row_col, row_row, seg_col, seg_row = block_frame(block, first, second)
    seg_start = jnp.where(seg_col == 0, 0, jnp.where(seg_col == 1, first, second))
    within = row_col - seg_start
    product = dot_nn(here, weights[layer, :, inner:])
    gate = product[:, :inner]
    mixed_in = product[:, inner : inner + mixed]
    dt_raw = product[:, inner + mixed :]
    z_ref[...] = gate.astype(BF16)
    in_ref[...] = mixed_in.astype(BF16)
    dt_ref[...] = dt_raw
    padded[pl.ds(8, BLK), :] = mixed_in
    taps = taps_ref[layer]
    conv = taps[CONV : CONV + 1] + taps[CONV - 1 : CONV] * mixed_in
    for delay in range(1, CONV):
        shifted_in = padded[pl.ds(8 - delay, BLK), :]
        conv = conv + taps[CONV - 1 - delay : CONV - delay] * jnp.where(within >= delay, shifted_in, 0.0)
    padded[pl.ds(0, 8), :] = padded[pl.ds(BLK, 8), :]
    pre_ref[...] = conv
    mixed_low = (conv * sigmoid(conv)).astype(BF16)
    x_low = mixed_low[:, :inner]
    b_low = mixed_low[:, inner : inner + STATE]
    c_low = mixed_low[:, inner + STATE :]
    head = head_ref[layer]
    spread = spread_ref[...]
    shifted, steps, cum2, entering, tail, retained = decay_parts(block, dt_raw, head, seg_col, first, second)
    cum_row = jnp.transpose(cum2)
    x_in = x_low.astype(F32)
    x_steps = spread_heads(steps, spread) * x_in
    x_steps_low = x_steps.astype(BF16)
    allowed = (seg_col == seg_row) & (row_col >= row_row)
    scores = jnp.where(allowed, dot_nt(c_low, b_low), 0.0)
    old_state = state[...]
    st_ref[0] = old_state
    carried = spread_heads(entering, spread) * dot_nn(c_low, old_state.astype(BF16))
    wide = wide_ref[layer]
    pieces = []
    for pair in range(inner // LANES):
        columns = slice(pair * LANES, (pair + 1) * LANES)
        total = None
        for head_index in (2 * pair, 2 * pair + 1):
            gaps = cum2[:, head_index : head_index + 1] - cum_row[head_index : head_index + 1, :]
            coupling = (jnp.exp2(jnp.minimum(gaps, 0.0)) * scores).astype(BF16)
            term = dot_nn(coupling, head_half(x_steps_low[:, columns], head_index))
            total = term if total is None else total + term
        pieces.append(total)
    mixed_out = jnp.concatenate(pieces, axis=1) + carried + wide[0:1] * x_in
    tailed = (spread_heads(tail, spread) * x_steps).astype(BF16)
    keep = spread_heads(jnp.broadcast_to(retained, (8, LANES)), spread)[0:1]
    state[...] = old_state * keep + dot_tn(b_low, tailed)
    y_ref[...] = mixed_out
    gated = mixed_out * (gate * sigmoid(gate))
    gained = (gated * wide[1:2]).astype(BF16)
    gg_ref[...] = gained
    now = Ring(sems.at[layer])
    high, low = split_two(gated * gated)
    ones = jnp.ones((8, inner), BF16)
    sq_own[step] = dot_nt(ones, high) + dot_nt(ones, low)
    sq_pair_copy(now, step).start()

    def free_parts(at_layer, at):
        if at_layer == 0:
            gather(0, AG_PASS, at).wait_send()
        else:
            pair_copy(ring, at, parts, from_pair).wait_send()
            across_copy(ring, at, parts, from_across).wait_send()

    def send_parts(at_ring, at, values, out_weights):
        store_parts(at_ring, at, dot_nt(values, out_weights), parts)
        pair_copy(at_ring, at, parts, from_pair).start()

    @pl.when(block < DEFER)
    def _():
        kept[block] = gained

    for at_layer in range(LAYERS):
        first_step = at_layer * blocks
        if four:
            for stage in (1, 2, 3):
                when = min(stage - 1, DEFER) if at_layer == 0 else 2 * stage + 2

                @pl.when(step == when)
                def _(at_layer=at_layer, stage=stage):
                    out_lines[at_layer].stage(stage)

        @pl.when(step == first_step + DEFER)
        def _(at_layer=at_layer):
            if not four:

                @pl.loop(1, line.line)
                def _(stage):
                    out_lines[at_layer].stage(stage)

            out_lines[at_layer].finish()
            keep_weights(at_layer).start()

            @pl.loop(0, DEFER)
            def _(at):
                free_parts(at_layer, at)
                send_parts(rings[at_layer], at, kept[at], weights[at_layer, :, :inner])

    @pl.when(block >= DEFER)
    def _():
        for at_layer in range(LAYERS):

            @pl.when(layer == at_layer)
            def _(at_layer=at_layer):
                free_parts(at_layer, block)

        send_parts(now, block, gained, weights[layer, :, :inner])

    def second_stage(slot):
        at_layer, at = slot // blocks, slot % blocks
        at_ring = Ring(sems.at[at_layer])
        pair_copy(at_ring, at, parts, from_pair).wait_recv()
        sq_pair_copy(at_ring, slot).wait_recv()

        add_pair(at, parts, from_pair)
        sq_sums[slot] = sq_own[slot] + sq_pair[slot]
        across_copy(at_ring, at, parts, from_across).start()
        sq_across_copy(at_ring, slot).start()

    def last_stage(at_layer, at):
        at_ring, slot = rings[at_layer], at_layer * blocks + at
        across_copy(at_ring, at, parts, from_across).wait_recv()
        sq_across_copy(at_ring, slot).wait_recv()
        total = add_all(at, parts, from_pair, from_across)
        squares = own_column((sq_sums[slot] + sq_across[slot])[0:1], ring.me * SHARE)
        scale = lax.rsqrt(squares / INNER + eps)
        here = pl.ds(at * SHARE, SHARE)
        mine = pl.ds(ring.me * SHARE, SHARE)
        tot_buf[slot] = total.astype(BF16)
        scale_buf[slot] = scale
        if at_layer == 0:
            before = rows[at, mine, :]
            before_buf[at] = before
            hidden = before.astype(F32) + total * scale
            middle[at] = hidden
            middle_buf[at] = hidden.astype(BF16)
            mean = jnp.sum(hidden * hidden, axis=1, keepdims=True) / hidden.shape[1]
            later = (hidden * lax.rsqrt(mean + eps) * gains[1:2]).astype(BF16)
            rows[at, mine, :] = later
            gather(1, AG_ACROSS, at).start()
            gather(1, AG_OWN, at).start()
        else:
            final_buf[at] = (middle[at] + total * scale).astype(BF16)

    @pl.when((step >= LAG) & (step < blocks + LAG))
    def _():
        last_stage(0, step - LAG)

    @pl.when(step >= blocks + LAG)
    def _():
        last_stage(1, step - LAG - blocks)

    if four:
        for stage, when in ((1, 1), (2, 3), (3, 5)):

            @pl.when(step == when)
            def _(stage=stage):
                line.stage(stage)

    @pl.when(step == blocks)
    def _():
        cot_bins.start()

    @pl.when((step >= blocks - PASS_AHEAD) & (step < 2 * blocks - PASS_AHEAD))
    def _():
        gather(1, AG_ACROSS, (step + PASS_AHEAD) % blocks).wait_recv()
        gather(1, AG_PASS, (step + PASS_AHEAD) % blocks).start()

    @pl.when((step % blocks == DEFER + 1) & (step > 0))
    def _():
        @pl.loop(0, DEFER)
        def _(at):
            second_stage(layer * blocks + at)

    @pl.when((step > 0) & ((step - 1 + blocks) % blocks >= DEFER))
    def _():
        second_stage(step - 1)

    @pl.when(step == blocks - 1)
    def _():
        if not four:

            @pl.loop(1, line.line)
            def _(stage):
                line.stage(stage)

        line.finish()

    @pl.when(step == 2 * blocks - 1)
    def _():
        second_stage(step)
        cot_bins.wait()
        pick_all(off_ref, cot_arrived, cot_cols)

        before_keep, middle_keep, *late_keep, cot_keep = keep_copies()
        for copy in (before_keep, middle_keep, cot_keep):
            copy.start()

        @pl.loop(blocks - LAG, blocks)
        def _(at):
            last_stage(1, at)

        for copy in late_keep:
            copy.start()

        @pl.loop(0, blocks)
        def _(at):
            gather(0, AG_OWN, at).wait_send()
            gather(0, AG_ACROSS, at).wait_send()
            for kind in (AG_OWN, AG_ACROSS, AG_PASS):
                gather(1, kind, at).wait_send()
            pair_copy(rings[1], at, parts, from_pair).wait_send()
            across_copy(rings[1], at, parts, from_across).wait_send()
            for at_layer in range(LAYERS):
                sq_pair_copy(rings[at_layer], at_layer * blocks + at).wait_send()
                sq_across_copy(rings[at_layer], at_layer * blocks + at).wait_send()

        for at in range(LAYERS):
            keep_weights(at).wait()
        for copy in (before_keep, middle_keep, *late_keep, cot_keep):
            copy.wait()


def own_line(column):
    lanes = lax.broadcasted_iota(jnp.int32, (SHARE, LANES), 1)
    rows = lax.broadcasted_iota(jnp.int32, (SHARE, LANES), 0)
    return jnp.sum(jnp.where(lanes == rows, column, 0.0), axis=0, keepdims=True)


TILE_KINDS = (5, 6, 7)
AHEAD = 2
QUEUED = 4
BACK_LAG = 4


def backward_kernel(
    off_ref, cot_in, tot_in, scale_in, before_ref, middle_ref, gains_ref, taps_ref, head_ref, wide_ref, spread_ref,
    weights_ref, final_ref,
    z_ref, in_ref, pre_ref, dt_ref, y_ref, st_ref, normed_ref, gg_ref,
    gcols_out, small_ref, pack_ref, packs_ref, back_ref,
    dstate, padded, rows, parts, from_pair, from_across, tiles, held, running, weights, acc_out, acc_in,
    packs, pair_buf, arrivals, cols, slots,
    cot_ref, tot_ref, scale_ref, ginput, gcols_ref, sems, copy_sems, line_sems, row_sems, bin_sems, load_sems, col_sems,
):
    step = pl.program_id(0)
    inner = y_ref.shape[1]
    mixed = in_ref.shape[1]
    first, second = off_ref[0], off_ref[1]
    blocks = rows.shape[0]
    phase, block = step // blocks, blocks - 1 - step % blocks
    layer = LAYERS - 1 - phase
    rings = (Ring(sems.at[0]), Ring(sems.at[1]))
    ring = rings[0]
    line = LineReduce(packs, pack_ref, pair_buf, arrivals, line_sems)
    four = line.line == 4
    final_rows = RowExchange(False, final_ref, cols.reshape(blocks, BLK, cols.shape[1]), row_sems)
    bins = BinExchange(False, slots, back_ref, bin_sems)
    mine = pl.ds(ring.me * SHARE, SHARE)

    def gather(at_phase, kind, at):
        own, place = ((cot_ref, column_place), (None, row_place))[at_phase]
        return gather_copy(rings[at_phase], kind, at, own, rows, place)

    def tile_copies(at_phase, at):
        at_ring = rings[at_phase]
        here = tiles.at[at_phase, ring.me, at]
        return [
            at_ring.copy(kind, at, here, here, other)
            for kind, other in zip(TILE_KINDS, (ring.sibling, ring.across, ring.beyond))
        ]

    def make_tile(at_phase, at, grad_low):
        slot = (LAYERS - 1 - at_phase) * blocks + at
        scale = scale_ref[slot]
        weighted = jnp.sum(grad_low.astype(F32) * tot_ref[slot].astype(F32), axis=1, keepdims=True)
        twice = -(scale * scale * scale) / INNER * weighted
        row = lax.broadcasted_iota(jnp.int32, (8, LANES), 0)
        tiles[at_phase, ring.me, at] = jnp.where(row == 0, own_line(twice), own_line(scale))
        for copy in tile_copies(at_phase, at):
            copy.start()

    def prepare(at):
        gather(0, AG_OWN, at).wait_recv()
        gather(0, AG_PASS, at).wait_recv()
        make_tile(0, at, rows[at, mine, :])

    def pass_rows(at_phase, at):
        gather(at_phase, AG_ACROSS, at).wait_recv()
        gather(at_phase, AG_PASS, at).start()

    def load_inputs():
        pairs = ((cot_in, cot_ref), (tot_in, tot_ref), (scale_in, scale_ref))
        return [pltpu.make_async_copy(a, b, load_sems.at[at]) for at, (a, b) in enumerate(pairs)]

    def column_copy(at, hop):
        other = (ring.me + hop) % 4
        columns = gcols_ref.shape[2]
        source = ginput.at[at, :, pl.ds(pl.multiple_of(other * columns, LANES), columns)]
        target = gcols_ref.at[at, mine, :]
        if hop == 0:
            return pltpu.make_async_copy(source, target, col_sems.at[at, 0, 0])
        return pltpu.make_async_remote_copy(
            src_ref=source, dst_ref=target, send_sem=col_sems.at[at, hop, 0], recv_sem=col_sems.at[at, hop, 1],
            device_id={"tensor": other}, device_id_type=pl.DeviceIdType.MESH,
        )

    def send_rows(at):
        gather(0, AG_ACROSS, at).start()
        gather(0, AG_OWN, at).start()

    def own_copy():
        return pltpu.make_async_copy(cot_ref, column_place(rows, ring.me), copy_sems.at[0])

    def load_weights(at_layer):
        return pltpu.make_async_copy(weights_ref.at[at_layer], weights, copy_sems.at[1])

    def load_held(at_phase):
        return pltpu.make_async_copy((middle_ref, before_ref)[at_phase], held, copy_sems.at[3 + at_phase])

    def store_packs():
        return pltpu.make_async_copy(packs, packs_ref, copy_sems.at[2])

    def clear():
        dstate[...] = jnp.zeros_like(dstate)
        padded[pl.ds(BLK, 8), :] = jnp.zeros((8, mixed), F32)
        acc_out[...] = jnp.zeros_like(acc_out)
        acc_in[...] = jnp.zeros_like(acc_in)

    @pl.when(step == 0)
    def _():
        cot_load, *loads = load_inputs()
        for copy in (cot_load, *loads):
            copy.start()
        load_weights(LAYERS - 1).start()
        load_held(0).start()
        cot_load.wait()
        own_copy().start()
        ring.greet()

        send_rows(blocks - 1)
        clear()
        small_ref[...] = jnp.zeros_like(small_ref)
        own_copy().wait()
        pass_rows(0, blocks - 1)
        for at in range(1, QUEUED):
            send_rows(blocks - 1 - at)
        for copy in loads:
            copy.wait()
        prepare(blocks - 1)
        for at in range(1, AHEAD + 1):
            pass_rows(0, blocks - 1 - at)
        for at in range(1, AHEAD):
            prepare(blocks - 1 - at)
        load_weights(LAYERS - 1).wait()

    @pl.when(step == blocks)
    def _():
        load_weights(0).start()
        clear()
        load_weights(0).wait()

    @pl.when(phase > 0)
    def _():
        gather(1, AG_OWN, block).wait_recv()
        gather(1, AG_PASS, block).wait_recv()

    for at_phase in range(LAYERS):

        @pl.when(phase == at_phase)
        def _(at_phase=at_phase):
            for copy in tile_copies(at_phase, block):
                copy.wait_recv()

    here = rows[block]
    tile_rows = [tiles[phase, owner, block] for owner in range(4)]
    twice_here = jnp.concatenate([own_column(tile[0:1], 0) for tile in tile_rows], axis=0)
    scale_here = jnp.concatenate([own_column(tile[1:2], 0) for tile in tile_rows], axis=0)
    row_col, row_row, seg_col, seg_row = block_frame(block, first, second)
    seg_end = jnp.where(seg_col == 0, first, jnp.where(seg_col == 1, second, BIN))
    remaining = seg_end - row_col
    head = head_ref[layer]
    wide = wide_ref[layer]
    spread = spread_ref[...]
    skip, gain = wide[0:1], wide[1:2]
    gate = z_ref[...].astype(F32)
    mixed_out = y_ref[...]
    conv = pre_ref[...]
    gate_sig = sigmoid(gate)
    gate_silu = gate * gate_sig
    gated = mixed_out * gate_silu
    grad_scaled = dot_nn(here, weights[:, :inner]) * scale_here
    grad_gated = grad_scaled * gain + twice_here * gated
    grad_out = grad_gated * gate_silu
    grad_gate = grad_gated * mixed_out * (gate_sig * (1.0 + gate * (1.0 - gate_sig)))
    grad_out_low = grad_out.astype(BF16)

    conv_sig = sigmoid(conv)
    mixed_low = (conv * conv_sig).astype(BF16)
    x_low = mixed_low[:, :inner]
    b_low = mixed_low[:, inner : inner + STATE]
    c_low = mixed_low[:, inner + STATE :]
    x_in = x_low.astype(F32)
    shifted, steps, cum2, entering, tail, retained = decay_parts(block, dt_ref[...], head, seg_col, first, second)
    cum_row = jnp.transpose(cum2)
    steps_wide = spread_heads(steps, spread)
    x_steps_low = (steps_wide * x_in).astype(BF16)
    x_steps = x_steps_low.astype(F32)

    allowed = (seg_col == seg_row) & (row_col <= row_row)
    scores = jnp.where(allowed, dot_nt(b_low, c_low), 0.0)
    grad_scores = jnp.zeros((BLK, BLK), F32)
    pieces = []
    for pair in range(inner // LANES):
        columns = slice(pair * LANES, (pair + 1) * LANES)
        total = None
        for head_index in (2 * pair, 2 * pair + 1):
            gaps = cum_row[head_index : head_index + 1, :] - cum2[:, head_index : head_index + 1]
            decays = jnp.exp2(jnp.minimum(gaps, 0.0))
            coupling = (decays * scores).astype(BF16)
            term = dot_nn(coupling, head_half(grad_out_low[:, columns], head_index))
            total = term if total is None else total + term
            grad_scores = grad_scores + decays * dot_nt(
                head_half(x_steps_low[:, columns], head_index), grad_out_low[:, columns]
            )
        pieces.append(total)
    grad_scores_low = jnp.where(allowed, grad_scores, 0.0).astype(BF16)
    old_dstate = dstate[...]
    old_dstate_low = old_dstate.astype(BF16)
    old_state = st_ref[0]
    tail_wide = spread_heads(tail, spread)
    from_state = tail_wide * dot_nn(b_low, old_dstate_low)
    grad_unit = jnp.concatenate(pieces, axis=1) + from_state
    entered = (spread_heads(entering, spread) * grad_out).astype(BF16)
    tailed = (tail_wide * x_steps).astype(BF16)
    grad_c = dot_tn(grad_scores_low, b_low) + dot_nt(entered, old_state.astype(BF16))
    grad_b = dot_nn(grad_scores_low, c_low) + dot_nt(tailed, old_dstate_low)
    keep = spread_heads(jnp.broadcast_to(retained, (8, LANES)), spread)[0:1]
    dstate[...] = old_dstate * keep + dot_tn(c_low, entered)

    balance = gather_heads(grad_out_low.astype(F32) * (mixed_out - skip * x_in) - x_steps * grad_unit, spread)
    direct = gather_heads(x_in * grad_unit, spread)
    final_wide = jnp.sum(x_steps * from_state, axis=0, keepdims=True) + keep * jnp.sum(
        old_dstate * old_state, axis=0, keepdims=True
    )
    final = gather_heads(jnp.broadcast_to(final_wide, (8, inner)), spread)[0:1]
    above = lax.broadcasted_iota(jnp.int32, (BLK, BLK), 0)
    below = lax.broadcasted_iota(jnp.int32, (BLK, BLK), 1)
    upper = jnp.where(above <= below, 1.0, 0.0).astype(BF16)
    thirds = dot_nn(upper, jnp.concatenate(split_three(balance), axis=1))
    grad_log = thirds[:, :LANES] + thirds[:, LANES : 2 * LANES] + thirds[:, 2 * LANES :] + final
    grad_steps = direct + grad_log * head[1:2]
    grad_dt = grad_steps * sigmoid(shifted)
    small_ref[layer, 7:8, :LANES] += jnp.sum(grad_dt, axis=0, keepdims=True)
    small_ref[layer, 7:8, LANES : 2 * LANES] += jnp.sum(grad_log * steps, axis=0, keepdims=True) * head[1:2]
    small_ref[layer, 6:7, :inner] += jnp.sum(grad_out * x_in, axis=0, keepdims=True)
    small_ref[layer, 6:7, inner : 2 * inner] += jnp.sum(grad_scaled * gated, axis=0, keepdims=True)

    grad_x = steps_wide * grad_unit + skip * grad_out
    grad_conv = jnp.concatenate([grad_x, grad_b, grad_c], axis=1) * (
        conv_sig * (1.0 + conv * (1.0 - conv_sig))
    )
    padded[pl.ds(0, BLK), :] = grad_conv
    mixed_in = in_ref[...].astype(F32)
    taps = taps_ref[layer]
    grad_in = taps[CONV - 1 : CONV] * grad_conv
    small_ref[layer, CONV : CONV + 1, :mixed] += jnp.sum(grad_conv, axis=0, keepdims=True)
    small_ref[layer, CONV - 1 : CONV, :mixed] += jnp.sum(mixed_in * grad_conv, axis=0, keepdims=True)
    for delay in range(1, CONV):
        later = jnp.where(remaining > delay, padded[pl.ds(delay, BLK), :], 0.0)
        grad_in = grad_in + taps[CONV - 1 - delay : CONV - delay] * later
        small_ref[layer, CONV - 1 - delay : CONV - delay, :mixed] += jnp.sum(mixed_in * later, axis=0, keepdims=True)
    padded[pl.ds(BLK, 8), :] = padded[pl.ds(0, 8), :]
    gproj = jnp.concatenate([grad_gate.astype(BF16), grad_in.astype(BF16), grad_dt.astype(BF16)], axis=1)
    acc_out[...] += dot_tn(here, (gg_ref[...].astype(F32) * scale_here).astype(BF16))
    acc_in[...] += dot_tn(normed_ref[...], gproj)
    part = dot_nt(gproj, weights[:, inner:])

    @pl.when(phase > 0)
    def _():
        pair_copy(ring, block, parts, from_pair).wait_send()
        across_copy(ring, block, parts, from_across).wait_send()

    @pl.when(phase == 0)
    def _():
        gather(0, AG_PASS, block).wait_send()

    now = Ring(sems.at[phase])
    store_parts(now, block, part, parts)
    pair_copy(now, block, parts, from_pair).start()

    def second_stage(turn):
        at_phase, at = turn // blocks, blocks - 1 - turn % blocks
        at_ring = Ring(sems.at[at_phase])
        pair_copy(at_ring, at, parts, from_pair).wait_recv()

        add_pair(at, parts, from_pair)
        across_copy(at_ring, at, parts, from_across).start()

    def last_stage(at_phase, at):
        at_layer = LAYERS - 1 - at_phase
        across_copy(rings[at_phase], at, parts, from_across).wait_recv()
        grad_normed = add_all(at, parts, from_pair, from_across)
        hidden = held[at].astype(F32)
        width = hidden.shape[1]
        root = lax.rsqrt(jnp.sum(hidden * hidden, axis=1, keepdims=True) / width + eps)
        gained = grad_normed * gains_ref[at_layer : at_layer + 1, :]
        small_ref[at_layer, 5:6, :] += jnp.sum(grad_normed * hidden * root, axis=0, keepdims=True)
        along = jnp.sum(gained * hidden, axis=1, keepdims=True) * (root * root * root) / width
        change = gained * root - hidden * along
        if at_phase == 0:
            grad = rows[at, mine, :].astype(F32) + change
            running[at] = grad
            grad_low = grad.astype(BF16)
            rows[at, mine, :] = grad_low
            gather(1, AG_ACROSS, at).start()
            gather(1, AG_OWN, at).start()
            make_tile(1, at, grad_low)
        else:
            ginput[at] = (running[at] + change).astype(BF16)
            for hop in range(4):
                column_copy(at, hop).start()

    @pl.when(step == BACK_LAG)
    def _():
        load_held(0).wait()

    @pl.when(step == blocks + BACK_LAG)
    def _():
        load_held(1).start()
        load_held(1).wait()

    @pl.when((step >= BACK_LAG) & (step < blocks + BACK_LAG))
    def _():
        last_stage(0, blocks - 1 - (step - BACK_LAG))

    @pl.when(step >= blocks + BACK_LAG)
    def _():
        last_stage(1, blocks - 1 - (step - BACK_LAG - blocks))

    @pl.when(step + QUEUED < blocks)
    def _():
        send_rows(blocks - 1 - (step + QUEUED))

    @pl.when(step + AHEAD + 1 < blocks)
    def _():
        pass_rows(0, blocks - 1 - (step + AHEAD + 1))

    @pl.when(step + AHEAD < blocks)
    def _():
        prepare(blocks - 1 - (step + AHEAD))

    @pl.when((step >= blocks - PASS_AHEAD) & (step < 2 * blocks - PASS_AHEAD))
    def _():
        pass_rows(1, blocks - 1 - (step + PASS_AHEAD) % blocks)

    @pl.when(step >= 1)
    def _():
        second_stage(step - 1)

    @pl.when(step == 1)
    def _():
        final_rows.start()

    @pl.when(step == 4)
    def _():
        final_rows.wait()
        place_all(off_ref, cols, slots)
        bins.start()

    @pl.when(step == blocks - 1)
    def _():
        packs[:, :inner] = acc_out[...].astype(BF16)
        packs[:, inner:] = acc_in[...].astype(BF16)
        line.send_pairs()

    if four:
        for stage in (0, 1, 2):

            @pl.when(step == blocks + 1 + 2 * stage)
            def _(stage=stage):
                line.stage(stage)

    @pl.when(step == 2 * blocks - 1)
    def _():
        second_stage(step)
        if not four:

            @pl.loop(0, line.line - 1)
            def _(stage):
                line.stage(stage)

        line.finish()
        packs[:, :inner] = acc_out[...].astype(BF16)
        packs[:, inner:] = acc_in[...].astype(BF16)
        store_packs().start()

        @pl.loop(0, BACK_LAG)
        def _(turn):
            last_stage(1, BACK_LAG - 1 - turn)

        @pl.loop(0, blocks)
        def _(at):
            gather(0, AG_OWN, at).wait_send()
            gather(0, AG_ACROSS, at).wait_send()
            for kind in (AG_OWN, AG_ACROSS, AG_PASS):
                gather(1, kind, at).wait_send()
            pair_copy(rings[1], at, parts, from_pair).wait_send()
            across_copy(rings[1], at, parts, from_across).wait_send()
            for at_phase in range(LAYERS):
                for copy in tile_copies(at_phase, at):
                    copy.wait_send()

        @pl.loop(0, blocks)
        def _(at):
            for hop in range(4):
                column_copy(at, hop).wait()

        keep_columns = pltpu.make_async_copy(gcols_ref, gcols_out, load_sems.at[0])
        keep_columns.start()
        keep_columns.wait()
        store_packs().wait()
        bins.wait()


def whole(shape):
    return pl.BlockSpec(shape, lambda *at: (0,) * len(shape))


def exchange_scratch(blocks, width):
    return [
        pltpu.VMEM((blocks, BLK, width), BF16),
        pltpu.VMEM((blocks, BLK, width), BF16),
        pltpu.VMEM((blocks, 2 * SHARE, width), BF16),
        pltpu.VMEM((blocks, SHARE, width), BF16),
    ]


def layers_forward(offsets, given, packs, given_cot, taps, head, wide, spread):
    blocks, width = BIN // BLK, given_cot.shape[0] * packs.shape[1]
    inner, mixed = wide.shape[2], taps.shape[2]
    dp_count, members, span, columns = given_cot.shape
    total = packs.shape[2]
    steps = LAYERS * blocks
    vmem, hbm = pl.BlockSpec(memory_space=pltpu.VMEM), pl.BlockSpec(memory_space=pltpu.HBM)

    def by_block(size):
        return pl.BlockSpec((BLK, size), lambda s: (s, 0))

    return pl.pallas_call(
        forward_kernel,
        grid=(steps,),
        in_specs=[pl.BlockSpec(memory_space=pltpu.SMEM), hbm, vmem, hbm] + [vmem] * 4,
        out_specs=[
            by_block(width), by_block(inner), by_block(mixed), by_block(mixed),
            by_block(LANES), by_block(inner), by_block(inner),
            pl.BlockSpec((1, STATE, inner), lambda s: (s, 0, 0)),
            hbm, hbm, hbm, hbm, hbm, vmem, hbm, hbm,
        ],
        out_shape=[
            jax.ShapeDtypeStruct((steps * BLK, width), BF16),
            jax.ShapeDtypeStruct((steps * BLK, inner), BF16),
            jax.ShapeDtypeStruct((steps * BLK, mixed), BF16),
            jax.ShapeDtypeStruct((steps * BLK, mixed), F32),
            jax.ShapeDtypeStruct((steps * BLK, LANES), F32),
            jax.ShapeDtypeStruct((steps * BLK, inner), F32),
            jax.ShapeDtypeStruct((steps * BLK, inner), BF16),
            jax.ShapeDtypeStruct((steps, STATE, inner), F32),
            jax.ShapeDtypeStruct((blocks, SHARE, width), BF16),
            jax.ShapeDtypeStruct((blocks, SHARE, width), BF16),
            jax.ShapeDtypeStruct((steps, SHARE, width), BF16),
            jax.ShapeDtypeStruct((steps, SHARE, 1), F32),
            jax.ShapeDtypeStruct((blocks, SHARE, width), BF16),
            jax.ShapeDtypeStruct((8, width), F32),
            jax.ShapeDtypeStruct((blocks, BLK, columns), BF16),
            jax.ShapeDtypeStruct((LAYERS, width, total), BF16),
        ],
        scratch_shapes=[pltpu.VMEM((STATE, inner), F32), pltpu.VMEM((BLK + 8, mixed), F32)]
        + exchange_scratch(blocks, width)
        + [pltpu.VMEM((steps, 8, BLK), F32)] * 4
        + [
            pltpu.VMEM((LAYERS, width, total), BF16),
            pltpu.VMEM((members, dp_count * span, columns), BF16),
            pltpu.VMEM((blocks, BLK, columns), BF16),
            pltpu.VMEM((members, dp_count * span, columns), BF16),
            pltpu.VMEM((blocks, SHARE, width), F32),
            pltpu.VMEM((DEFER, BLK, inner), BF16),
            pltpu.VMEM((blocks, SHARE, width), BF16),
            pltpu.VMEM((blocks, SHARE, width), BF16),
            pltpu.VMEM((steps, SHARE, width), BF16),
            pltpu.VMEM((steps, SHARE, 1), F32),
            pltpu.VMEM((blocks, SHARE, width), BF16),
            pltpu.VMEM((blocks, BLK, columns), BF16),
            pltpu.SemaphoreType.DMA((6,)),
            pltpu.SemaphoreType.DMA((LAYERS, 7, blocks, 2)),
            pltpu.SemaphoreType.DMA((LAYERS + 1,)),
            pltpu.SemaphoreType.DMA((3 * LAYERS, 6, dp_count // 2)),
            pltpu.SemaphoreType.DMA((dp_count, 2)),
            pltpu.SemaphoreType.DMA((dp_count, 2)),
        ],
        compiler_params=pltpu.CompilerParams(
            vmem_limit_bytes=48 * 1024 * 1024, collective_id=1, has_side_effects=True
        ),
        cost_estimate=pl.CostEstimate(flops=6 * 10**10, bytes_accessed=6 * 10**7, transcendentals=10**7),
        name="layers_forward",
    )(offsets, given, packs, given_cot, taps, head, wide, spread)


def layers_backward(offsets, cot, totals, scales, before, middle, gains, taps, head, wide, spread, weights, final, saved, span):
    gate, mixed_in, conv, dt_raw, mixed_out, states, normed, gained = saved
    blocks, _, columns = cot.shape
    width = gains.shape[1]
    inner, mixed = wide.shape[2], taps.shape[2]
    total = weights.shape[2]
    steps = LAYERS * blocks
    count = lax.axis_size("dp")
    vmem, hbm = pl.BlockSpec(memory_space=pltpu.VMEM), pl.BlockSpec(memory_space=pltpu.HBM)

    def by_block(size):
        return pl.BlockSpec((BLK, size), lambda s: (steps - 1 - s, 0))

    return pl.pallas_call(
        backward_kernel,
        grid=(steps,),
        in_specs=[pl.BlockSpec(memory_space=pltpu.SMEM)]
        + [hbm] * 5
        + [vmem] * 5
        + [hbm, hbm]
        + [
            by_block(inner), by_block(mixed), by_block(mixed), by_block(LANES), by_block(inner),
            pl.BlockSpec((1, STATE, inner), lambda s: (steps - 1 - s, 0, 0)),
            by_block(width), by_block(inner),
        ],
        out_specs=[hbm, vmem, vmem, hbm, hbm],
        out_shape=[
            jax.ShapeDtypeStruct((blocks, BLK, columns), BF16),
            jax.ShapeDtypeStruct((LAYERS, 8, width), F32),
            jax.ShapeDtypeStruct((width // count, total), F32),
            jax.ShapeDtypeStruct((width, total), BF16),
            jax.ShapeDtypeStruct((count, 3, span, columns), BF16),
        ],
        scratch_shapes=[pltpu.VMEM((STATE, inner), F32), pltpu.VMEM((BLK + 8, mixed), F32)]
        + exchange_scratch(blocks, width)
        + [
            pltpu.VMEM((LAYERS, 4, blocks, 8, LANES), F32),
            pltpu.VMEM((blocks, SHARE, width), BF16),
            pltpu.VMEM((blocks, SHARE, width), F32),
            pltpu.VMEM((width, total), BF16),
            pltpu.VMEM((width, inner), F32),
            pltpu.VMEM((width, total - inner), F32),
            pltpu.VMEM((width, total), BF16),
        ]
        + [
            pltpu.VMEM((count // 2, width // count, total), BF16),
            pltpu.VMEM((count // 2 + 1, width // count, total), BF16),
            pltpu.VMEM((BIN, columns), BF16),
            pltpu.VMEM((3, count * span, columns), BF16),
            pltpu.VMEM(cot.shape, BF16),
            pltpu.VMEM(totals.shape, BF16),
            pltpu.VMEM(scales.shape, F32),
            pltpu.VMEM((blocks, SHARE, width), BF16),
            pltpu.VMEM((blocks, BLK, columns), BF16),
            pltpu.SemaphoreType.DMA((LAYERS, 8, blocks, 2)),
            pltpu.SemaphoreType.DMA((3 + LAYERS,)),
            pltpu.SemaphoreType.DMA((5, count // 2)),
            pltpu.SemaphoreType.DMA((4, 2)),
            pltpu.SemaphoreType.DMA((count, 2)),
            pltpu.SemaphoreType.DMA((3,)),
            pltpu.SemaphoreType.DMA((blocks, 4, 2)),
        ],
        compiler_params=pltpu.CompilerParams(
            vmem_limit_bytes=61 * 1024 * 1024, collective_id=2, has_side_effects=True
        ),
        cost_estimate=pl.CostEstimate(flops=6 * 10**10, bytes_accessed=6 * 10**7, transcendentals=10**7),
        name="layers_backward",
    )(
        offsets, cot, totals, scales, before, middle, gains, taps, head, wide, spread, weights, final,
        gate, mixed_in, conv, dt_raw, mixed_out, states, normed, gained,
    )


def spread_matrix(inner, heads):
    lane_head = lax.broadcasted_iota(jnp.int32, (2 * LANES, inner), 1) // (inner // heads)
    row_head = lax.broadcasted_iota(jnp.int32, (2 * LANES, inner), 0) % LANES
    return jnp.where(lane_head == row_head, 1.0, 0.0).astype(BF16)


SEQ_MIN = 512


def choose_rows(wanted, valid, begin, end):
    slots = begin + lax.broadcasted_iota(jnp.int32, (wanted.shape[0], end - begin), 1)
    return jnp.where((slots == wanted) & valid, 1.0, 0.0).astype(BF16)


def pick_all(off_ref, arrived, cols):
    first, second = off_ref[0], off_ref[1]
    length = arrived.shape[1]
    for block in range(cols.shape[0]):
        low, high = block * BLK, (block + 1) * BLK
        row = low + lax.broadcasted_iota(jnp.int32, (BLK, 1), 0)
        total = None
        for member, begin, least, most in ((1, first, SEQ_MIN, length), (2, second, BIN - length, BIN - SEQ_MIN)):
            reach = BIN - SEQ_MIN if member == 1 else BIN
            start, end = max(low - most, 0), min(high - least, length)
            if end <= 0 or start >= length or low >= reach:
                continue
            valid = (row >= first) & (row < second) if member == 1 else row >= second
            term = dot_nn(choose_rows(row - begin, valid, start, end), arrived[member, start:end, :])
            total = term if total is None else total + term
        if high <= length:
            own = arrived[0, low:high, :].astype(F32)
            own = jnp.where(row < first, own, 0.0)
            total = own if total is None else total + own
        cols[block] = total.astype(BF16)


def place_all(off_ref, cols, slots):
    first, second = off_ref[0], off_ref[1]
    length = slots.shape[1]
    for chunk in range(length // BLK):
        low, high = chunk * BLK, (chunk + 1) * BLK
        position = low + lax.broadcasted_iota(jnp.int32, (BLK, 1), 0)
        slots[0, low:high, :] = jnp.where(position < first, cols[low:high, :].astype(F32), 0.0).astype(BF16)
        for member, begin, stop, least, most, reach in (
            (1, first, second, SEQ_MIN, length, BIN - SEQ_MIN),
            (2, second, BIN, BIN - length, BIN - SEQ_MIN, BIN),
        ):
            wanted = begin + position
            start, end = least + low, min(most + high, reach)
            choose = choose_rows(wanted, wanted < stop, start, end)
            slots[member, low:high, :] = dot_nn(choose, cols[start:end, :]).astype(BF16)


class LineGather:
    def __init__(self, own, target, sems):
        self.own, self.target, self.sems = own, target, sems
        me = lax.axis_index("dp")
        self.me, self.low, self.high = me, me % 2, me // 2
        self.line = lax.axis_size("dp") // 2
        self.span = own.shape[0]

    def copy(self, kind, place, other, own):
        here = self.target.at[pl.ds((place * 2 + self.low) * self.span, self.span), :]
        arrival = 2 if kind == 2 else 3
        return pltpu.make_async_remote_copy(
            src_ref=self.own if own else here, dst_ref=here,
            send_sem=self.sems.at[kind, place], recv_sem=self.sems.at[arrival + 1, place],
            device_id={"dp": other}, device_id_type=pl.DeviceIdType.MESH,
        )

    def right(self, place, own=False):
        return self.copy(0, place, (self.high + 1) * 2 + self.low, own)

    def left(self, place, own=False):
        return self.copy(1, place, (self.high - 1) * 2 + self.low, own)

    def pair(self, place, own=False):
        return self.copy(2, place, self.high * 2 + 1 - self.low, own)

    def local(self):
        here = self.target.at[pl.ds(self.me * self.span, self.span), :]
        return pltpu.make_async_copy(self.own, here, self.sems.at[5, 0])

    def start_pair(self):
        self.local().start()
        self.pair(self.high, True).start()

    def start_line(self):
        @pl.when(self.high < self.line - 1)
        def _():
            self.right(self.high, True).start()

        @pl.when(self.high > 0)
        def _():
            self.left(self.high, True).start()

    def start(self):
        self.start_line()
        self.start_pair()

    def stage(self, step):
        @pl.when(self.high - step >= 0)
        def _():
            self.right(self.high - step).wait_recv()

            @pl.when(self.high < self.line - 1)
            def _():
                self.right(self.high - step).start()

            self.pair(self.high - step).start()

        @pl.when(self.high + step < self.line)
        def _():
            self.left(self.high + step).wait_recv()

            @pl.when(self.high > 0)
            def _():
                self.left(self.high + step).start()

            self.pair(self.high + step).start()

    def finish(self):
        self.local().wait()

        @pl.loop(0, self.line)
        def _(place):
            self.pair(place).wait_recv()
            self.pair(place).wait_send()

            @pl.when((self.high < self.line - 1) & (place <= self.high))
            def _():
                self.right(place).wait_send()

            @pl.when((self.high > 0) & (place >= self.high))
            def _():
                self.left(place).wait_send()


class Lines:
    def __init__(self, parts):
        self.parts, self.line = parts, parts[0].line

    def each(self, name, *given):
        for part in self.parts:
            getattr(part, name)(*given)

    def start(self):
        self.each("start")

    def start_pair(self):
        self.each("start_pair")

    def start_line(self):
        self.each("start_line")

    def stage(self, step):
        self.each("stage", step)

    def finish(self):
        self.each("finish")


class LineReduce:
    def __init__(self, given, out, pair_buf, arrivals, sems):
        self.given, self.out, self.pair_buf = given, out, pair_buf
        self.arrivals, self.sems = arrivals, sems
        me = lax.axis_index("dp")
        self.low, self.high = me % 2, me // 2
        self.line = lax.axis_size("dp") // 2
        self.span = out.shape[0]

    def chunk(self, place, low):
        return pl.ds((place * 2 + low) * self.span, self.span)

    def pair(self, place):
        return pltpu.make_async_remote_copy(
            src_ref=self.given.at[self.chunk(place, 1 - self.low), :], dst_ref=self.pair_buf.at[place],
            send_sem=self.sems.at[0, place], recv_sem=self.sems.at[1, place],
            device_id={"dp": self.high * 2 + 1 - self.low}, device_id_type=pl.DeviceIdType.MESH,
        )

    def onward(self, place, right):
        slot = place + 1 if right else place
        other = (self.high + 1 if right else self.high - 1) * 2 + self.low
        return pltpu.make_async_remote_copy(
            src_ref=self.pair_buf.at[place], dst_ref=self.arrivals.at[slot],
            send_sem=self.sems.at[2, place], recv_sem=self.sems.at[3 if right else 4, place],
            device_id={"dp": other}, device_id_type=pl.DeviceIdType.MESH,
        )

    def by_distance(self, step, act):
        distance = self.line - 1 - step

        @pl.when(self.high + distance < self.line)
        def _():
            act(self.high + distance, True)

        @pl.when(self.high - distance >= 0)
        def _():
            act(self.high - distance, False)

    def send_pairs(self):
        @pl.loop(0, self.line - 1)
        def _(step):
            self.by_distance(step, lambda place, right: self.pair(place).start())

        self.pair(self.high).start()

    def fold(self, place):
        return self.given[self.chunk(place, self.low), :].astype(F32) + self.pair_buf[place].astype(F32)

    def pass_on(self, place, right):
        self.pair(place).wait_recv()
        upstream = (self.high > 0) if right else (self.high < self.line - 1)
        slot = place + 1 if right else place

        @pl.when(upstream)
        def _():
            self.onward(place, right).wait_recv()
            self.pair_buf[place] = (self.fold(place) + self.arrivals[slot].astype(F32)).astype(BF16)

        @pl.when(jnp.logical_not(upstream))
        def _():
            self.pair_buf[place] = self.fold(place).astype(BF16)

        self.onward(place, right).start()

    def stage(self, step):
        self.by_distance(step, self.pass_on)

    def finish(self):
        here = self.high
        self.pair(here).wait_recv()
        self.out[...] = self.fold(here)

        @pl.when(here > 0)
        def _():
            self.onward(here, True).wait_recv()
            self.out[...] += self.arrivals[here + 1].astype(F32)

        @pl.when(here < self.line - 1)
        def _():
            self.onward(here, False).wait_recv()
            self.out[...] += self.arrivals[here].astype(F32)

        @pl.loop(0, self.line)
        def _(place):
            self.pair(place).wait_send()

            @pl.when(place != here)
            def _():
                self.onward(place, True).wait_send()


def line_scratch(count, span, columns):
    line = count // 2
    return [
        pltpu.VMEM((line, span, columns), BF16),
        pltpu.VMEM((line + 1, span, columns), BF16),
        pltpu.SemaphoreType.DMA((5, line)),
    ]


class MemberGather:
    def __init__(self, target, sems):
        self.target, self.sems = target, sems
        self.me = lax.axis_index("tensor")

    def remote(self, step):
        return pltpu.make_async_remote_copy(
            src_ref=self.target.at[self.me], dst_ref=self.target.at[self.me],
            send_sem=self.sems.at[step, 0], recv_sem=self.sems.at[step, 1],
            device_id={"tensor": (self.me + step) % 4}, device_id_type=pl.DeviceIdType.MESH,
        )

    def start(self):
        for step in range(1, 4):
            self.remote(step).start()

    def wait(self):
        for step in range(1, 4):
            self.remote(step).wait()


def end_kernel(
    off_ref, cols_ref, packs_ref, small_ref, later_ref,
    back_ref, pack_ref, sum_ref, shared_ref, maps_ref,
    slots, pair_buf, arrivals, line_sems, smalls, shared, maps,
    bin_sems, small_sems, shared_sems, maps_sems,
):
    ring = Ring(None)
    ring.greet()
    inner = (pack_ref.shape[1] - 2 * STATE - LANES) // 3
    first_map = 3 * inner
    bins = BinExchange(False, slots, back_ref, bin_sems)
    cut = pack_ref.shape[1] // (2 * LANES) * LANES
    line = Lines(
        [
            LineReduce(
                packs_ref.at[:, part], pack_ref.at[:, part], pair_buf.at[:, :, part], arrivals.at[:, :, part], line_sems.at[at]
            )
            for at, part in enumerate((pl.ds(cut, pack_ref.shape[1] - cut), pl.ds(0, cut)))
        ]
    )
    dp_smalls = LineGather(small_ref, smalls, small_sems)
    shared_smalls = MemberGather(shared, shared_sems)
    shared_maps = [MemberGather(maps.at[at], maps_sems.at[at]) for at in range(LAYERS)]
    maps[1, ring.me] = later_ref[:, first_map : first_map + 2 * STATE].astype(BF16)
    dp_smalls.start()
    line.each("send_pairs")
    shared_maps[1].start()
    place_all(off_ref, cols_ref, slots)
    bins.start()

    @pl.loop(0, line.line - 1)
    def _(step):
        dp_smalls.stage(step + 1)
        line.stage(step)

    dp_smalls.finish()
    small_rows = sum_ref.shape[0]
    sum_ref[...] = smalls[:small_rows, :]

    @pl.loop(1, 2 * line.line)
    def _(at):
        sum_ref[...] += smalls[pl.ds(at * small_rows, small_rows), :]

    shared[ring.me] = sum_ref[...]
    shared_smalls.start()
    line.parts[0].finish()
    maps[0, ring.me] = pack_ref[:, first_map : first_map + 2 * STATE].astype(BF16)
    shared_maps[0].start()
    shared_smalls.wait()
    shared_ref[...] = (shared[0] + shared[1]) + (shared[2] + shared[3])
    line.parts[1].finish()
    for layer in range(LAYERS):
        shared_maps[layer].wait()
        maps_ref[layer] = (maps[layer, 0].astype(F32) + maps[layer, 1].astype(F32)) + (
            maps[layer, 2].astype(F32) + maps[layer, 3].astype(F32)
        )
    bins.wait()


def end_exchange(offsets, grad_columns, packs, small, later_pack, span):
    count = lax.axis_size("dp")
    width, total = packs.shape
    columns = width // 4
    vmem = pl.BlockSpec(memory_space=pltpu.VMEM)
    pack_rows = width // count
    return pl.pallas_call(
        end_kernel,
        in_specs=[pl.BlockSpec(memory_space=pltpu.SMEM)] + [vmem] * 4,
        out_specs=[pl.BlockSpec(memory_space=pltpu.HBM), vmem, vmem, vmem, vmem],
        out_shape=[
            jax.ShapeDtypeStruct((count, 3, span, columns), BF16),
            jax.ShapeDtypeStruct((pack_rows, total), F32),
            jax.ShapeDtypeStruct(small.shape, F32),
            jax.ShapeDtypeStruct(small.shape, F32),
            jax.ShapeDtypeStruct((LAYERS, pack_rows, 2 * STATE), F32),
        ],
        scratch_shapes=[pltpu.VMEM((3, count * span, columns), BF16)]
        + line_scratch(count, pack_rows, total)[:2]
        + [
            pltpu.SemaphoreType.DMA((2, 5, count // 2)),
            pltpu.VMEM((count * small.shape[0], width), F32),
            pltpu.VMEM((4,) + small.shape, F32),
            pltpu.VMEM((LAYERS, 4, pack_rows, 2 * STATE), BF16),
            pltpu.SemaphoreType.DMA((count, 2)),
            pltpu.SemaphoreType.DMA((6, count // 2)),
            pltpu.SemaphoreType.DMA((4, 2)),
            pltpu.SemaphoreType.DMA((LAYERS, 4, 2)),
        ],
        compiler_params=pltpu.CompilerParams(
            vmem_limit_bytes=56 * 1024 * 1024, collective_id=3, has_side_effects=True
        ),
        cost_estimate=pl.CostEstimate(flops=6 * 10**10, bytes_accessed=6 * 10**7, transcendentals=0),
        name="end_exchange",
    )(offsets, grad_columns.reshape(BIN, columns), packs, small, later_pack)


def pad_to(values, rows, columns):
    return jnp.pad(values, ((0, rows - values.shape[0]), (0, columns - values.shape[1])))


def on_device(
    tokens, cotangent, lengths, packing, pre_gain, w_z, w_x, w_bc, w_dt, conv_x, conv_bc, head_params, norm_gain, w_out,
):
    dp_count = lax.axis_size("dp")
    bin_index = lax.axis_index("dp")
    seq_total, pos_here, cols_here = tokens.shape
    inner_part = conv_x.shape[2]
    heads_here = head_params.shape[2]
    dp_rows = w_z.shape[1]
    mixed = inner_part + 2 * STATE
    triples = lengths[packing].reshape(dp_count, 3)
    offsets = jnp.cumsum(triples, axis=1) - triples
    my_offsets = offsets[bin_index]
    bounds = my_offsets[1:3]
    by_bin = (dp_count, 3, pos_here, cols_here)
    given_tokens, given_cot = (array[packing].reshape(by_bin) for array in (tokens, cotangent))

    spread = spread_matrix(inner_part, heads_here)
    last_columns = [jnp.concatenate([w_dt[0], pre_gain.T], axis=1), w_dt[1]]
    packs = []
    for layer in range(LAYERS):
        own = jnp.concatenate(
            [w_out[layer].T, w_z[layer], w_x[layer], w_bc[layer], pad_to(last_columns[layer], dp_rows, LANES)], axis=1
        )
        taps = jnp.concatenate([conv_x[layer], conv_bc[layer]], axis=1).astype(F32)
        head = jnp.stack([head_params[layer, 0], -jnp.exp(head_params[layer, 1])])
        wide = jnp.stack(
            [jnp.repeat(head_params[layer, 2], inner_part // heads_here), norm_gain[layer].astype(F32)]
        )
        packs.append((own, pad_to(taps, 8, mixed), pad_to(head, 8, LANES), pad_to(wide, 8, inner_part)))

    taps_all, head_all, wide_all = (jnp.stack([pack[at] for pack in packs]) for at in (1, 2, 3))
    (
        rows_all, gate, mixed_in, conv, dt_raw, mixed_out, gained_all, states, first_before, middle, totals, scales,
        final_rows, gains, cot_columns, all_weights,
    ) = layers_forward(
        bounds, given_tokens, jnp.stack([pack[0] for pack in packs]), given_cot,
        taps_all, head_all, wide_all, spread,
    )
    grad_columns, small, later_pack, first_packs, activations_back = layers_backward(
        bounds, cot_columns, totals, scales, first_before, middle, gains, taps_all, head_all, wide_all, spread,
        all_weights, final_rows, (gate, mixed_in, conv, dt_raw, mixed_out, states, rows_all, gained_all), pos_here,
    )
    returned, first_pack, sums, shared, maps = end_exchange(
        bounds, grad_columns, first_packs, small.reshape(LAYERS * 8, -1), later_pack, pos_here
    )
    sums, shared = sums.reshape(small.shape), shared.reshape(small.shape)
    grad_convx = sums[:, : CONV + 1, :inner_part]
    grad_convbc = shared[:, : CONV + 1, inner_part:mixed]
    shard_pre = lax.dynamic_slice_in_dim(shared[:, 5], bin_index * dp_rows, dp_rows, 1)
    skips = jnp.sum(sums[:, 6, :inner_part].reshape(LAYERS, heads_here, -1), axis=2)
    grad_head = jnp.stack([sums[:, 7, :heads_here], sums[:, 7, LANES : LANES + heads_here], skips], axis=1)
    grad_norm = sums[:, 6, inner_part : 2 * inner_part]
    own_weights = jnp.stack([first_pack, later_pack])
    grad_bc = maps
    grad_out = jnp.swapaxes(own_weights[:, :, :inner_part], 1, 2)
    grad_z = own_weights[:, :, inner_part : 2 * inner_part]
    grad_x = own_weights[:, :, 2 * inner_part : 3 * inner_part]
    grad_dt = own_weights[:, :, 3 * inner_part + 2 * STATE : 3 * inner_part + 2 * STATE + heads_here]

    rank_of = jnp.zeros_like(packing).at[packing].set(jnp.arange(seq_total, dtype=jnp.int32))

    def in_order(returned):
        return returned.reshape(seq_total, pos_here, cols_here)[rank_of]

    activations = in_order(activations_back)
    input_grad = in_order(returned)
    return (
        activations, input_grad, shard_pre, grad_z, grad_x, grad_bc, grad_dt,
        grad_convx, grad_convbc, grad_head, grad_norm, grad_out,
    )


def solution(mesh):
    placed = (
        P(None, "dp", "tensor"), P(None, "dp", "tensor"), P(), P(), P(None, "dp"),
        P(None, "dp", "tensor"), P(None, "dp", "tensor"), P(None, "dp", None), P(None, "dp", "tensor"),
        P(None, None, "tensor"), P(), P(None, None, "tensor"), P(None, "tensor"), P(None, "tensor", "dp"),
    )
    results = (
        P(None, "dp", "tensor"), P(None, "dp", "tensor"), P(None, "dp"),
        P(None, "dp", "tensor"), P(None, "dp", "tensor"), P(None, "dp", None), P(None, "dp", "tensor"),
        P(None, None, "tensor"), P(), P(None, None, "tensor"), P(None, "tensor"), P(None, "tensor", "dp"),
    )
    return jax.shard_map(on_device, mesh=mesh, in_specs=placed, out_specs=results, check_vma=False)
```

```python
import functools
import jax
import jax.numpy as jnp
from jax import lax
from jax.experimental import pallas as pl
from jax.experimental.pallas import tpu as pltpu
from jax.sharding import PartitionSpec as P

CONV = 4
INNER = 2048
LAYERS = 2
BIN = 2048
eps = 1e-05
STATE = 128
BLK = 256
LANES = 128
LOG2E = 1.4426950408889634
F32 = jnp.float32
BF16 = jnp.bfloat16


def dot_nn(left, right):
    return lax.dot_general(left, right, (((1,), (0,)), ((), ())), preferred_element_type=F32)


def dot_nt(left, right):
    return lax.dot_general(left, right, (((1,), (1,)), ((), ())), preferred_element_type=F32)


def dot_tn(left, right):
    return lax.dot_general(left, right, (((0,), (0,)), ((), ())), preferred_element_type=F32)


def split_two(values):
    high = values.astype(BF16)
    return high, (values - high.astype(F32)).astype(BF16)


def split_three(values):
    high = values.astype(BF16)
    rest = values - high.astype(F32)
    middle = rest.astype(BF16)
    return high, middle, (rest - middle.astype(F32)).astype(BF16)


def spread_heads(values, spread):
    high, low = split_two(values)
    return dot_nn(jnp.concatenate([high, low], axis=1), spread)


def gather_heads(values, spread):
    high, low = split_two(values)
    half = spread[:LANES]
    return dot_nt(high, half) + dot_nt(low, half)


def sigmoid(values):
    return 0.5 * jnp.tanh(0.5 * values) + 0.5


def softplus(values):
    return jnp.maximum(values, 0.0) + jnp.log1p(jnp.exp(-jnp.abs(values)))


def segment_of(rows, first, second):
    return (rows >= first).astype(jnp.int32) + (rows >= second).astype(jnp.int32)


def block_frame(block, first, second):
    row_col = block * BLK + lax.broadcasted_iota(jnp.int32, (BLK, 1), 0)
    row_row = block * BLK + lax.broadcasted_iota(jnp.int32, (1, BLK), 1)
    return row_col, row_row, segment_of(row_col, first, second), segment_of(row_row, first, second)


def decay_parts(block, dt_raw, head, seg_col, first, second):
    shifted = dt_raw + head[0:1]
    steps = softplus(shifted)
    log_decay = steps * head[1:2]
    above = lax.broadcasted_iota(jnp.int32, (BLK, BLK), 0)
    below = lax.broadcasted_iota(jnp.int32, (BLK, BLK), 1)
    lower = jnp.where(above >= below, 1.0, 0.0).astype(BF16)
    parts = dot_nn(lower, jnp.concatenate(split_three(log_decay), axis=1))
    cumulative = parts[:, :LANES] + parts[:, LANES : 2 * LANES] + parts[:, 2 * LANES :]
    cum2 = cumulative * LOG2E
    final2 = cum2[BLK - 1 : BLK]
    last_seg = segment_of(block * BLK + BLK - 1, first, second)
    prior_seg = jnp.where(block == 0, -1, segment_of(block * BLK - 1, first, second))
    entering = jnp.where(seg_col == prior_seg, jnp.exp2(cum2), 0.0)
    tail = jnp.where(seg_col == last_seg, jnp.exp2(final2 - cum2), 0.0)
    retained = jnp.where(last_seg == prior_seg, jnp.exp2(final2), 0.0)
    return shifted, steps, cum2, entering, tail, retained


def head_half(pair, head):
    lanes = lax.broadcasted_iota(jnp.int32, pair.shape, 1)
    keep = (lanes < LANES // 2) if head % 2 == 0 else (lanes >= LANES // 2)
    return jnp.where(keep, pair, jnp.zeros_like(pair))


SHARE = BLK // 4
AG_OWN, AG_ACROSS, AG_PASS, RS_PAIR, RS_ACROSS, SM_PAIR, SM_ACROSS = range(7)


class Ring:
    def __init__(self, sems):
        me = lax.axis_index("tensor")
        self.low, self.high = me % 2, me // 2
        self.me = me
        self.sibling = self.high * 2 + (1 - self.low)
        self.across = (1 - self.high) * 2 + self.low
        self.beyond = (1 - self.high) * 2 + (1 - self.low)
        self.sems = sems

    def greet(self):
        barrier = pltpu.get_barrier_semaphore()
        for other in (self.sibling, self.across, self.beyond):
            pl.semaphore_signal(barrier, inc=1, device_id={"tensor": other}, device_id_type=pl.DeviceIdType.MESH)
        pl.semaphore_wait(barrier, greet_dp(barrier) + 3)

    def slot(self, owner):
        return ((self.low + owner % 2) % 2) * 2 + (self.high + owner // 2) % 2

    def copy(self, kind, block, source, target, other):
        return pltpu.make_async_remote_copy(
            src_ref=source, dst_ref=target,
            send_sem=self.sems.at[kind, block, 0], recv_sem=self.sems.at[kind, block, 1],
            device_id={"tensor": other}, device_id_type=pl.DeviceIdType.MESH,
        )


def greet_dp(barrier):
    count, me = lax.axis_size("dp"), lax.axis_index("dp")

    @pl.loop(1, count)
    def _(step):
        pl.semaphore_signal(
            barrier, inc=1, device_id={"dp": (me + step) % count}, device_id_type=pl.DeviceIdType.MESH
        )

    return count - 1


class BinExchange:
    def __init__(self, to_bins, source, target, sems):
        self.to_bins, self.source, self.target, self.sems = to_bins, source, target, sems
        self.count, self.me = lax.axis_size("dp"), lax.axis_index("dp")
        self.span = source.shape[2] if to_bins else target.shape[2]

    def pieces(self, other):
        if self.to_bins:
            return self.source.at[other], self.target.at[:, pl.ds(self.me * self.span, self.span), :]
        return self.source.at[:, pl.ds(other * self.span, self.span), :], self.target.at[self.me]

    def remote(self, step, other):
        source, target = self.pieces(other)
        return pltpu.make_async_remote_copy(
            src_ref=source, dst_ref=target, send_sem=self.sems.at[step, 0], recv_sem=self.sems.at[step, 1],
            device_id={"dp": other}, device_id_type=pl.DeviceIdType.MESH,
        )

    def local(self):
        source, target = self.pieces(self.me)
        return pltpu.make_async_copy(source, target, self.sems.at[0, 0])

    def start(self):
        self.local().start()
        self.start_steps(1, self.count)

    def wait(self):
        self.local().wait()
        self.wait_steps(1, self.count)

    def start_steps(self, begin, end):
        @pl.loop(begin, end)
        def _(step):
            self.remote(step, (self.me + step) % self.count).start()

    def wait_steps(self, begin, end):
        @pl.loop(begin, end)
        def _(step):
            self.remote(step, (self.me + step) % self.count).wait()


class RowExchange:
    def __init__(self, to_rows, source, target, sems):
        self.to_rows, self.source, self.target, self.sems = to_rows, source, target, sems
        self.me = lax.axis_index("tensor")
        self.columns = source.shape[2] if to_rows else target.shape[2]

    def pieces(self, other):
        if self.to_rows:
            return (
                self.source.at[:, pl.ds(other * SHARE, SHARE), :],
                self.target.at[:, :, pl.ds(pl.multiple_of(self.me * self.columns, LANES), self.columns)],
            )
        return (
            self.source.at[:, :, pl.ds(pl.multiple_of(other * self.columns, LANES), self.columns)],
            self.target.at[:, pl.ds(self.me * SHARE, SHARE), :],
        )

    def remote(self, step):
        other = (self.me + step) % 4
        source, target = self.pieces(other)
        return pltpu.make_async_remote_copy(
            src_ref=source, dst_ref=target, send_sem=self.sems.at[step, 0], recv_sem=self.sems.at[step, 1],
            device_id={"tensor": other}, device_id_type=pl.DeviceIdType.MESH,
        )

    def local(self):
        source, target = self.pieces(self.me)
        return pltpu.make_async_copy(source, target, self.sems.at[0, 0])

    def start(self):
        self.local().start()
        for step in range(1, 4):
            self.remote(step).start()

    def wait(self):
        self.local().wait()
        for step in range(1, 4):
            self.remote(step).wait()


def row_place(rows, member):
    return rows.at[:, pl.ds(member * SHARE, SHARE), :]


def column_place(rows, member):
    columns = rows.shape[2] // 4
    return rows.at[:, :, pl.ds(pl.multiple_of(member * columns, LANES), columns)]


def gather_copy(ring, kind, block, own, rows, place):
    if kind == AG_PASS:
        passed = place(rows, ring.across).at[block]
        return ring.copy(kind, block, passed, passed, ring.sibling)
    other = ring.sibling if kind == AG_OWN else ring.across
    target = place(rows, ring.me).at[block]
    return ring.copy(kind, block, target if own is None else own.at[block], target, other)


def pair_copy(ring, block, parts, from_pair):
    return ring.copy(RS_PAIR, block, parts.at[block, pl.ds(2 * SHARE, 2 * SHARE), :], from_pair.at[block], ring.sibling)


def across_copy(ring, block, parts, from_across):
    return ring.copy(RS_ACROSS, block, parts.at[block, pl.ds(SHARE, SHARE), :], from_across.at[block], ring.across)


def store_parts(ring, block, part, parts):
    for owner in range(4):
        parts[block, pl.ds(ring.slot(owner) * SHARE, SHARE), :] = part[owner * SHARE : (owner + 1) * SHARE].astype(BF16)


def add_pair(block, parts, from_pair):
    parts[block, pl.ds(SHARE, SHARE), :] = (
        parts[block, pl.ds(SHARE, SHARE), :].astype(F32) + from_pair[block, pl.ds(SHARE, SHARE), :].astype(F32)
    ).astype(BF16)


def add_all(block, parts, from_pair, from_across):
    return (
        parts[block, pl.ds(0, SHARE), :].astype(F32)
        + from_pair[block, pl.ds(0, SHARE), :].astype(F32)
        + from_across[block].astype(F32)
    )


def own_column(line, first_lane):
    lanes = lax.broadcasted_iota(jnp.int32, (SHARE, line.shape[1]), 1)
    rows = lax.broadcasted_iota(jnp.int32, (SHARE, line.shape[1]), 0)
    return jnp.sum(jnp.where(lanes == rows + first_lane, line, 0.0), axis=1, keepdims=True)


LAG = 4
DEFER = 2
PASS_AHEAD = 2


def forward_kernel(
    off_ref, tok_ref, packs_ref, cot_ref, taps_ref, head_ref, wide_ref, spread_ref,
    rows_ref, z_ref, in_ref, pre_ref, dt_ref, y_ref, gg_ref, st_ref,
    before_ref, middle_ref, tot_ref, scale_ref, final_ref, gains_ref, cot_cols_ref, weights_ref,
    state, padded, rows, parts, from_pair, from_across, sq_own, sq_pair, sq_sums, sq_across,
    weights, arrived, cols, cot_arrived, middle, kept,
    before_buf, middle_buf, tot_buf, scale_buf, final_buf, cot_cols, keep_sems,
    sems, copy_sems, line_sems, bin_sems, cot_sems,
):
    step = pl.program_id(0)
    inner = y_ref.shape[1]
    mixed = in_ref.shape[1]
    first, second = off_ref[0], off_ref[1]
    blocks = rows.shape[0]
    layer, block = step // blocks, step % blocks
    rings = (Ring(sems.at[0]), Ring(sems.at[1]))
    ring = rings[0]
    total_columns = weights.shape[2]

    def line_of(at_layer, begin, end, slot):
        part = pl.ds(begin, end - begin)
        return LineGather(packs_ref.at[at_layer, :, part], weights.at[at_layer, :, part], line_sems.at[slot])

    cut = inner + (total_columns - inner) // (2 * LANES) * LANES
    in_lines = [Lines([line_of(at, inner, cut, 3 * at), line_of(at, cut, total_columns, 3 * at + 1)]) for at in range(LAYERS)]
    out_lines = [line_of(at, 0, inner, 3 * at + 2) for at in range(LAYERS)]
    in_line, line = in_lines
    bins = BinExchange(True, tok_ref, arrived, bin_sems)
    cot_bins = BinExchange(True, cot_ref, cot_arrived, cot_sems)
    four = line.line == 4

    def gather(at_layer, kind, at):
        own, place = ((cols, column_place), (None, row_place))[at_layer]
        return gather_copy(rings[at_layer], kind, at, own, rows, place)

    def sq_pair_copy(at_ring, slot):
        return at_ring.copy(SM_PAIR, slot % blocks, sq_own.at[slot], sq_pair.at[slot], at_ring.sibling)

    def sq_across_copy(at_ring, slot):
        return at_ring.copy(SM_ACROSS, slot % blocks, sq_sums.at[slot], sq_across.at[slot], at_ring.across)

    def own_copy():
        return pltpu.make_async_copy(cols, column_place(rows, ring.me), copy_sems.at[LAYERS])

    def keep_weights(at):
        return pltpu.make_async_copy(weights.at[at], weights_ref.at[at], copy_sems.at[at])

    def keep_copies():
        kept_pairs = (
            (before_buf, before_ref), (middle_buf, middle_ref), (tot_buf, tot_ref),
            (scale_buf, scale_ref), (final_buf, final_ref), (cot_cols, cot_cols_ref),
        )
        return [pltpu.make_async_copy(a, b, keep_sems.at[at]) for at, (a, b) in enumerate(kept_pairs)]

    def clear():
        state[...] = jnp.zeros_like(state)
        padded[pl.ds(0, 8), :] = jnp.zeros((8, mixed), F32)

    @pl.when(step == 0)
    def _():
        ring.greet()
        half = bins.count // 2
        bins.local().start()
        bins.start_steps(half - 1, half + 2)
        in_line.start_pair()
        for part in (out_lines[0], line, out_lines[1]):
            part.start_pair()
        clear()
        bins.wait_steps(half - 1, half + 2)
        in_line.start_line()
        bins.start_steps(1, half - 1)
        bins.start_steps(half + 2, bins.count)
        bins.local().wait()
        bins.wait_steps(1, half - 1)
        bins.wait_steps(half + 2, bins.count)
        pick_all(off_ref, arrived, cols)
        own_copy().start()

        @pl.loop(0, blocks)
        def _(at):
            gather(0, AG_ACROSS, at).start()
            gather(0, AG_OWN, at).start()

        own_copy().wait()

        def pass_rows(begin, end):
            @pl.loop(begin, end)
            def _(at):
                gather(0, AG_ACROSS, at).wait_recv()
                gather(0, AG_PASS, at).start()

        if four:
            in_line.stage(1)
            pass_rows(0, blocks // 2)
            in_line.stage(2)
            pass_rows(blocks // 2, blocks)
            in_line.stage(3)
            for part in (out_lines[0], line, out_lines[1]):
                part.start_line()
        else:
            pass_rows(0, blocks)

            @pl.loop(1, line.line)
            def _(stage):
                in_line.stage(stage)

        in_line.finish()
        last_columns = weights[0, :, total_columns - LANES :].astype(F32)
        gains_ref[...] = jnp.transpose(last_columns)[8:16]
        if not four:
            for part in (out_lines[0], line, out_lines[1]):
                part.start_line()

    @pl.when(step == blocks)
    def _():
        clear()

    for at_layer in range(LAYERS):

        @pl.when(layer == at_layer)
        def _(at_layer=at_layer):
            gather(at_layer, AG_OWN, block).wait_recv()
            gather(at_layer, AG_PASS, block).wait_recv()

    gains = gains_ref[...]
    raw = rows[block].astype(F32)
    mean = jnp.sum(raw * raw, axis=1, keepdims=True) / raw.shape[1]
    normed = raw * lax.rsqrt(mean + eps) * gains[0:1]
    here = jnp.where(layer == 0, normed, raw).astype(BF16)
    rows_ref[...] = here
    row_col, row_row, seg_col, seg_row = block_frame(block, first, second)
    seg_start = jnp.where(seg_col == 0, 0, jnp.where(seg_col == 1, first, second))
    within = row_col - seg_start
    product = dot_nn(here, weights[layer, :, inner:])
    gate = product[:, :inner]
    mixed_in = product[:, inner : inner + mixed]
    dt_raw = product[:, inner + mixed :]
    z_ref[...] = gate.astype(BF16)
    in_ref[...] = mixed_in.astype(BF16)
    dt_ref[...] = dt_raw
    padded[pl.ds(8, BLK), :] = mixed_in
    taps = taps_ref[layer]
    conv = taps[CONV : CONV + 1] + taps[CONV - 1 : CONV] * mixed_in
    for delay in range(1, CONV):
        shifted_in = padded[pl.ds(8 - delay, BLK), :]
        conv = conv + taps[CONV - 1 - delay : CONV - delay] * jnp.where(within >= delay, shifted_in, 0.0)
    padded[pl.ds(0, 8), :] = padded[pl.ds(BLK, 8), :]
    pre_ref[...] = conv
    mixed_low = (conv * sigmoid(conv)).astype(BF16)
    x_low = mixed_low[:, :inner]
    b_low = mixed_low[:, inner : inner + STATE]
    c_low = mixed_low[:, inner + STATE :]
    head = head_ref[layer]
    spread = spread_ref[...]
    shifted, steps, cum2, entering, tail, retained = decay_parts(block, dt_raw, head, seg_col, first, second)
    cum_row = jnp.transpose(cum2)
    x_in = x_low.astype(F32)
    x_steps = spread_heads(steps, spread) * x_in
    x_steps_low = x_steps.astype(BF16)
    allowed = (seg_col == seg_row) & (row_col >= row_row)
    scores = jnp.where(allowed, dot_nt(c_low, b_low), 0.0)
    old_state = state[...]
    st_ref[0] = old_state
    carried = spread_heads(entering, spread) * dot_nn(c_low, old_state.astype(BF16))
    wide = wide_ref[layer]
    pieces = []
    for pair in range(inner // LANES):
        columns = slice(pair * LANES, (pair + 1) * LANES)
        total = None
        for head_index in (2 * pair, 2 * pair + 1):
            gaps = cum2[:, head_index : head_index + 1] - cum_row[head_index : head_index + 1, :]
            coupling = (jnp.exp2(jnp.minimum(gaps, 0.0)) * scores).astype(BF16)
            term = dot_nn(coupling, head_half(x_steps_low[:, columns], head_index))
            total = term if total is None else total + term
        pieces.append(total)
    mixed_out = jnp.concatenate(pieces, axis=1) + carried + wide[0:1] * x_in
    tailed = (spread_heads(tail, spread) * x_steps).astype(BF16)
    keep = spread_heads(jnp.broadcast_to(retained, (8, LANES)), spread)[0:1]
    state[...] = old_state * keep + dot_tn(b_low, tailed)
    y_ref[...] = mixed_out
    gated = mixed_out * (gate * sigmoid(gate))
    gained = (gated * wide[1:2]).astype(BF16)
    gg_ref[...] = gained
    now = Ring(sems.at[layer])
    high, low = split_two(gated * gated)
    ones = jnp.ones((8, inner), BF16)
    sq_own[step] = dot_nt(ones, high) + dot_nt(ones, low)
    sq_pair_copy(now, step).start()

    def free_parts(at_layer, at):
        if at_layer == 0:
            gather(0, AG_PASS, at).wait_send()
        else:
            pair_copy(ring, at, parts, from_pair).wait_send()
            across_copy(ring, at, parts, from_across).wait_send()

    def send_parts(at_ring, at, values, out_weights):
        store_parts(at_ring, at, dot_nt(values, out_weights), parts)
        pair_copy(at_ring, at, parts, from_pair).start()

    @pl.when(block < DEFER)
    def _():
        kept[block] = gained

    for at_layer in range(LAYERS):
        first_step = at_layer * blocks
        if four:
            for stage in (1, 2, 3):
                when = min(stage - 1, DEFER) if at_layer == 0 else 2 * stage + 2

                @pl.when(step == when)
                def _(at_layer=at_layer, stage=stage):
                    out_lines[at_layer].stage(stage)

        @pl.when(step == first_step + DEFER)
        def _(at_layer=at_layer):
            if not four:

                @pl.loop(1, line.line)
                def _(stage):
                    out_lines[at_layer].stage(stage)

            out_lines[at_layer].finish()
            keep_weights(at_layer).start()

            @pl.loop(0, DEFER)
            def _(at):
                free_parts(at_layer, at)
                send_parts(rings[at_layer], at, kept[at], weights[at_layer, :, :inner])

    @pl.when(block >= DEFER)
    def _():
        for at_layer in range(LAYERS):

            @pl.when(layer == at_layer)
            def _(at_layer=at_layer):
                free_parts(at_layer, block)

        send_parts(now, block, gained, weights[layer, :, :inner])

    def second_stage(slot):
        at_layer, at = slot // blocks, slot % blocks
        at_ring = Ring(sems.at[at_layer])
        pair_copy(at_ring, at, parts, from_pair).wait_recv()
        sq_pair_copy(at_ring, slot).wait_recv()

        add_pair(at, parts, from_pair)
        sq_sums[slot] = sq_own[slot] + sq_pair[slot]
        across_copy(at_ring, at, parts, from_across).start()
        sq_across_copy(at_ring, slot).start()

    def last_stage(at_layer, at):
        at_ring, slot = rings[at_layer], at_layer * blocks + at
        across_copy(at_ring, at, parts, from_across).wait_recv()
        sq_across_copy(at_ring, slot).wait_recv()
        total = add_all(at, parts, from_pair, from_across)
        squares = own_column((sq_sums[slot] + sq_across[slot])[0:1], ring.me * SHARE)
        scale = lax.rsqrt(squares / INNER + eps)
        here = pl.ds(at * SHARE, SHARE)
        mine = pl.ds(ring.me * SHARE, SHARE)
        tot_buf[slot] = total.astype(BF16)
        scale_buf[slot] = scale
        if at_layer == 0:
            before = rows[at, mine, :]
            before_buf[at] = before
            hidden = before.astype(F32) + total * scale
            middle[at] = hidden
            middle_buf[at] = hidden.astype(BF16)
            mean = jnp.sum(hidden * hidden, axis=1, keepdims=True) / hidden.shape[1]
            later = (hidden * lax.rsqrt(mean + eps) * gains[1:2]).astype(BF16)
            rows[at, mine, :] = later
            gather(1, AG_ACROSS, at).start()
            gather(1, AG_OWN, at).start()
        else:
            final_buf[at] = (middle[at] + total * scale).astype(BF16)

    @pl.when((step >= LAG) & (step < blocks + LAG))
    def _():
        last_stage(0, step - LAG)

    @pl.when(step >= blocks + LAG)
    def _():
        last_stage(1, step - LAG - blocks)

    if four:
        for stage, when in ((1, 1), (2, 3), (3, 5)):

            @pl.when(step == when)
            def _(stage=stage):
                line.stage(stage)

    @pl.when(step == blocks)
    def _():
        cot_bins.start()

    @pl.when((step >= blocks - PASS_AHEAD) & (step < 2 * blocks - PASS_AHEAD))
    def _():
        gather(1, AG_ACROSS, (step + PASS_AHEAD) % blocks).wait_recv()
        gather(1, AG_PASS, (step + PASS_AHEAD) % blocks).start()

    @pl.when((step % blocks == DEFER + 1) & (step > 0))
    def _():
        @pl.loop(0, DEFER)
        def _(at):
            second_stage(layer * blocks + at)

    @pl.when((step > 0) & ((step - 1 + blocks) % blocks >= DEFER))
    def _():
        second_stage(step - 1)

    @pl.when(step == blocks - 1)
    def _():
        if not four:

            @pl.loop(1, line.line)
            def _(stage):
                line.stage(stage)

        line.finish()

    @pl.when(step == 2 * blocks - 1)
    def _():
        second_stage(step)
        cot_bins.wait()
        pick_all(off_ref, cot_arrived, cot_cols)

        before_keep, middle_keep, *late_keep, cot_keep = keep_copies()
        for copy in (before_keep, middle_keep, cot_keep):
            copy.start()

        @pl.loop(blocks - LAG, blocks)
        def _(at):
            last_stage(1, at)

        for copy in late_keep:
            copy.start()

        @pl.loop(0, blocks)
        def _(at):
            gather(0, AG_OWN, at).wait_send()
            gather(0, AG_ACROSS, at).wait_send()
            for kind in (AG_OWN, AG_ACROSS, AG_PASS):
                gather(1, kind, at).wait_send()
            pair_copy(rings[1], at, parts, from_pair).wait_send()
            across_copy(rings[1], at, parts, from_across).wait_send()
            for at_layer in range(LAYERS):
                sq_pair_copy(rings[at_layer], at_layer * blocks + at).wait_send()
                sq_across_copy(rings[at_layer], at_layer * blocks + at).wait_send()

        for at in range(LAYERS):
            keep_weights(at).wait()
        for copy in (before_keep, middle_keep, *late_keep, cot_keep):
            copy.wait()


def own_line(column):
    lanes = lax.broadcasted_iota(jnp.int32, (SHARE, LANES), 1)
    rows = lax.broadcasted_iota(jnp.int32, (SHARE, LANES), 0)
    return jnp.sum(jnp.where(lanes == rows, column, 0.0), axis=0, keepdims=True)


TILE_KINDS = (5, 6, 7)
AHEAD = 2
QUEUED = 4
BACK_LAG = 4


def backward_kernel(
    off_ref, cot_in, tot_in, scale_in, before_ref, middle_ref, gains_ref, taps_ref, head_ref, wide_ref, spread_ref,
    weights_ref, final_ref,
    z_ref, in_ref, pre_ref, dt_ref, y_ref, st_ref, normed_ref, gg_ref,
    gcols_out, small_ref, pack_ref, packs_ref, back_ref,
    dstate, padded, rows, parts, from_pair, from_across, tiles, held, running, weights, acc_out, acc_in,
    packs, pair_buf, arrivals, cols, slots,
    cot_ref, tot_ref, scale_ref, ginput, gcols_ref, sems, copy_sems, line_sems, row_sems, bin_sems, load_sems, col_sems,
):
    step = pl.program_id(0)
    inner = y_ref.shape[1]
    mixed = in_ref.shape[1]
    first, second = off_ref[0], off_ref[1]
    blocks = rows.shape[0]
    phase, block = step // blocks, blocks - 1 - step % blocks
    layer = LAYERS - 1 - phase
    rings = (Ring(sems.at[0]), Ring(sems.at[1]))
    ring = rings[0]
    line = LineReduce(packs, pack_ref, pair_buf, arrivals, line_sems)
    four = line.line == 4
    final_rows = RowExchange(False, final_ref, cols.reshape(blocks, BLK, cols.shape[1]), row_sems)
    bins = BinExchange(False, slots, back_ref, bin_sems)
    mine = pl.ds(ring.me * SHARE, SHARE)

    def gather(at_phase, kind, at):
        own, place = ((cot_ref, column_place), (None, row_place))[at_phase]
        return gather_copy(rings[at_phase], kind, at, own, rows, place)

    def tile_copies(at_phase, at):
        at_ring = rings[at_phase]
        here = tiles.at[at_phase, ring.me, at]
        return [
            at_ring.copy(kind, at, here, here, other)
            for kind, other in zip(TILE_KINDS, (ring.sibling, ring.across, ring.beyond))
        ]

    def make_tile(at_phase, at, grad_low):
        slot = (LAYERS - 1 - at_phase) * blocks + at
        scale = scale_ref[slot]
        weighted = jnp.sum(grad_low.astype(F32) * tot_ref[slot].astype(F32), axis=1, keepdims=True)
        twice = -(scale * scale * scale) / INNER * weighted
        row = lax.broadcasted_iota(jnp.int32, (8, LANES), 0)
        tiles[at_phase, ring.me, at] = jnp.where(row == 0, own_line(twice), own_line(scale))
        for copy in tile_copies(at_phase, at):
            copy.start()

    def prepare(at):
        gather(0, AG_OWN, at).wait_recv()
        gather(0, AG_PASS, at).wait_recv()
        make_tile(0, at, rows[at, mine, :])

    def pass_rows(at_phase, at):
        gather(at_phase, AG_ACROSS, at).wait_recv()
        gather(at_phase, AG_PASS, at).start()

    def load_inputs():
        pairs = ((cot_in, cot_ref), (tot_in, tot_ref), (scale_in, scale_ref))
        return [pltpu.make_async_copy(a, b, load_sems.at[at]) for at, (a, b) in enumerate(pairs)]

    def column_copy(at, hop):
        other = (ring.me + hop) % 4
        columns = gcols_ref.shape[2]
        source = ginput.at[at, :, pl.ds(pl.multiple_of(other * columns, LANES), columns)]
        target = gcols_ref.at[at, mine, :]
        if hop == 0:
            return pltpu.make_async_copy(source, target, col_sems.at[at, 0, 0])
        return pltpu.make_async_remote_copy(
            src_ref=source, dst_ref=target, send_sem=col_sems.at[at, hop, 0], recv_sem=col_sems.at[at, hop, 1],
            device_id={"tensor": other}, device_id_type=pl.DeviceIdType.MESH,
        )

    def send_rows(at):
        gather(0, AG_ACROSS, at).start()
        gather(0, AG_OWN, at).start()

    def own_copy():
        return pltpu.make_async_copy(cot_ref, column_place(rows, ring.me), copy_sems.at[0])

    def load_weights(at_layer):
        return pltpu.make_async_copy(weights_ref.at[at_layer], weights, copy_sems.at[1])

    def load_held(at_phase):
        return pltpu.make_async_copy((middle_ref, before_ref)[at_phase], held, copy_sems.at[3 + at_phase])

    def store_packs():
        return pltpu.make_async_copy(packs, packs_ref, copy_sems.at[2])

    def clear():
        dstate[...] = jnp.zeros_like(dstate)
        padded[pl.ds(BLK, 8), :] = jnp.zeros((8, mixed), F32)
        acc_out[...] = jnp.zeros_like(acc_out)
        acc_in[...] = jnp.zeros_like(acc_in)

    @pl.when(step == 0)
    def _():
        cot_load, *loads = load_inputs()
        for copy in (cot_load, *loads):
            copy.start()
        load_weights(LAYERS - 1).start()
        load_held(0).start()
        cot_load.wait()
        own_copy().start()
        ring.greet()

        send_rows(blocks - 1)
        clear()
        small_ref[...] = jnp.zeros_like(small_ref)
        own_copy().wait()
        pass_rows(0, blocks - 1)
        for at in range(1, QUEUED):
            send_rows(blocks - 1 - at)
        for copy in loads:
            copy.wait()
        prepare(blocks - 1)
        for at in range(1, AHEAD + 1):
            pass_rows(0, blocks - 1 - at)
        for at in range(1, AHEAD):
            prepare(blocks - 1 - at)
        load_weights(LAYERS - 1).wait()

    @pl.when(step == blocks)
    def _():
        load_weights(0).start()
        clear()
        load_weights(0).wait()

    @pl.when(phase > 0)
    def _():
        gather(1, AG_OWN, block).wait_recv()
        gather(1, AG_PASS, block).wait_recv()

    for at_phase in range(LAYERS):

        @pl.when(phase == at_phase)
        def _(at_phase=at_phase):
            for copy in tile_copies(at_phase, block):
                copy.wait_recv()

    here = rows[block]
    tile_rows = [tiles[phase, owner, block] for owner in range(4)]
    twice_here = jnp.concatenate([own_column(tile[0:1], 0) for tile in tile_rows], axis=0)
    scale_here = jnp.concatenate([own_column(tile[1:2], 0) for tile in tile_rows], axis=0)
    row_col, row_row, seg_col, seg_row = block_frame(block, first, second)
    seg_end = jnp.where(seg_col == 0, first, jnp.where(seg_col == 1, second, BIN))
    remaining = seg_end - row_col
    head = head_ref[layer]
    wide = wide_ref[layer]
    spread = spread_ref[...]
    skip, gain = wide[0:1], wide[1:2]
    gate = z_ref[...].astype(F32)
    mixed_out = y_ref[...]
    conv = pre_ref[...]
    gate_sig = sigmoid(gate)
    gate_silu = gate * gate_sig
    gated = mixed_out * gate_silu
    grad_scaled = dot_nn(here, weights[:, :inner]) * scale_here
    grad_gated = grad_scaled * gain + twice_here * gated
    grad_out = grad_gated * gate_silu
    grad_gate = grad_gated * mixed_out * (gate_sig * (1.0 + gate * (1.0 - gate_sig)))
    grad_out_low = grad_out.astype(BF16)

    conv_sig = sigmoid(conv)
    mixed_low = (conv * conv_sig).astype(BF16)
    x_low = mixed_low[:, :inner]
    b_low = mixed_low[:, inner : inner + STATE]
    c_low = mixed_low[:, inner + STATE :]
    x_in = x_low.astype(F32)
    shifted, steps, cum2, entering, tail, retained = decay_parts(block, dt_ref[...], head, seg_col, first, second)
    cum_row = jnp.transpose(cum2)
    steps_wide = spread_heads(steps, spread)
    x_steps_low = (steps_wide * x_in).astype(BF16)
    x_steps = x_steps_low.astype(F32)

    allowed = (seg_col == seg_row) & (row_col <= row_row)
    scores = jnp.where(allowed, dot_nt(b_low, c_low), 0.0)
    grad_scores = jnp.zeros((BLK, BLK), F32)
    pieces = []
    for pair in range(inner // LANES):
        columns = slice(pair * LANES, (pair + 1) * LANES)
        total = None
        for head_index in (2 * pair, 2 * pair + 1):
            gaps = cum_row[head_index : head_index + 1, :] - cum2[:, head_index : head_index + 1]
            decays = jnp.exp2(jnp.minimum(gaps, 0.0))
            coupling = (decays * scores).astype(BF16)
            term = dot_nn(coupling, head_half(grad_out_low[:, columns], head_index))
            total = term if total is None else total + term
            grad_scores = grad_scores + decays * dot_nt(
                head_half(x_steps_low[:, columns], head_index), grad_out_low[:, columns]
            )
        pieces.append(total)
    grad_scores_low = jnp.where(allowed, grad_scores, 0.0).astype(BF16)
    old_dstate = dstate[...]
    old_dstate_low = old_dstate.astype(BF16)
    old_state = st_ref[0]
    tail_wide = spread_heads(tail, spread)
    from_state = tail_wide * dot_nn(b_low, old_dstate_low)
    grad_unit = jnp.concatenate(pieces, axis=1) + from_state
    entered = (spread_heads(entering, spread) * grad_out).astype(BF16)
    tailed = (tail_wide * x_steps).astype(BF16)
    grad_c = dot_tn(grad_scores_low, b_low) + dot_nt(entered, old_state.astype(BF16))
    grad_b = dot_nn(grad_scores_low, c_low) + dot_nt(tailed, old_dstate_low)
    keep = spread_heads(jnp.broadcast_to(retained, (8, LANES)), spread)[0:1]
    dstate[...] = old_dstate * keep + dot_tn(c_low, entered)

    balance = gather_heads(grad_out_low.astype(F32) * (mixed_out - skip * x_in) - x_steps * grad_unit, spread)
    direct = gather_heads(x_in * grad_unit, spread)
    final_wide = jnp.sum(x_steps * from_state, axis=0, keepdims=True) + keep * jnp.sum(
        old_dstate * old_state, axis=0, keepdims=True
    )
    final = gather_heads(jnp.broadcast_to(final_wide, (8, inner)), spread)[0:1]
    above = lax.broadcasted_iota(jnp.int32, (BLK, BLK), 0)
    below = lax.broadcasted_iota(jnp.int32, (BLK, BLK), 1)
    upper = jnp.where(above <= below, 1.0, 0.0).astype(BF16)
    thirds = dot_nn(upper, jnp.concatenate(split_three(balance), axis=1))
    grad_log = thirds[:, :LANES] + thirds[:, LANES : 2 * LANES] + thirds[:, 2 * LANES :] + final
    grad_steps = direct + grad_log * head[1:2]
    grad_dt = grad_steps * sigmoid(shifted)
    small_ref[layer, 7:8, :LANES] += jnp.sum(grad_dt, axis=0, keepdims=True)
    small_ref[layer, 7:8, LANES : 2 * LANES] += jnp.sum(grad_log * steps, axis=0, keepdims=True) * head[1:2]
    small_ref[layer, 6:7, :inner] += jnp.sum(grad_out * x_in, axis=0, keepdims=True)
    small_ref[layer, 6:7, inner : 2 * inner] += jnp.sum(grad_scaled * gated, axis=0, keepdims=True)

    grad_x = steps_wide * grad_unit + skip * grad_out
    grad_conv = jnp.concatenate([grad_x, grad_b, grad_c], axis=1) * (
        conv_sig * (1.0 + conv * (1.0 - conv_sig))
    )
    padded[pl.ds(0, BLK), :] = grad_conv
    mixed_in = in_ref[...].astype(F32)
    taps = taps_ref[layer]
    grad_in = taps[CONV - 1 : CONV] * grad_conv
    small_ref[layer, CONV : CONV + 1, :mixed] += jnp.sum(grad_conv, axis=0, keepdims=True)
    small_ref[layer, CONV - 1 : CONV, :mixed] += jnp.sum(mixed_in * grad_conv, axis=0, keepdims=True)
    for delay in range(1, CONV):
        later = jnp.where(remaining > delay, padded[pl.ds(delay, BLK), :], 0.0)
        grad_in = grad_in + taps[CONV - 1 - delay : CONV - delay] * later
        small_ref[layer, CONV - 1 - delay : CONV - delay, :mixed] += jnp.sum(mixed_in * later, axis=0, keepdims=True)
    padded[pl.ds(BLK, 8), :] = padded[pl.ds(0, 8), :]
    gproj = jnp.concatenate([grad_gate.astype(BF16), grad_in.astype(BF16), grad_dt.astype(BF16)], axis=1)
    acc_out[...] += dot_tn(here, (gg_ref[...].astype(F32) * scale_here).astype(BF16))
    acc_in[...] += dot_tn(normed_ref[...], gproj)
    part = dot_nt(gproj, weights[:, inner:])

    @pl.when(phase > 0)
    def _():
        pair_copy(ring, block, parts, from_pair).wait_send()
        across_copy(ring, block, parts, from_across).wait_send()

    @pl.when(phase == 0)
    def _():
        gather(0, AG_PASS, block).wait_send()

    now = Ring(sems.at[phase])
    store_parts(now, block, part, parts)
    pair_copy(now, block, parts, from_pair).start()

    def second_stage(turn):
        at_phase, at = turn // blocks, blocks - 1 - turn % blocks
        at_ring = Ring(sems.at[at_phase])
        pair_copy(at_ring, at, parts, from_pair).wait_recv()

        add_pair(at, parts, from_pair)
        across_copy(at_ring, at, parts, from_across).start()

    def last_stage(at_phase, at):
        at_layer = LAYERS - 1 - at_phase
        across_copy(rings[at_phase], at, parts, from_across).wait_recv()
        grad_normed = add_all(at, parts, from_pair, from_across)
        hidden = held[at].astype(F32)
        width = hidden.shape[1]
        root = lax.rsqrt(jnp.sum(hidden * hidden, axis=1, keepdims=True) / width + eps)
        gained = grad_normed * gains_ref[at_layer : at_layer + 1, :]
        small_ref[at_layer, 5:6, :] += jnp.sum(grad_normed * hidden * root, axis=0, keepdims=True)
        along = jnp.sum(gained * hidden, axis=1, keepdims=True) * (root * root * root) / width
        change = gained * root - hidden * along
        if at_phase == 0:
            grad = rows[at, mine, :].astype(F32) + change
            running[at] = grad
            grad_low = grad.astype(BF16)
            rows[at, mine, :] = grad_low
            gather(1, AG_ACROSS, at).start()
            gather(1, AG_OWN, at).start()
            make_tile(1, at, grad_low)
        else:
            ginput[at] = (running[at] + change).astype(BF16)
            for hop in range(4):
                column_copy(at, hop).start()

    @pl.when(step == BACK_LAG)
    def _():
        load_held(0).wait()

    @pl.when(step == blocks + BACK_LAG)
    def _():
        load_held(1).start()
        load_held(1).wait()

    @pl.when((step >= BACK_LAG) & (step < blocks + BACK_LAG))
    def _():
        last_stage(0, blocks - 1 - (step - BACK_LAG))

    @pl.when(step >= blocks + BACK_LAG)
    def _():
        last_stage(1, blocks - 1 - (step - BACK_LAG - blocks))

    @pl.when(step + QUEUED < blocks)
    def _():
        send_rows(blocks - 1 - (step + QUEUED))

    @pl.when(step + AHEAD + 1 < blocks)
    def _():
        pass_rows(0, blocks - 1 - (step + AHEAD + 1))

    @pl.when(step + AHEAD < blocks)
    def _():
        prepare(blocks - 1 - (step + AHEAD))

    @pl.when((step >= blocks - PASS_AHEAD) & (step < 2 * blocks - PASS_AHEAD))
    def _():
        pass_rows(1, blocks - 1 - (step + PASS_AHEAD) % blocks)

    @pl.when(step >= 1)
    def _():
        second_stage(step - 1)

    @pl.when(step == 1)
    def _():
        final_rows.start()

    @pl.when(step == 4)
    def _():
        final_rows.wait()
        place_all(off_ref, cols, slots)
        bins.start()

    @pl.when(step == blocks - 1)
    def _():
        packs[:, :inner] = acc_out[...].astype(BF16)
        packs[:, inner:] = acc_in[...].astype(BF16)
        line.send_pairs()

    if four:
        for stage in (0, 1, 2):

            @pl.when(step == blocks + 1 + 2 * stage)
            def _(stage=stage):
                line.stage(stage)

    @pl.when(step == 2 * blocks - 1)
    def _():
        second_stage(step)
        if not four:

            @pl.loop(0, line.line - 1)
            def _(stage):
                line.stage(stage)

        line.finish()
        packs[:, :inner] = acc_out[...].astype(BF16)
        packs[:, inner:] = acc_in[...].astype(BF16)
        store_packs().start()

        @pl.loop(0, BACK_LAG)
        def _(turn):
            last_stage(1, BACK_LAG - 1 - turn)

        @pl.loop(0, blocks)
        def _(at):
            gather(0, AG_OWN, at).wait_send()
            gather(0, AG_ACROSS, at).wait_send()
            for kind in (AG_OWN, AG_ACROSS, AG_PASS):
                gather(1, kind, at).wait_send()
            pair_copy(rings[1], at, parts, from_pair).wait_send()
            across_copy(rings[1], at, parts, from_across).wait_send()
            for at_phase in range(LAYERS):
                for copy in tile_copies(at_phase, at):
                    copy.wait_send()

        @pl.loop(0, blocks)
        def _(at):
            for hop in range(4):
                column_copy(at, hop).wait()

        keep_columns = pltpu.make_async_copy(gcols_ref, gcols_out, load_sems.at[0])
        keep_columns.start()
        keep_columns.wait()
        store_packs().wait()
        bins.wait()


def whole(shape):
    return pl.BlockSpec(shape, lambda *at: (0,) * len(shape))


def exchange_scratch(blocks, width):
    return [
        pltpu.VMEM((blocks, BLK, width), BF16),
        pltpu.VMEM((blocks, BLK, width), BF16),
        pltpu.VMEM((blocks, 2 * SHARE, width), BF16),
        pltpu.VMEM((blocks, SHARE, width), BF16),
    ]


def layers_forward(offsets, given, packs, given_cot, taps, head, wide, spread):
    blocks, width = BIN // BLK, given_cot.shape[0] * packs.shape[1]
    inner, mixed = wide.shape[2], taps.shape[2]
    dp_count, members, span, columns = given_cot.shape
    total = packs.shape[2]
    steps = LAYERS * blocks
    vmem, hbm = pl.BlockSpec(memory_space=pltpu.VMEM), pl.BlockSpec(memory_space=pltpu.HBM)

    def by_block(size):
        return pl.BlockSpec((BLK, size), lambda s: (s, 0))

    return pl.pallas_call(
        forward_kernel,
        grid=(steps,),
        in_specs=[pl.BlockSpec(memory_space=pltpu.SMEM), hbm, vmem, hbm] + [vmem] * 4,
        out_specs=[
            by_block(width), by_block(inner), by_block(mixed), by_block(mixed),
            by_block(LANES), by_block(inner), by_block(inner),
            pl.BlockSpec((1, STATE, inner), lambda s: (s, 0, 0)),
            hbm, hbm, hbm, hbm, hbm, vmem, hbm, hbm,
        ],
        out_shape=[
            jax.ShapeDtypeStruct((steps * BLK, width), BF16),
            jax.ShapeDtypeStruct((steps * BLK, inner), BF16),
            jax.ShapeDtypeStruct((steps * BLK, mixed), BF16),
            jax.ShapeDtypeStruct((steps * BLK, mixed), F32),
            jax.ShapeDtypeStruct((steps * BLK, LANES), F32),
            jax.ShapeDtypeStruct((steps * BLK, inner), F32),
            jax.ShapeDtypeStruct((steps * BLK, inner), BF16),
            jax.ShapeDtypeStruct((steps, STATE, inner), F32),
            jax.ShapeDtypeStruct((blocks, SHARE, width), BF16),
            jax.ShapeDtypeStruct((blocks, SHARE, width), BF16),
            jax.ShapeDtypeStruct((steps, SHARE, width), BF16),
            jax.ShapeDtypeStruct((steps, SHARE, 1), F32),
            jax.ShapeDtypeStruct((blocks, SHARE, width), BF16),
            jax.ShapeDtypeStruct((8, width), F32),
            jax.ShapeDtypeStruct((blocks, BLK, columns), BF16),
            jax.ShapeDtypeStruct((LAYERS, width, total), BF16),
        ],
        scratch_shapes=[pltpu.VMEM((STATE, inner), F32), pltpu.VMEM((BLK + 8, mixed), F32)]
        + exchange_scratch(blocks, width)
        + [pltpu.VMEM((steps, 8, BLK), F32)] * 4
        + [
            pltpu.VMEM((LAYERS, width, total), BF16),
            pltpu.VMEM((members, dp_count * span, columns), BF16),
            pltpu.VMEM((blocks, BLK, columns), BF16),
            pltpu.VMEM((members, dp_count * span, columns), BF16),
            pltpu.VMEM((blocks, SHARE, width), F32),
            pltpu.VMEM((DEFER, BLK, inner), BF16),
            pltpu.VMEM((blocks, SHARE, width), BF16),
            pltpu.VMEM((blocks, SHARE, width), BF16),
            pltpu.VMEM((steps, SHARE, width), BF16),
            pltpu.VMEM((steps, SHARE, 1), F32),
            pltpu.VMEM((blocks, SHARE, width), BF16),
            pltpu.VMEM((blocks, BLK, columns), BF16),
            pltpu.SemaphoreType.DMA((6,)),
            pltpu.SemaphoreType.DMA((LAYERS, 7, blocks, 2)),
            pltpu.SemaphoreType.DMA((LAYERS + 1,)),
            pltpu.SemaphoreType.DMA((3 * LAYERS, 6, dp_count // 2)),
            pltpu.SemaphoreType.DMA((dp_count, 2)),
            pltpu.SemaphoreType.DMA((dp_count, 2)),
        ],
        compiler_params=pltpu.CompilerParams(
            vmem_limit_bytes=48 * 1024 * 1024, collective_id=1, has_side_effects=True
        ),
        cost_estimate=pl.CostEstimate(flops=6 * 10**10, bytes_accessed=6 * 10**7, transcendentals=10**7),
        name="layers_forward",
    )(offsets, given, packs, given_cot, taps, head, wide, spread)


def layers_backward(offsets, cot, totals, scales, before, middle, gains, taps, head, wide, spread, weights, final, saved, span):
    gate, mixed_in, conv, dt_raw, mixed_out, states, normed, gained = saved
    blocks, _, columns = cot.shape
    width = gains.shape[1]
    inner, mixed = wide.shape[2], taps.shape[2]
    total = weights.shape[2]
    steps = LAYERS * blocks
    count = lax.axis_size("dp")
    vmem, hbm = pl.BlockSpec(memory_space=pltpu.VMEM), pl.BlockSpec(memory_space=pltpu.HBM)

    def by_block(size):
        return pl.BlockSpec((BLK, size), lambda s: (steps - 1 - s, 0))

    return pl.pallas_call(
        backward_kernel,
        grid=(steps,),
        in_specs=[pl.BlockSpec(memory_space=pltpu.SMEM)]
        + [hbm] * 5
        + [vmem] * 5
        + [hbm, hbm]
        + [
            by_block(inner), by_block(mixed), by_block(mixed), by_block(LANES), by_block(inner),
            pl.BlockSpec((1, STATE, inner), lambda s: (steps - 1 - s, 0, 0)),
            by_block(width), by_block(inner),
        ],
        out_specs=[hbm, vmem, vmem, hbm, hbm],
        out_shape=[
            jax.ShapeDtypeStruct((blocks, BLK, columns), BF16),
            jax.ShapeDtypeStruct((LAYERS, 8, width), F32),
            jax.ShapeDtypeStruct((width // count, total), F32),
            jax.ShapeDtypeStruct((width, total), BF16),
            jax.ShapeDtypeStruct((count, 3, span, columns), BF16),
        ],
        scratch_shapes=[pltpu.VMEM((STATE, inner), F32), pltpu.VMEM((BLK + 8, mixed), F32)]
        + exchange_scratch(blocks, width)
        + [
            pltpu.VMEM((LAYERS, 4, blocks, 8, LANES), F32),
            pltpu.VMEM((blocks, SHARE, width), BF16),
            pltpu.VMEM((blocks, SHARE, width), F32),
            pltpu.VMEM((width, total), BF16),
            pltpu.VMEM((width, inner), F32),
            pltpu.VMEM((width, total - inner), F32),
            pltpu.VMEM((width, total), BF16),
        ]
        + [
            pltpu.VMEM((count // 2, width // count, total), BF16),
            pltpu.VMEM((count // 2 + 1, width // count, total), BF16),
            pltpu.VMEM((BIN, columns), BF16),
            pltpu.VMEM((3, count * span, columns), BF16),
            pltpu.VMEM(cot.shape, BF16),
            pltpu.VMEM(totals.shape, BF16),
            pltpu.VMEM(scales.shape, F32),
            pltpu.VMEM((blocks, SHARE, width), BF16),
            pltpu.VMEM((blocks, BLK, columns), BF16),
            pltpu.SemaphoreType.DMA((LAYERS, 8, blocks, 2)),
            pltpu.SemaphoreType.DMA((3 + LAYERS,)),
            pltpu.SemaphoreType.DMA((5, count // 2)),
            pltpu.SemaphoreType.DMA((4, 2)),
            pltpu.SemaphoreType.DMA((count, 2)),
            pltpu.SemaphoreType.DMA((3,)),
            pltpu.SemaphoreType.DMA((blocks, 4, 2)),
        ],
        compiler_params=pltpu.CompilerParams(
            vmem_limit_bytes=61 * 1024 * 1024, collective_id=2, has_side_effects=True
        ),
        cost_estimate=pl.CostEstimate(flops=6 * 10**10, bytes_accessed=6 * 10**7, transcendentals=10**7),
        name="layers_backward",
    )(
        offsets, cot, totals, scales, before, middle, gains, taps, head, wide, spread, weights, final,
        gate, mixed_in, conv, dt_raw, mixed_out, states, normed, gained,
    )


def spread_matrix(inner, heads):
    lane_head = lax.broadcasted_iota(jnp.int32, (2 * LANES, inner), 1) // (inner // heads)
    row_head = lax.broadcasted_iota(jnp.int32, (2 * LANES, inner), 0) % LANES
    return jnp.where(lane_head == row_head, 1.0, 0.0).astype(BF16)


SEQ_MIN = 512


def choose_rows(wanted, valid, begin, end):
    slots = begin + lax.broadcasted_iota(jnp.int32, (wanted.shape[0], end - begin), 1)
    return jnp.where((slots == wanted) & valid, 1.0, 0.0).astype(BF16)


def pick_all(off_ref, arrived, cols):
    first, second = off_ref[0], off_ref[1]
    length = arrived.shape[1]
    for block in range(cols.shape[0]):
        low, high = block * BLK, (block + 1) * BLK
        row = low + lax.broadcasted_iota(jnp.int32, (BLK, 1), 0)
        total = None
        for member, begin, least, most in ((1, first, SEQ_MIN, length), (2, second, BIN - length, BIN - SEQ_MIN)):
            reach = BIN - SEQ_MIN if member == 1 else BIN
            start, end = max(low - most, 0), min(high - least, length)
            if end <= 0 or start >= length or low >= reach:
                continue
            valid = (row >= first) & (row < second) if member == 1 else row >= second
            term = dot_nn(choose_rows(row - begin, valid, start, end), arrived[member, start:end, :])
            total = term if total is None else total + term
        if high <= length:
            own = arrived[0, low:high, :].astype(F32)
            own = jnp.where(row < first, own, 0.0)
            total = own if total is None else total + own
        cols[block] = total.astype(BF16)


def place_all(off_ref, cols, slots):
    first, second = off_ref[0], off_ref[1]
    length = slots.shape[1]
    for chunk in range(length // BLK):
        low, high = chunk * BLK, (chunk + 1) * BLK
        position = low + lax.broadcasted_iota(jnp.int32, (BLK, 1), 0)
        slots[0, low:high, :] = jnp.where(position < first, cols[low:high, :].astype(F32), 0.0).astype(BF16)
        for member, begin, stop, least, most, reach in (
            (1, first, second, SEQ_MIN, length, BIN - SEQ_MIN),
            (2, second, BIN, BIN - length, BIN - SEQ_MIN, BIN),
        ):
            wanted = begin + position
            start, end = least + low, min(most + high, reach)
            choose = choose_rows(wanted, wanted < stop, start, end)
            slots[member, low:high, :] = dot_nn(choose, cols[start:end, :]).astype(BF16)


class LineGather:
    def __init__(self, own, target, sems):
        self.own, self.target, self.sems = own, target, sems
        me = lax.axis_index("dp")
        self.me, self.low, self.high = me, me % 2, me // 2
        self.line = lax.axis_size("dp") // 2
        self.span = own.shape[0]

    def copy(self, kind, place, other, own):
        here = self.target.at[pl.ds((place * 2 + self.low) * self.span, self.span), :]
        arrival = 2 if kind == 2 else 3
        return pltpu.make_async_remote_copy(
            src_ref=self.own if own else here, dst_ref=here,
            send_sem=self.sems.at[kind, place], recv_sem=self.sems.at[arrival + 1, place],
            device_id={"dp": other}, device_id_type=pl.DeviceIdType.MESH,
        )

    def right(self, place, own=False):
        return self.copy(0, place, (self.high + 1) % self.line * 2 + self.low, own)

    def left(self, place, own=False):
        return self.copy(1, place, (self.high + self.line - 1) % self.line * 2 + self.low, own)

    def pair(self, place, own=False):
        return self.copy(2, place, self.high * 2 + 1 - self.low, own)

    def local(self):
        here = self.target.at[pl.ds(self.me * self.span, self.span), :]
        return pltpu.make_async_copy(self.own, here, self.sems.at[5, 0])

    def start_pair(self):
        self.local().start()
        self.pair(self.high, True).start()

    def start_line(self):
        @pl.when(self.high < self.line - 1)
        def _():
            self.right(self.high, True).start()

        @pl.when(self.high > 0)
        def _():
            self.left(self.high, True).start()

    def start(self):
        self.start_line()
        self.start_pair()

    def stage(self, step):
        @pl.when(self.high - step >= 0)
        def _():
            self.right(self.high - step).wait_recv()

            @pl.when(self.high < self.line - 1)
            def _():
                self.right(self.high - step).start()

            self.pair(self.high - step).start()

        @pl.when(self.high + step < self.line)
        def _():
            self.left(self.high + step).wait_recv()

            @pl.when(self.high > 0)
            def _():
                self.left(self.high + step).start()

            self.pair(self.high + step).start()

    def finish(self):
        self.local().wait()

        @pl.loop(0, self.line)
        def _(place):
            self.pair(place).wait_recv()
            self.pair(place).wait_send()

            @pl.when((self.high < self.line - 1) & (place <= self.high))
            def _():
                self.right(place).wait_send()

            @pl.when((self.high > 0) & (place >= self.high))
            def _():
                self.left(place).wait_send()


class Lines:
    def __init__(self, parts):
        self.parts, self.line = parts, parts[0].line

    def each(self, name, *given):
        for part in self.parts:
            getattr(part, name)(*given)

    def start(self):
        self.each("start")

    def start_pair(self):
        self.each("start_pair")

    def start_line(self):
        self.each("start_line")

    def stage(self, step):
        self.each("stage", step)

    def finish(self):
        self.each("finish")


class LineReduce:
    def __init__(self, given, out, pair_buf, arrivals, sems):
        self.given, self.out, self.pair_buf = given, out, pair_buf
        self.arrivals, self.sems = arrivals, sems
        me = lax.axis_index("dp")
        self.low, self.high = me % 2, me // 2
        self.line = lax.axis_size("dp") // 2
        self.span = out.shape[0]

    def chunk(self, place, low):
        return pl.ds((place * 2 + low) * self.span, self.span)

    def pair(self, place):
        return pltpu.make_async_remote_copy(
            src_ref=self.given.at[self.chunk(place, 1 - self.low), :], dst_ref=self.pair_buf.at[place],
            send_sem=self.sems.at[0, place], recv_sem=self.sems.at[1, place],
            device_id={"dp": self.high * 2 + 1 - self.low}, device_id_type=pl.DeviceIdType.MESH,
        )

    def onward(self, place, right):
        slot = place + 1 if right else place
        other = (self.high + (1 if right else self.line - 1)) % self.line * 2 + self.low
        return pltpu.make_async_remote_copy(
            src_ref=self.pair_buf.at[place], dst_ref=self.arrivals.at[slot],
            send_sem=self.sems.at[2, place], recv_sem=self.sems.at[3 if right else 4, place],
            device_id={"dp": other}, device_id_type=pl.DeviceIdType.MESH,
        )

    def by_distance(self, step, act):
        distance = self.line - 1 - step

        @pl.when(self.high + distance < self.line)
        def _():
            act(self.high + distance, True)

        @pl.when(self.high - distance >= 0)
        def _():
            act(self.high - distance, False)

    def send_pairs(self):
        @pl.loop(0, self.line - 1)
        def _(step):
            self.by_distance(step, lambda place, right: self.pair(place).start())

        self.pair(self.high).start()

    def fold(self, place):
        return self.given[self.chunk(place, self.low), :].astype(F32) + self.pair_buf[place].astype(F32)

    def pass_on(self, place, right):
        self.pair(place).wait_recv()
        upstream = (self.high > 0) if right else (self.high < self.line - 1)
        slot = place + 1 if right else place

        @pl.when(upstream)
        def _():
            self.onward(place, right).wait_recv()
            self.pair_buf[place] = (self.fold(place) + self.arrivals[slot].astype(F32)).astype(BF16)

        @pl.when(jnp.logical_not(upstream))
        def _():
            self.pair_buf[place] = self.fold(place).astype(BF16)

        self.onward(place, right).start()

    def stage(self, step):
        self.by_distance(step, self.pass_on)

    def finish(self):
        here = self.high
        self.pair(here).wait_recv()
        self.out[...] = self.fold(here)

        @pl.when(here > 0)
        def _():
            self.onward(here, True).wait_recv()
            self.out[...] += self.arrivals[here + 1].astype(F32)

        @pl.when(here < self.line - 1)
        def _():
            self.onward(here, False).wait_recv()
            self.out[...] += self.arrivals[here].astype(F32)

        @pl.loop(0, self.line)
        def _(place):
            self.pair(place).wait_send()

            @pl.when(place != here)
            def _():
                self.onward(place, True).wait_send()


def line_scratch(count, span, columns):
    line = count // 2
    return [
        pltpu.VMEM((line, span, columns), BF16),
        pltpu.VMEM((line + 1, span, columns), BF16),
        pltpu.SemaphoreType.DMA((5, line)),
    ]


class MemberGather:
    def __init__(self, target, sems):
        self.target, self.sems = target, sems
        self.me = lax.axis_index("tensor")

    def remote(self, step):
        return pltpu.make_async_remote_copy(
            src_ref=self.target.at[self.me], dst_ref=self.target.at[self.me],
            send_sem=self.sems.at[step, 0], recv_sem=self.sems.at[step, 1],
            device_id={"tensor": (self.me + step) % 4}, device_id_type=pl.DeviceIdType.MESH,
        )

    def start(self):
        for step in range(1, 4):
            self.remote(step).start()

    def wait(self):
        for step in range(1, 4):
            self.remote(step).wait()


def end_kernel(
    off_ref, cols_ref, packs_ref, small_ref, later_ref,
    back_ref, pack_ref, sum_ref, shared_ref, maps_ref,
    slots, pair_buf, arrivals, line_sems, smalls, shared, maps,
    bin_sems, small_sems, shared_sems, maps_sems,
):
    ring = Ring(None)
    ring.greet()
    inner = (pack_ref.shape[1] - 2 * STATE - LANES) // 3
    first_map = 3 * inner
    bins = BinExchange(False, slots, back_ref, bin_sems)
    cut = pack_ref.shape[1] // (2 * LANES) * LANES
    line = Lines(
        [
            LineReduce(
                packs_ref.at[:, part], pack_ref.at[:, part], pair_buf.at[:, :, part], arrivals.at[:, :, part], line_sems.at[at]
            )
            for at, part in enumerate((pl.ds(cut, pack_ref.shape[1] - cut), pl.ds(0, cut)))
        ]
    )
    dp_smalls = LineGather(small_ref, smalls, small_sems)
    shared_smalls = MemberGather(shared, shared_sems)
    shared_maps = [MemberGather(maps.at[at], maps_sems.at[at]) for at in range(LAYERS)]
    maps[1, ring.me] = later_ref[:, first_map : first_map + 2 * STATE].astype(BF16)
    dp_smalls.start()
    line.each("send_pairs")
    shared_maps[1].start()
    place_all(off_ref, cols_ref, slots)
    bins.start()

    @pl.loop(0, line.line - 1)
    def _(step):
        dp_smalls.stage(step + 1)
        line.stage(step)

    dp_smalls.finish()
    small_rows = sum_ref.shape[0]
    sum_ref[...] = smalls[:small_rows, :]

    @pl.loop(1, 2 * line.line)
    def _(at):
        sum_ref[...] += smalls[pl.ds(at * small_rows, small_rows), :]

    shared[ring.me] = sum_ref[...]
    shared_smalls.start()
    line.parts[0].finish()
    maps[0, ring.me] = pack_ref[:, first_map : first_map + 2 * STATE].astype(BF16)
    shared_maps[0].start()
    shared_smalls.wait()
    shared_ref[...] = (shared[0] + shared[1]) + (shared[2] + shared[3])
    line.parts[1].finish()
    for layer in range(LAYERS):
        shared_maps[layer].wait()
        maps_ref[layer] = (maps[layer, 0].astype(F32) + maps[layer, 1].astype(F32)) + (
            maps[layer, 2].astype(F32) + maps[layer, 3].astype(F32)
        )
    bins.wait()


def end_exchange(offsets, grad_columns, packs, small, later_pack, span):
    count = lax.axis_size("dp")
    width, total = packs.shape
    columns = width // 4
    vmem = pl.BlockSpec(memory_space=pltpu.VMEM)
    pack_rows = width // count
    return pl.pallas_call(
        end_kernel,
        in_specs=[pl.BlockSpec(memory_space=pltpu.SMEM)] + [vmem] * 4,
        out_specs=[pl.BlockSpec(memory_space=pltpu.HBM), vmem, vmem, vmem, vmem],
        out_shape=[
            jax.ShapeDtypeStruct((count, 3, span, columns), BF16),
            jax.ShapeDtypeStruct((pack_rows, total), F32),
            jax.ShapeDtypeStruct(small.shape, F32),
            jax.ShapeDtypeStruct(small.shape, F32),
            jax.ShapeDtypeStruct((LAYERS, pack_rows, 2 * STATE), F32),
        ],
        scratch_shapes=[pltpu.VMEM((3, count * span, columns), BF16)]
        + line_scratch(count, pack_rows, total)[:2]
        + [
            pltpu.SemaphoreType.DMA((2, 5, count // 2)),
            pltpu.VMEM((count * small.shape[0], width), F32),
            pltpu.VMEM((4,) + small.shape, F32),
            pltpu.VMEM((LAYERS, 4, pack_rows, 2 * STATE), BF16),
            pltpu.SemaphoreType.DMA((count, 2)),
            pltpu.SemaphoreType.DMA((6, count // 2)),
            pltpu.SemaphoreType.DMA((4, 2)),
            pltpu.SemaphoreType.DMA((LAYERS, 4, 2)),
        ],
        compiler_params=pltpu.CompilerParams(
            vmem_limit_bytes=56 * 1024 * 1024, collective_id=3, has_side_effects=True
        ),
        cost_estimate=pl.CostEstimate(flops=6 * 10**10, bytes_accessed=6 * 10**7, transcendentals=0),
        name="end_exchange",
    )(offsets, grad_columns.reshape(BIN, columns), packs, small, later_pack)


def pad_to(values, rows, columns):
    return jnp.pad(values, ((0, rows - values.shape[0]), (0, columns - values.shape[1])))


def on_device(
    tokens, cotangent, lengths, packing, pre_gain, w_z, w_x, w_bc, w_dt, conv_x, conv_bc, head_params, norm_gain, w_out,
):
    dp_count = lax.axis_size("dp")
    bin_index = lax.axis_index("dp")
    seq_total, pos_here, cols_here = tokens.shape
    inner_part = conv_x.shape[2]
    heads_here = head_params.shape[2]
    dp_rows = w_z.shape[1]
    mixed = inner_part + 2 * STATE
    triples = lengths[packing].reshape(dp_count, 3)
    offsets = jnp.cumsum(triples, axis=1) - triples
    my_offsets = offsets[bin_index]
    bounds = my_offsets[1:3]
    by_bin = (dp_count, 3, pos_here, cols_here)
    given_tokens, given_cot = (array[packing].reshape(by_bin) for array in (tokens, cotangent))

    spread = spread_matrix(inner_part, heads_here)
    last_columns = [jnp.concatenate([w_dt[0], pre_gain.T], axis=1), w_dt[1]]
    packs = []
    for layer in range(LAYERS):
        own = jnp.concatenate(
            [w_out[layer].T, w_z[layer], w_x[layer], w_bc[layer], pad_to(last_columns[layer], dp_rows, LANES)], axis=1
        )
        taps = jnp.concatenate([conv_x[layer], conv_bc[layer]], axis=1).astype(F32)
        head = jnp.stack([head_params[layer, 0], -jnp.exp(head_params[layer, 1])])
        wide = jnp.stack(
            [jnp.repeat(head_params[layer, 2], inner_part // heads_here), norm_gain[layer].astype(F32)]
        )
        packs.append((own, pad_to(taps, 8, mixed), pad_to(head, 8, LANES), pad_to(wide, 8, inner_part)))

    taps_all, head_all, wide_all = (jnp.stack([pack[at] for pack in packs]) for at in (1, 2, 3))
    (
        rows_all, gate, mixed_in, conv, dt_raw, mixed_out, gained_all, states, first_before, middle, totals, scales,
        final_rows, gains, cot_columns, all_weights,
    ) = layers_forward(
        bounds, given_tokens, jnp.stack([pack[0] for pack in packs]), given_cot,
        taps_all, head_all, wide_all, spread,
    )
    grad_columns, small, later_pack, first_packs, activations_back = layers_backward(
        bounds, cot_columns, totals, scales, first_before, middle, gains, taps_all, head_all, wide_all, spread,
        all_weights, final_rows, (gate, mixed_in, conv, dt_raw, mixed_out, states, rows_all, gained_all), pos_here,
    )
    returned, first_pack, sums, shared, maps = end_exchange(
        bounds, grad_columns, first_packs, small.reshape(LAYERS * 8, -1), later_pack, pos_here
    )
    sums, shared = sums.reshape(small.shape), shared.reshape(small.shape)
    grad_convx = sums[:, : CONV + 1, :inner_part]
    grad_convbc = shared[:, : CONV + 1, inner_part:mixed]
    shard_pre = lax.dynamic_slice_in_dim(shared[:, 5], bin_index * dp_rows, dp_rows, 1)
    skips = jnp.sum(sums[:, 6, :inner_part].reshape(LAYERS, heads_here, -1), axis=2)
    grad_head = jnp.stack([sums[:, 7, :heads_here], sums[:, 7, LANES : LANES + heads_here], skips], axis=1)
    grad_norm = sums[:, 6, inner_part : 2 * inner_part]
    own_weights = jnp.stack([first_pack, later_pack])
    grad_bc = maps
    grad_out = jnp.swapaxes(own_weights[:, :, :inner_part], 1, 2)
    grad_z = own_weights[:, :, inner_part : 2 * inner_part]
    grad_x = own_weights[:, :, 2 * inner_part : 3 * inner_part]
    grad_dt = own_weights[:, :, 3 * inner_part + 2 * STATE : 3 * inner_part + 2 * STATE + heads_here]

    rank_of = jnp.zeros_like(packing).at[packing].set(jnp.arange(seq_total, dtype=jnp.int32))

    def in_order(returned):
        return returned.reshape(seq_total, pos_here, cols_here)[rank_of]

    activations = in_order(activations_back)
    input_grad = in_order(returned)
    return (
        activations, input_grad, shard_pre, grad_z, grad_x, grad_bc, grad_dt,
        grad_convx, grad_convbc, grad_head, grad_norm, grad_out,
    )


def solution(mesh):
    placed = (
        P(None, "dp", "tensor"), P(None, "dp", "tensor"), P(), P(), P(None, "dp"),
        P(None, "dp", "tensor"), P(None, "dp", "tensor"), P(None, "dp", None), P(None, "dp", "tensor"),
        P(None, None, "tensor"), P(), P(None, None, "tensor"), P(None, "tensor"), P(None, "tensor", "dp"),
    )
    results = (
        P(None, "dp", "tensor"), P(None, "dp", "tensor"), P(None, "dp"),
        P(None, "dp", "tensor"), P(None, "dp", "tensor"), P(None, "dp", None), P(None, "dp", "tensor"),
        P(None, None, "tensor"), P(), P(None, None, "tensor"), P(None, "tensor"), P(None, "tensor", "dp"),
    )
    return jax.shard_map(on_device, mesh=mesh, in_specs=placed, out_specs=results, check_vma=False)
```
